32 devices in a mesh: clip: 4 (over z), ha: 4 (over y, x), wa: 2 (over core).
Axes of the slice: x: 2, y: 2, z: 4, core: 2. Of those that a mesh axis runs over, the one named last changes fastest.
Arguments:
- slow_in: float32 [4, 8, 16, 16, 1024], P('clip', None, 'ha', 'wa'), may hold values from -6 to 6
- fast_in: float32 [4, 32, 16, 16, 128], P('clip', None, 'ha', 'wa'), may hold values from -6 to 6
- valid_frames: int32 [4], replicated, may hold values from 1 to 8, as said below
- lateral_w: bfloat16 [2, 5, 128, 256], replicated, may hold values from -0.25 to 0.25
- slow_temporal_w: bfloat16 [2, 3, 1280, 256], replicated, may hold values from -0.09375 to 0.09375
- slow_spatial_w: bfloat16 [2, 3, 3, 256, 256], replicated, may hold values from -0.125 to 0.125
- slow_expand_w: bfloat16 [2, 256, 1024], replicated, may hold values from -0.375 to 0.375
- slow_skip_w: bfloat16 [2, 1280, 1024], replicated, may hold values from -0.15625 to 0.15625
- fast_temporal_w: bfloat16 [2, 3, 128, 32], replicated, may hold values from -0.3125 to 0.3125
- fast_spatial_w: bfloat16 [2, 3, 3, 32, 32], replicated, may hold values from -0.375 to 0.375
- fast_expand_w: bfloat16 [2, 32, 128], replicated, may hold values from -1 to 1
- fast_skip_w: bfloat16 [2, 128, 128], replicated, may hold values from -0.5 to 0.5
- gains: float32 [2, 3136], replicated, may hold values from 0.25 to 1.75
- biases: float32 [2, 3136], replicated, may hold values from -1.5 to 1.5
- slow_cot: float32 [4, 8, 16, 16, 1024], P('clip', None, 'ha', 'wa'), may hold values from -6 to 6
- fast_cot: float32 [4, 32, 16, 16, 128], P('clip', None, 'ha', 'wa'), may hold values from -6 to 6
Outputs:
- out_slow: float32 [4, 8, 16, 16, 1024], P('clip', None, 'ha', 'wa')
- out_fast: float32 [4, 32, 16, 16, 128], P('clip', None, 'ha', 'wa')
- grad_slow_in: float32 [4, 8, 16, 16, 1024], P('clip', None, 'ha', 'wa')
- grad_fast_in: float32 [4, 32, 16, 16, 128], P('clip', None, 'ha', 'wa')
- grad_lateral_w: float32 [2, 5, 128, 256], P(None, None, ('ha', 'wa'), 'clip')
- grad_slow_temporal_w: float32 [2, 3, 1280, 256], P(None, None, ('ha', 'wa'), 'clip')
- grad_slow_spatial_w: float32 [2, 3, 3, 256, 256], P(None, None, None, ('ha', 'wa'), 'clip')
- grad_slow_expand_w: float32 [2, 256, 1024], P(None, ('ha', 'wa'), 'clip')
- grad_slow_skip_w: float32 [2, 1280, 1024], P(None, ('ha', 'wa'), 'clip')
- grad_fast_temporal_w: float32 [2, 3, 128, 32], P(None, None, ('ha', 'wa'), 'clip')
- grad_fast_spatial_w: float32 [2, 3, 3, 32, 32], P(None, None, None, ('ha', 'wa'), 'clip')
- grad_fast_expand_w: float32 [2, 32, 128], P(None, ('ha', 'wa'), 'clip')
- grad_fast_skip_w: float32 [2, 128, 128], P(None, ('ha', 'wa'), 'clip')
- grad_gains: float32 [2, 3136], replicated
- grad_biases: float32 [2, 3136], replicated
The draws below stay inside these ranges and needn't reach their ends.
Inputs may be any that keep to these rules, and one draw needn't show every extreme that they name: valid_frames[c] sets the masks and counts of the steps for clip c; the last clip has all 8.
All inputs are finite; a program needn't handle non-finite values.
Results may differ from the reference program's by a relative error of at most 0.024.
Values may be sent and summed in bfloat16 or wider, within the bound.
No kernel may reach another device: no remote copies, remote signals or barrier semaphores. Data moves between devices by JAX's collectives and lax.ppermute only.
A program may use at most 256 MiB of HBM per device.

```python
import jax
import jax.numpy as jnp
from jax import lax

DS = 1024
DL = 256
BS = 256
DF = 128
BF = 32
ST = 8
ALPHA = 4
HT = 16
WD = 16
LAYERS = 2
CLIPS = 4
FT = 32
NORMS = 3136


def draw_valid_frames(key, part):
    key = jax.random.fold_in(key, 11)
    places = jnp.arange(CLIPS)
    baseline = 2 + places * (ST - 2) // max(CLIPS - 1, 1)
    jitter = jax.random.randint(key, (CLIPS,), -1, 2)
    drawn = jnp.clip(baseline + jitter, 1, ST)
    return jnp.where(places == CLIPS - 1, ST, drawn).astype(jnp.int32)


def levels(stream_key, shape, cuts, smallest, largest):
    level = 1.0
    for dim, parts in cuts:
        heights = jax.random.uniform(jax.random.fold_in(jax.random.fold_in(stream_key, 6), dim), (parts,), jnp.float32, smallest / len(cuts), largest / len(cuts))
        level = level * jnp.repeat(jnp.exp(heights), shape[dim] // parts).reshape((-1,) + (1,) * (len(shape) - 1 - dim))
    return level


def gaussian(key, shape, deviation, limit, shards=(), kind=jnp.bfloat16):
    values = deviation * jax.random.normal(key, shape, jnp.float32)
    if shards:
        values = values * levels(key, shape, shards, -0.22, 0.18)
    return jnp.clip(values, -limit, limit).astype(kind)


def setup_inputs(seed: int = 0) -> dict:
    seeds = jax.random.split(jax.random.key(seed), 17)
    slow_in = gaussian(seeds[0], (CLIPS, ST, HT, WD, DS), 1.0, 6.0, ((0, 4), (2, 4), (3, 2)), jnp.float32)
    fast_in = gaussian(seeds[1], (CLIPS, FT, HT, WD, DF), 1.0, 6.0, ((0, 4), (2, 4), (3, 2)), jnp.float32)
    valid_frames = draw_valid_frames(jax.random.fold_in(seeds[16], 71), 0)
    lateral_w = gaussian(seeds[3], (LAYERS, 5, DF, DL), (5 * DF) ** -0.5, 0.25)
    slow_temporal_w = gaussian(seeds[4], (LAYERS, 3, DS + DL, BS), (3 * (DS + DL)) ** -0.5, 0.09375)
    slow_spatial_w = gaussian(seeds[5], (LAYERS, 3, 3, BS, BS), (9 * BS) ** -0.5, 0.125)
    slow_expand_w = gaussian(seeds[6], (LAYERS, BS, DS), BS ** -0.5, 0.375)
    slow_skip_w = gaussian(seeds[7], (LAYERS, DS + DL, DS), (DS + DL) ** -0.5, 0.15625)
    fast_temporal_w = gaussian(seeds[8], (LAYERS, 3, DF, BF), (3 * DF) ** -0.5, 0.3125)
    fast_spatial_w = gaussian(seeds[9], (LAYERS, 3, 3, BF, BF), (9 * BF) ** -0.5, 0.375)
    fast_expand_w = gaussian(seeds[10], (LAYERS, BF, DF), BF ** -0.5, 1.0)
    fast_skip_w = gaussian(seeds[11], (LAYERS, DF, DF), DF ** -0.5, 0.5)
    gains = jnp.clip(1.0 + 0.15 * jax.random.normal(seeds[12], (LAYERS, NORMS), jnp.float32), 0.25, 1.75)
    biases = gaussian(seeds[13], (LAYERS, NORMS), 0.3, 1.5, (), jnp.float32)
    slow_cot = gaussian(seeds[14], (CLIPS, ST, HT, WD, DS), 1.0, 6.0, ((0, 4), (2, 4), (3, 2)), jnp.float32)
    fast_cot = gaussian(seeds[15], (CLIPS, FT, HT, WD, DF), 1.0, 6.0, ((0, 4), (2, 4), (3, 2)), jnp.float32)
    return dict(slow_in=slow_in, fast_in=fast_in, valid_frames=valid_frames, lateral_w=lateral_w, slow_temporal_w=slow_temporal_w, slow_spatial_w=slow_spatial_w, slow_expand_w=slow_expand_w, slow_skip_w=slow_skip_w, fast_temporal_w=fast_temporal_w, fast_spatial_w=fast_spatial_w, fast_expand_w=fast_expand_w, fast_skip_w=fast_skip_w, gains=gains, biases=biases, slow_cot=slow_cot, fast_cot=fast_cot)


@jax.custom_vjp
def low(v):
    return lax.optimization_barrier(v.astype(jnp.bfloat16)).astype(jnp.float32)

@jax.custom_vjp
def low_back(v):
    return v

def low_keep(v):
    return (low(v), None)

def low_pass(kept, grad):
    return (grad,)

def back_keep(v):
    return (v, None)

def back_low(kept, grad):
    return (low(grad),)
low.defvjp(low_keep, low_pass)
low_back.defvjp(back_keep, back_low)
EPSILON = 1e-05

def swish_unit(values):
    return values * jax.nn.sigmoid(values)

def matmul_high(inputs, weight):
    return jnp.einsum('...k,kn->...n', inputs, weight, precision=lax.Precision.HIGHEST)

def split_norms(vector):
    pieces = []
    offset = 0
    for column_count in [DL, BS, BS, DS, DS, BF, BF, DF, DF]:
        pieces.append(vector[offset:offset + column_count])
        offset += column_count
    return pieces

def time_taps(values):
    frames = values.shape[1]
    padded = jnp.pad(values, ((0, 0), (1, 1), (0, 0), (0, 0), (0, 0)))
    return jnp.concatenate([padded[:, 0:frames], padded[:, 1:frames + 1], padded[:, 2:frames + 2]], axis=-1)

def lateral_taps(values):
    frames = values.shape[1] // ALPHA
    padded = jnp.pad(values, ((0, 0), (2, 2), (0, 0), (0, 0), (0, 0)))
    return jnp.concatenate([padded[:, k:k + ALPHA * frames:ALPHA] for k in range(5)], axis=-1)

def pixel_taps(values):
    height = values.shape[2]
    breadth = values.shape[3]
    padded = jnp.pad(values, ((0, 0), (0, 0), (1, 1), (1, 1), (0, 0)))
    return jnp.concatenate([padded[:, :, a:a + height, b:b + breadth] for a in range(3) for b in range(3)], axis=-1)

def batch_norm(values, mask_vals, count_all, gain_part, bias_part):
    centre = lax.optimization_barrier(jnp.sum(values * mask_vals, axis=(0, 1, 2, 3))) / count_all
    square = lax.optimization_barrier(jnp.sum(values * values * mask_vals, axis=(0, 1, 2, 3))) / count_all
    inv_std = lax.rsqrt(square - centre * centre + EPSILON)
    return gain_part * (values - centre) * inv_std + bias_part

def block(slow_act, fast_act, weights, gain_parts, bias_parts, mask_slow, mask_fast, count_slow, count_fast):
    lateral_w, slow_temporal_w, slow_spatial_w, slow_expand_w, slow_skip_w, fast_temporal_w, fast_spatial_w, fast_expand_w, fast_skip_w = weights
    fast_low = low(fast_act)
    lateral_pre = low_back(matmul_high(lateral_taps(fast_low), lateral_w.reshape(-1, DL)))
    lateral_act = swish_unit(batch_norm(lateral_pre, mask_slow, count_slow, gain_parts[0], bias_parts[0]))
    cat_low = low(jnp.concatenate([slow_act, lateral_act], axis=-1))
    slow_temporal_pre = low_back(matmul_high(time_taps(cat_low), slow_temporal_w.reshape(-1, BS)))
    slow_mid = low(swish_unit(batch_norm(slow_temporal_pre, mask_slow, count_slow, gain_parts[1], bias_parts[1])))
    slow_spatial_pre = low_back(matmul_high(pixel_taps(slow_mid), slow_spatial_w.reshape(-1, BS)))
    slow_top = low(swish_unit(batch_norm(slow_spatial_pre, mask_slow, count_slow, gain_parts[2], bias_parts[2])))
    slow_expand = batch_norm(low_back(matmul_high(slow_top, slow_expand_w)), mask_slow, count_slow, gain_parts[3], bias_parts[3])
    slow_skip = batch_norm(low_back(matmul_high(cat_low, slow_skip_w)), mask_slow, count_slow, gain_parts[4], bias_parts[4])
    slow_next = mask_slow * swish_unit(slow_expand + slow_skip)
    fast_temporal_pre = low_back(matmul_high(time_taps(fast_low), fast_temporal_w.reshape(-1, BF)))
    fast_mid = low(swish_unit(batch_norm(fast_temporal_pre, mask_fast, count_fast, gain_parts[5], bias_parts[5])))
    fast_spatial_pre = low_back(matmul_high(pixel_taps(fast_mid), fast_spatial_w.reshape(-1, BF)))
    fast_top = low(swish_unit(batch_norm(fast_spatial_pre, mask_fast, count_fast, gain_parts[6], bias_parts[6])))
    fast_expand = batch_norm(low_back(matmul_high(fast_top, fast_expand_w)), mask_fast, count_fast, gain_parts[7], bias_parts[7])
    fast_skip = batch_norm(low_back(matmul_high(fast_low, fast_skip_w)), mask_fast, count_fast, gain_parts[8], bias_parts[8])
    fast_next = mask_fast * swish_unit(fast_expand + fast_skip)
    return (slow_next, fast_next)

def reference(slow_in, fast_in, valid_frames, lateral_w, slow_temporal_w, slow_spatial_w, slow_expand_w, slow_skip_w, fast_temporal_w, fast_spatial_w, fast_expand_w, fast_skip_w, gains, biases, slow_cot, fast_cot):
    frame_slow = jnp.arange(ST).astype(jnp.int32)
    frame_fast = jnp.arange(ST * ALPHA).astype(jnp.int32)
    mask_slow = (frame_slow[None, :] < valid_frames[:, None]).astype(jnp.float32)[:, :, None, None, None]
    mask_fast = (frame_fast[None, :] < ALPHA * valid_frames[:, None]).astype(jnp.float32)[:, :, None, None, None]
    count_slow = jnp.sum(valid_frames).astype(jnp.float32) * (HT * WD)
    count_fast = count_slow * ALPHA
    all_weights = (lateral_w.astype(jnp.float32), slow_temporal_w.astype(jnp.float32), slow_spatial_w.astype(jnp.float32), slow_expand_w.astype(jnp.float32), slow_skip_w.astype(jnp.float32), fast_temporal_w.astype(jnp.float32), fast_spatial_w.astype(jnp.float32), fast_expand_w.astype(jnp.float32), fast_skip_w.astype(jnp.float32))

    def forward(slow_act, fast_act, weight_set, gain_set, bias_set):
        for layer_index in range(LAYERS):
            slow_act, fast_act = block(slow_act, fast_act, [w[layer_index] for w in weight_set], split_norms(gain_set[layer_index]), split_norms(bias_set[layer_index]), mask_slow, mask_fast, count_slow, count_fast)
        return (slow_act, fast_act)
    outputs, pullback = jax.vjp(forward, slow_in, fast_in, all_weights, gains, biases)
    grad_slow, grad_fast, grad_weights, grad_gains, grad_biases = pullback((slow_cot, fast_cot))
    return (outputs[0], outputs[1], grad_slow, grad_fast, grad_weights[0], grad_weights[1], grad_weights[2], grad_weights[3], grad_weights[4], grad_weights[5], grad_weights[6], grad_weights[7], grad_weights[8], grad_gains, grad_biases)
```

```python
import jax
import jax.numpy as jnp
from jax import lax
from jax.sharding import PartitionSpec as P

DS = 1024
DL = 256
BS = 256
DF = 128
BF = 32
ST = 8
ALPHA = 4
HT = 16
WD = 16
LAYERS = 2


EPSILON = 1e-05


def with_halo(shard, sides, width):
    for axis, dim in sides:
        count, length = (lax.axis_size(axis), shard.shape[dim])
        up = [(i, (i + 1) % count) for i in range(count - 1)]
        down = [(j, i) for i, j in up]
        last = lax.slice_in_dim(shard, length - width, length, axis=dim)
        leading = lax.slice_in_dim(shard, 0, width, axis=dim)
        before = lax.ppermute(last, axis, up)
        after = lax.ppermute(leading, axis, down)
        shard = jnp.concatenate([before, shard, after], axis=dim)
    return shard


def for_sending(shard):

    def short(part):
        return part.astype(jnp.bfloat16) if part.dtype == jnp.float32 else part

    return jax.tree.map(short, shard)


def swish_unit(values):
    return values * jax.nn.sigmoid(values)


def swish_slope(values):
    sigma = jax.nn.sigmoid(values)
    return sigma * (1.0 + values * (1.0 - sigma))


def split_norms(vector):
    pieces = []
    offset = 0
    for column_count in [DL, BS, BS, DS, DS, BF, BF, DF, DF]:
        pieces.append(vector[offset : offset + column_count])
        offset += column_count
    return pieces


def apply_weight(inputs, weight):
    return jnp.einsum("...k,kn->...n", inputs, weight, preferred_element_type=jnp.float32)


def apply_back(gradient, weight):
    return jnp.einsum("...n,kn->...k", gradient, weight, preferred_element_type=jnp.float32)


def weight_grad(inputs, gradient):
    rows_in = inputs.reshape(-1, inputs.shape[-1])
    rows_out = gradient.reshape(-1, gradient.shape[-1])
    return jnp.einsum("rk,rn->kn", rows_in, rows_out, preferred_element_type=jnp.float32)


def time_taps(values):
    frames = values.shape[1]
    padded = jnp.pad(values, ((0, 0), (1, 1), (0, 0), (0, 0), (0, 0)))
    return jnp.concatenate(
        [padded[:, 0:frames], padded[:, 1 : frames + 1], padded[:, 2 : frames + 2]], axis=-1
    )


def time_untaps(gradient, column_count):
    before = gradient[..., :column_count]
    centre = gradient[..., column_count : 2 * column_count]
    later_tap = gradient[..., 2 * column_count :]
    zero_frame = jnp.zeros_like(centre[:, :1])
    return (
        centre
        + jnp.concatenate([before[:, 1:], zero_frame], axis=1)
        + jnp.concatenate([zero_frame, later_tap[:, :-1]], axis=1)
    )


def lateral_taps(values):
    frames = values.shape[1] // ALPHA
    padded = jnp.pad(values, ((0, 0), (2, 2), (0, 0), (0, 0), (0, 0)))
    return jnp.concatenate([padded[:, k : k + ALPHA * frames : ALPHA] for k in range(5)], axis=-1)


def lateral_untaps(gradient, column_count):
    frames = gradient.shape[1]
    target = jnp.zeros(
        (gradient.shape[0], ALPHA * frames + 4, gradient.shape[2], gradient.shape[3], column_count),
        jnp.float32,
    )
    for k in range(5):
        target = target.at[:, k : k + ALPHA * frames : ALPHA].add(
            gradient[..., k * column_count : (k + 1) * column_count]
        )
    return target[:, 2 : 2 + ALPHA * frames]


def pixel_taps(padded):
    height = padded.shape[2] - 2
    breadth = padded.shape[3] - 2
    return jnp.concatenate(
        [padded[:, :, a : a + height, b : b + breadth] for a in range(3) for b in range(3)], axis=-1
    )


def pixel_back(padded, weight):
    height = padded.shape[2] - 2
    breadth = padded.shape[3] - 2
    stacked = jnp.concatenate(
        [
            padded[:, :, 2 - a : 2 - a + height, 2 - b : 2 - b + breadth]
            for a in range(3)
            for b in range(3)
        ],
        axis=-1,
    )
    turned = jnp.transpose(weight, (0, 1, 3, 2)).reshape(-1, weight.shape[2])
    return apply_weight(stacked, turned)


def pixel_rim(values):
    return with_halo(values, (("ha", 2), ("wa", 3)), 1)


def grad_rim(values):
    return with_halo(values, (("ha", 2), ("wa", 3)), 1)


def local_moments(values, mask_vals):
    masked = values * mask_vals
    return jnp.stack(
        [jnp.sum(masked, axis=(0, 1, 2, 3)), jnp.sum(masked * values, axis=(0, 1, 2, 3))]
    )


def local_back(gradient, normed):
    return jnp.stack(
        [jnp.sum(gradient, axis=(0, 1, 2, 3)), jnp.sum(gradient * normed, axis=(0, 1, 2, 3))]
    )


ALL_AXES = ("clip", "ha", "wa")


def moment_totals(term_list):
    flat = jnp.concatenate([one_term.reshape(-1) for one_term in term_list])
    length = flat.shape[0]
    padded = -(-length // 1024) * 1024
    rows = jnp.pad(flat, (0, padded - length)).reshape(8, padded // 8)
    count = lax.axis_size(ALL_AXES)
    sent = jnp.broadcast_to(rows[None], (count,) + rows.shape)
    total = jnp.sum(lax.all_to_all(sent, ALL_AXES, 0, 0), axis=0).reshape(-1)
    results = []
    offset = 0
    for one_term in term_list:
        results.append(total[offset : offset + one_term.size].reshape(one_term.shape))
        offset += one_term.size
    return results


grad_totals = moment_totals


def normalize(values, totals, count_all, gain_part, bias_part):
    centre = totals[0] / count_all
    inv_std = lax.rsqrt(totals[1] / count_all - centre * centre + EPSILON)
    normed = (values - centre) * inv_std
    return (gain_part * normed + bias_part, normed, inv_std)


def norm_back(gradient, normed, inv_std, gain_part, mask_vals, count_all, totals):
    return (
        gain_part * inv_std * (gradient - mask_vals * (totals[0] + normed * totals[1]) / count_all)
    ).astype(jnp.bfloat16)


def block_forward(
    slow_act,
    fast_act,
    weights,
    gain_parts,
    bias_parts,
    mask_slow,
    mask_fast,
    count_slow,
    count_fast,
):
    (
        lateral_w,
        slow_temporal_w,
        slow_spatial_w,
        slow_expand_w,
        slow_skip_w,
        fast_temporal_w,
        fast_spatial_w,
        fast_expand_w,
        fast_skip_w,
    ) = weights
    fast_low = fast_act.astype(jnp.bfloat16)
    lateral_pre = apply_weight(lateral_taps(fast_low), lateral_w.reshape(-1, DL))
    fast_temporal_pre = apply_weight(time_taps(fast_low), fast_temporal_w.reshape(-1, BF))
    fast_skip_pre = apply_weight(fast_low, fast_skip_w)
    totals_one = moment_totals(
        [
            local_moments(lateral_pre, mask_slow),
            local_moments(fast_temporal_pre, mask_fast),
            local_moments(fast_skip_pre, mask_fast),
        ]
    )
    lateral_out = normalize(lateral_pre, totals_one[0], count_slow, gain_parts[0], bias_parts[0])
    fast_temporal_out = normalize(
        fast_temporal_pre, totals_one[1], count_fast, gain_parts[5], bias_parts[5]
    )
    fast_skip_out = normalize(
        fast_skip_pre, totals_one[2], count_fast, gain_parts[8], bias_parts[8]
    )
    cat_low = jnp.concatenate(
        [slow_act.astype(jnp.bfloat16), swish_unit(lateral_out[0]).astype(jnp.bfloat16)], axis=-1
    )
    slow_temporal_pre = apply_weight(time_taps(cat_low), slow_temporal_w.reshape(-1, BS))
    slow_skip_pre = apply_weight(cat_low, slow_skip_w)
    fast_mid_pad = pixel_rim(swish_unit(fast_temporal_out[0]).astype(jnp.bfloat16))
    fast_spatial_pre = apply_weight(pixel_taps(fast_mid_pad), fast_spatial_w.reshape(-1, BF))
    totals_two = moment_totals(
        [
            local_moments(slow_temporal_pre, mask_slow),
            local_moments(slow_skip_pre, mask_slow),
            local_moments(fast_spatial_pre, mask_fast),
        ]
    )
    slow_temporal_out = normalize(
        slow_temporal_pre, totals_two[0], count_slow, gain_parts[1], bias_parts[1]
    )
    slow_skip_out = normalize(
        slow_skip_pre, totals_two[1], count_slow, gain_parts[4], bias_parts[4]
    )
    fast_spatial_out = normalize(
        fast_spatial_pre, totals_two[2], count_fast, gain_parts[6], bias_parts[6]
    )
    slow_mid_pad = pixel_rim(swish_unit(slow_temporal_out[0]).astype(jnp.bfloat16))
    slow_spatial_pre = apply_weight(pixel_taps(slow_mid_pad), slow_spatial_w.reshape(-1, BS))
    fast_top_low = swish_unit(fast_spatial_out[0]).astype(jnp.bfloat16)
    fast_expand_pre = apply_weight(fast_top_low, fast_expand_w)
    totals_three = moment_totals(
        [local_moments(slow_spatial_pre, mask_slow), local_moments(fast_expand_pre, mask_fast)]
    )
    slow_spatial_out = normalize(
        slow_spatial_pre, totals_three[0], count_slow, gain_parts[2], bias_parts[2]
    )
    fast_expand_out = normalize(
        fast_expand_pre, totals_three[1], count_fast, gain_parts[7], bias_parts[7]
    )
    slow_top_low = swish_unit(slow_spatial_out[0]).astype(jnp.bfloat16)
    slow_expand_pre = apply_weight(slow_top_low, slow_expand_w)
    totals_four = moment_totals([local_moments(slow_expand_pre, mask_slow)])
    slow_expand_out = normalize(
        slow_expand_pre, totals_four[0], count_slow, gain_parts[3], bias_parts[3]
    )
    slow_sum = slow_expand_out[0] + slow_skip_out[0]
    fast_sum = fast_expand_out[0] + fast_skip_out[0]
    stored = {
        "fast_low": fast_low,
        "cat_low": cat_low,
        "lateral": lateral_out,
        "slow_temporal": slow_temporal_out,
        "slow_spatial": slow_spatial_out,
        "slow_expand": slow_expand_out,
        "slow_skip": slow_skip_out,
        "fast_temporal": fast_temporal_out,
        "fast_spatial": fast_spatial_out,
        "fast_expand": fast_expand_out,
        "fast_skip": fast_skip_out,
        "slow_mid_pad": slow_mid_pad,
        "fast_mid_pad": fast_mid_pad,
        "slow_top_low": slow_top_low,
        "fast_top_low": fast_top_low,
        "slow_sum": slow_sum,
        "fast_sum": fast_sum,
    }
    return (mask_slow * swish_unit(slow_sum), mask_fast * swish_unit(fast_sum), stored)


def block_backward(
    grad_slow, grad_fast, stored, weights, gain_parts, mask_slow, mask_fast, count_slow, count_fast
):
    (
        lateral_w,
        slow_temporal_w,
        slow_spatial_w,
        slow_expand_w,
        slow_skip_w,
        fast_temporal_w,
        fast_spatial_w,
        fast_expand_w,
        fast_skip_w,
    ) = weights
    fast_low = stored["fast_low"]
    cat_low = stored["cat_low"]
    lateral_out = stored["lateral"]
    slow_temporal_out = stored["slow_temporal"]
    slow_spatial_out = stored["slow_spatial"]
    slow_expand_out = stored["slow_expand"]
    slow_skip_out = stored["slow_skip"]
    fast_temporal_out = stored["fast_temporal"]
    fast_spatial_out = stored["fast_spatial"]
    fast_expand_out = stored["fast_expand"]
    fast_skip_out = stored["fast_skip"]
    slow_final = grad_slow * mask_slow * swish_slope(stored["slow_sum"])
    fast_final = grad_fast * mask_fast * swish_slope(stored["fast_sum"])
    totals_one = grad_totals(
        [
            local_back(slow_final, slow_expand_out[1]),
            local_back(slow_final, slow_skip_out[1]),
            local_back(fast_final, fast_expand_out[1]),
            local_back(fast_final, fast_skip_out[1]),
        ]
    )
    slow_expand_grad = norm_back(
        slow_final,
        slow_expand_out[1],
        slow_expand_out[2],
        gain_parts[3],
        mask_slow,
        count_slow,
        totals_one[0],
    )
    slow_skip_grad = norm_back(
        slow_final,
        slow_skip_out[1],
        slow_skip_out[2],
        gain_parts[4],
        mask_slow,
        count_slow,
        totals_one[1],
    )
    fast_expand_grad = norm_back(
        fast_final,
        fast_expand_out[1],
        fast_expand_out[2],
        gain_parts[7],
        mask_fast,
        count_fast,
        totals_one[2],
    )
    fast_skip_grad = norm_back(
        fast_final,
        fast_skip_out[1],
        fast_skip_out[2],
        gain_parts[8],
        mask_fast,
        count_fast,
        totals_one[3],
    )
    slow_expand_wg = weight_grad(stored["slow_top_low"], slow_expand_grad)
    slow_skip_wg = weight_grad(cat_low, slow_skip_grad)
    fast_expand_wg = weight_grad(stored["fast_top_low"], fast_expand_grad)
    fast_skip_wg = weight_grad(fast_low, fast_skip_grad)
    slow_spatial_top = apply_back(slow_expand_grad, slow_expand_w) * swish_slope(
        slow_spatial_out[0]
    )
    cat_grad = apply_back(slow_skip_grad, slow_skip_w)
    fast_spatial_top = apply_back(fast_expand_grad, fast_expand_w) * swish_slope(
        fast_spatial_out[0]
    )
    fast_grad = apply_back(fast_skip_grad, fast_skip_w)
    totals_two = grad_totals(
        [
            local_back(slow_spatial_top, slow_spatial_out[1]),
            local_back(fast_spatial_top, fast_spatial_out[1]),
        ]
    )
    slow_spatial_grad = norm_back(
        slow_spatial_top,
        slow_spatial_out[1],
        slow_spatial_out[2],
        gain_parts[2],
        mask_slow,
        count_slow,
        totals_two[0],
    )
    fast_spatial_grad = norm_back(
        fast_spatial_top,
        fast_spatial_out[1],
        fast_spatial_out[2],
        gain_parts[6],
        mask_fast,
        count_fast,
        totals_two[1],
    )
    slow_spatial_wg = weight_grad(pixel_taps(stored["slow_mid_pad"]), slow_spatial_grad).reshape(
        slow_spatial_w.shape
    )
    fast_spatial_wg = weight_grad(pixel_taps(stored["fast_mid_pad"]), fast_spatial_grad).reshape(
        fast_spatial_w.shape
    )
    slow_temporal_top = pixel_back(grad_rim(slow_spatial_grad), slow_spatial_w) * swish_slope(
        slow_temporal_out[0]
    )
    fast_temporal_top = pixel_back(grad_rim(fast_spatial_grad), fast_spatial_w) * swish_slope(
        fast_temporal_out[0]
    )
    totals_three = grad_totals(
        [
            local_back(slow_temporal_top, slow_temporal_out[1]),
            local_back(fast_temporal_top, fast_temporal_out[1]),
        ]
    )
    slow_temporal_grad = norm_back(
        slow_temporal_top,
        slow_temporal_out[1],
        slow_temporal_out[2],
        gain_parts[1],
        mask_slow,
        count_slow,
        totals_three[0],
    )
    fast_temporal_grad = norm_back(
        fast_temporal_top,
        fast_temporal_out[1],
        fast_temporal_out[2],
        gain_parts[5],
        mask_fast,
        count_fast,
        totals_three[1],
    )
    slow_temporal_wg = weight_grad(time_taps(cat_low), slow_temporal_grad).reshape(
        slow_temporal_w.shape
    )
    fast_temporal_wg = weight_grad(time_taps(fast_low), fast_temporal_grad).reshape(
        fast_temporal_w.shape
    )
    cat_grad = cat_grad + time_untaps(
        apply_back(slow_temporal_grad, slow_temporal_w.reshape(-1, BS)), DS + DL
    )
    fast_grad = fast_grad + time_untaps(
        apply_back(fast_temporal_grad, fast_temporal_w.reshape(-1, BF)), DF
    )
    lateral_top = cat_grad[..., DS:] * swish_slope(lateral_out[0])
    totals_four = grad_totals([local_back(lateral_top, lateral_out[1])])
    lateral_grad = norm_back(
        lateral_top,
        lateral_out[1],
        lateral_out[2],
        gain_parts[0],
        mask_slow,
        count_slow,
        totals_four[0],
    )
    lateral_wg = weight_grad(lateral_taps(fast_low), lateral_grad).reshape(lateral_w.shape)
    fast_grad = fast_grad + lateral_untaps(apply_back(lateral_grad, lateral_w.reshape(-1, DL)), DF)
    ordered = [
        totals_four[0],
        totals_three[0],
        totals_two[0],
        totals_one[0],
        totals_one[1],
        totals_three[1],
        totals_two[1],
        totals_one[2],
        totals_one[3],
    ]
    gain_grad = jnp.concatenate([member[1] for member in ordered])
    bias_grad = jnp.concatenate([member[0] for member in ordered])
    gradient_list = [
        lateral_wg,
        slow_temporal_wg,
        slow_spatial_wg,
        slow_expand_wg,
        slow_skip_wg,
        fast_temporal_wg,
        fast_spatial_wg,
        fast_expand_wg,
        fast_skip_wg,
    ]
    return (cat_grad[..., :DS], fast_grad, gradient_list, gain_grad, bias_grad)


def scatter_sum(blocks):
    for axis, dim in (("wa", 2), ("ha", 1), ("clip", 0)):
        place = lax.axis_index(axis)
        count = lax.axis_size(axis)
        step = 1
        while step < count:
            step *= 2
        step //= 2
        while step >= 1:
            half = blocks.shape[dim] // 2
            bit = (place // step) % 2
            kept = lax.dynamic_slice_in_dim(blocks, bit * half, half, dim)
            sent = lax.dynamic_slice_in_dim(blocks, (1 - bit) * half, half, dim)
            got = lax.ppermute(sent, axis, [(i, i ^ step) for i in range(count)])
            blocks = (kept.astype(jnp.float32) + got.astype(jnp.float32)).astype(jnp.bfloat16)
            step //= 2
    return blocks


def sum_weights(weight_grads):
    clips = lax.axis_size("clip")
    tiles = lax.axis_size(("ha", "wa"))
    per_layer = []
    for layer_grads in weight_grads:
        pieces = []
        shapes = []
        for member in layer_grads:
            rows, columns = member.shape[-2:]
            low = member.astype(jnp.bfloat16).reshape(-1, tiles, rows // tiles, clips, columns // clips)
            pieces.append(jnp.transpose(low, (3, 1, 0, 2, 4)).reshape(clips * tiles, -1))
            shapes.append(member.shape[:-2] + (rows // tiles, columns // clips))
        flat = jnp.concatenate(pieces, axis=1)
        length = -(-flat.shape[1] // 2048) * 2048
        flat = jnp.pad(flat, ((0, 0), (0, length - flat.shape[1])))
        summed = scatter_sum(flat.reshape(clips, -1, lax.axis_size("wa"), length // 128, 128)).reshape(-1)
        offset = 0
        shares = []
        for shape in shapes:
            size = 1
            for d in shape:
                size *= d
            shares.append(summed[offset : offset + size].reshape(shape).astype(jnp.float32))
            offset += size
        per_layer.append(shares)
    return [jnp.stack(group) for group in zip(*per_layer)]


def local(
    slow_in,
    fast_in,
    valid_frames,
    lateral_w,
    slow_temporal_w,
    slow_spatial_w,
    slow_expand_w,
    slow_skip_w,
    fast_temporal_w,
    fast_spatial_w,
    fast_expand_w,
    fast_skip_w,
    gains,
    biases,
    slow_cot,
    fast_cot,
):
    clips_here = slow_in.shape[0]
    local_frames = lax.dynamic_slice_in_dim(
        valid_frames, lax.axis_index("clip") * clips_here, clips_here
    )
    frame_slow = jnp.arange(ST, dtype=jnp.int32)
    frame_fast = jnp.arange(ST * ALPHA, dtype=jnp.int32)
    mask_slow = (frame_slow[None, :] < local_frames[:, None]).astype(jnp.float32)[
        :, :, None, None, None
    ]
    mask_fast = (frame_fast[None, :] < ALPHA * local_frames[:, None]).astype(jnp.float32)[
        :, :, None, None, None
    ]
    count_slow = jnp.sum(valid_frames).astype(jnp.float32) * (HT * WD)
    count_fast = count_slow * ALPHA
    all_weights = (
        lateral_w,
        slow_temporal_w,
        slow_spatial_w,
        slow_expand_w,
        slow_skip_w,
        fast_temporal_w,
        fast_spatial_w,
        fast_expand_w,
        fast_skip_w,
    )
    slow_act = slow_in
    fast_act = fast_in
    stored_list = []
    for layer_index in range(LAYERS):
        weights = [w[layer_index] for w in all_weights]
        slow_act, fast_act, stored = block_forward(
            slow_act,
            fast_act,
            weights,
            split_norms(gains[layer_index]),
            split_norms(biases[layer_index]),
            mask_slow,
            mask_fast,
            count_slow,
            count_fast,
        )
        stored_list.append(stored)
    grad_slow = slow_cot
    grad_fast = fast_cot
    weight_grads = [None] * LAYERS
    gain_grads = [None] * LAYERS
    bias_grads = [None] * LAYERS
    for layer_index in reversed(range(LAYERS)):
        weights = [w[layer_index] for w in all_weights]
        grad_slow, grad_fast, gradient_list, gain_grad, bias_grad = block_backward(
            grad_slow,
            grad_fast,
            stored_list[layer_index],
            weights,
            split_norms(gains[layer_index]),
            mask_slow,
            mask_fast,
            count_slow,
            count_fast,
        )
        weight_grads[layer_index] = gradient_list
        gain_grads[layer_index] = gain_grad
        bias_grads[layer_index] = bias_grad
    shares = sum_weights(weight_grads)
    return (
        slow_act,
        fast_act,
        grad_slow,
        grad_fast,
        shares[0],
        shares[1],
        shares[2],
        shares[3],
        shares[4],
        shares[5],
        shares[6],
        shares[7],
        shares[8],
        jnp.stack(gain_grads),
        jnp.stack(bias_grads),
    )


def solution(mesh):
    return jax.shard_map(
        local,
        mesh=mesh,
        in_specs=(
            P("clip", None, "ha", "wa", None),
            P("clip", None, "ha", "wa", None),
            P(),
            P(),
            P(),
            P(),
            P(),
            P(),
            P(),
            P(),
            P(),
            P(),
            P(),
            P(),
            P("clip", None, "ha", "wa", None),
            P("clip", None, "ha", "wa", None),
        ),
        out_specs=(
            P("clip", None, "ha", "wa", None),
            P("clip", None, "ha", "wa", None),
            P("clip", None, "ha", "wa", None),
            P("clip", None, "ha", "wa", None),
            P(None, None, ("ha", "wa"), "clip"),
            P(None, None, ("ha", "wa"), "clip"),
            P(None, None, None, ("ha", "wa"), "clip"),
            P(None, ("ha", "wa"), "clip"),
            P(None, ("ha", "wa"), "clip"),
            P(None, None, ("ha", "wa"), "clip"),
            P(None, None, None, ("ha", "wa"), "clip"),
            P(None, ("ha", "wa"), "clip"),
            P(None, ("ha", "wa"), "clip"),
            P(),
            P(),
        ),
        check_vma=False,
    )
```

```python
import functools

import jax
import jax.numpy as jnp
from jax import lax
from jax.experimental import pallas as pl
from jax.experimental.pallas import tpu as pltpu
from jax.sharding import PartitionSpec as P

DS = 1024
DL = 256
BS = 256
DF = 128
BF = 32
ST = 8
ALPHA = 4
HT = 16
WD = 16
LAYERS = 2
CC = DS + DL
EPSILON = 1e-05
LANES = 128
ALL_AXES = ("clip", "ha", "wa")


LAT, STM, SSP, SEX, SSK, FTM, FSP, FEX, FSK = 0, 2, 4, 6, 14, 22, 23, 24, 25
GB_ROWS = 32

F32 = jnp.float32
BF16 = jnp.bfloat16


def dot(a, b):
    return jnp.dot(a, b, preferred_element_type=F32)


def dot_nt(a, b):
    return lax.dot_general(a, b, (((1,), (1,)), ((), ())), preferred_element_type=F32)


def dot_tn(a, b):
    return lax.dot_general(a, b, (((0,), (0,)), ((), ())), preferred_element_type=F32)


def sigmoid(v):
    return 0.5 * jnp.tanh(0.5 * v) + 0.5


def silu(v):
    return v * sigmoid(v)


def slope(v):
    s = sigmoid(v)
    return s + v * s * (1.0 - s)


def silu_and_slope(v):
    s = sigmoid(v)
    act = v * s
    return act, s + act * (1.0 - s)


def wide(tile, row, count):
    if count == 1:
        return tile[row : row + 1, :]
    return jnp.concatenate([tile[row + i : row + i + 1, :] for i in range(count)], axis=1)


def fold_phases(tile):
    return tile + pltpu.roll(tile, 32, 1) + pltpu.roll(tile, 64, 1) + pltpu.roll(tile, 96, 1)


def down(x, frame):
    return jnp.concatenate([jnp.zeros_like(x[:frame]), x[:-frame]], axis=0)


def up(x, frame):
    return jnp.concatenate([x[frame:], jnp.zeros_like(x[:frame])], axis=0)


def col_sum(x):
    return jnp.sum(x, axis=0, keepdims=True)


class Norm:
    def __init__(self, total, row, gb, gb_row, count, inv_count):
        mean = wide(total, row, count) * inv_count
        square = wide(total, row + count, count) * inv_count
        self.mean = mean
        self.rstd = lax.rsqrt(square - mean * mean + EPSILON)
        self.gain = wide(gb[0], gb_row, count)
        self.bias = wide(gb[1], gb_row, count)
        self.scale = self.gain * self.rstd
        self.shift = self.bias - mean * self.scale

    def columns(self, start, size):
        other = object.__new__(Norm)
        for name in ("mean", "rstd", "gain", "bias", "scale", "shift"):
            setattr(other, name, getattr(self, name)[:, start : start + size])
        return other

    def out(self, z):
        return z * self.scale + self.shift

    def hat(self, z):
        return (z - self.mean) * self.rstd

    def back(self, dy, hat, inside, a_sum, b_sum, inv_count):
        return self.scale * (dy - jnp.where(inside, a_sum * inv_count + hat * (b_sum * inv_count), 0.0))


def inside_rows(rows, columns, limit):
    return lax.broadcasted_iota(jnp.int32, (rows, columns), 0) < limit


def moments(z, inside):
    masked = jnp.where(inside, z, 0.0)
    return col_sum(masked), col_sum(masked * z)


def put_rows(ref, row, vector):
    for i in range(vector.shape[1] // LANES):
        ref[0, row + i : row + i + 1, :] = vector[:, i * LANES : (i + 1) * LANES]


def spread(ref):
    tile = ref[0]

    def body(i, carry):
        ref[i] = tile
        return carry

    lax.fori_loop(1, ref.shape[0], body, 0)


def gather_total(ref):
    return jnp.sum(ref[...], axis=0)


def phase(ref, p):
    return ref[:, p].reshape(ref.shape[0] * ref.shape[2], ref.shape[3])


def fill_padded(pad, shape, own, above, below, other, has_left, has_right):
    t, h, w = shape
    edge = t * w
    c = own.shape[1]
    pad[:, 1 : h + 1, w : 2 * w, :] = own.reshape(t, h, w, c)
    pad[:, 0, w : 2 * w, :] = above.reshape(t, w, c)
    pad[:, h + 1, w : 2 * w, :] = below.reshape(t, w, c)
    o_above, o_own, o_below = other[:edge], other[edge : edge + t * h * w], other[edge + t * h * w :]
    for start, has in ((0, has_left), (2 * w, has_right)):
        pad[:, 1 : h + 1, start : start + w, :] = (o_own * has).reshape(t, h, w, c)
        pad[:, 0, start : start + w, :] = (o_above * has).reshape(t, w, c)
        pad[:, h + 1, start : start + w, :] = (o_below * has).reshape(t, w, c)


def tap(pad, shape, a, b):
    t, h, w = shape
    part = pad[:, a : a + h, w - 1 + b : 2 * w - 1 + b, :]
    return part.reshape(t * h * w, part.shape[-1]).astype(BF16)


def activate_padded(pad, shape, norm, own, above_ref, below_ref, other_ref, sf):
    def act(z):
        return silu(norm.out(z)).astype(BF16).astype(F32)

    has_up, has_down = sf[2], sf[3]
    t, h, w = shape
    edge = t * w
    other = act(other_ref[...].astype(F32))
    other = jnp.concatenate(
        [other[:edge] * has_up, other[edge:-edge], other[-edge:] * has_down], axis=0
    )
    fill_padded(
        pad,
        shape,
        act(own),
        act(above_ref[...].astype(F32)) * has_up,
        act(below_ref[...].astype(F32)) * has_down,
        other,
        sf[4],
        sf[5],
    )


def fast_head(phases, frame, inside, lat_w, ft_band, fk_w, fb_out, zlat_out, zft_out, zft16_out, zfk_out, pay, row):
    low = [v.astype(BF16) for v in phases]
    for p in range(ALPHA):
        fb_out[:, p * DF : (p + 1) * DF] = low[p]
    before2, before3, after0 = down(low[2], frame), down(low[3], frame), up(low[0], frame)
    z = (
        dot(before2, lat_w[0, 0])
        + dot(before3, lat_w[0, 1])
        + dot(low[0], lat_w[0, 2])
        + dot(low[1], lat_w[0, 3])
        + dot(low[2], lat_w[0, 4])
    )
    zlat_out[...] = z
    total, square = moments(z, inside[:, :DL])
    put_rows(pay, row, total)
    put_rows(pay, row + 2, square)
    six = [before3] + low + [after0]
    z = dot(six[0], ft_band[0])
    for j in range(1, 6):
        z = z + dot(six[j], ft_band[j])
    zft_out[...] = z
    zft16_out[...] = z.astype(BF16)
    total, square = moments(z, inside[:, :LANES])
    put_rows(pay, row + 4, total)
    put_rows(pay, row + 5, square)
    total, square = 0.0, 0.0
    for p in range(ALPHA):
        z = dot(low[p], fk_w[0])
        zfk_out[:, p * DF : (p + 1) * DF] = z
        one, two = moments(z, inside[:, :LANES])
        total, square = total + one, square + two
    put_rows(pay, row + 6, total)
    put_rows(pay, row + 7, square)


def kernel_start(shape, si, fast, lat_w, ft_band, fk_w, fb, zlat, zft, zft16, zfk, pay):
    t, h, w = shape
    inside = inside_rows(t * h * w, DL, si[0])
    fast_head(
        [phase(fast, p) for p in range(ALPHA)],
        h * w, inside, lat_w, ft_band, fk_w, fb, zlat, zft, zft16, zfk, pay, 0,
    )
    spread(pay)


def kernel_temporal(first, shape, si, sf, *refs):
    t, h, w = shape
    rows, frame = t * h * w, h * w
    if first:
        (recv, slow, gb, zlat, zft, above, below, other, st_w, sk_w, fs_bd,
         low_out, zst, zst16, zsk, af9, zfs, pay, tot_out, pad) = refs
        row = 0
        total = gather_total(recv)
        tot_out[...] = total
    else:
        (recv, gb_before, tot_sk, zse_in, zsk_in, gb, zlat, zft, above, below, other, st_w, sk_w, fs_bd,
         low_out, zst, zst16, zsk, af9, zfs, pay, tot_out, pad) = refs
        row = 16
        total = gather_total(recv)
        tot_out[...] = total
        inside = inside_rows(rows, 256, si[0])
        one = Norm(total, 0, gb_before, SEX, 8, sf[0])
        two = Norm(tot_sk[...], 8, gb_before, SSK, 8, sf[0])
        for c in range(0, DS, 256):
            u = one.columns(c, 256).out(zse_in[:, c : c + 256]) + two.columns(c, 256).out(zsk_in[:, c : c + 256])
            low_out[:, c : c + 256] = jnp.where(inside, silu(u), 0.0).astype(BF16)
    inside = inside_rows(rows, 256, si[0])
    lat = Norm(total, row, gb, LAT, 2, sf[0])
    ft = Norm(fold_phases(total), row + 4, gb, FTM, 1, sf[1])
    if first:
        low_out[:, :DS] = slow[...].astype(BF16)
    low_out[:, DS:] = silu(lat.out(zlat[...])).astype(BF16)
    activate_padded(pad, shape, ft, zft[...], above, below, other, sf)
    low = low_out[...]
    z = dot(low, st_w[0, 1])
    z = z + down(dot(low, st_w[0, 0]), frame)
    z = z + up(dot(low, st_w[0, 2]), frame)
    zst[...] = z
    zst16[...] = z.astype(BF16)
    one, two = moments(z, inside)
    put_rows(pay, 0, one)
    put_rows(pay, 2, two)
    for a in range(3):
        for b in range(3):
            k = 3 * a + b
            af9[:, k * LANES : (k + 1) * LANES] = tap(pad, shape, a, b)
    z = dot(af9[...], fs_bd[...].reshape(9 * LANES, LANES))
    zfs[...] = z
    one, two = moments(z, inside[:, :LANES])
    put_rows(pay, 4, one)
    put_rows(pay, 5, two)
    pay[0, 6:8, :] = jnp.zeros((2, LANES), F32)
    for c in range(0, DS, 256):
        z = dot(low, sk_w[0, :, c : c + 256])
        zsk[:, c : c + 256] = z
        one, two = moments(z, inside)
        put_rows(pay, 8 + c // LANES, one)
        put_rows(pay, 16 + c // LANES, two)
    spread(pay)


def kernel_spatial(shape, si, sf, recv, gb, zst, above, below, other, zfs, ss_w, fe_bd,
                   a9, zss, bf, zfe, pay, tot_out, pad):
    t, h, w = shape
    inside = inside_rows(t * h * w, 256, si[0])
    total = gather_total(recv)
    tot_out[...] = total
    st = Norm(total, 0, gb, STM, 2, sf[0])
    fs = Norm(fold_phases(total), 4, gb, FSP, 1, sf[1])
    activate_padded(pad, shape, st, zst[...], above, below, other, sf)
    for a in range(3):
        for b in range(3):
            k = 3 * a + b
            a9[:, k * BS : (k + 1) * BS] = tap(pad, shape, a, b)
    z = dot(a9[...], ss_w[...].reshape(9 * BS, BS))
    zss[...] = z
    one, two = moments(z, inside)
    put_rows(pay, 0, one)
    put_rows(pay, 2, two)
    low = silu(fs.out(zfs[...])).astype(BF16)
    bf[...] = low
    total, square = 0.0, 0.0
    for p in range(ALPHA):
        z = dot(low, fe_bd[:, p * DF : (p + 1) * DF])
        zfe[:, p * DF : (p + 1) * DF] = z
        one, two = moments(z, inside[:, :LANES])
        total, square = total + one, square + two
    put_rows(pay, 4, total)
    put_rows(pay, 5, square)
    pay[0, 6:8, :] = jnp.zeros((2, LANES), F32)
    spread(pay)


def kernel_expand(last, shape, si, sf, *refs):
    t, h, w = shape
    inside = inside_rows(t * h * w, 256, si[0])
    if last:
        recv, gb, zss, se_w, bt, zse, pay, tot_out = refs
    else:
        (recv, gb, zss, se_w, tot_fk, zfe, zfk, lat_w, ft_band, fk_w,
         bt, zse, pay, tot_out, fb, zlat, zft, zft16, zfk_out) = refs
    total = gather_total(recv)
    tot_out[...] = total
    ss = Norm(total, 0, gb, SSP, 2, sf[0])
    low = silu(ss.out(zss[...])).astype(BF16)
    bt[...] = low
    for c in range(0, DS, 256):
        z = dot(low, se_w[0, :, c : c + 256])
        zse[:, c : c + 256] = z
        one, two = moments(z, inside)
        put_rows(pay, c // LANES, one)
        put_rows(pay, 8 + c // LANES, two)
    if not last:
        fe = Norm(total, 4, gb, FEX, 1, sf[1])
        fk = Norm(tot_fk[...], tot_fk.shape[0] - 2, gb, FSK, 1, sf[1])
        phases = []
        for p in range(ALPHA):
            cols = slice(p * DF, (p + 1) * DF)
            u = fe.out(zfe[:, cols]) + fk.out(zfk[:, cols])
            phases.append(jnp.where(inside[:, :LANES], silu(u), 0.0))
        fast_head(
            phases, h * w, inside, lat_w, ft_band, fk_w, fb, zlat, zft, zft16, zfk_out, pay, 16
        )
    spread(pay)


def top_of_block(shape, si, sf, se, sk, fe, fk, zse, zsk, zfe, zfk, slow_grad, fast_grad, du_s, du_f, pay, outs):
    t, h, w = shape
    inside = inside_rows(t * h * w, 256, si[0])
    for c in range(0, DS, 256):
        cols = slice(c, c + 256)
        one, two = se.columns(c, 256), sk.columns(c, 256)
        hat1, hat2 = one.hat(zse[:, cols]), two.hat(zsk[:, cols])
        u = one.gain * hat1 + one.bias + (two.gain * hat2 + two.bias)
        act, rate = silu_and_slope(u)
        if outs is not None:
            outs[0][:, cols] = jnp.where(inside, act, 0.0)
        du = jnp.where(inside, slow_grad(cols) * rate, 0.0)
        du_s[:, cols] = du
        put_rows(pay, c // LANES, col_sum(du))
        put_rows(pay, 8 + c // LANES, col_sum(du * hat1))
        put_rows(pay, 16 + c // LANES, col_sum(du * hat2))
    sums = [0.0, 0.0, 0.0]
    for p in range(ALPHA):
        cols = slice(p * DF, (p + 1) * DF)
        hat1, hat2 = fe.hat(zfe[:, cols]), fk.hat(zfk[:, cols])
        u = fe.gain * hat1 + fe.bias + (fk.gain * hat2 + fk.bias)
        act, rate = silu_and_slope(u)
        if outs is not None:
            outs[1][:, p] = jnp.where(inside[:, :LANES], act, 0.0).reshape(t, h * w, DF)
        du = jnp.where(inside[:, :LANES], fast_grad(p) * rate, 0.0)
        du_f[:, cols] = du
        sums = [sums[0] + col_sum(du), sums[1] + col_sum(du * hat1), sums[2] + col_sum(du * hat2)]
    for i in range(3):
        put_rows(pay, 24 + i, sums[i])
    pay[0, 27:32, :] = jnp.zeros((5, LANES), F32)
    spread(pay)


def kernel_turn(shape, si, sf, recv, gb, tot_sk, tot_fk, tot_fe, zse, zsk, zfe, zfk, slow_cot, fast_cot,
                out_slow, out_fast, du_s, du_f, pay, tot_out):
    total = gather_total(recv)
    tot_out[...] = total
    top_of_block(
        shape, si, sf,
        Norm(total, 0, gb, SEX, 8, sf[0]),
        Norm(tot_sk[...], 8, gb, SSK, 8, sf[0]),
        Norm(tot_fe[...], 4, gb, FEX, 1, sf[1]),
        Norm(tot_fk[...], tot_fk.shape[0] - 2, gb, FSK, 1, sf[1]),
        zse, zsk, zfe, zfk,
        lambda cols: slow_cot[:, cols],
        lambda p: phase(fast_cot, p),
        du_s, du_f, pay, (out_slow, out_fast),
    )


def kernel_back_expand(shape, si, sf, recv, gb, tot_se, tot_sk, tot_ss, tot_fk, zse, zsk, zss, zfe, zfk, zfs,
                       du_s, du_f, se_w, fe_bd,
                       dz_se, dz_sk, dz_fe, dz_fk, dy_ss, dy_fs, pay, tot_out):
    t, h, w = shape
    inside = inside_rows(t * h * w, 256, si[0])
    total = gather_total(recv)
    tot_out[...] = total
    inv, inv_f = sf[0], sf[1]
    se = Norm(tot_se[...], 0, gb, SEX, 8, inv)
    sk = Norm(tot_sk[...], 8, gb, SSK, 8, inv)
    ss = Norm(tot_ss[...], 0, gb, SSP, 2, inv)
    fe = Norm(tot_ss[...], 4, gb, FEX, 1, inv_f)
    fk = Norm(tot_fk[...], tot_fk.shape[0] - 2, gb, FSK, 1, inv_f)
    fs = Norm(fold_phases(tot_sk[...]), 4, gb, FSP, 1, inv_f)
    back = 0.0
    for c in range(0, DS, 256):
        cols = slice(c, c + 256)
        r = c // LANES
        du = du_s[:, cols]
        a_sum = wide(total, r, 2)
        one, two = se.columns(c, 256), sk.columns(c, 256)
        dz = one.back(du, one.hat(zse[:, cols]), inside, a_sum, wide(total, 8 + r, 2), inv).astype(BF16)
        dz_se[:, cols] = dz
        back = back + dot_nt(dz, se_w[0, :, cols])
        dz_sk[:, cols] = two.back(du, two.hat(zsk[:, cols]), inside, a_sum, wide(total, 16 + r, 2), inv).astype(BF16)
    dy = back * slope(ss.out(zss[...]))
    dy_ss[...] = dy
    put_rows(pay, 0, col_sum(dy))
    put_rows(pay, 2, col_sum(dy * ss.hat(zss[...])))
    back = 0.0
    for p in range(ALPHA):
        cols = slice(p * DF, (p + 1) * DF)
        du = du_f[:, cols]
        a_sum = wide(total, 24, 1)
        dz = fe.back(du, fe.hat(zfe[:, cols]), inside[:, :LANES], a_sum, wide(total, 25, 1), inv_f).astype(BF16)
        dz_fe[:, cols] = dz
        back = back + dot_nt(dz, fe_bd[:, cols])
        dz_fk[:, cols] = fk.back(
            du, fk.hat(zfk[:, cols]), inside[:, :LANES], a_sum, wide(total, 26, 1), inv_f
        ).astype(BF16)
    dy = back * slope(fs.out(zfs[...]))
    dy_fs[...] = dy
    put_rows(pay, 4, col_sum(dy))
    put_rows(pay, 5, col_sum(dy * fs.hat(zfs[...])))
    pay[0, 6:8, :] = jnp.zeros((2, LANES), F32)
    spread(pay)


def kernel_back_spatial_in(shape, si, sf, recv, gb, tot_ss, tot_sk, zss, zfs, dy_ss, dy_fs, dz, tot_out):
    t, h, w = shape
    inside = inside_rows(t * h * w, 256, si[0])
    total = gather_total(recv)
    folded = fold_phases(total)
    tot_out[0] = total
    tot_out[1] = folded
    ss = Norm(tot_ss[...], 0, gb, SSP, 2, sf[0])
    fs = Norm(fold_phases(tot_sk[...]), 4, gb, FSP, 1, sf[1])
    dz[:, :BS] = ss.back(
        dy_ss[...], ss.hat(zss[...]), inside, wide(total, 0, 2), wide(total, 2, 2), sf[0]
    ).astype(BF16)
    dz[:, BS:] = fs.back(
        dy_fs[...], fs.hat(zfs[...]), inside[:, :LANES], wide(folded, 4, 1), wide(folded, 5, 1), sf[1]
    ).astype(BF16)


def kernel_back_spatial(shape, si, sf, gb, tot_st, tot_ft, zst, zft, dz, above, below, other, ss_w, fs_bd,
                        dy_st, dy_ft, pay, pad):
    fill_padded(
        pad, shape,
        dz[...].astype(F32), above[...].astype(F32), below[...].astype(F32), other[...].astype(F32),
        sf[4], sf[5],
    )
    st = Norm(tot_st[...], 0, gb, STM, 2, sf[0])
    ft = Norm(fold_phases(tot_ft[...]), tot_ft.shape[0] - 4, gb, FTM, 1, sf[1])
    back, back_f = 0.0, 0.0
    for a in range(3):
        for b in range(3):
            part = tap(pad, shape, 2 - a, 2 - b)
            back = back + dot_nt(part[:, :BS], ss_w[0, a, b])
            back_f = back_f + dot_nt(part[:, BS:], fs_bd[a, b])
    dy = back * slope(st.out(zst[...]))
    dy_st[...] = dy
    put_rows(pay, 0, col_sum(dy))
    put_rows(pay, 2, col_sum(dy * st.hat(zst[...])))
    dy = back_f * slope(ft.out(zft[...]))
    dy_ft[...] = dy
    put_rows(pay, 4, col_sum(dy))
    put_rows(pay, 5, col_sum(dy * ft.hat(zft[...])))
    pay[0, 6:8, :] = jnp.zeros((2, LANES), F32)
    spread(pay)


def kernel_back_skip(dz_sk, sk_w, dlow):
    for k in range(0, CC, 256):
        dlow[:, k : k + 256] = dot_nt(dz_sk[...], sk_w[0, k : k + 256, :])


def kernel_back_temporal(shape, si, sf, recv, gb, tot_lat, tot_st, zst, zft, zlat, dy_st, dy_ft, dlow,
                         dz_fk, st_w, ft_band, fk_w,
                         dz_st, dz_ft, dslow, dfast, dy_lat, pay, tot_out):
    t, h, w = shape
    rows, frame = t * h * w, h * w
    inside = inside_rows(rows, 256, si[0])
    total = gather_total(recv)
    folded = fold_phases(total)
    tot_out[0] = total
    tot_out[1] = folded
    st = Norm(tot_st[...], 0, gb, STM, 2, sf[0])
    base = tot_lat.shape[0] - 8
    ft = Norm(fold_phases(tot_lat[...]), base + 4, gb, FTM, 1, sf[1])
    lat = Norm(tot_lat[...], base, gb, LAT, 2, sf[0])
    dz = st.back(
        dy_st[...], st.hat(zst[...]), inside, wide(total, 0, 2), wide(total, 2, 2), sf[0]
    ).astype(BF16)
    dz_st[:, :BS] = up(dz, frame)
    dz_st[:, BS : 2 * BS] = dz
    dz_st[:, 2 * BS :] = down(dz, frame)

    def back(k):
        cols = slice(k, k + 256)
        part = dlow[:, cols]
        for j in range(3):
            part = part + dot_nt(dz_st[:, j * BS : (j + 1) * BS], st_w[0, j, cols, :])
        return part

    dy = back(DS) * slope(lat.out(zlat[...]))
    dy_lat[...] = dy
    put_rows(pay, 0, col_sum(dy))
    put_rows(pay, 2, col_sum(dy * lat.hat(zlat[...])))
    pay[0, 4:8, :] = jnp.zeros((4, LANES), F32)
    spread(pay)
    for k in range(0, DS, 256):
        dslow[:, k : k + 256] = back(k)
    dzf = ft.back(
        dy_ft[...], ft.hat(zft[...]), inside[:, :LANES], wide(folded, 4, 1), wide(folded, 5, 1), sf[1]
    ).astype(BF16)
    dz_ft[...] = dzf
    for p in range(ALPHA):
        part = dot_nt(dz_fk[:, p * DF : (p + 1) * DF], fk_w[0]) + dot_nt(dzf, ft_band[p + 1])
        if p == ALPHA - 1:
            part = part + up(dot_nt(dzf, ft_band[0]), frame)
        if p == 0:
            part = part + down(dot_nt(dzf, ft_band[5]), frame)
        dfast[:, p * DF : (p + 1) * DF] = part


def kernel_back_lateral(last, shape, si, sf, *refs):
    t, h, w = shape
    rows, frame = t * h * w, h * w
    if last:
        recv, gb, tot_lat, zlat, dy_lat, dfast, lat_w, dz_lat, tot_out, dfast_out = refs
    else:
        (recv, gb, tot_lat, zlat, dy_lat, dfast, lat_w,
         gb_below, tot_se, tot_sk, tot_fe, tot_fk, zse, zsk, zfe, zfk, dslow,
         dz_lat, tot_out, du_s, du_f, pay) = refs
    inside = inside_rows(rows, 256, si[0])
    total = gather_total(recv)
    tot_out[...] = total
    lat = Norm(tot_lat[...], tot_lat.shape[0] - 8, gb, LAT, 2, sf[0])
    dz = lat.back(
        dy_lat[...], lat.hat(zlat[...]), inside, wide(total, 0, 2), wide(total, 2, 2), sf[0]
    ).astype(BF16)
    dz_lat[...] = dz

    def fast_grad(p):
        part = dfast[:, p * DF : (p + 1) * DF]
        if p < 3:
            part = part + dot_nt(dz, lat_w[0, p + 2])
        if p >= 2:
            part = part + up(dot_nt(dz, lat_w[0, p - 2]), frame)
        return part

    if last:
        for p in range(ALPHA):
            dfast_out[:, p] = fast_grad(p).reshape(t, frame, DF)
    else:
        top_of_block(
            shape, si, sf,
            Norm(tot_se[...], 0, gb_below, SEX, 8, sf[0]),
            Norm(tot_sk[...], 8, gb_below, SSK, 8, sf[0]),
            Norm(tot_fe[...], 4, gb_below, FEX, 1, sf[1]),
            Norm(tot_fk[...], tot_fk.shape[0] - 2, gb_below, FSK, 1, sf[1]),
            zse, zsk, zfe, zfk, lambda cols: dslow[:, cols], fast_grad, du_s, du_f, pay, None,
        )


def kernel_weights_one(tiles, low, bt, fb, bf, dz_se, dz_sk, dz_fe, dz_fk, bundle, d_fe, d_fk):
    ksk, kse = CC // tiles, BS // tiles
    for j in range(4):
        cols = slice(j * 256, (j + 1) * 256)
        d = dot_tn(low[...], dz_sk[:, cols]).astype(BF16)
        bundle[:, j, :ksk, :] = d.reshape(tiles, ksk, 256)
        d = dot_tn(bt[...], dz_se[:, cols]).astype(BF16)
        bundle[:, j, ksk:, :] = d.reshape(tiles, kse, 256)
    fe, fk = 0.0, 0.0
    for p in range(ALPHA):
        cols = slice(p * DF, (p + 1) * DF)
        fk = fk + dot_tn(fb[:, cols], dz_fk[:, cols])
        fe = fe + dot_tn(bf[...], dz_fe[:, cols])[p * BF : (p + 1) * BF, :]
    d_fe[...] = fe
    d_fk[...] = fk


def kernel_weights_two(tiles, frame, low, a9, af9, fb, dz_s, dz_st, dz_ft, dz_lat, bundle, d_fs, d_ft):
    kst, kss, kla = CC // tiles, BS // tiles, DF // tiles
    for j in range(3):
        d = dot_tn(low[...], dz_st[:, j * BS : (j + 1) * BS]).astype(BF16)
        bundle[:, j * kst : (j + 1) * kst, :] = d.reshape(tiles, kst, BS)
    base = 3 * kst
    for k in range(9):
        d = dot_tn(a9[:, k * BS : (k + 1) * BS], dz_s[:, :BS]).astype(BF16)
        bundle[:, base + k * kss : base + (k + 1) * kss, :] = d.reshape(tiles, kss, BS)
        d_fs[k] = dot_tn(af9[:, k * LANES : (k + 1) * LANES], dz_s[:, BS:])
    base += 9 * kss
    f = [fb[:, p * DF : (p + 1) * DF] for p in range(ALPHA)]
    five = [down(f[2], frame), down(f[3], frame), f[0], f[1], f[2]]
    for k in range(5):
        d = dot_tn(five[k], dz_lat[...]).astype(BF16)
        bundle[:, base + k * kla : base + (k + 1) * kla, :] = d.reshape(tiles, kla, DL)
    six = [five[1]] + f + [up(f[0], frame)]
    for j in range(6):
        d_ft[j] = dot_tn(six[j], dz_ft[...])


SMEM = pltpu.MemorySpace.SMEM
VMEM = pltpu.MemorySpace.VMEM


class Weight:
    def __init__(self, array, layer):
        self.array = array
        self.layer = layer


class Arriving:
    def __init__(self, copy, ref, layered):
        self.copy = copy
        self.ref = ref
        self.layered = layered
        self.shape = ref.shape

    def __getitem__(self, place):
        if self.copy is not None:
            self.copy.wait()
            self.copy = None
        if self.layered:
            return self.ref[place[1:]] if isinstance(place, tuple) else self.ref[...]
        return self.ref[place]


class Leaving:
    def __init__(self, copy, ref):
        self.copy = copy
        self.ref = ref
        self.shape = ref.shape
        self.sent = False

    def __getitem__(self, place):
        return self.ref[place]

    def __setitem__(self, place, value):
        self.ref[place] = value

    def flush(self):
        self.copy.start()
        self.sent = True


def call(body, scalars, operands, outs, scratch=(), limit=61):
    layered = [isinstance(operand, Weight) for operand in operands]
    arrays = [operand.array if one else operand for operand, one in zip(operands, layered)]
    first, count = len(scalars), len(arrays)
    buffers = [pltpu.VMEM(x.shape[1:] if one else x.shape, x.dtype) for x, one in zip(arrays, layered)]
    buffers += [pltpu.VMEM(shape, kind) for shape, kind in outs]
    own = first + count + len(outs)

    def wrapped(*refs):
        inner = refs[own : own + len(buffers)]
        sems = refs[-1]
        arriving, leaving = [], []
        for i in range(count):
            source = refs[first + i]
            if layered[i]:
                source = source.at[operands[i].layer]
            copy = pltpu.make_async_copy(source, inner[i], sems.at[i])
            copy.start()
            arriving.append(Arriving(copy, inner[i], layered[i]))
        for i in range(len(outs)):
            copy = pltpu.make_async_copy(inner[count + i], refs[first + count + i], sems.at[count + i])
            leaving.append(Leaving(copy, inner[count + i]))
        body(*refs[:first], *arriving, *leaving, *refs[own + len(buffers) : -1])
        for one in leaving:
            if not one.sent:
                one.copy.start()
        for one in arriving:
            if one.copy is not None:
                one.copy.wait()
        for one in leaving:
            one.copy.wait()

    return pl.pallas_call(
        wrapped,
        out_shape=[jax.ShapeDtypeStruct(shape, kind) for shape, kind in outs],
        in_specs=[pl.BlockSpec(memory_space=SMEM) for _ in scalars] + [pl.BlockSpec(memory_space=pl.ANY)] * count,
        out_specs=[pl.BlockSpec(memory_space=pl.ANY)] * len(outs),
        scratch_shapes=buffers
        + [pltpu.VMEM(shape, kind) for shape, kind in scratch]
        + [pltpu.SemaphoreType.DMA((count + len(outs),))],
        compiler_params=pltpu.CompilerParams(vmem_limit_bytes=limit << 20),
    )(*scalars, *arrays)


def exchange(block):
    return lax.all_to_all(block, ALL_AXES, 0, 0)


def halo(z, shape):
    t, h, w = shape
    c = z.shape[1]
    count = lax.axis_size("ha")
    four = z.reshape(t, h, w, c)
    above = lax.ppermute(four[:, h - 1].reshape(t * w, c), "ha", [(i, i + 1) for i in range(count - 1)])
    below = lax.ppermute(four[:, 0].reshape(t * w, c), "ha", [(i + 1, i) for i in range(count - 1)])
    mine = jnp.concatenate([above, z, below], axis=0)
    other = lax.ppermute(mine, "wa", [(0, 1), (1, 0)])
    return above, below, other


def scatter_sum(blocks):
    for axis, dim in (("wa", 1), ("ha", 0), ("clip", 2)):
        place = lax.axis_index(axis)
        count = lax.axis_size(axis)
        step = count // 2
        while step >= 1:
            half = blocks.shape[dim] // 2
            bit = (place // step) % 2
            kept = lax.dynamic_slice_in_dim(blocks, bit * half, half, dim)
            sent = lax.dynamic_slice_in_dim(blocks, (1 - bit) * half, half, dim)
            got = lax.ppermute(sent, axis, [(i, i ^ step) for i in range(count)])
            blocks = (kept.astype(F32) + got.astype(F32)).astype(BF16)
            step //= 2
    return blocks.reshape(blocks.shape[3:])


def local(
    slow_in,
    fast_in,
    valid_frames,
    lateral_w,
    slow_temporal_w,
    slow_spatial_w,
    slow_expand_w,
    slow_skip_w,
    fast_temporal_w,
    fast_spatial_w,
    fast_expand_w,
    fast_skip_w,
    gains,
    biases,
    slow_cot,
    fast_cot,
):
    devices = lax.axis_size(ALL_AXES)
    clips, n_ha, n_wa = (lax.axis_size(a) for a in ALL_AXES)
    tiles = n_ha * n_wa
    _, t, h, w, _ = slow_in.shape
    shape = (t, h, w)
    frame = h * w
    rows = t * frame

    clip, ha, wa = (lax.axis_index(a) for a in ALL_AXES)
    si = (lax.dynamic_slice_in_dim(valid_frames, clip, 1) * frame).astype(jnp.int32)
    count_slow = jnp.sum(valid_frames).astype(F32) * (HT * WD)
    sf = jnp.stack(
        [
            1.0 / count_slow,
            1.0 / (count_slow * ALPHA),
            (ha > 0).astype(F32),
            (ha < n_ha - 1).astype(F32),
            (wa > 0).astype(F32),
            (wa < n_wa - 1).astype(F32),
        ]
    )
    both = jnp.stack([gains, biases], axis=1)
    slow_part = both[:, :, : 2816].reshape(LAYERS, 2, 22, LANES)
    narrow = jnp.tile(both[:, :, 2816 : 2880].reshape(LAYERS, 2, 2, BF), (1, 1, 1, ALPHA))
    fast_part = both[:, :, 2880:].reshape(LAYERS, 2, 2, LANES)
    gb_all = jnp.pad(
        jnp.concatenate([slow_part, narrow, fast_part], axis=2), ((0, 0), (0, 0), (0, GB_ROWS - 26), (0, 0))
    )
    gb = [gb_all[l] for l in range(LAYERS)]

    zero = jnp.zeros((LAYERS, DF, BF), BF16)
    taps = [fast_temporal_w[:, k] for k in range(3)]
    band = jnp.stack(
        [
            jnp.concatenate([taps[j - p] if 0 <= j - p <= 2 else zero for p in range(ALPHA)], axis=-1)
            for j in range(6)
        ],
        axis=1,
    )
    eye = jnp.eye(ALPHA, dtype=BF16)
    fs_bd = jnp.einsum("pq,labio->labpiqo", eye, fast_spatial_w).reshape(LAYERS, 3, 3, LANES, LANES)
    fe_bd = jnp.einsum("pq,lio->lpiqo", eye, fast_expand_w).reshape(LAYERS, LANES, ALPHA * DF)

    slow2 = slow_in.reshape(rows, DS)
    fast4 = fast_in.reshape(t, ALPHA, frame, DF)
    slow_cot2 = slow_cot.reshape(rows, DS)
    fast_cot4 = fast_cot.reshape(t, ALPHA, frame, DF)

    def act(columns, kind=F32):
        return ((rows, columns), kind)

    def pay(count):
        return ((devices, count, LANES), F32)

    def tot(count):
        return ((count, LANES), F32)

    def bind(body, *static):
        return functools.partial(body, *static)

    pad_slow = ((t, h + 2, 3 * w, BS), F32)
    pad_fast = ((t, h + 2, 3 * w, LANES), F32)
    pad_both = ((t, h + 2, 3 * w, BS + LANES), F32)
    scalars = (si, sf)

    saved = []
    fb, zlat, zft, zft16, zfk, sent = call(
        bind(kernel_start, shape),
        (si,),
        [fast4, Weight(lateral_w, 0), band[0], Weight(fast_skip_w, 0)],
        [act(512, BF16), act(DL), act(LANES), act(LANES, BF16), act(512), pay(8)],
    )
    recv = exchange(sent)
    before = None
    for l in range(LAYERS):
        above, below, other = halo(zft16, shape)
        last = l == LAYERS - 1
        start = [recv, slow2, gb[l]] if l == 0 else [recv, gb[l - 1], before["tot_sk"], before["zse"], before["zsk"], gb[l]]
        low, zst, zst16, zsk, af9, zfs, sent, tot_lat = call(
            bind(kernel_temporal, l == 0, shape),
            scalars,
            start + [zlat, zft, above, below, other, Weight(slow_temporal_w, l), Weight(slow_skip_w, l), fs_bd[l]],
            [act(CC, BF16), act(BS), act(BS, BF16), act(DS), act(9 * LANES, BF16), act(LANES), pay(24), tot(recv.shape[1])],
            [pad_fast],
        )
        if l > 0:
            before["tot_se"] = tot_lat
        recv = exchange(sent)
        above, below, other = halo(zst16, shape)
        a9, zss, bf, zfe, sent, tot_st = call(
            bind(kernel_spatial, shape),
            scalars,
            [recv, gb[l], zst, above, below, other, zfs, Weight(slow_spatial_w, l), fe_bd[l]],
            [act(9 * BS, BF16), act(BS), act(LANES, BF16), act(512), pay(8), tot(24)],
            [pad_slow],
        )
        recv = exchange(sent)
        keep = dict(
            fb=fb, zlat=zlat, zft=zft, zfk=zfk, low=low, zst=zst, zsk=zsk, af9=af9, zfs=zfs, a9=a9, zss=zss, bf=bf,
            zfe=zfe, tot_lat=tot_lat, tot_fk=tot_lat, tot_st=tot_st, tot_sk=tot_st,
        )
        if last:
            bt, zse, sent, tot_ss = call(
                bind(kernel_expand, True, shape),
                scalars,
                [recv, gb[l], zss, Weight(slow_expand_w, l)],
                [act(BS, BF16), act(DS), pay(16), tot(8)],
            )
        else:
            bt, zse, sent, tot_ss, fb, zlat, zft, zft16, zfk = call(
                bind(kernel_expand, False, shape),
                scalars,
                [recv, gb[l], zss, Weight(slow_expand_w, l), tot_lat, zfe, zfk,
                 Weight(lateral_w, l + 1), band[l + 1], Weight(fast_skip_w, l + 1)],
                [act(BS, BF16), act(DS), pay(24), tot(8),
                 act(512, BF16), act(DL), act(LANES), act(LANES, BF16), act(512)],
            )
        recv = exchange(sent)
        keep.update(bt=bt, zse=zse, tot_ss=tot_ss, tot_fe=tot_ss)
        saved.append(keep)
        before = keep

    keep = saved[-1]
    out_slow, out_fast, du_s, du_f, sent, keep["tot_se"] = call(
        bind(kernel_turn, shape),
        scalars,
        [recv, gb[-1], keep["tot_sk"], keep["tot_fk"], keep["tot_fe"], keep["zse"], keep["zsk"], keep["zfe"],
         keep["zfk"], slow_cot2, fast_cot4],
        [act(DS), ((t, ALPHA, frame, DF), F32), act(DS), act(512), pay(32), tot(16)],
    )

    shares = [None] * LAYERS
    sums = [None] * LAYERS
    for l in reversed(range(LAYERS)):
        k = saved[l]
        recv = exchange(sent)
        dz_se, dz_sk, dz_fe, dz_fk, dy_ss, dy_fs, sent, tot_one = call(
            bind(kernel_back_expand, shape),
            scalars,
            [recv, gb[l], k["tot_se"], k["tot_sk"], k["tot_ss"], k["tot_fk"], k["zse"], k["zsk"], k["zss"], k["zfe"],
             k["zfk"], k["zfs"], du_s, du_f, Weight(slow_expand_w, l), fe_bd[l]],
            [act(DS, BF16), act(DS, BF16), act(512, BF16), act(512, BF16), act(BS), act(LANES), pay(8), tot(32)],
        )
        recv = exchange(sent)
        (dlow,) = call(kernel_back_skip, (), [dz_sk, Weight(slow_skip_w, l)], [act(CC)])
        bundle_one, d_fe, d_fk = call(
            bind(kernel_weights_one, tiles),
            (),
            [k["low"], k["bt"], k["fb"], k["bf"], dz_se, dz_sk, dz_fe, dz_fk],
            [((tiles, 4, (CC + BS) // tiles, 256), BF16), ((BF, DF), F32), ((DF, DF), F32)],
        )
        dz, tot_two = call(
            bind(kernel_back_spatial_in, shape),
            scalars,
            [recv, gb[l], k["tot_ss"], k["tot_sk"], k["zss"], k["zfs"], dy_ss, dy_fs],
            [act(BS + LANES, BF16), ((2, 8, LANES), F32)],
        )
        above, below, other = halo(dz, shape)
        dy_st, dy_ft, sent = call(
            bind(kernel_back_spatial, shape),
            scalars,
            [gb[l], k["tot_st"], k["tot_lat"], k["zst"], k["zft"], dz, above, below, other,
             Weight(slow_spatial_w, l), fs_bd[l]],
            [act(BS), act(LANES), pay(8)],
            [pad_both],
        )
        recv = exchange(sent)
        dz_st, dz_ft, dslow, dfast, dy_lat, sent, tot_three = call(
            bind(kernel_back_temporal, shape),
            scalars,
            [recv, gb[l], k["tot_lat"], k["tot_st"], k["zst"], k["zft"], k["zlat"], dy_st, dy_ft, dlow, dz_fk,
             Weight(slow_temporal_w, l), band[l], Weight(fast_skip_w, l)],
            [act(3 * BS, BF16), act(LANES, BF16), act(DS), act(512), act(DL), pay(8), ((2, 8, LANES), F32)],
        )
        recv = exchange(sent)
        start = [recv, gb[l], k["tot_lat"], k["zlat"], dy_lat, dfast, Weight(lateral_w, l)]
        if l > 0:
            b = saved[l - 1]
            dz_lat, tot_four, du_s, du_f, sent = call(
                bind(kernel_back_lateral, False, shape),
                scalars,
                start + [gb[l - 1], b["tot_se"], b["tot_sk"], b["tot_fe"], b["tot_fk"], b["zse"], b["zsk"], b["zfe"],
                         b["zfk"], dslow],
                [act(DL, BF16), tot(8), act(DS), act(512), pay(32)],
            )
        else:
            dz_lat, tot_four, grad_fast = call(
                bind(kernel_back_lateral, True, shape),
                scalars,
                start,
                [act(DL, BF16), tot(8), ((t, ALPHA, frame, DF), F32)],
            )
            grad_slow = dslow
        rows_two = (3 * CC + 9 * BS + 5 * DF) // tiles
        bundle_two, d_fs, d_ft = call(
            bind(kernel_weights_two, tiles, frame),
            (),
            [k["low"], k["a9"], k["af9"], k["fb"], dz, dz_st, dz_ft, dz_lat],
            [((tiles, rows_two, 256), BF16), ((9, LANES, LANES), F32), ((6, LANES, LANES), F32)],
        )
        g_ft = jnp.stack(
            [
                sum(d_ft[p + j][:, p * BF : (p + 1) * BF] for p in range(ALPHA))
                for j in range(3)
            ]
        )
        g_fs = sum(d_fs[:, p * BF : (p + 1) * BF, p * BF : (p + 1) * BF] for p in range(ALPHA))
        pieces = []
        for g in (g_ft, g_fs, d_fe, d_fk):
            r, c = g.shape[-2:]
            g = g.astype(BF16).reshape(-1, tiles, r // tiles, clips, c // clips)
            pieces.append(jnp.transpose(g, (1, 3, 0, 2, 4)).reshape(tiles, clips, -1))
        small = jnp.concatenate(pieces, axis=-1)
        small_size = small.shape[-1]
        small_rows = -(-small_size // (16 * LANES)) * 16
        small = jnp.pad(small, ((0, 0), (0, 0), (0, small_rows * LANES - small_size)))
        small = scatter_sum(small.reshape(n_ha, n_wa, clips, small_rows, LANES)).reshape(-1)
        columns = DS // clips
        one = bundle_one.reshape(tiles, 4, -1, 256)
        if clips != 4:
            one = jnp.transpose(one, (0, 2, 1, 3)).reshape(tiles, -1, clips, columns)
            one = jnp.transpose(one, (0, 2, 1, 3))
        one = scatter_sum(one.reshape((n_ha, n_wa) + one.shape[1:]))
        two = jnp.transpose(bundle_two.reshape(tiles, rows_two, clips, BS // clips), (0, 2, 1, 3))
        two = scatter_sum(two.reshape((n_ha, n_wa) + two.shape[1:]))
        kst, kss, kla = CC // tiles, BS // tiles, DF // tiles
        n = BS // clips
        g_st = two[: 3 * kst].reshape(3, kst, n)
        g_ss = two[3 * kst : 3 * kst + 9 * kss].reshape(3, 3, kss, n)
        g_lat = two[3 * kst + 9 * kss :].reshape(5, kla, n)
        g_sk, g_se = one[:kst], one[kst:]
        fast_shares = []
        offset = 0
        for dims in ((3, DF // tiles, BF // clips), (3, 3, BF // tiles, BF // clips),
                     (BF // tiles, DF // clips), (DF // tiles, DF // clips)):
            size = functools.reduce(lambda x, y: x * y, dims)
            fast_shares.append(small[offset : offset + size].reshape(dims))
            offset += size
        shares[l] = [g_lat, g_st, g_ss, g_se, g_sk] + fast_shares
        flat = lambda tile, row, count: tile[row : row + count].reshape(-1)
        two_fold, three_fold = tot_two[1], tot_three[1]
        sums[l] = [
            jnp.concatenate(
                [
                    flat(tot_four, 2 * i, 2),
                    flat(tot_three[0], 2 * i, 2),
                    flat(tot_two[0], 2 * i, 2),
                    flat(tot_one, 8 * i, 8),
                    flat(tot_one, 16 * i, 8),
                    three_fold[4 + i, :BF],
                    two_fold[4 + i, :BF],
                    tot_one[24 + i],
                    tot_one[24 + 2 * i],
                ]
            )
            for i in range(2)
        ]
    weights = [jnp.stack(group).astype(F32) for group in zip(*shares)]
    return (
        out_slow.reshape(slow_in.shape),
        out_fast.reshape(fast_in.shape),
        grad_slow.reshape(slow_in.shape),
        grad_fast.reshape(fast_in.shape),
        *weights,
        jnp.stack([s[1] for s in sums]),
        jnp.stack([s[0] for s in sums]),
    )


def solution(mesh):
    pixels = P("clip", None, "ha", "wa", None)
    tile = ("ha", "wa")
    return jax.shard_map(
        local,
        mesh=mesh,
        in_specs=(pixels, pixels) + (P(),) * 12 + (pixels, pixels),
        out_specs=(
            (pixels,) * 4
            + (P(None, None, tile, "clip"),) * 2
            + (P(None, None, None, tile, "clip"),)
            + (P(None, tile, "clip"),) * 2
            + (P(None, None, tile, "clip"),)
            + (P(None, None, None, tile, "clip"),)
            + (P(None, tile, "clip"),) * 2
            + (P(),) * 2
        ),
        check_vma=False,
    )
```

```python
import functools

import jax
import jax.numpy as jnp
from jax import lax
from jax.experimental import pallas as pl
from jax.experimental.pallas import tpu as pltpu
from jax.sharding import PartitionSpec as P

DS = 1024
DL = 256
BS = 256
DF = 128
BF = 32
ST = 8
ALPHA = 4
HT = 16
WD = 16
LAYERS = 2
CC = DS + DL
EPSILON = 1e-05
LANES = 128
ALL_AXES = ("clip", "ha", "wa")


LAT, STM, SSP, SEX, SSK, FTM, FSP, FEX, FSK = 0, 2, 4, 6, 14, 22, 23, 24, 25
GB_ROWS = 32

F32 = jnp.float32
BF16 = jnp.bfloat16


def dot(a, b):
    return jnp.dot(a, b, preferred_element_type=F32)


def dot_nt(a, b):
    return lax.dot_general(a, b, (((1,), (1,)), ((), ())), preferred_element_type=F32)


def dot_tn(a, b):
    return lax.dot_general(a, b, (((0,), (0,)), ((), ())), preferred_element_type=F32)


def sigmoid(v):
    return 0.5 * jnp.tanh(0.5 * v) + 0.5


def silu(v):
    return v * sigmoid(v)


def slope(v):
    s = sigmoid(v)
    return s + v * s * (1.0 - s)


def silu_and_slope(v):
    s = sigmoid(v)
    act = v * s
    return act, s + act * (1.0 - s)


def wide(tile, row, count):
    if count == 1:
        return tile[row : row + 1, :]
    return jnp.concatenate([tile[row + i : row + i + 1, :] for i in range(count)], axis=1)


def fold_phases(tile):
    return tile + pltpu.roll(tile, 32, 1) + pltpu.roll(tile, 64, 1) + pltpu.roll(tile, 96, 1)


def down(x, frame):
    return jnp.concatenate([jnp.zeros_like(x[:frame]), x[:-frame]], axis=0)


def up(x, frame):
    return jnp.concatenate([x[frame:], jnp.zeros_like(x[:frame])], axis=0)


def col_sum(x):
    return jnp.sum(x, axis=0, keepdims=True)


class Norm:
    def __init__(self, total, row, gb, gb_row, count, inv_count):
        mean = wide(total, row, count) * inv_count
        square = wide(total, row + count, count) * inv_count
        self.mean = mean
        self.rstd = lax.rsqrt(square - mean * mean + EPSILON)
        self.gain = wide(gb[0], gb_row, count)
        self.bias = wide(gb[1], gb_row, count)
        self.scale = self.gain * self.rstd
        self.shift = self.bias - mean * self.scale

    def columns(self, start, size):
        other = object.__new__(Norm)
        for name in ("mean", "rstd", "gain", "bias", "scale", "shift"):
            setattr(other, name, getattr(self, name)[:, start : start + size])
        return other

    def out(self, z):
        return z * self.scale + self.shift

    def hat(self, z):
        return (z - self.mean) * self.rstd

    def back(self, dy, hat, inside, a_sum, b_sum, inv_count):
        return self.scale * (dy - jnp.where(inside, a_sum * inv_count + hat * (b_sum * inv_count), 0.0))


def inside_rows(rows, columns, limit):
    return lax.broadcasted_iota(jnp.int32, (rows, columns), 0) < limit


def moments(z, inside):
    masked = jnp.where(inside, z, 0.0)
    return col_sum(masked), col_sum(masked * z)


def put_rows(ref, row, vector):
    for i in range(vector.shape[1] // LANES):
        ref[row + i : row + i + 1, :] = vector[:, i * LANES : (i + 1) * LANES]


def phase(ref, p):
    return ref[:, p].reshape(ref.shape[0] * ref.shape[2], ref.shape[3])


def send_halo(z, shape, whole, top, bottom):
    t, h, w = shape
    four = z.reshape(t, h, w, z.shape[1])
    whole[...] = z.astype(BF16)
    top[...] = four[:, 0].reshape(t * w, z.shape[1]).astype(BF16)
    bottom[...] = four[:, h - 1].reshape(t * w, z.shape[1]).astype(BF16)


def fill_padded(pad, shape, own, above, below, others, has_left, has_right):
    t, h, w = shape
    c = own.shape[1]
    pad[:, 1 : h + 1, w : 2 * w, :] = own.reshape(t, h, w, c)
    pad[:, 0, w : 2 * w, :] = above.reshape(t, w, c)
    pad[:, h + 1, w : 2 * w, :] = below.reshape(t, w, c)
    o_above, o_own, o_below = others
    for start, has in ((0, has_left), (2 * w, has_right)):
        pad[:, 1 : h + 1, start : start + w, :] = (o_own * has).reshape(t, h, w, c)
        pad[:, 0, start : start + w, :] = (o_above * has).reshape(t, w, c)
        pad[:, h + 1, start : start + w, :] = (o_below * has).reshape(t, w, c)


def tap(pad, shape, a, b):
    t, h, w = shape
    part = pad[:, a : a + h, w - 1 + b : 2 * w - 1 + b, :]
    return part.reshape(t * h * w, part.shape[-1]).astype(BF16)


def activate_padded(pad, shape, norm, own, halo_refs, sf):
    def act(z):
        return silu(norm.out(z.astype(F32))).astype(BF16).astype(F32)

    above, below, o_above, o_own, o_below = (act(ref[...]) for ref in halo_refs)
    has_up, has_down = sf[2], sf[3]
    others = (o_above * has_up, o_own, o_below * has_down)
    fill_padded(pad, shape, act(own), above * has_up, below * has_down, others, sf[4], sf[5])


def fast_head(phases, shape, inside, lat_w, ft_band, fk_w, fb_out, zlat_out, zft_out, halo_out, zfk_out, pay, row):
    frame = shape[1] * shape[2]
    low = [v.astype(BF16) for v in phases]
    for p in range(ALPHA):
        fb_out[:, p * DF : (p + 1) * DF] = low[p]
    before2, before3, after0 = down(low[2], frame), down(low[3], frame), up(low[0], frame)
    z = (
        dot(before2, lat_w[0, 0])
        + dot(before3, lat_w[0, 1])
        + dot(low[0], lat_w[0, 2])
        + dot(low[1], lat_w[0, 3])
        + dot(low[2], lat_w[0, 4])
    )
    zlat_out[...] = z
    total, square = moments(z, inside[:, :DL])
    put_rows(pay, row, total)
    put_rows(pay, row + 2, square)
    six = [before3] + low + [after0]
    z = dot(six[0], ft_band[0])
    for j in range(1, 6):
        z = z + dot(six[j], ft_band[j])
    zft_out[...] = z
    send_halo(z, shape, *halo_out)
    total, square = moments(z, inside[:, :LANES])
    put_rows(pay, row + 4, total)
    put_rows(pay, row + 5, square)
    total, square = 0.0, 0.0
    for p in range(ALPHA):
        z = dot(low[p], fk_w[0])
        zfk_out[:, p * DF : (p + 1) * DF] = z
        one, two = moments(z, inside[:, :LANES])
        total, square = total + one, square + two
    put_rows(pay, row + 6, total)
    put_rows(pay, row + 7, square)


def place_columns(p):
    row = lax.broadcasted_iota(jnp.int32, (BF, LANES), 0)
    column = lax.broadcasted_iota(jnp.int32, (BF, LANES), 1)
    return jnp.where(column == row + BF * p, 1.0, 0.0).astype(BF16)


def kernel_start(shape, si, sf, fast, lat_w, ft_w, fk_w, fb, zlat, zft, z16, top, bottom, zfk, pay, ft_band):
    t, h, w = shape
    inside = inside_rows(t * h * w, DL, si[0])
    places = [place_columns(p) for p in range(ALPHA)]
    for l in range(LAYERS):
        for j in range(6):
            part = 0.0
            for p in range(ALPHA):
                if 0 <= j - p <= 2:
                    part = part + dot(ft_w[l, j - p], places[p])
            ft_band[l, j] = part.astype(BF16)
    fast_head(
        [phase(fast, p) for p in range(ALPHA)],
        shape, inside, lat_w, ft_band.at[0], fk_w, fb, zlat, zft, (z16, top, bottom), zfk, pay, 0,
    )


def lane(shape):
    return lax.broadcasted_iota(jnp.int32, shape, len(shape) - 1)


def kernel_prepare(gains, biases, fs_w, fe_w, gb, fs_bd, fe_bd):
    for i, source in enumerate((gains, biases)):
        for l in range(LAYERS):
            for r in range(22):
                gb[l, i, r : r + 1, :] = source[l : l + 1, r * LANES : (r + 1) * LANES]
            v = source[l : l + 1, 22 * LANES : 23 * LANES]
            v2 = source[l : l + 1, 23 * LANES : 24 * LANES]
            v3 = jnp.concatenate([source[l : l + 1, 24 * LANES :], jnp.zeros((1, 64), F32)], axis=1)
            place = lane((1, LANES))
            gb[l, i, FTM : FTM + 1, :] = fold_phases(jnp.where(place < 32, v, 0.0))
            gb[l, i, FSP : FSP + 1, :] = fold_phases(jnp.where((place >= 32) & (place < 64), v, 0.0))
            v, v2, v3 = (pltpu.roll(x, 64, 1) for x in (v, v2, v3))
            gb[l, i, FEX : FEX + 1, :] = jnp.where(place < 64, v, v2)
            gb[l, i, FSK : FSK + 1, :] = jnp.where(place < 64, v2, v3)
            gb[l, i, 26:32, :] = jnp.zeros((6, LANES), F32)
    row = lax.broadcasted_iota(jnp.int32, (LANES, LANES), 0)
    column = lane((LANES, LANES))
    same = (row // BF) == (column // BF)
    spread_columns = 0.0
    for p in range(ALPHA):
        spread_columns = spread_columns + place_columns(p).astype(F32)
    spread_columns = spread_columns.astype(BF16)
    for l in range(LAYERS):
        for a in range(3):
            for b in range(3):
                part = dot(fs_w[l, a, b], spread_columns).astype(BF16)
                fs_bd[l, a, b] = jnp.where(same, dot_tn(spread_columns, part), 0.0).astype(BF16)
        fe_bd[l] = jnp.zeros((LANES, ALPHA * DF), BF16)
        for p in range(ALPHA):
            fe_bd[l, p * BF : (p + 1) * BF, p * DF : (p + 1) * DF] = fe_w[l]


def kernel_temporal(first, shape, si, sf, *refs):
    t, h, w = shape
    rows, frame = t * h * w, h * w
    if first:
        (recv, slow, gb, zlat, zft, h1, h2, h3, h4, h5, st_w, sk_w, fs_bd,
         low_out, zst, z16, top, bottom, zsk, af9, zfs, pay, pad) = refs
        row = 0
        total = recv[...]
    else:
        (recv, gb_before, tot_sk, zse_in, zsk_in, gb, zlat, zft, h1, h2, h3, h4, h5, st_w, sk_w, fs_bd,
         low_out, zst, z16, top, bottom, zsk, af9, zfs, pay, pad) = refs
        row = 16
        total = recv[...]
        inside = inside_rows(rows, 256, si[0])
        one = Norm(total, 0, gb_before, SEX, 8, sf[0])
        two = Norm(tot_sk[...], 8, gb_before, SSK, 8, sf[0])
        for c in range(0, DS, 256):
            u = one.columns(c, 256).out(zse_in[:, c : c + 256]) + two.columns(c, 256).out(zsk_in[:, c : c + 256])
            low_out[:, c : c + 256] = jnp.where(inside, silu(u), 0.0).astype(BF16)
    inside = inside_rows(rows, 256, si[0])
    lat = Norm(total, row, gb, LAT, 2, sf[0])
    ft = Norm(fold_phases(total), row + 4, gb, FTM, 1, sf[1])
    if first:
        low_out[:, :DS] = slow[...].astype(BF16)
    low_out[:, DS:] = silu(lat.out(zlat[...])).astype(BF16)
    activate_padded(pad, shape, ft, zft[...], (h1, h2, h3, h4, h5), sf)
    low = low_out[...]
    z = dot(low, st_w[0, 1])
    z = z + down(dot(low, st_w[0, 0]), frame)
    z = z + up(dot(low, st_w[0, 2]), frame)
    zst[...] = z
    send_halo(z, shape, z16, top, bottom)
    one, two = moments(z, inside)
    put_rows(pay, 0, one)
    put_rows(pay, 2, two)
    for a in range(3):
        for b in range(3):
            k = 3 * a + b
            af9[:, k * LANES : (k + 1) * LANES] = tap(pad, shape, a, b)
    z = dot(af9[...], fs_bd[...].reshape(9 * LANES, LANES))
    zfs[...] = z
    one, two = moments(z, inside[:, :LANES])
    put_rows(pay, 4, one)
    put_rows(pay, 5, two)
    pay[6:8, :] = jnp.zeros((2, LANES), F32)
    for c in range(0, DS, 256):
        z = dot(low, sk_w[0, :, c : c + 256])
        zsk[:, c : c + 256] = z
        one, two = moments(z, inside)
        put_rows(pay, 8 + c // LANES, one)
        put_rows(pay, 16 + c // LANES, two)


def kernel_spatial(shape, si, sf, recv, gb, zst, h1, h2, h3, h4, h5, zfs, ss_w, fe_bd,
                   a9, zss, bf, zfe, pay, pad):
    t, h, w = shape
    inside = inside_rows(t * h * w, 256, si[0])
    total = recv[...]
    st = Norm(total, 0, gb, STM, 2, sf[0])
    fs = Norm(fold_phases(total), 4, gb, FSP, 1, sf[1])
    activate_padded(pad, shape, st, zst[...], (h1, h2, h3, h4, h5), sf)
    for a in range(3):
        for b in range(3):
            k = 3 * a + b
            a9[:, k * BS : (k + 1) * BS] = tap(pad, shape, a, b)
    z = dot(a9[...], ss_w[...].reshape(9 * BS, BS))
    zss[...] = z
    one, two = moments(z, inside)
    put_rows(pay, 0, one)
    put_rows(pay, 2, two)
    low = silu(fs.out(zfs[...])).astype(BF16)
    bf[...] = low
    total, square = 0.0, 0.0
    for p in range(ALPHA):
        z = dot(low, fe_bd[:, p * DF : (p + 1) * DF])
        zfe[:, p * DF : (p + 1) * DF] = z
        one, two = moments(z, inside[:, :LANES])
        total, square = total + one, square + two
    put_rows(pay, 4, total)
    put_rows(pay, 5, square)
    pay[6:8, :] = jnp.zeros((2, LANES), F32)


def kernel_expand(last, shape, si, sf, *refs):
    t, h, w = shape
    inside = inside_rows(t * h * w, 256, si[0])
    if last:
        recv, gb, zss, se_w, bt, zse, pay = refs
    else:
        (recv, gb, zss, se_w, tot_fk, zfe, zfk, lat_w, ft_band, fk_w,
         bt, zse, pay, fb, zlat, zft, z16, top, bottom, zfk_out) = refs
    total = recv[...]
    ss = Norm(total, 0, gb, SSP, 2, sf[0])
    low = silu(ss.out(zss[...])).astype(BF16)
    bt[...] = low
    for c in range(0, DS, 256):
        z = dot(low, se_w[0, :, c : c + 256])
        zse[:, c : c + 256] = z
        one, two = moments(z, inside)
        put_rows(pay, c // LANES, one)
        put_rows(pay, 8 + c // LANES, two)
    if not last:
        fe = Norm(total, 4, gb, FEX, 1, sf[1])
        fk = Norm(tot_fk[...], tot_fk.shape[0] - 2, gb, FSK, 1, sf[1])
        phases = []
        for p in range(ALPHA):
            cols = slice(p * DF, (p + 1) * DF)
            u = fe.out(zfe[:, cols]) + fk.out(zfk[:, cols])
            phases.append(jnp.where(inside[:, :LANES], silu(u), 0.0))
        fast_head(
            phases, shape, inside, lat_w, ft_band, fk_w, fb, zlat, zft, (z16, top, bottom), zfk_out, pay, 16
        )


def top_of_block(shape, si, sf, se, sk, fe, fk, zse, zsk, zfe, zfk, slow_grad, fast_grad, du_s, du_f, pay, outs):
    t, h, w = shape
    inside = inside_rows(t * h * w, 256, si[0])
    for c in range(0, DS, 256):
        cols = slice(c, c + 256)
        one, two = se.columns(c, 256), sk.columns(c, 256)
        hat1, hat2 = one.hat(zse[:, cols]), two.hat(zsk[:, cols])
        u = one.gain * hat1 + one.bias + (two.gain * hat2 + two.bias)
        act, rate = silu_and_slope(u)
        if outs is not None:
            outs[0][:, cols] = jnp.where(inside, act, 0.0)
        du = jnp.where(inside, slow_grad(cols) * rate, 0.0)
        du_s[:, cols] = du
        put_rows(pay, c // LANES, col_sum(du))
        put_rows(pay, 8 + c // LANES, col_sum(du * hat1))
        put_rows(pay, 16 + c // LANES, col_sum(du * hat2))
    sums = [0.0, 0.0, 0.0]
    for p in range(ALPHA):
        cols = slice(p * DF, (p + 1) * DF)
        hat1, hat2 = fe.hat(zfe[:, cols]), fk.hat(zfk[:, cols])
        u = fe.gain * hat1 + fe.bias + (fk.gain * hat2 + fk.bias)
        act, rate = silu_and_slope(u)
        if outs is not None:
            outs[1][:, p] = jnp.where(inside[:, :LANES], act, 0.0).reshape(t, h * w, DF)
        du = jnp.where(inside[:, :LANES], fast_grad(p) * rate, 0.0)
        du_f[:, cols] = du
        sums = [sums[0] + col_sum(du), sums[1] + col_sum(du * hat1), sums[2] + col_sum(du * hat2)]
    for i in range(3):
        put_rows(pay, 24 + i, sums[i])
    pay[27:32, :] = jnp.zeros((5, LANES), F32)


def kernel_turn(shape, si, sf, recv, gb, tot_sk, tot_fk, tot_fe, zse, zsk, zfe, zfk, slow_cot, fast_cot,
                out_slow, out_fast, du_s, du_f, pay):
    total = recv[...]
    top_of_block(
        shape, si, sf,
        Norm(total, 0, gb, SEX, 8, sf[0]),
        Norm(tot_sk[...], 8, gb, SSK, 8, sf[0]),
        Norm(tot_fe[...], 4, gb, FEX, 1, sf[1]),
        Norm(tot_fk[...], tot_fk.shape[0] - 2, gb, FSK, 1, sf[1]),
        zse, zsk, zfe, zfk,
        lambda cols: slow_cot[:, cols],
        lambda p: phase(fast_cot, p),
        du_s, du_f, pay, (out_slow, out_fast),
    )


def kernel_back_expand(shape, si, sf, recv, gb, tot_se, tot_sk, tot_ss, tot_fk, zse, zsk, zss, zfe, zfk, zfs,
                       du_s, du_f, se_w, fe_bd,
                       dz_se, dz_sk, dz_fe, dz_fk, dy_ss, dy_fs, pay):
    t, h, w = shape
    inside = inside_rows(t * h * w, 256, si[0])
    total = recv[...]
    inv, inv_f = sf[0], sf[1]
    se = Norm(tot_se[...], 0, gb, SEX, 8, inv)
    sk = Norm(tot_sk[...], 8, gb, SSK, 8, inv)
    ss = Norm(tot_ss[...], 0, gb, SSP, 2, inv)
    fe = Norm(tot_ss[...], 4, gb, FEX, 1, inv_f)
    fk = Norm(tot_fk[...], tot_fk.shape[0] - 2, gb, FSK, 1, inv_f)
    fs = Norm(fold_phases(tot_sk[...]), 4, gb, FSP, 1, inv_f)
    back = 0.0
    for c in range(0, DS, 256):
        cols = slice(c, c + 256)
        r = c // LANES
        du = du_s[:, cols]
        a_sum = wide(total, r, 2)
        one, two = se.columns(c, 256), sk.columns(c, 256)
        dz = one.back(du, one.hat(zse[:, cols]), inside, a_sum, wide(total, 8 + r, 2), inv).astype(BF16)
        dz_se[:, cols] = dz
        back = back + dot_nt(dz, se_w[0, :, cols])
        dz_sk[:, cols] = two.back(du, two.hat(zsk[:, cols]), inside, a_sum, wide(total, 16 + r, 2), inv).astype(BF16)
    dy = back * slope(ss.out(zss[...]))
    dy_ss[...] = dy
    put_rows(pay, 0, col_sum(dy))
    put_rows(pay, 2, col_sum(dy * ss.hat(zss[...])))
    back = 0.0
    for p in range(ALPHA):
        cols = slice(p * DF, (p + 1) * DF)
        du = du_f[:, cols]
        a_sum = wide(total, 24, 1)
        dz = fe.back(du, fe.hat(zfe[:, cols]), inside[:, :LANES], a_sum, wide(total, 25, 1), inv_f).astype(BF16)
        dz_fe[:, cols] = dz
        back = back + dot_nt(dz, fe_bd[:, cols])
        dz_fk[:, cols] = fk.back(
            du, fk.hat(zfk[:, cols]), inside[:, :LANES], a_sum, wide(total, 26, 1), inv_f
        ).astype(BF16)
    dy = back * slope(fs.out(zfs[...]))
    dy_fs[...] = dy
    put_rows(pay, 4, col_sum(dy))
    put_rows(pay, 5, col_sum(dy * fs.hat(zfs[...])))
    pay[6:8, :] = jnp.zeros((2, LANES), F32)


def kernel_back_spatial_in(shape, si, sf, recv, gb, tot_ss, tot_sk, zss, zfs, dy_ss, dy_fs,
                           dz, top, bottom):
    t, h, w = shape
    inside = inside_rows(t * h * w, 256, si[0])
    total = recv[...]
    folded = fold_phases(total)
    ss = Norm(tot_ss[...], 0, gb, SSP, 2, sf[0])
    fs = Norm(fold_phases(tot_sk[...]), 4, gb, FSP, 1, sf[1])
    one = ss.back(dy_ss[...], ss.hat(zss[...]), inside, wide(total, 0, 2), wide(total, 2, 2), sf[0])
    two = fs.back(
        dy_fs[...], fs.hat(zfs[...]), inside[:, :LANES], wide(folded, 4, 1), wide(folded, 5, 1), sf[1]
    )
    send_halo(jnp.concatenate([one, two], axis=1), shape, dz, top, bottom)


def kernel_back_spatial(shape, si, sf, gb, tot_st, tot_ft, zst, zft, dz, h1, h2, h3, h4, h5, ss_w, fs_bd,
                        dy_st, dy_ft, pay, pad):
    above, below, *others = (ref[...].astype(F32) for ref in (h1, h2, h3, h4, h5))
    fill_padded(pad, shape, dz[...].astype(F32), above, below, others, sf[4], sf[5])
    st = Norm(tot_st[...], 0, gb, STM, 2, sf[0])
    ft = Norm(fold_phases(tot_ft[...]), tot_ft.shape[0] - 4, gb, FTM, 1, sf[1])
    back, back_f = 0.0, 0.0
    for a in range(3):
        for b in range(3):
            part = tap(pad, shape, 2 - a, 2 - b)
            back = back + dot_nt(part[:, :BS], ss_w[0, a, b])
            back_f = back_f + dot_nt(part[:, BS:], fs_bd[a, b])
    dy = back * slope(st.out(zst[...]))
    dy_st[...] = dy
    put_rows(pay, 0, col_sum(dy))
    put_rows(pay, 2, col_sum(dy * st.hat(zst[...])))
    dy = back_f * slope(ft.out(zft[...]))
    dy_ft[...] = dy
    put_rows(pay, 4, col_sum(dy))
    put_rows(pay, 5, col_sum(dy * ft.hat(zft[...])))
    pay[6:8, :] = jnp.zeros((2, LANES), F32)


def kernel_back_skip(dz_sk, sk_w, dlow):
    for k in range(0, CC, 256):
        dlow[:, k : k + 256] = dot_nt(dz_sk[...], sk_w[0, k : k + 256, :])


def kernel_back_temporal(shape, si, sf, recv, gb, tot_lat, tot_st, zst, zft, zlat, dy_st, dy_ft, dlow,
                         dz_fk, st_w, ft_band, fk_w,
                         dz_st, dz_ft, dslow, dfast, dy_lat, pay):
    t, h, w = shape
    rows, frame = t * h * w, h * w
    inside = inside_rows(rows, 256, si[0])
    total = recv[...]
    folded = fold_phases(total)
    st = Norm(tot_st[...], 0, gb, STM, 2, sf[0])
    base = tot_lat.shape[0] - 8
    ft = Norm(fold_phases(tot_lat[...]), base + 4, gb, FTM, 1, sf[1])
    lat = Norm(tot_lat[...], base, gb, LAT, 2, sf[0])
    dz = st.back(
        dy_st[...], st.hat(zst[...]), inside, wide(total, 0, 2), wide(total, 2, 2), sf[0]
    ).astype(BF16)
    dz_st[:, :BS] = up(dz, frame)
    dz_st[:, BS : 2 * BS] = dz
    dz_st[:, 2 * BS :] = down(dz, frame)

    def back(k):
        cols = slice(k, k + 256)
        part = dlow[:, cols]
        for j in range(3):
            part = part + dot_nt(dz_st[:, j * BS : (j + 1) * BS], st_w[0, j, cols, :])
        return part

    dy = back(DS) * slope(lat.out(zlat[...]))
    dy_lat[...] = dy
    put_rows(pay, 0, col_sum(dy))
    put_rows(pay, 2, col_sum(dy * lat.hat(zlat[...])))
    pay[4:8, :] = jnp.zeros((4, LANES), F32)
    for k in range(0, DS, 256):
        dslow[:, k : k + 256] = back(k)
    dzf = ft.back(
        dy_ft[...], ft.hat(zft[...]), inside[:, :LANES], wide(folded, 4, 1), wide(folded, 5, 1), sf[1]
    ).astype(BF16)
    dz_ft[...] = dzf
    for p in range(ALPHA):
        part = dot_nt(dz_fk[:, p * DF : (p + 1) * DF], fk_w[0]) + dot_nt(dzf, ft_band[p + 1])
        if p == ALPHA - 1:
            part = part + up(dot_nt(dzf, ft_band[0]), frame)
        if p == 0:
            part = part + down(dot_nt(dzf, ft_band[5]), frame)
        dfast[:, p * DF : (p + 1) * DF] = part


def kernel_back_lateral(last, shape, si, sf, *refs):
    t, h, w = shape
    rows, frame = t * h * w, h * w
    if last:
        recv, gb, tot_lat, zlat, dy_lat, dfast, lat_w, dz_lat, dfast_out = refs
    else:
        (recv, gb, tot_lat, zlat, dy_lat, dfast, lat_w,
         gb_below, tot_se, tot_sk, tot_fe, tot_fk, zse, zsk, zfe, zfk, dslow,
         dz_lat, du_s, du_f, pay) = refs
    inside = inside_rows(rows, 256, si[0])
    total = recv[...]
    lat = Norm(tot_lat[...], tot_lat.shape[0] - 8, gb, LAT, 2, sf[0])
    dz = lat.back(
        dy_lat[...], lat.hat(zlat[...]), inside, wide(total, 0, 2), wide(total, 2, 2), sf[0]
    ).astype(BF16)
    dz_lat[...] = dz

    def fast_grad(p):
        part = dfast[:, p * DF : (p + 1) * DF]
        if p < 3:
            part = part + dot_nt(dz, lat_w[0, p + 2])
        if p >= 2:
            part = part + up(dot_nt(dz, lat_w[0, p - 2]), frame)
        return part

    if last:
        for p in range(ALPHA):
            dfast_out[:, p] = fast_grad(p).reshape(t, frame, DF)
    else:
        top_of_block(
            shape, si, sf,
            Norm(tot_se[...], 0, gb_below, SEX, 8, sf[0]),
            Norm(tot_sk[...], 8, gb_below, SSK, 8, sf[0]),
            Norm(tot_fe[...], 4, gb_below, FEX, 1, sf[1]),
            Norm(tot_fk[...], tot_fk.shape[0] - 2, gb_below, FSK, 1, sf[1]),
            zse, zsk, zfe, zfk, lambda cols: dslow[:, cols], fast_grad, du_s, du_f, pay, None,
        )


SMALL_ROWS = 64


def turned(i, count):
    out = 0
    while count > 1:
        out, i, count = 2 * out + i % 2, i // 2, count // 2
    return out


def part_tiles(si, tiles, low_first, ref, keep, send):
    side = si[2]
    for i in range(tiles // 2):
        place = turned(i, tiles // 2) if low_first else i
        keep[place] = ref[2 * i + side]
        send[place] = ref[2 * i + 1 - side]


def kernel_weights_one(tiles, si, low, bt, dz_se, dz_sk, keep, send, blocks):
    ksk, kse = CC // tiles, BS // tiles
    for j in range(4):
        cols = slice(j * 256, (j + 1) * 256)
        d = dot_tn(low[...], dz_sk[:, cols]).astype(BF16)
        blocks[:, j, :ksk, :] = d.reshape(tiles, ksk, 256)
        d = dot_tn(bt[...], dz_se[:, cols]).astype(BF16)
        blocks[:, j, ksk:, :] = d.reshape(tiles, kse, 256)
    part_tiles(si, tiles, True, blocks, keep, send)


def pick_phases(parts):
    place = lane(parts[0].shape) // BF
    return fold_phases(sum(jnp.where(place == p, part, 0.0) for p, part in enumerate(parts)))


def kernel_weights_two(tiles, frame, si, low, a9, af9, fb, bf, dz_s, dz_st, dz_ft, dz_lat, dz_fe, dz_fk,
                       keep, send, blocks, small):
    kst, kss, kla, ksm = CC // tiles, BS // tiles, DF // tiles, BF // tiles
    for j in range(3):
        d = dot_tn(low[...], dz_st[:, j * BS : (j + 1) * BS]).astype(BF16)
        blocks[:, j * kst : (j + 1) * kst, :] = d.reshape(tiles, kst, BS)
    base = 3 * kst
    small[...] = jnp.zeros(small.shape, F32)
    for k in range(9):
        d = dot_tn(a9[:, k * BS : (k + 1) * BS], dz_s[:, :BS]).astype(BF16)
        blocks[:, base + k * kss : base + (k + 1) * kss, :] = d.reshape(tiles, kss, BS)
        d = dot_tn(af9[:, k * LANES : (k + 1) * LANES], dz_s[:, BS:])
        d = pick_phases([d[p * BF : (p + 1) * BF] for p in range(ALPHA)])
        for i in range(tiles):
            small[i, k * ksm : (k + 1) * ksm, LANES:] = d[i * ksm : (i + 1) * ksm]
    base += 9 * kss
    f = [fb[:, p * DF : (p + 1) * DF] for p in range(ALPHA)]
    five = [down(f[2], frame), down(f[3], frame), f[0], f[1], f[2]]
    for k in range(5):
        d = dot_tn(five[k], dz_lat[...]).astype(BF16)
        blocks[:, base + k * kla : base + (k + 1) * kla, :] = d.reshape(tiles, kla, DL)
    base += 5 * kla
    six = [five[1]] + f + [up(f[0], frame)]
    six = [dot_tn(x, dz_ft[...]) for x in six]
    for k in range(3):
        d = pick_phases([six[k + p] for p in range(ALPHA)])
        small[:, k * kla : (k + 1) * kla, :LANES] = d.reshape(tiles, kla, LANES)
    fe, fk = 0.0, 0.0
    for p in range(ALPHA):
        cols = slice(p * DF, (p + 1) * DF)
        fk = fk + dot_tn(fb[:, cols], dz_fk[:, cols])
        fe = fe + dot_tn(bf[...], dz_fe[:, cols])[p * BF : (p + 1) * BF, :]
    for i in range(tiles):
        small[i, 9 * ksm : 10 * ksm, LANES:] = fe[i * ksm : (i + 1) * ksm]
        small[i, 10 * ksm : 10 * ksm + kla, LANES:] = fk[i * kla : (i + 1) * kla]
    end = blocks.shape[1] - SMALL_ROWS
    if end > base:
        blocks[:, base:end, :] = jnp.zeros((tiles, end - base, 256), BF16)
    blocks[:, end:, :] = small[...].astype(BF16)
    part_tiles(si, tiles, False, blocks, keep, send)


def add(one, two):
    return (one.astype(F32) + two.astype(F32)).astype(BF16)


def kernel_halve(slot, step, si, kept, got, keep, send):
    half = keep.shape[0]
    bit = (si[slot] // step) % 2
    for i in range(half):
        keep[i] = add(kept[bit * half + i], got[bit * half + i])
        other = (1 - bit) * half + i
        send[i] = add(kept[other], got[other])


def columns_of(x, j):
    half = x.shape[0] // 2
    base = (j // 2) * LANES
    a, b = x[:half, base : base + LANES], x[half:, base : base + LANES]
    left = lane(a.shape) < 64
    if j % 2 == 0:
        return jnp.where(left, a, pltpu.roll(b, 64, 1))
    return jnp.where(left, pltpu.roll(a, 64, 1), b)


def kernel_halve_columns(si, kept, got, keep, send, planes):
    big = kept.shape[1] - SMALL_ROWS
    total = kept[0].astype(F32) + got[0].astype(F32)
    packed = big // 2
    for j in range(4):
        planes[j] = columns_of(total[:big], j).astype(BF16)
    bit = si[3] // 2
    small = total[big:].astype(BF16)
    for ref, start in ((keep, bit * 2), (send, (1 - bit) * 2)):
        for i in range(2):
            ref[i * packed : (i + 1) * packed, :] = planes[start + i]
        ref[2 * packed : 2 * packed + SMALL_ROWS, :] = small[:, :LANES]
        ref[2 * packed + SMALL_ROWS :, :] = small[:, LANES:]


def kernel_halve_planes(si, kept, got, keep, send):
    packed = (kept.shape[0] - 2 * SMALL_ROWS) // 2
    bit = si[3] % 2
    small = add(kept[2 * packed :, :], got[2 * packed :, :])
    for ref, place in ((keep, bit), (send, 1 - bit)):
        start = pl.multiple_of(place * packed, 16)
        ref[:packed, :] = add(kept[pl.ds(start, packed), :], got[pl.ds(start, packed), :])
        ref[packed:, :] = small


def kernel_add(one, two, out):
    out[...] = add(one[...], two[...])


def kernel_finish(tiles, si, *refs):
    kst, kss, kla, ksm = CC // tiles, BS // tiles, DF // tiles, BF // tiles
    inputs, outs = refs[: 4 * LAYERS], refs[4 * LAYERS :]
    g_lat, g_st, g_ss, g_se, g_sk, g_ft, g_fs, g_fe, g_fk = outs
    for l in range(LAYERS):
        kept1, got1, kept2, got2 = inputs[4 * l : 4 * (l + 1)]
        planes = kept1[0].astype(F32) + got1[0].astype(F32)
        g_sk[l] = planes[:kst]
        g_se[l] = planes[kst:]
        total = kept2[...].astype(F32) + got2[...].astype(F32)
        packed = total.shape[0] - 2 * SMALL_ROWS
        rows = [total[:packed, :64], pltpu.roll(total[:packed], 64, 1)[:, :64]]

        def part(start, size):
            end = start + size
            if end <= packed:
                return rows[0][start:end]
            if start >= packed:
                return rows[1][start - packed : end - packed]
            return jnp.concatenate([rows[0][start:], rows[1][: end - packed]], axis=0)

        for k in range(3):
            g_st[l, k] = part(k * kst, kst)
        for k in range(9):
            g_ss[l, k // 3, k % 3] = part(3 * kst + k * kss, kss)
        for k in range(5):
            g_lat[l, k] = part(3 * kst + 9 * kss + k * kla, kla)
        small = total[packed : packed + SMALL_ROWS]
        eight = pltpu.roll(small, (LANES - 8 * si[3]) % LANES, 1)[:, :8]
        for k in range(3):
            g_ft[l, k] = eight[k * kla : (k + 1) * kla]
        small = total[packed + SMALL_ROWS :]
        eight = pltpu.roll(small, (LANES - 8 * si[3]) % LANES, 1)[:, :8]
        for k in range(9):
            g_fs[l, k // 3, k % 3] = eight[k * ksm : (k + 1) * ksm]
        part32 = pltpu.roll(small, (LANES - 32 * si[3]) % LANES, 1)[:, :32]
        g_fe[l] = part32[9 * ksm : 10 * ksm]
        g_fk[l] = part32[10 * ksm : 10 * ksm + kla]


def kernel_norm_sums(*refs):
    d_gains, d_biases = refs[4 * LAYERS :]
    for l in range(LAYERS):
        one, two, three, four = refs[4 * l : 4 * (l + 1)]
        for i, out in ((0, d_biases), (1, d_gains)):
            vectors = [
                (four, 2 * i, 2), (three, 2 * i, 2), (two, 2 * i, 2), (one, 8 * i, 8), (one, 16 * i, 8),
            ]
            column = 0
            for ref, row, count in vectors:
                for r in range(row, row + count):
                    out[l : l + 1, column : column + LANES] = ref[r : r + 1, :]
                    column += LANES
            ft, fs = fold_phases(three[4 + i : 5 + i, :]), fold_phases(two[4 + i : 5 + i, :])
            fe = pltpu.roll(one[24 + i : 25 + i, :], 64, 1)
            fk = pltpu.roll(one[24 + 2 * i : 25 + 2 * i, :], 64, 1)
            place = lane((1, LANES))
            out[l : l + 1, column : column + LANES] = jnp.where(place < 32, ft, jnp.where(place < 64, fs, fe))
            out[l : l + 1, column + LANES : column + 2 * LANES] = jnp.where(place < 64, fe, fk)
            out[l : l + 1, column + 2 * LANES :] = fk[:, :64]


SMEM = pltpu.MemorySpace.SMEM
VMEM = pltpu.MemorySpace.VMEM


class Weight:
    def __init__(self, array, layer):
        self.array = array
        self.layer = layer


class Layer:
    def __init__(self, array, layer):
        self.array = array
        self.layer = layer


class Load:
    def __init__(self, array):
        self.array = array


class Arriving:
    def __init__(self, copy, ref, layered):
        self.copy = copy
        self.ref = ref
        self.layered = layered
        self.shape = ref.shape

    def __getitem__(self, place):
        if self.copy is not None:
            self.copy.wait()
            self.copy = None
        if not self.layered:
            return self.ref[place]
        return self.ref[place[1:]] if isinstance(place, tuple) else self.ref[...]


class Out:
    def __init__(self, shape, kind):
        self.shape = shape
        self.kind = kind


def scalar_values(place, valid, frame, tiles):
    ha, wa, clip = place[0], place[1], place[2]
    total = valid[0]
    for i in range(1, valid.shape[0]):
        total = total + valid[i]
    count = jnp.full((1, LANES), total * (HT * WD), jnp.int32).astype(F32)
    inverse = 1.0 / count
    flags = [ha > 0, ha < tiles[0] - 1, wa > 0, wa < tiles[1] - 1]
    vectors = [jnp.where(jnp.full((1, LANES), jnp.where(f, 1, 0), jnp.int32) > 0, 1.0, 0.0) for f in flags]
    vectors = [inverse, inverse * (1.0 / ALPHA)] + vectors
    return (valid[clip] * frame, ha, wa, clip), [v[:, :1] for v in vectors]


def call(body, scalars, operands, outs, scratch=(), limit=16):
    mode, scalars = (None, ()) if not scalars else (scalars[0], scalars[1:3])
    count, first = len(operands), len(scalars)
    weights = [i for i, x in enumerate(operands) if isinstance(x, (Weight, Load))]
    results = [i for i, x in enumerate(outs) if isinstance(x, Out)]
    arrays = [x.array if isinstance(x, (Weight, Layer, Load)) else x for x in operands]
    layered = [isinstance(x, Weight) for x in operands]
    shapes = [(x.shape, x.kind) if isinstance(x, Out) else x for x in outs]
    buffers = [pltpu.VMEM(arrays[i].shape[1:] if layered[i] else arrays[i].shape, arrays[i].dtype) for i in weights]
    buffers += [pltpu.VMEM(*shapes[i]) for i in results]
    own = first + count + len(outs)

    def wrapped(*refs):
        refs = list(refs)
        inner, rest = refs[own : own + len(buffers)], refs[own + len(buffers) :]
        arriving, leaving = [], []
        for n, i in enumerate(weights):
            source = refs[first + i].at[operands[i].layer] if layered[i] else refs[first + i]
            copy = pltpu.make_async_copy(source, inner[n], rest[-1].at[n])
            copy.start()
            refs[first + i] = Arriving(copy, inner[n], layered[i])
            arriving.append(refs[first + i])
        for i, x in enumerate(operands):
            if isinstance(x, Layer):
                refs[first + i] = refs[first + i].at[x.layer]
        for n, i in enumerate(results):
            n += len(weights)
            leaving.append(pltpu.make_async_copy(inner[n], refs[first + count + i], rest[-1].at[n]))
            refs[first + count + i] = inner[n]
        given = ()
        if mode is not None:
            t_frame, tiles = mode[1], mode[2]
            ints, vectors = scalar_values(refs[0], refs[1], t_frame, tiles) if mode[0] == "all" else (
                (None, refs[0][0], refs[0][1], refs[0][2]), None)
            given = (ints, vectors) if mode[0] == "all" else (ints,)
        body(*given, *refs[first:own], *(rest[:-1] if buffers else rest))
        for copy in leaving:
            copy.start()
        for one in arriving:
            if one.copy is not None:
                one.copy.wait()
        for copy in leaving:
            copy.wait()

    def space(i, some):
        return pl.BlockSpec(memory_space=pl.ANY if i in some else VMEM)

    return pl.pallas_call(
        wrapped,
        out_shape=[jax.ShapeDtypeStruct(shape, kind) for shape, kind in shapes],
        in_specs=[pl.BlockSpec(memory_space=SMEM) for _ in scalars] + [space(i, weights) for i in range(count)],
        out_specs=[space(i, results) for i in range(len(outs))],
        scratch_shapes=buffers
        + [pltpu.VMEM(shape, kind) for shape, kind in scratch]
        + ([pltpu.SemaphoreType.DMA((len(buffers),))] if buffers else []),
        cost_estimate=pl.CostEstimate(flops=20000000000, bytes_accessed=80000000, transcendentals=0),
        compiler_params=pltpu.CompilerParams(vmem_limit_bytes=limit << 20),
    )(*scalars, *arrays)


def sum_all(x):
    for axis in ("wa", "ha", "clip"):
        step, count = 1, lax.axis_size(axis)
        while step < count:
            pair = x + flip(x, axis, step)
            if 4 * step <= count:
                pair = pair + (flip(x, axis, 2 * step) + flip(x, axis, 3 * step))
                step *= 2
            x = pair
            step *= 2
    return x


def swap(x):
    return lax.ppermute(x, "wa", [(0, 1), (1, 0)])


def halo(z, top, bottom):
    count = lax.axis_size("ha")
    above = lax.ppermute(bottom, "ha", [(i, i + 1) for i in range(count - 1)])
    below = lax.ppermute(top, "ha", [(i + 1, i) for i in range(count - 1)])
    return [above, below, swap(above), swap(z), swap(below)]


def after(first, *rest):
    return lax.optimization_barrier((first,) + rest)


def flip(x, axis, step):
    return lax.ppermute(x, axis, [(i, i ^ step) for i in range(lax.axis_size(axis))])


def local(
    slow_in,
    fast_in,
    valid_frames,
    lateral_w,
    slow_temporal_w,
    slow_spatial_w,
    slow_expand_w,
    slow_skip_w,
    fast_temporal_w,
    fast_spatial_w,
    fast_expand_w,
    fast_skip_w,
    gains,
    biases,
    slow_cot,
    fast_cot,
):
    clips, n_ha, n_wa = (lax.axis_size(a) for a in ALL_AXES)
    tiles = n_ha * n_wa
    _, t, h, w, _ = slow_in.shape
    shape = (t, h, w)
    frame = h * w
    rows = t * frame

    place = jnp.stack([lax.axis_index(a) for a in ("ha", "wa", "clip")]).astype(jnp.int32)
    scalars = (("all", frame, (n_ha, n_wa)), place, valid_frames)
    places = (("place", frame, (n_ha, n_wa)), place, valid_frames)

    slow2 = slow_in.reshape(rows, DS)
    fast4 = fast_in.reshape(t, ALPHA, frame, DF)
    slow_cot2 = slow_cot.reshape(rows, DS)
    fast_cot4 = fast_cot.reshape(t, ALPHA, frame, DF)

    def act(columns, kind=F32):
        return ((rows, columns), kind)

    def edges(columns):
        return [act(columns, BF16), ((t * w, columns), BF16), ((t * w, columns), BF16)]

    def pay(count):
        return ((count, LANES), F32)

    def bind(body, *static):
        return functools.partial(body, *static)

    pad_slow = ((t, h + 2, 3 * w, BS), F32)
    pad_fast = ((t, h + 2, 3 * w, LANES), F32)
    pad_both = ((t, h + 2, 3 * w, BS + LANES), F32)
    saved = []
    fb, zlat, zft, z16, top, bottom, zfk, sent, band = call(
        bind(kernel_start, shape),
        scalars,
        [Load(fast4), Weight(lateral_w, 0), Load(fast_temporal_w), Weight(fast_skip_w, 0)],
        [act(512, BF16), act(DL), act(LANES), *edges(LANES), act(512), pay(8), ((LAYERS, 6, LANES, LANES), BF16)],
    )
    recv = sum_all(sent)
    gb_all, fs_bd, fe_bd = call(
        kernel_prepare,
        (),
        [Load(gains), Load(biases), Load(fast_spatial_w), Load(fast_expand_w)],
        [((LAYERS, 2, GB_ROWS, LANES), F32), ((LAYERS, 3, 3, LANES, LANES), BF16), ((LAYERS, LANES, ALPHA * DF), BF16)],
    )
    gb = [Layer(gb_all, l) for l in range(LAYERS)]
    before = None
    for l in range(LAYERS):
        around = halo(z16, top, bottom)
        last = l == LAYERS - 1
        start = [recv, Load(slow2), gb[l]] if l == 0 else [recv, gb[l - 1], before["tot_sk"], before["zse"], before["zsk"], gb[l]]
        low, zst, z16, top, bottom, zsk, af9, zfs, sent = call(
            bind(kernel_temporal, l == 0, shape),
            scalars,
            start + [zlat, zft, *around, Weight(slow_temporal_w, l), Weight(slow_skip_w, l), Layer(fs_bd, l)],
            [act(CC, BF16), act(BS), *edges(BS), act(DS), act(9 * LANES, BF16), act(LANES), pay(24)],
            [pad_fast],
        )
        tot_lat = recv
        if l > 0:
            before["tot_se"] = tot_lat
        recv = sum_all(sent)
        around = halo(z16, top, bottom)
        a9, zss, bf, zfe, sent = call(
            bind(kernel_spatial, shape),
            scalars,
            [recv, gb[l], zst, *around, zfs, Weight(slow_spatial_w, l), Layer(fe_bd, l)],
            [act(9 * BS, BF16), act(BS), act(LANES, BF16), act(512), pay(8)],
            [pad_slow],
        )
        tot_st = recv
        recv = sum_all(sent)
        keep = dict(
            fb=fb, zlat=zlat, zft=zft, zfk=zfk, low=low, zst=zst, zsk=zsk, af9=af9, zfs=zfs, a9=a9, zss=zss, bf=bf,
            zfe=zfe, tot_lat=tot_lat, tot_fk=tot_lat, tot_st=tot_st, tot_sk=tot_st,
        )
        if last:
            bt, zse, sent = call(
                bind(kernel_expand, True, shape),
                scalars,
                [recv, gb[l], zss, Weight(slow_expand_w, l)],
                [act(BS, BF16), act(DS), pay(16)],
            )
        else:
            bt, zse, sent, fb, zlat, zft, z16, top, bottom, zfk = call(
                bind(kernel_expand, False, shape),
                scalars,
                [recv, gb[l], zss, Weight(slow_expand_w, l), tot_lat, zfe, zfk,
                 Weight(lateral_w, l + 1), Layer(band, l + 1), Weight(fast_skip_w, l + 1)],
                [act(BS, BF16), act(DS), pay(24),
                 act(512, BF16), act(DL), act(LANES), *edges(LANES), act(512)],
            )
        tot_ss = recv
        recv = sum_all(sent)
        keep.update(bt=bt, zse=zse, tot_ss=tot_ss, tot_fe=tot_ss)
        saved.append(keep)
        before = keep

    keep = saved[-1]
    keep["tot_se"] = recv
    out_slow, out_fast, du_s, du_f, sent = call(
        bind(kernel_turn, shape),
        scalars,
        [recv, gb[-1], keep["tot_sk"], keep["tot_fk"], keep["tot_fe"], keep["zse"], keep["zsk"], keep["zfe"],
         keep["zfk"], Load(slow_cot2), Load(fast_cot4)],
        [Out((rows, DS), F32), Out((t, ALPHA, frame, DF), F32), act(DS), act(512), pay(32)],
    )

    plane_rows = (CC + BS) // tiles
    rows_two = -(-((3 * CC + 9 * BS + 5 * DF) // tiles) // 32) * 32 + SMALL_ROWS
    packed = (rows_two - SMALL_ROWS) // 2

    def halve(body, keep, got, shape):
        return call(body, places, [keep, got], [(shape, BF16)] * 2)

    def halve_ha(keep, send, steps, block):
        got = swap(send)
        size = tiles // 2
        for step in steps:
            keep, got = yield keep, got
            size //= 2
            keep, send = halve(bind(kernel_halve, 1, step), keep, got, (size,) + block)
            got = flip(send, "ha", step)
        return (yield keep, got)

    descending = []
    while 2 ** (len(descending) + 1) <= n_ha:
        descending.insert(0, 2 ** len(descending))
    narrow = clips == 4

    def chain_one(keep, send):
        keep, got = yield from halve_ha(keep, send, descending[::-1], (4, plane_rows, 256))
        keep, got = (x.reshape(4, plane_rows, 256) for x in (keep, got))
        if narrow:
            keep, send = halve(bind(kernel_halve, 3, 2), keep, got, (2, plane_rows, 256))
            got = flip(send, "clip", 2)
            keep, got = yield keep, got
            keep, send = halve(bind(kernel_halve, 3, 1), keep, got, (1, plane_rows, 256))
            got = flip(send, "clip", 1)
        yield keep, got, True

    def chain_two(keep, send):
        keep, got = yield from halve_ha(keep, send, descending, (rows_two, 256))
        if narrow:
            keep, send = call(
                kernel_halve_columns,
                places,
                [keep, got],
                [((2 * packed + 2 * SMALL_ROWS, LANES), BF16)] * 2,
                [((4, packed, LANES), BF16)],
            )
            got = flip(send, "clip", 2)
            keep, got = yield keep, got
            keep, send = halve(kernel_halve_planes, keep, got, (packed + 2 * SMALL_ROWS, LANES))
            got = flip(send, "clip", 1)
        yield keep, got, True

    class Running:
        def __init__(self, chain):
            self.chain = chain
            self.state = next(chain)

        def done(self):
            return len(self.state) == 3

        def step(self, token=None):
            if self.done():
                return
            keep, got = self.state
            if token is not None:
                _, keep = after(token, keep)
            self.state = self.chain.send((keep, got))

    running = {}
    totals = [None] * LAYERS

    def advance(token):
        for chain in running.values():
            chain.step(token)

    for l in reversed(range(LAYERS)):
        k = saved[l]
        recv = sum_all(sent)
        tot_one = recv
        dz_se, dz_sk, dz_fe, dz_fk, dy_ss, dy_fs, sent = call(
            bind(kernel_back_expand, shape),
            scalars,
            [recv, gb[l], k["tot_se"], k["tot_sk"], k["tot_ss"], k["tot_fk"], k["zse"], k["zsk"], k["zss"], k["zfe"],
             k["zfk"], k["zfs"], du_s, du_f, Weight(slow_expand_w, l), Layer(fe_bd, l)],
            [act(DS, BF16), act(DS, BF16), act(512, BF16), act(512, BF16), act(BS), act(LANES), pay(8)],
        )
        recv = sum_all(sent)
        tot_two, late = recv, dz_sk
        dz, top, bottom = call(
            bind(kernel_back_spatial_in, shape),
            scalars,
            [recv, gb[l], k["tot_ss"], k["tot_sk"], k["zss"], k["zfs"], dy_ss, dy_fs],
            [*edges(BS + LANES)],
        )
        (dlow,) = call(kernel_back_skip, (), [late, Weight(slow_skip_w, l)], [act(CC)])
        one = call(
            bind(kernel_weights_one, tiles),
            places,
            [k["low"], k["bt"], dz_se, late],
            [((tiles // 2, 4, plane_rows, 256), BF16)] * 2,
            [((tiles, 4, plane_rows, 256), BF16)],
        )
        running[l, 0] = Running(chain_one(*one))
        around = halo(dz, top, bottom)
        dy_st, dy_ft, sent = call(
            bind(kernel_back_spatial, shape),
            scalars,
            [gb[l], k["tot_st"], k["tot_lat"], k["zst"], k["zft"], dz, *around,
             Weight(slow_spatial_w, l), Layer(fs_bd, l)],
            [act(BS), act(LANES), pay(8)],
            [pad_both],
        )
        recv = sum_all(sent)
        tot_three = recv
        dz_st, dz_ft, dslow, dfast, dy_lat, sent = call(
            bind(kernel_back_temporal, shape),
            scalars,
            [recv, gb[l], k["tot_lat"], k["tot_st"], k["zst"], k["zft"], k["zlat"], dy_st, dy_ft, dlow, dz_fk,
             Weight(slow_temporal_w, l), Layer(band, l), Weight(fast_skip_w, l)],
            [act(3 * BS, BF16), act(LANES, BF16), Out((rows, DS), F32) if l == 0 else act(DS), act(512), act(DL), pay(8)],
        )
        recv = sum_all(sent)
        tot_four = recv
        start = [recv, gb[l], k["tot_lat"], k["zlat"], dy_lat, dfast, Weight(lateral_w, l)]
        if l > 0:
            b = saved[l - 1]
            dz_lat, du_s, du_f, sent = call(
                bind(kernel_back_lateral, False, shape),
                scalars,
                start + [gb[l - 1], b["tot_se"], b["tot_sk"], b["tot_fe"], b["tot_fk"], b["zse"], b["zsk"], b["zfe"],
                         b["zfk"], dslow],
                [act(DL, BF16), act(DS), act(512), pay(32)],
            )
        else:
            dz_lat, grad_fast = call(
                bind(kernel_back_lateral, True, shape),
                scalars,
                start,
                [act(DL, BF16), Out((t, ALPHA, frame, DF), F32)],
            )
            grad_slow = dslow
        two = call(
            bind(kernel_weights_two, tiles, frame),
            places,
            [k["low"], k["a9"], k["af9"], k["fb"], k["bf"], dz, dz_st, dz_ft, dz_lat, dz_fe, dz_fk],
            [((tiles // 2, rows_two, 256), BF16)] * 2,
            [((tiles, rows_two, 256), BF16), ((tiles, SMALL_ROWS, 256), F32)],
            limit=24,
        )
        running[l, 1] = Running(chain_two(*two))
        totals[l] = [tot_one, tot_two, tot_three, tot_four]
    while not all(chain.done() for chain in running.values()):
        advance(None)
    nst, nss, nla, nsm = CC // tiles, BS // tiles, DF // tiles, BF // tiles
    n, f, g = BS // clips, BF // clips, DF // clips
    sums = call(kernel_norm_sums, (), totals[0] + totals[1], [Out(gains.shape, F32), Out(biases.shape, F32)])
    weights = [(LAYERS,) + dims for dims in (
        (5, nla, n), (3, nst, n), (3, 3, nss, n), (nss, DS // clips), (nst, DS // clips),
        (3, nla, f), (3, 3, nsm, f), (nsm, g), (nla, g),
    )]
    if narrow:
        parts = [x for l in range(LAYERS) for i in range(2) for x in running[l, i].state[:2]]
        weights = call(bind(kernel_finish, tiles), places, parts, [Out(dims, F32) for dims in weights])
    else:
        layers = []
        for l in range(LAYERS):
            one, two = (running[l, i].state[0].astype(F32) + running[l, i].state[1].astype(F32) for i in range(2))
            one = jnp.transpose(one, (1, 0, 2)).reshape(plane_rows, clips, DS // clips).astype(BF16)
            one = lax.psum_scatter(one, "clip", scatter_dimension=1)
            two = two.reshape(rows_two, BS).astype(BF16)
            small = lax.psum(two[-SMALL_ROWS:], "clip")
            two = lax.psum_scatter(two[:-SMALL_ROWS].reshape(-1, clips, n), "clip", scatter_dimension=1)
            left = lax.dynamic_slice_in_dim(small[:, :LANES], place[2] * f, f, 1)
            right = lax.dynamic_slice_in_dim(small[:, LANES:], place[2] * f, f, 1)
            last = lax.dynamic_slice_in_dim(small[:, LANES:], place[2] * g, g, 1)
            ends = [0, 3 * nst, 3 * nst + 9 * nss, 3 * nst + 9 * nss + 5 * nla]
            st, ss, la = (two[i:j] for i, j in zip(ends, ends[1:]))
            layers.append([la, st, ss, one[nst:], one[:nst], left[: 3 * nla], right[: 9 * nsm],
                           last[9 * nsm : 10 * nsm], last[10 * nsm : 10 * nsm + nla]])
        weights = [jnp.stack(x).astype(F32).reshape(dims) for x, dims in zip(zip(*layers), weights)]
    return (
        out_slow.reshape(slow_in.shape),
        out_fast.reshape(fast_in.shape),
        grad_slow.reshape(slow_in.shape),
        grad_fast.reshape(fast_in.shape),
        *weights,
        *sums,
    )


def solution(mesh):
    pixels = P("clip", None, "ha", "wa", None)
    tile = ("ha", "wa")
    return jax.shard_map(
        local,
        mesh=mesh,
        in_specs=(pixels, pixels) + (P(),) * 12 + (pixels, pixels),
        out_specs=(
            (pixels,) * 4
            + (P(None, None, tile, "clip"),) * 2
            + (P(None, None, None, tile, "clip"),)
            + (P(None, tile, "clip"),) * 2
            + (P(None, None, tile, "clip"),)
            + (P(None, None, None, tile, "clip"),)
            + (P(None, tile, "clip"),) * 2
            + (P(),) * 2
        ),
        check_vma=False,
    )
```

```python
import functools

import jax
import jax.numpy as jnp
from jax import lax
from jax.experimental import pallas as pl
from jax.experimental.pallas import tpu as pltpu
from jax.sharding import PartitionSpec as P

DS = 1024
DL = 256
BS = 256
DF = 128
BF = 32
ST = 8
ALPHA = 4
HT = 16
WD = 16
LAYERS = 2
CC = DS + DL
EPSILON = 1e-05
LANES = 128
ALL_AXES = ("clip", "ha", "wa")


LAT, STM, SSP, SEX, SSK, FTM, FSP, FEX, FSK = 0, 2, 4, 6, 14, 22, 23, 24, 25
GB_ROWS = 32

F32 = jnp.float32
BF16 = jnp.bfloat16


def dot(a, b):
    return jnp.dot(a, b, preferred_element_type=F32)


def dot_nt(a, b):
    return lax.dot_general(a, b, (((1,), (1,)), ((), ())), preferred_element_type=F32)


def dot_tn(a, b):
    return lax.dot_general(a, b, (((0,), (0,)), ((), ())), preferred_element_type=F32)


def sigmoid(v):
    return 0.5 * jnp.tanh(0.5 * v) + 0.5


def silu(v):
    return v * sigmoid(v)


def slope(v):
    s = sigmoid(v)
    return s + v * s * (1.0 - s)


def silu_and_slope(v):
    s = sigmoid(v)
    act = v * s
    return act, s + act * (1.0 - s)


def wide(tile, row, count):
    if count == 1:
        return tile[row : row + 1, :]
    return jnp.concatenate([tile[row + i : row + i + 1, :] for i in range(count)], axis=1)


def fold_phases(tile):
    return tile + pltpu.roll(tile, 32, 1) + pltpu.roll(tile, 64, 1) + pltpu.roll(tile, 96, 1)


def down(x, frame):
    return jnp.concatenate([jnp.zeros_like(x[:frame]), x[:-frame]], axis=0)


def up(x, frame):
    return jnp.concatenate([x[frame:], jnp.zeros_like(x[:frame])], axis=0)


def col_sum(x):
    return jnp.sum(x, axis=0, keepdims=True)


class Norm:
    def __init__(self, total, row, gb, gb_row, count, inv_count):
        mean = wide(total, row, count) * inv_count
        square = wide(total, row + count, count) * inv_count
        self.mean = mean
        self.rstd = lax.rsqrt(square - mean * mean + EPSILON)
        self.gain = wide(gb[0], gb_row, count)
        self.bias = wide(gb[1], gb_row, count)
        self.scale = self.gain * self.rstd
        self.shift = self.bias - mean * self.scale

    def columns(self, start, size):
        other = object.__new__(Norm)
        for name in ("mean", "rstd", "gain", "bias", "scale", "shift"):
            setattr(other, name, getattr(self, name)[:, start : start + size])
        return other

    def out(self, z):
        return z * self.scale + self.shift

    def hat(self, z):
        return (z - self.mean) * self.rstd

    def back(self, dy, hat, inside, a_sum, b_sum, inv_count):
        return self.scale * (dy - jnp.where(inside, a_sum * inv_count + hat * (b_sum * inv_count), 0.0))


def inside_rows(rows, columns, limit):
    return lax.broadcasted_iota(jnp.int32, (rows, columns), 0) < limit


def moments(z, inside):
    masked = jnp.where(inside, z, 0.0)
    return col_sum(masked), col_sum(masked * z)


def put_rows(ref, row, vector):
    for i in range(vector.shape[1] // LANES):
        ref[row + i : row + i + 1, :] = vector[:, i * LANES : (i + 1) * LANES]


def phase(ref, p):
    return ref[:, p].reshape(ref.shape[0] * ref.shape[2], ref.shape[3])


def send_halo(z, shape, whole, top, bottom):
    t, h, w = shape
    four = z.reshape(t, h, w, z.shape[1])
    whole[...] = z.astype(BF16)
    top[...] = four[:, 0].reshape(t * w, z.shape[1]).astype(BF16)
    bottom[...] = four[:, h - 1].reshape(t * w, z.shape[1]).astype(BF16)


def fill_padded(pad, shape, own, above, below, others, has_left, has_right):
    t, h, w = shape
    c = own.shape[1]
    pad[:, 1 : h + 1, w : 2 * w, :] = own.reshape(t, h, w, c)
    pad[:, 0, w : 2 * w, :] = above.reshape(t, w, c)
    pad[:, h + 1, w : 2 * w, :] = below.reshape(t, w, c)
    o_above, o_own, o_below = others
    for start, has in ((0, has_left), (2 * w, has_right)):
        pad[:, 1 : h + 1, start : start + w, :] = (o_own * has).reshape(t, h, w, c)
        pad[:, 0, start : start + w, :] = (o_above * has).reshape(t, w, c)
        pad[:, h + 1, start : start + w, :] = (o_below * has).reshape(t, w, c)


def tap(pad, shape, a, b):
    t, h, w = shape
    part = pad[:, a : a + h, w - 1 + b : 2 * w - 1 + b, :]
    return part.reshape(t * h * w, part.shape[-1]).astype(BF16)


def activate_padded(pad, shape, norm, own, halo_refs, sf):
    def act(z):
        return silu(norm.out(z.astype(F32))).astype(BF16).astype(F32)

    above, below, o_above, o_own, o_below = (act(ref[...]) for ref in halo_refs)
    has_up, has_down = sf[2], sf[3]
    others = (o_above * has_up, o_own, o_below * has_down)
    fill_padded(pad, shape, act(own), above * has_up, below * has_down, others, sf[4], sf[5])


def fast_head(phases, shape, inside, lat_w, ft_band, fk_w, fb_out, zlat_out, zft_out, halo_out, zfk_out, pay, row):
    frame = shape[1] * shape[2]
    low = [v.astype(BF16) for v in phases]
    for p in range(ALPHA):
        fb_out[:, p * DF : (p + 1) * DF] = low[p]
    before2, before3, after0 = down(low[2], frame), down(low[3], frame), up(low[0], frame)
    z = (
        dot(before2, lat_w[0, 0])
        + dot(before3, lat_w[0, 1])
        + dot(low[0], lat_w[0, 2])
        + dot(low[1], lat_w[0, 3])
        + dot(low[2], lat_w[0, 4])
    )
    zlat_out[...] = z
    total, square = moments(z, inside[:, :DL])
    put_rows(pay, row, total)
    put_rows(pay, row + 2, square)
    six = [before3] + low + [after0]
    z = dot(six[0], ft_band[0])
    for j in range(1, 6):
        z = z + dot(six[j], ft_band[j])
    zft_out[...] = z
    send_halo(z, shape, *halo_out)
    total, square = moments(z, inside[:, :LANES])
    put_rows(pay, row + 4, total)
    put_rows(pay, row + 5, square)
    total, square = 0.0, 0.0
    for p in range(ALPHA):
        z = dot(low[p], fk_w[0])
        zfk_out[:, p * DF : (p + 1) * DF] = z
        one, two = moments(z, inside[:, :LANES])
        total, square = total + one, square + two
    put_rows(pay, row + 6, total)
    put_rows(pay, row + 7, square)


def place_columns(p):
    row = lax.broadcasted_iota(jnp.int32, (BF, LANES), 0)
    column = lax.broadcasted_iota(jnp.int32, (BF, LANES), 1)
    return jnp.where(column == row + BF * p, 1.0, 0.0).astype(BF16)


def kernel_start(shape, si, sf, fast, lat_w, ft_w, fk_w, fb, zlat, zft, z16, top, bottom, zfk, pay, ft_band):
    t, h, w = shape
    inside = inside_rows(t * h * w, DL, si[0])
    places = [place_columns(p) for p in range(ALPHA)]
    for l in range(LAYERS):
        for j in range(6):
            part = 0.0
            for p in range(ALPHA):
                if 0 <= j - p <= 2:
                    part = part + dot(ft_w[l, j - p], places[p])
            ft_band[l, j] = part.astype(BF16)
    fast_head(
        [phase(fast, p) for p in range(ALPHA)],
        shape, inside, lat_w, ft_band.at[0], fk_w, fb, zlat, zft, (z16, top, bottom), zfk, pay, 0,
    )


def lane(shape):
    return lax.broadcasted_iota(jnp.int32, shape, len(shape) - 1)


def kernel_prepare(gains, biases, fs_w, fe_w, gb, fs_bd, fe_bd):
    for i, source in enumerate((gains, biases)):
        for l in range(LAYERS):
            for r in range(22):
                gb[l, i, r : r + 1, :] = source[l : l + 1, r * LANES : (r + 1) * LANES]
            v = source[l : l + 1, 22 * LANES : 23 * LANES]
            v2 = source[l : l + 1, 23 * LANES : 24 * LANES]
            v3 = jnp.concatenate([source[l : l + 1, 24 * LANES :], jnp.zeros((1, 64), F32)], axis=1)
            place = lane((1, LANES))
            gb[l, i, FTM : FTM + 1, :] = fold_phases(jnp.where(place < 32, v, 0.0))
            gb[l, i, FSP : FSP + 1, :] = fold_phases(jnp.where((place >= 32) & (place < 64), v, 0.0))
            v, v2, v3 = (pltpu.roll(x, 64, 1) for x in (v, v2, v3))
            gb[l, i, FEX : FEX + 1, :] = jnp.where(place < 64, v, v2)
            gb[l, i, FSK : FSK + 1, :] = jnp.where(place < 64, v2, v3)
            gb[l, i, 26:32, :] = jnp.zeros((6, LANES), F32)
    row = lax.broadcasted_iota(jnp.int32, (LANES, LANES), 0)
    column = lane((LANES, LANES))
    same = (row // BF) == (column // BF)
    spread_columns = 0.0
    for p in range(ALPHA):
        spread_columns = spread_columns + place_columns(p).astype(F32)
    spread_columns = spread_columns.astype(BF16)
    for l in range(LAYERS):
        for a in range(3):
            for b in range(3):
                part = dot(fs_w[l, a, b], spread_columns).astype(BF16)
                fs_bd[l, a, b] = jnp.where(same, dot_tn(spread_columns, part), 0.0).astype(BF16)
        fe_bd[l] = jnp.zeros((LANES, ALPHA * DF), BF16)
        for p in range(ALPHA):
            fe_bd[l, p * BF : (p + 1) * BF, p * DF : (p + 1) * DF] = fe_w[l]


def kernel_temporal(first, shape, si, sf, *refs):
    t, h, w = shape
    rows, frame = t * h * w, h * w
    if first:
        (recv, slow, gb, zlat, zft, h1, h2, h3, h4, h5, st_w, sk_w, fs_bd,
         low_out, zst, z16, top, bottom, zsk, af9, zfs, pay, pad) = refs
        row = 0
        total = recv[...]
    else:
        (recv, gb_before, tot_sk, zse_in, zsk_in, gb, zlat, zft, h1, h2, h3, h4, h5, st_w, sk_w, fs_bd,
         low_out, zst, z16, top, bottom, zsk, af9, zfs, pay, pad) = refs
        row = 16
        total = recv[...]
        inside = inside_rows(rows, 256, si[0])
        one = Norm(total, 0, gb_before, SEX, 8, sf[0])
        two = Norm(tot_sk[...], 8, gb_before, SSK, 8, sf[0])
        for c in range(0, DS, 256):
            u = one.columns(c, 256).out(zse_in[:, c : c + 256]) + two.columns(c, 256).out(zsk_in[:, c : c + 256])
            low_out[:, c : c + 256] = jnp.where(inside, silu(u), 0.0).astype(BF16)
    inside = inside_rows(rows, 256, si[0])
    lat = Norm(total, row, gb, LAT, 2, sf[0])
    ft = Norm(fold_phases(total), row + 4, gb, FTM, 1, sf[1])
    if first:
        low_out[:, :DS] = slow[...].astype(BF16)
    low_out[:, DS:] = silu(lat.out(zlat[...])).astype(BF16)
    activate_padded(pad, shape, ft, zft[...], (h1, h2, h3, h4, h5), sf)
    low = low_out[...]
    z = dot(low, st_w[0, 1])
    z = z + down(dot(low, st_w[0, 0]), frame)
    z = z + up(dot(low, st_w[0, 2]), frame)
    zst[...] = z
    send_halo(z, shape, z16, top, bottom)
    one, two = moments(z, inside)
    put_rows(pay, 0, one)
    put_rows(pay, 2, two)
    for a in range(3):
        for b in range(3):
            k = 3 * a + b
            af9[:, k * LANES : (k + 1) * LANES] = tap(pad, shape, a, b)
    z = dot(af9[...], fs_bd[...].reshape(9 * LANES, LANES))
    zfs[...] = z
    one, two = moments(z, inside[:, :LANES])
    put_rows(pay, 4, one)
    put_rows(pay, 5, two)
    pay[6:8, :] = jnp.zeros((2, LANES), F32)
    for c in range(0, DS, 256):
        z = dot(low, sk_w[0, :, c : c + 256])
        zsk[:, c : c + 256] = z
        one, two = moments(z, inside)
        put_rows(pay, 8 + c // LANES, one)
        put_rows(pay, 16 + c // LANES, two)


def kernel_spatial(shape, si, sf, recv, gb, zst, h1, h2, h3, h4, h5, zfs, ss_w, fe_bd,
                   a9, zss, bf, zfe, pay, pad):
    t, h, w = shape
    inside = inside_rows(t * h * w, 256, si[0])
    total = recv[...]
    st = Norm(total, 0, gb, STM, 2, sf[0])
    fs = Norm(fold_phases(total), 4, gb, FSP, 1, sf[1])
    activate_padded(pad, shape, st, zst[...], (h1, h2, h3, h4, h5), sf)
    for a in range(3):
        for b in range(3):
            k = 3 * a + b
            a9[:, k * BS : (k + 1) * BS] = tap(pad, shape, a, b)
    z = dot(a9[...], ss_w[...].reshape(9 * BS, BS))
    zss[...] = z
    one, two = moments(z, inside)
    put_rows(pay, 0, one)
    put_rows(pay, 2, two)
    low = silu(fs.out(zfs[...])).astype(BF16)
    bf[...] = low
    total, square = 0.0, 0.0
    for p in range(ALPHA):
        z = dot(low, fe_bd[:, p * DF : (p + 1) * DF])
        zfe[:, p * DF : (p + 1) * DF] = z
        one, two = moments(z, inside[:, :LANES])
        total, square = total + one, square + two
    put_rows(pay, 4, total)
    put_rows(pay, 5, square)
    pay[6:8, :] = jnp.zeros((2, LANES), F32)


def kernel_expand(last, shape, si, sf, *refs):
    t, h, w = shape
    inside = inside_rows(t * h * w, 256, si[0])
    if last:
        recv, gb, zss, se_w, bt, zse, pay = refs
    else:
        (recv, gb, zss, se_w, tot_fk, zfe, zfk, lat_w, ft_band, fk_w,
         bt, zse, pay, fb, zlat, zft, z16, top, bottom, zfk_out) = refs
    total = recv[...]
    ss = Norm(total, 0, gb, SSP, 2, sf[0])
    low = silu(ss.out(zss[...])).astype(BF16)
    bt[...] = low
    for c in range(0, DS, 256):
        z = dot(low, se_w[0, :, c : c + 256])
        zse[:, c : c + 256] = z
        one, two = moments(z, inside)
        put_rows(pay, c // LANES, one)
        put_rows(pay, 8 + c // LANES, two)
    if not last:
        fe = Norm(total, 4, gb, FEX, 1, sf[1])
        fk = Norm(tot_fk[...], tot_fk.shape[0] - 2, gb, FSK, 1, sf[1])
        phases = []
        for p in range(ALPHA):
            cols = slice(p * DF, (p + 1) * DF)
            u = fe.out(zfe[:, cols]) + fk.out(zfk[:, cols])
            phases.append(jnp.where(inside[:, :LANES], silu(u), 0.0))
        fast_head(
            phases, shape, inside, lat_w, ft_band, fk_w, fb, zlat, zft, (z16, top, bottom), zfk_out, pay, 16
        )


class Refs:
    def __init__(self, names, refs):
        self.__dict__.update(zip(names, refs))

    def layer(self, prefix):
        own = {k[len(prefix) :]: v for k, v in self.__dict__.items() if k.startswith(prefix)}
        return Refs(own.keys(), own.values())


def norms_of(L, sf, *names):
    def make(name):
        if name == "se":
            return Norm(L.tot_se[...], 0, L.gb, SEX, 8, sf[0])
        if name == "sk":
            return Norm(L.tot_sk[...], 8, L.gb, SSK, 8, sf[0])
        if name == "ss":
            return Norm(L.tot_ss[...], 0, L.gb, SSP, 2, sf[0])
        if name == "st":
            return Norm(L.tot_sk[...], 0, L.gb, STM, 2, sf[0])
        if name == "lat":
            return Norm(L.tot_lat[...], L.tot_lat.shape[0] - 8, L.gb, LAT, 2, sf[0])
        if name == "ft":
            return Norm(fold_phases(L.tot_lat[...]), L.tot_lat.shape[0] - 4, L.gb, FTM, 1, sf[1])
        if name == "fk":
            return Norm(L.tot_lat[...], L.tot_lat.shape[0] - 2, L.gb, FSK, 1, sf[1])
        if name == "fs":
            return Norm(fold_phases(L.tot_sk[...]), 4, L.gb, FSP, 1, sf[1])
        return Norm(L.tot_ss[...], 4, L.gb, FEX, 1, sf[1])

    return [make(name) for name in names]


def fill_rows(pay, start, end):
    pay[start:end, :] = jnp.zeros((end - start, LANES), F32)


def top_slow(L, inside, sf, grad, du_out, pay, row, out=None):
    se, sk = norms_of(L, sf, "se", "sk")
    for c in range(0, DS, 256):
        cols = slice(c, c + 256)
        one, two = se.columns(c, 256), sk.columns(c, 256)
        hat1, hat2 = one.hat(L.zse[:, cols]), two.hat(L.zsk[:, cols])
        u = one.gain * hat1 + one.bias + (two.gain * hat2 + two.bias)
        act, rate = silu_and_slope(u)
        if out is not None:
            out[:, cols] = jnp.where(inside, act, 0.0)
        du = jnp.where(inside, grad(cols) * rate, 0.0)
        du_out[:, cols] = du
        put_rows(pay, row + c // LANES, col_sum(du))
        put_rows(pay, row + 8 + c // LANES, col_sum(du * hat1))
        put_rows(pay, row + 16 + c // LANES, col_sum(du * hat2))


def top_fast(L, inside, sf, grad, du_out, pay, row, out=None):
    fe, fk = norms_of(L, sf, "fe", "fk")
    inside = inside[:, :LANES]
    sums = [0.0, 0.0, 0.0]
    for p in range(ALPHA):
        cols = slice(p * DF, (p + 1) * DF)
        hat1, hat2 = fe.hat(L.zfe[:, cols]), fk.hat(L.zfk[:, cols])
        u = fe.gain * hat1 + fe.bias + (fk.gain * hat2 + fk.bias)
        act, rate = silu_and_slope(u)
        if out is not None:
            out[:, p] = jnp.where(inside, act, 0.0).reshape(out.shape[0], out.shape[2], DF)
        du = jnp.where(inside, grad(p) * rate, 0.0)
        du_out[:, cols] = du
        sums = [sums[0] + col_sum(du), sums[1] + col_sum(du * hat1), sums[2] + col_sum(du * hat2)]
    for i in range(3):
        put_rows(pay, row + i, sums[i])


def expand_slow(L, inside, sf, total, row, du_in, se_w, dz_se, dz_sk, pay, out_row):
    se, sk, ss = norms_of(L, sf, "se", "sk", "ss")
    back = 0.0
    for c in range(0, DS, 256):
        cols = slice(c, c + 256)
        r = row + c // LANES
        du = du_in[:, cols]
        a_sum = wide(total, r, 2)
        one, two = se.columns(c, 256), sk.columns(c, 256)
        dz = one.back(du, one.hat(L.zse[:, cols]), inside, a_sum, wide(total, 8 + r, 2), sf[0]).astype(BF16)
        dz_se[:, cols] = dz
        back = back + dot_nt(dz, se_w[0, :, cols])
        dz = two.back(du, two.hat(L.zsk[:, cols]), inside, a_sum, wide(total, 16 + r, 2), sf[0])
        dz_sk[:, cols] = dz.astype(BF16)
    z = L.zss[...]
    dy = back * slope(ss.out(z))
    put_rows(pay, out_row, col_sum(dy))
    put_rows(pay, out_row + 2, col_sum(dy * ss.hat(z)))
    return dy, z


def expand_fast(L, inside, sf, total, row, du_in, fe_bd, dz_fe, dz_fk, pay, out_row):
    fe, fk, fs = norms_of(L, sf, "fe", "fk", "fs")
    inside = inside[:, :LANES]
    back = 0.0
    a_sum = wide(total, row, 1)
    for p in range(ALPHA):
        cols = slice(p * DF, (p + 1) * DF)
        du = du_in[:, cols]
        dz = fe.back(du, fe.hat(L.zfe[:, cols]), inside, a_sum, wide(total, row + 1, 1), sf[1]).astype(BF16)
        dz_fe[:, cols] = dz
        back = back + dot_nt(dz, fe_bd[:, cols])
        dz = fk.back(du, fk.hat(L.zfk[:, cols]), inside, a_sum, wide(total, row + 2, 1), sf[1])
        dz_fk[:, cols] = dz.astype(BF16)
    z = L.zfs[...]
    dy = back * slope(fs.out(z))
    put_rows(pay, out_row, col_sum(dy))
    put_rows(pay, out_row + 1, col_sum(dy * fs.hat(z)))
    return dy, z


def pack_halo(pairs, shape, dy_out, halo_out):
    dy = jnp.concatenate([one for one, _ in pairs], axis=1) if len(pairs) > 1 else pairs[0][0]
    dy_out[...] = dy
    send_halo(jnp.concatenate([dy] + [z for _, z in pairs], axis=1), shape, *halo_out)


def spatial_gradient(parts, shape, si, sf, dy_in, halo_refs, pad, dz_out):
    t, h, w = shape
    width = dy_in.shape[1]

    def dz(dy, z, frame):
        inside = inside_rows(dy.shape[0], width, si[0] // (h * w) * frame)
        pieces, column = [], 0
        for norm, _, a_sum, b_sum, inv in parts:
            cols = slice(column, column + norm.mean.shape[1])
            pieces.append(norm.back(dy[:, cols], norm.hat(z[:, cols]), inside[:, cols], a_sum, b_sum, inv))
            column = cols.stop
        value = jnp.concatenate(pieces, axis=1) if len(pieces) > 1 else pieces[0]
        return value.astype(BF16)

    def arrived(ref, frame):
        value = ref[...].astype(F32)
        return dz(value[:, :width], value[:, width:], frame).astype(F32)

    z = jnp.concatenate([part[1] for part in parts], axis=1) if len(parts) > 1 else parts[0][1]
    own = dz(dy_in[...], z, h * w)
    dz_out[...] = own
    above, below, o_above, o_own, o_below = (
        arrived(ref, h * w if i == 3 else w) for i, ref in enumerate(halo_refs)
    )
    others = (o_above * sf[2], o_own, o_below * sf[3])
    fill_padded(pad, shape, own.astype(F32), above * sf[2], below * sf[3], others, sf[4], sf[5])


def spatial_part(norm, z, total, row, columns, inv):
    count = columns // LANES
    if columns == LANES:
        total = fold_phases(total)
    return norm, z, wide(total, row, count), wide(total, row + count, count), inv


def spatial_back(pad, shape, slow_w, fast_w):
    back, back_f = 0.0, 0.0
    for a in range(3):
        for b in range(3):
            part = tap(pad, shape, 2 - a, 2 - b)
            if slow_w is not None:
                back = back + dot_nt(part[:, :BS], slow_w[0, a, b])
            if fast_w is not None:
                back_f = back_f + dot_nt(part[:, part.shape[1] - LANES :], fast_w[a, b])
    return back, back_f


def finish_spatial(norm, z, back, dy_out, pay, row):
    dy = back * slope(norm.out(z))
    dy_out[...] = dy
    put_rows(pay, row, col_sum(dy))
    put_rows(pay, row + dy.shape[1] // LANES, col_sum(dy * norm.hat(z)))


def temporal_slow(L, frame, inside, sf, total, row, dy_in, dlow, st_w, dz_st, dy_lat, pay, out_row):
    st, lat = norms_of(L, sf, "st", "lat")
    dz = st.back(
        dy_in[...], st.hat(L.zst[...]), inside, wide(total, row, 2), wide(total, row + 2, 2), sf[0]
    ).astype(BF16)
    dz_st[:, :BS] = up(dz, frame)
    dz_st[:, BS : 2 * BS] = dz
    dz_st[:, 2 * BS :] = down(dz, frame)

    def back(cols):
        part = dlow[:, cols]
        for j in range(3):
            part = part + dot_nt(dz_st[:, j * BS : (j + 1) * BS], st_w[0, j, cols, :])
        return part

    z = L.zlat[...]
    dy = back(slice(DS, CC)) * slope(lat.out(z))
    dy_lat[...] = dy
    put_rows(pay, out_row, col_sum(dy))
    put_rows(pay, out_row + 2, col_sum(dy * lat.hat(z)))
    return back


def temporal_fast(L, frame, inside, sf, total, row, dy_in, dz_ft, dz_fk, fk_w, ft_band):
    (ft,) = norms_of(L, sf, "ft")
    folded = fold_phases(total)
    dz = ft.back(
        dy_in[...], ft.hat(L.zft[...]), inside[:, :LANES], wide(folded, row, 1), wide(folded, row + 1, 1), sf[1]
    ).astype(BF16)
    dz_ft[...] = dz

    def grad(p):
        part = dot_nt(dz_fk[:, p * DF : (p + 1) * DF], fk_w[0]) + dot_nt(dz, ft_band[p + 1])
        if p == ALPHA - 1:
            part = part + up(dot_nt(dz, ft_band[0]), frame)
        if p == 0:
            part = part + down(dot_nt(dz, ft_band[5]), frame)
        return part

    return grad


def lateral_back(L, frame, inside, sf, total, row, dy_in, lat_w, dz_lat, grad):
    (lat,) = norms_of(L, sf, "lat")
    dz = lat.back(
        dy_in[...], lat.hat(L.zlat[...]), inside, wide(total, row, 2), wide(total, row + 2, 2), sf[0]
    ).astype(BF16)
    dz_lat[...] = dz

    def whole(p):
        part = grad(p)
        if p < 3:
            part = part + dot_nt(dz, lat_w[0, p + 2])
        if p >= 2:
            part = part + up(dot_nt(dz, lat_w[0, p - 2]), frame)
        return part

    return whole


def back_turn(shape, R, inside, si, sf):
    L = R.layer("a_")
    total = R.recv[...]
    L.tot_se = R.recv
    top_slow(L, inside, sf, lambda cols: R.slow_cot[:, cols], R.du_s, R.pay, 0, R.out_slow)
    top_fast(L, inside, sf, lambda p: phase(R.fast_cot, p), R.du_f, R.pay, 24, R.out_fast)
    fill_rows(R.pay, 27, 32)


def back_expand(shape, R, inside, si, sf):
    L = R.layer("a_")
    total = R.recv[...]
    slow = expand_slow(L, inside, sf, total, 0, R.du_s, R.se_w, R.dz_se, R.dz_sk, R.pay, 0)
    fast = expand_fast(L, inside, sf, total, 24, R.du_f, R.fe_bd, R.dz_fe, R.dz_fk, R.pay, 4)
    fill_rows(R.pay, 6, 8)
    pack_halo([slow, fast], shape, R.dy, (R.whole, R.top, R.bottom))


def back_spatial(shape, R, inside, si, sf):
    L = R.layer("a_")
    total = R.recv[...]
    ss, fs, st, ft = norms_of(L, sf, "ss", "fs", "st", "ft")
    parts = [
        spatial_part(ss, L.zss[...], total, 0, BS, sf[0]),
        spatial_part(fs, L.zfs[...], total, 4, LANES, sf[1]),
    ]
    spatial_gradient(parts, shape, si, sf, R.dy, (R.h0, R.h1, R.h2, R.h3, R.h4), R.pad, R.dz)
    back, back_f = spatial_back(R.pad, shape, R.ss_w, R.fs_bd)
    finish_spatial(st, L.zst[...], back, R.dy_st, R.pay, 0)
    finish_spatial(ft, L.zft[...], back_f, R.dy_ft, R.pay, 4)
    fill_rows(R.pay, 6, 8)


def back_temporal(shape, R, inside, si, sf):
    L, below = R.layer("a_"), R.layer("b_")
    frame = shape[1] * shape[2]
    total = R.recv[...]
    back = temporal_slow(L, frame, inside, sf, total, 0, R.dy_st, R.dlow, R.st_w, R.dz_st, R.dy_lat, R.pay, 0)
    top_slow(below, inside, sf, back, R.du_s, R.pay, 8)
    fill_rows(R.pay, 4, 8)
    grad = temporal_fast(L, frame, inside, sf, total, 4, R.dy_ft, R.dz_ft, R.dz_fk, R.fk_w, R.ft_band)
    for p in range(ALPHA):
        R.dfast[:, p * DF : (p + 1) * DF] = grad(p)


def back_lateral(shape, R, inside, si, sf):
    L, below = R.layer("a_"), R.layer("b_")
    frame = shape[1] * shape[2]
    total = R.recv[...]
    slow = expand_slow(below, inside, sf, total, 8, R.du_s, R.se_w, R.dz_se, R.dz_sk, R.pay, 0)
    pack_halo([slow], shape, R.dy, (R.whole, R.top, R.bottom))
    grad = lateral_back(
        L, frame, inside, sf, total, 0, R.dy_lat, R.lat_w, R.dz_lat, lambda p: R.dfast[:, p * DF : (p + 1) * DF]
    )
    top_fast(below, inside, sf, grad, R.du_f, R.pay, 4)
    fill_rows(R.pay, 7, 8)


def back_low_spatial(shape, R, inside, si, sf):
    L = R.layer("b_")
    total = R.recv[...]
    fast = expand_fast(L, inside, sf, total, 4, R.du_f, R.fe_bd, R.dz_fe, R.dz_fk, R.pay, 4)
    pack_halo([fast], shape, R.dy_fs, (R.whole, R.top, R.bottom))
    ss, st = norms_of(L, sf, "ss", "st")
    parts = [spatial_part(ss, L.zss[...], total, 0, BS, sf[0])]
    spatial_gradient(parts, shape, si, sf, R.dy, (R.h0, R.h1, R.h2, R.h3, R.h4), R.pad, R.dz)
    back, _ = spatial_back(R.pad, shape, R.ss_w, None)
    finish_spatial(st, L.zst[...], back, R.dy_st, R.pay, 0)
    fill_rows(R.pay, 6, 8)


def back_low_temporal(shape, R, inside, si, sf):
    L = R.layer("b_")
    frame = shape[1] * shape[2]
    total = R.recv[...]
    fs, ft = norms_of(L, sf, "fs", "ft")
    parts = [spatial_part(fs, L.zfs[...], total, 4, LANES, sf[1])]
    spatial_gradient(parts, shape, si, sf, R.dy_fs, (R.h0, R.h1, R.h2, R.h3, R.h4), R.pad, R.dz_f)
    _, back_f = spatial_back(R.pad, shape, None, R.fs_bd)
    finish_spatial(ft, L.zft[...], back_f, R.dy_ft, R.pay, 4)
    back = temporal_slow(L, frame, inside, sf, total, 0, R.dy_st, R.dlow, R.st_w, R.dz_st, R.dy_lat, R.pay, 0)
    fill_rows(R.pay, 6, 8)
    for c in range(0, DS, 256):
        R.dslow[:, c : c + 256] = back(slice(c, c + 256))


def back_low_lateral(shape, R, inside, si, sf):
    L = R.layer("b_")
    frame = shape[1] * shape[2]
    total = R.recv[...]
    grad = temporal_fast(L, frame, inside, sf, total, 4, R.dy_ft, R.dz_ft, R.dz_fk, R.fk_w, R.ft_band)
    grad = lateral_back(L, frame, inside, sf, total, 0, R.dy_lat, R.lat_w, R.dz_lat, grad)
    for p in range(ALPHA):
        R.dfast[:, p] = grad(p).reshape(shape[0], frame, DF)


def kernel_back_skip(dz_sk, sk_w, dlow):
    for k in range(0, CC, 256):
        dlow[:, k : k + 256] = dot_nt(dz_sk[...], sk_w[0, k : k + 256, :])


def part_tiles(si, tiles, ref, keep, send):
    side = si[2]
    for i in range(tiles // 2):
        keep[i] = ref[2 * i + side]
        send[i] = ref[2 * i + 1 - side]


def kernel_weights_planes(tiles, si, low, bt, dz_se, dz_sk, keep, send, blocks):
    ksk, kse = CC // tiles, BS // tiles
    for j in range(4):
        cols, place = slice(j * 256, (j + 1) * 256), j
        d = dot_tn(low[...], dz_sk[:, cols]).astype(BF16)
        blocks[:, place, :ksk, :] = d.reshape(tiles, ksk, 256)
        d = dot_tn(bt[...], dz_se[:, cols]).astype(BF16)
        blocks[:, place, ksk:, :] = d.reshape(tiles, kse, 256)
    part_tiles(si, tiles, blocks, keep, send)


def pick_phases(parts):
    place = lane(parts[0].shape) // BF
    return fold_phases(sum(jnp.where(place == p, part, 0.0) for p, part in enumerate(parts)))


SMALL_ROWS = 64
ROW_JOBS = {"st": 2, "ss": 2, "lat": 2, "small": 7}


def job_rows(job, tiles):
    return {"st": 3 * CC, "ss": 9 * BS, "lat": 5 * DF, "small": SMALL_ROWS * tiles}[job] // tiles


def bundle_rows(jobs, tiles):
    small = SMALL_ROWS if "small" in jobs else 0
    rows = sum(job_rows(job, tiles) for job in jobs if job != "small")
    return -(-rows // 32) * 32 + small, small


def kernel_weights_rows(tiles, frame, jobs, si, *refs):
    kst, kss, kla, ksm = CC // tiles, BS // tiles, DF // tiles, BF // tiles
    count = sum(ROW_JOBS[job] for job in jobs)
    keep, send, blocks, small = refs[count:]
    rows, small_rows = bundle_rows(jobs, tiles)
    base = 0
    operands = list(refs[:count])
    for job in jobs:
        own = [operands.pop(0) for _ in range(ROW_JOBS[job])]
        if job == "st":
            low, dz = own
            for j in range(3):
                d = dot_tn(low[...], dz[:, j * BS : (j + 1) * BS]).astype(BF16)
                blocks[:, base + j * kst : base + (j + 1) * kst, :] = d.reshape(tiles, kst, BS)
        elif job == "ss":
            a9, dz = own
            for k in range(9):
                d = dot_tn(a9[:, k * BS : (k + 1) * BS], dz[:, :BS]).astype(BF16)
                blocks[:, base + k * kss : base + (k + 1) * kss, :] = d.reshape(tiles, kss, BS)
        elif job == "lat":
            fb, dz = own
            f = [fb[:, p * DF : (p + 1) * DF] for p in range(3)] + [fb[:, 3 * DF :]]
            for k, x in enumerate([down(f[2], frame), down(f[3], frame), f[0], f[1], f[2]]):
                d = dot_tn(x, dz[...]).astype(BF16)
                blocks[:, base + k * kla : base + (k + 1) * kla, :] = d.reshape(tiles, kla, DL)
        else:
            af9, fb, bf, dz_f, dz_ft, dz_fe, dz_fk = own
            small[...] = jnp.zeros(small.shape, F32)
            last = dz_f.shape[1] - LANES
            for k in range(9):
                d = dot_tn(af9[:, k * LANES : (k + 1) * LANES], dz_f[:, last:])
                d = pick_phases([d[p * BF : (p + 1) * BF] for p in range(ALPHA)])
                for i in range(tiles):
                    small[i, k * ksm : (k + 1) * ksm, LANES:] = d[i * ksm : (i + 1) * ksm]
            f = [fb[:, p * DF : (p + 1) * DF] for p in range(ALPHA)]
            six = [dot_tn(x, dz_ft[...]) for x in [down(f[3], frame)] + f + [up(f[0], frame)]]
            for k in range(3):
                d = pick_phases([six[k + p] for p in range(ALPHA)])
                small[:, k * kla : (k + 1) * kla, :LANES] = d.reshape(tiles, kla, LANES)
            fe, fk = 0.0, 0.0
            for p in range(ALPHA):
                cols = slice(p * DF, (p + 1) * DF)
                fk = fk + dot_tn(fb[:, cols], dz_fk[:, cols])
                fe = fe + dot_tn(bf[...], dz_fe[:, cols])[p * BF : (p + 1) * BF, :]
            for i in range(tiles):
                small[i, 9 * ksm : 10 * ksm, LANES:] = fe[i * ksm : (i + 1) * ksm]
                small[i, 10 * ksm : 10 * ksm + kla, LANES:] = fk[i * kla : (i + 1) * kla]
            blocks[:, rows - small_rows :, :] = small[...].astype(BF16)
            continue
        base += job_rows(job, tiles)
    if rows - small_rows > base:
        blocks[:, base : rows - small_rows, :] = jnp.zeros((tiles, rows - small_rows - base, 256), BF16)
    part_tiles(si, tiles, blocks, keep, send)


def add(one, two):
    return (one.astype(F32) + two.astype(F32)).astype(BF16)


def rows_from(ref, i, start, end):
    return ref[i, ..., start:end, :]


def kernel_halve_first(split, si, kept, got, keep_a, send_a, keep_b, send_b):
    low, high, end = si[1] % 2, si[1] // 2, kept.shape[-2]
    for i in range(2):
        for ref, side in ((keep_a, low), (send_a, 1 - low)):
            place = 2 * i + side
            ref[i] = add(rows_from(kept, place, 0, split), rows_from(got, place, 0, split))
        for ref, side in ((keep_b, high), (send_b, 1 - high)):
            place = 2 * side + i
            ref[i] = add(rows_from(kept, place, split, end), rows_from(got, place, split, end))


def kernel_halve_second(si, kept_a, got_a, kept_b, got_b, keep_a, send_a, keep_b, send_b):
    low, high = si[1] % 2, si[1] // 2
    for ref, place in ((keep_a, high), (send_a, 1 - high)):
        ref[...] = add(kept_a[place], got_a[place])
    for ref, place in ((keep_b, low), (send_b, 1 - low)):
        ref[...] = add(kept_b[place], got_b[place])


def kernel_join_planes(si, kept_a, got_a, kept_b, got_b, keep, send):
    split = kept_a.shape[-2]
    bit = si[3] % 2
    for ref, side in ((keep, bit), (send, 1 - bit)):
        for i in range(2):
            ref[i, :split, :] = add(kept_a[2 * i + side], got_a[2 * i + side])
            ref[i, split:, :] = add(kept_b[2 * i + side], got_b[2 * i + side])


def kernel_halve_last(si, kept, got, keep, send):
    bit = si[3] // 2
    for ref, place in ((keep, bit), (send, 1 - bit)):
        ref[...] = add(kept[place], got[place])


def kernel_pick_places(si, kept, got, *outs):
    for i, ref in enumerate(outs):
        place = si[1] ^ i
        ref[...] = add(kept[place], got[place])


def whole_sum(parts):
    total = parts[0][...].astype(F32)
    for part in parts[1:]:
        total = total + part[...].astype(F32)
    return total


def column_planes(small_rows, total, planes):
    big = total.shape[0] - small_rows
    packed = big // 2
    for j in range(4):
        planes[j, :packed, :] = columns_of(total[:big], j).astype(BF16)
        if small_rows:
            small = total[big:].astype(BF16)
            planes[j, packed : packed + small_rows, :] = small[:, :LANES]
            planes[j, packed + small_rows :, :] = small[:, LANES:]


def kernel_pick_columns(small_rows, si, a, b, c, d, out0, out1, out2, out3, planes):
    column_planes(small_rows, whole_sum((a, b, c, d)), planes)
    for i, ref in enumerate((out0, out1, out2, out3)):
        ref[...] = planes[si[3] ^ i]


def columns_of(x, j):
    half = x.shape[0] // 2
    base = (j // 2) * LANES
    a, b = x[:half, base : base + LANES], x[half:, base : base + LANES]
    left = lane(a.shape) < 64
    if j % 2 == 0:
        return jnp.where(left, a, pltpu.roll(b, 64, 1))
    return jnp.where(left, pltpu.roll(a, 64, 1), b)


def kernel_join_columns(small_rows, si, kept_a, got_a, kept_b, got_b, keep, send, planes):
    total = jnp.concatenate([whole_sum((kept_a, got_a)), whole_sum((kept_b, got_b))], axis=0)
    column_planes(small_rows, total, planes)
    bit = si[3] % 2
    for ref, side in ((keep, bit), (send, 1 - bit)):
        for i in range(2):
            ref[i] = planes[2 * i + side]


def kernel_finish(tiles, plan, si, *refs):
    kst, kss, kla, ksm = CC // tiles, BS // tiles, DF // tiles, BF // tiles
    refs = list(refs)
    g_lat, g_st, g_ss, g_se, g_sk, g_ft, g_fs, g_fe, g_fk = refs[-9:]
    for jobs, layers, count in plan:
        total, refs = whole_sum(refs[:count]), refs[count:]
        if jobs == ("planes",):
            g_sk[layers[0]] = total[:kst]
            g_se[layers[0]] = total[kst:]
            continue
        _, small_rows = bundle_rows(jobs, tiles)
        packed = total.shape[0] - 2 * small_rows
        rows = [total[:packed, :64], pltpu.roll(total[:packed], 64, 1)[:, :64]]

        def part(start, size):
            end = start + size
            if end <= packed:
                return rows[0][start:end]
            if start >= packed:
                return rows[1][start - packed : end - packed]
            return jnp.concatenate([rows[0][start:], rows[1][: end - packed]], axis=0)

        base = 0
        for job, l in zip(jobs, layers):
            if job == "st":
                for k in range(3):
                    g_st[l, k] = part(base + k * kst, kst)
            elif job == "ss":
                for k in range(9):
                    g_ss[l, k // 3, k % 3] = part(base + k * kss, kss)
            elif job == "lat":
                for k in range(5):
                    g_lat[l, k] = part(base + k * kla, kla)
            else:
                small = total[packed : packed + SMALL_ROWS]
                eight = pltpu.roll(small, (LANES - 8 * si[3]) % LANES, 1)[:, :8]
                for k in range(3):
                    g_ft[l, k] = eight[k * kla : (k + 1) * kla]
                small = total[packed + SMALL_ROWS :]
                eight = pltpu.roll(small, (LANES - 8 * si[3]) % LANES, 1)[:, :8]
                for k in range(9):
                    g_fs[l, k // 3, k % 3] = eight[k * ksm : (k + 1) * ksm]
                part32 = pltpu.roll(small, (LANES - 32 * si[3]) % LANES, 1)[:, :32]
                g_fe[l] = part32[9 * ksm : 10 * ksm]
                g_fk[l] = part32[10 * ksm : 10 * ksm + kla]
                continue
            base += job_rows(job, tiles)


def kernel_norm_sums(places, *refs):
    d_gains, d_biases = refs[-2:]
    for l in range(LAYERS):
        for i, out in ((0, d_biases), (1, d_gains)):
            column = 0
            for n, row, second, count in places[l][:5]:
                row += i * second
                for r in range(row, row + count):
                    out[l : l + 1, column : column + LANES] = refs[n][r : r + 1, :]
                    column += LANES
            ft, fs, fe, fk = (
                refs[n][row + i * second : row + i * second + 1, :] for n, row, second, _ in places[l][5:]
            )
            ft, fs = fold_phases(ft), fold_phases(fs)
            fe, fk = pltpu.roll(fe, 64, 1), pltpu.roll(fk, 64, 1)
            place = lane((1, LANES))
            out[l : l + 1, column : column + LANES] = jnp.where(place < 32, ft, jnp.where(place < 64, fs, fe))
            out[l : l + 1, column + LANES : column + 2 * LANES] = jnp.where(place < 64, fe, fk)
            out[l : l + 1, column + 2 * LANES :] = fk[:, :64]


SMEM = pltpu.MemorySpace.SMEM
VMEM = pltpu.MemorySpace.VMEM


class Weight:
    def __init__(self, array, layer):
        self.array = array
        self.layer = layer


class Layer:
    def __init__(self, array, layer):
        self.array = array
        self.layer = layer


class Load:
    def __init__(self, array):
        self.array = array


class Arriving:
    def __init__(self, copy, ref, layered):
        self.copy = copy
        self.ref = ref
        self.layered = layered
        self.shape = ref.shape

    def __getitem__(self, place):
        if self.copy is not None:
            self.copy.wait()
            self.copy = None
        if not self.layered:
            return self.ref[place]
        return self.ref[place[1:]] if isinstance(place, tuple) else self.ref[...]


class Out:
    def __init__(self, shape, kind):
        self.shape = shape
        self.kind = kind


def scalar_values(place, valid, frame, tiles):
    ha, wa, clip = place[0], place[1], place[2]
    total = valid[0]
    for i in range(1, valid.shape[0]):
        total = total + valid[i]
    count = jnp.full((1, LANES), total * (HT * WD), jnp.int32).astype(F32)
    inverse = 1.0 / count
    flags = [ha > 0, ha < tiles[0] - 1, wa > 0, wa < tiles[1] - 1]
    vectors = [jnp.where(jnp.full((1, LANES), jnp.where(f, 1, 0), jnp.int32) > 0, 1.0, 0.0) for f in flags]
    vectors = [inverse, inverse * (1.0 / ALPHA)] + vectors
    return (valid[clip] * frame, ha, wa, clip), [v[:, :1] for v in vectors]


def call(body, scalars, operands, outs, scratch=(), limit=16):
    mode, scalars = (None, ()) if not scalars else (scalars[0], scalars[1:3])
    count, first = len(operands), len(scalars)
    weights = [i for i, x in enumerate(operands) if isinstance(x, (Weight, Load))]
    results = [i for i, x in enumerate(outs) if isinstance(x, Out)]
    arrays = [x.array if isinstance(x, (Weight, Layer, Load)) else x for x in operands]
    layered = [isinstance(x, Weight) for x in operands]
    shapes = [(x.shape, x.kind) if isinstance(x, Out) else x for x in outs]
    buffers = [pltpu.VMEM(arrays[i].shape[1:] if layered[i] else arrays[i].shape, arrays[i].dtype) for i in weights]
    buffers += [pltpu.VMEM(*shapes[i]) for i in results]
    own = first + count + len(outs)

    def wrapped(*refs):
        refs = list(refs)
        inner, rest = refs[own : own + len(buffers)], refs[own + len(buffers) :]
        arriving, leaving = [], []
        for n, i in enumerate(weights):
            source = refs[first + i].at[operands[i].layer] if layered[i] else refs[first + i]
            copy = pltpu.make_async_copy(source, inner[n], rest[-1].at[n])
            copy.start()
            refs[first + i] = Arriving(copy, inner[n], layered[i])
            arriving.append(refs[first + i])
        for i, x in enumerate(operands):
            if isinstance(x, Layer):
                refs[first + i] = refs[first + i].at[x.layer]
        for n, i in enumerate(results):
            n += len(weights)
            leaving.append(pltpu.make_async_copy(inner[n], refs[first + count + i], rest[-1].at[n]))
            refs[first + count + i] = inner[n]
        given = ()
        if mode is not None:
            t_frame, tiles = mode[1], mode[2]
            ints, vectors = scalar_values(refs[0], refs[1], t_frame, tiles) if mode[0] == "all" else (
                (None, refs[0][0], refs[0][1], refs[0][2]), None)
            given = (ints, vectors) if mode[0] == "all" else (ints,)
        body(*given, *refs[first:own], *(rest[:-1] if buffers else rest))
        for copy in leaving:
            copy.start()
        for one in arriving:
            if one.copy is not None:
                one.copy.wait()
        for copy in leaving:
            copy.wait()

    def space(i, some):
        return pl.BlockSpec(memory_space=pltpu.HBM if i in some else VMEM)

    return pl.pallas_call(
        wrapped,
        out_shape=[jax.ShapeDtypeStruct(shape, kind) for shape, kind in shapes],
        in_specs=[pl.BlockSpec(memory_space=SMEM) for _ in scalars] + [space(i, weights) for i in range(count)],
        out_specs=[space(i, results) for i in range(len(outs))],
        scratch_shapes=buffers
        + [pltpu.VMEM(shape, kind) for shape, kind in scratch]
        + ([pltpu.SemaphoreType.DMA((len(buffers),))] if buffers else []),
        cost_estimate=pl.CostEstimate(flops=20000000000, bytes_accessed=80000000, transcendentals=0),
        compiler_params=pltpu.CompilerParams(vmem_limit_bytes=limit << 20),
    )(*scalars, *arrays)


def sum_over(x, axis):
    step, count = 1, lax.axis_size(axis)
    while step < count:
        pair = x + flip(x, axis, step)
        if 4 * step <= count:
            pair = pair + (flip(x, axis, 2 * step) + flip(x, axis, 3 * step))
            step *= 2
        x = pair
        step *= 2
    return x


def sum_all(x):
    for axis in ("wa", "ha", "clip"):
        x = sum_over(x, axis)
    return x


def swap(x):
    return lax.ppermute(x, "wa", [(0, 1), (1, 0)])


def halo(z, top, bottom):
    count = lax.axis_size("ha")
    above = lax.ppermute(bottom, "ha", [(i, i + 1) for i in range(count - 1)])
    below = lax.ppermute(top, "ha", [(i + 1, i) for i in range(count - 1)])
    return [above, below, swap(above), swap(z), swap(below)]


def after(first, *rest):
    return lax.optimization_barrier((first,) + rest)


def flip(x, axis, step):
    return lax.ppermute(x, axis, [(i, i ^ step) for i in range(lax.axis_size(axis))])


ORDERS = (("wa", "clip", "ha"), ("wa", "ha", "clip"))
LAUNCH = {
    (1, "wa"): ("A1",),
    (3, "wa"): ("ST1",),
    (3, "ha"): ("A1",),
    (4, "wa"): ("A0",),
    (4, "clip"): ("A1",),
    (5, "wa"): ("SL",),
    (5, "ha"): ("ST1", "A0"),
    (6, "wa"): ("T0",),
    (6, "clip"): ("A1", "ST1"),
    (6, "ha"): ("A0", "T0", "SL"),
}
LAND = {
    (1, "clip"): ("A1",),
    (2, "ha"): ("A1",),
    (3, "clip"): ("ST1",),
    (4, "ha"): ("A1", "ST1", "A0"),
    (5, "clip"): ("A1", "SL"),
    (6, "ha"): ("ST1", "A0", "T0"),
}
AT_ONCE = {(1, "clip", "A1"), (3, "clip", "ST1")}


def local(
    slow_in,
    fast_in,
    valid_frames,
    lateral_w,
    slow_temporal_w,
    slow_spatial_w,
    slow_expand_w,
    slow_skip_w,
    fast_temporal_w,
    fast_spatial_w,
    fast_expand_w,
    fast_skip_w,
    gains,
    biases,
    slow_cot,
    fast_cot,
):
    clips, n_ha, n_wa = (lax.axis_size(a) for a in ALL_AXES)
    tiles = n_ha * n_wa
    _, t, h, w, _ = slow_in.shape
    shape = (t, h, w)
    frame = h * w
    rows = t * frame

    place = jnp.stack([lax.axis_index(a) for a in ("ha", "wa", "clip")]).astype(jnp.int32)
    scalars = (("all", frame, (n_ha, n_wa)), place, valid_frames)
    places = (("place", frame, (n_ha, n_wa)), place, valid_frames)

    slow2 = slow_in.reshape(rows, DS)
    fast4 = fast_in.reshape(t, ALPHA, frame, DF)
    slow_cot2 = slow_cot.reshape(rows, DS)
    fast_cot4 = fast_cot.reshape(t, ALPHA, frame, DF)

    def act(columns, kind=F32):
        return ((rows, columns), kind)

    def edges(columns):
        return [act(columns, BF16), ((t * w, columns), BF16), ((t * w, columns), BF16)]

    def pay(count):
        return ((count, LANES), F32)

    def bind(body, *static):
        return functools.partial(body, *static)

    pad_slow = ((t, h + 2, 3 * w, BS), F32)
    pad_fast = ((t, h + 2, 3 * w, LANES), F32)
    pad_both = ((t, h + 2, 3 * w, BS + LANES), F32)
    saved = []
    fb, zlat, zft, z16, top, bottom, zfk, sent, band = call(
        bind(kernel_start, shape),
        scalars,
        [Load(fast4), Weight(lateral_w, 0), Load(fast_temporal_w), Weight(fast_skip_w, 0)],
        [act(512, BF16), act(DL), act(LANES), *edges(LANES), act(512), pay(8), ((LAYERS, 6, LANES, LANES), BF16)],
    )
    recv = sum_all(sent)
    gb_all, fs_bd, fe_bd = call(
        kernel_prepare,
        (),
        [Load(gains), Load(biases), Load(fast_spatial_w), Load(fast_expand_w)],
        [((LAYERS, 2, GB_ROWS, LANES), F32), ((LAYERS, 3, 3, LANES, LANES), BF16), ((LAYERS, LANES, ALPHA * DF), BF16)],
    )
    gb = [Layer(gb_all, l) for l in range(LAYERS)]
    before = None
    for l in range(LAYERS):
        around = halo(z16, top, bottom)
        last = l == LAYERS - 1
        start = [recv, Load(slow2), gb[l]] if l == 0 else [recv, gb[l - 1], before["tot_sk"], before["zse"], before["zsk"], gb[l]]
        low, zst, z16, top, bottom, zsk, af9, zfs, sent = call(
            bind(kernel_temporal, l == 0, shape),
            scalars,
            start + [zlat, zft, *around, Weight(slow_temporal_w, l), Weight(slow_skip_w, l), Layer(fs_bd, l)],
            [act(CC, BF16), act(BS), *edges(BS), act(DS), act(9 * LANES, BF16), act(LANES), pay(24)],
            [pad_fast],
        )
        tot_lat = recv
        if l > 0:
            before["tot_se"] = tot_lat
        recv = sum_all(sent)
        around = halo(z16, top, bottom)
        a9, zss, bf, zfe, sent = call(
            bind(kernel_spatial, shape),
            scalars,
            [recv, gb[l], zst, *around, zfs, Weight(slow_spatial_w, l), Layer(fe_bd, l)],
            [act(9 * BS, BF16), act(BS), act(LANES, BF16), act(512), pay(8)],
            [pad_slow],
        )
        tot_st = recv
        recv = sum_all(sent)
        keep = dict(
            fb=fb, zlat=zlat, zft=zft, zfk=zfk, low=low, zst=zst, zsk=zsk, af9=af9, zfs=zfs, a9=a9, zss=zss, bf=bf,
            zfe=zfe, tot_lat=tot_lat, tot_fk=tot_lat, tot_st=tot_st, tot_sk=tot_st,
        )
        if last:
            bt, zse, sent = call(
                bind(kernel_expand, True, shape),
                scalars,
                [recv, gb[l], zss, Weight(slow_expand_w, l)],
                [act(BS, BF16), act(DS), pay(16)],
            )
        else:
            bt, zse, sent, fb, zlat, zft, z16, top, bottom, zfk = call(
                bind(kernel_expand, False, shape),
                scalars,
                [recv, gb[l], zss, Weight(slow_expand_w, l), tot_lat, zfe, zfk,
                 Weight(lateral_w, l + 1), Layer(band, l + 1), Weight(fast_skip_w, l + 1)],
                [act(BS, BF16), act(DS), pay(24),
                 act(512, BF16), act(DL), act(LANES), *edges(LANES), act(512)],
            )
        tot_ss = recv
        recv = sum_all(sent)
        keep.update(bt=bt, zse=zse, tot_ss=tot_ss, tot_fe=tot_ss)
        saved.append(keep)
        before = keep

    saved[-1]["tot_se"] = recv
    for l in range(LAYERS):
        saved[l]["gb"] = gb[l]

    def stage(body, ins, outs, scratch=(), limit=16):
        names = list(ins) + list(outs) + [name for name, _ in scratch]

        def named(ints, vectors, *refs):
            body(shape, Refs(names, refs), inside_rows(rows, 256, ints[0]), ints, vectors)

        results = call(
            named, scalars, list(ins.values()), list(outs.values()), [kind for _, kind in scratch], limit
        )
        return dict(zip(outs, results))

    def layer(prefix, l, *names):
        return {prefix + name: saved[l][name] for name in names}

    def edge(columns):
        return dict(zip(("whole", "top", "bottom"), edges(columns)))

    def around_of(r):
        return {f"h{i}": x for i, x in enumerate(halo(r["whole"], r["top"], r["bottom"]))}

    plane_rows = (CC + BS) // tiles

    narrow = clips == 4

    def both_halves(keep, send, block):
        (got,) = yield [keep], [(send, "wa", 1)]
        split = block[-2] // 32 * 16
        a, b = (block[:-2] + (r, 256) for r in (split, block[-2] - split))
        keep_a, send_a, keep_b, send_b = call(
            bind(kernel_halve_first, split), places, [keep, got], [((2,) + x, BF16) for x in (a, a, b, b)]
        )
        got_a, got_b = yield [keep_a, keep_b], [(send_a, "ha", 1), (send_b, "ha", 2)]
        keep_a, send_a, keep_b, send_b = call(
            kernel_halve_second, places, [keep_a, got_a, keep_b, got_b], [(x, BF16) for x in (a, a, b, b)]
        )
        got_a, got_b = yield [keep_a, keep_b], [(send_a, "ha", 2), (send_b, "ha", 1)]
        return [keep_a, got_a, keep_b, got_b]

    def last_halves(keep, send, block):
        (got,) = yield [keep], [(send, "clip", 1)]
        keep, send = call(kernel_halve_last, places, [keep, got], [(block, BF16)] * 2)
        (got,) = yield [keep], [(send, "clip", 2)]
        yield [keep, got], None

    def planes_chain(keep, send):
        parts = yield from both_halves(keep, send, (4, plane_rows, 256))
        if narrow:
            block = (plane_rows, 256)
            yield from last_halves(*call(kernel_join_planes, places, parts, [((2,) + block, BF16)] * 2), block)
        yield parts, None

    def rows_chain(keep, send, jobs):
        count, small = bundle_rows(jobs, tiles)
        parts = yield from both_halves(keep, send, (count, 256))
        if narrow:
            block = ((count - small) // 2 + 2 * small, LANES)
            pair = call(
                bind(kernel_join_columns, small), places, parts, [((2,) + block, BF16)] * 2, [((4,) + block, BF16)]
            )
            yield from last_halves(*pair, block)
        yield parts, None

    def direct_chain(keep, send, jobs):
        count, small = bundle_rows(jobs, tiles)
        (got,) = yield [keep], [(send, "wa", 1)]
        mine, *others = call(kernel_pick_places, places, [keep, got], [((count, 256), BF16)] * 4)
        got = yield [mine], [(x, "ha", i + 1) for i, x in enumerate(others)]
        parts = [mine, *got]
        if narrow:
            block = ((count - small) // 2 + 2 * small, LANES)
            mine, *others = call(
                bind(kernel_pick_columns, small), places, parts, [(block, BF16)] * 4, [((4,) + block, BF16)]
            )
            got = yield [mine], [(x, "clip", i + 1) for i, x in enumerate(others)]
            parts = [mine, *got]
        yield parts, None

    class Running:
        def __init__(self, chain, jobs, layers):
            self.chain = chain
            self.jobs = jobs
            self.layers = layers
            self.got = None
            self.state = next(chain)

        def done(self):
            return self.state[1] is None

        def launch(self, x=None):
            if self.done() or self.got is not None:
                return
            sends = [send for send, _, _ in self.state[1]]
            if x is not None:
                _, *sends = after(x, *sends)
            self.got = [flip(send, axis, step) for send, (_, axis, step) in zip(sends, self.state[1])]

        def land(self, x):
            if self.got is None:
                return x
            x, *got = after(x, *self.got)
            self.got = None
            self.state = self.chain.send(got)
            return x

        def finish(self):
            while not self.done():
                self.launch()
                got, self.got = self.got, None
                self.state = self.chain.send(got)
                yield

    running = {}

    def planes(name, l, r):
        k = saved[l]
        pair = call(
            bind(kernel_weights_planes, tiles),
            places,
            [k["low"], k["bt"], r["dz_se"], r["dz_sk"]],
            [((tiles // 2, 4, plane_rows, 256), BF16)] * 2,
            [((tiles, 4, plane_rows, 256), BF16)],
        )
        running[name] = Running(planes_chain(*pair), ("planes",), (l,))

    def bundle(name, chain, *parts):
        jobs, layers = tuple(p[0] for p in parts), tuple(p[1] for p in parts)
        operands = []
        for job, l, r in parts:
            k = saved[l]
            operands += {
                "st": lambda: [k["low"], r["dz_st"]],
                "ss": lambda: [k["a9"], r["dz"]],
                "lat": lambda: [k["fb"], r["dz_lat"]],
                "small": lambda: [k["af9"], k["fb"], k["bf"], r["dz_f"], r["dz_ft"], r["dz_fe"], r["dz_fk"]],
            }[job]()
        count, _ = bundle_rows(jobs, tiles)
        pair = call(
            bind(kernel_weights_rows, tiles, frame, jobs),
            places,
            operands,
            [((tiles // 2, count, 256), BF16)] * 2,
            [((tiles, count, 256), BF16), ((tiles, SMALL_ROWS, 256), F32)],
            limit=24,
        )
        running[name] = Running(chain(*pair, jobs), jobs, layers)

    def skip_back(l, r):
        (r["dlow"],) = call(kernel_back_skip, (), [r["dz_sk"], Weight(slow_skip_w, l)], [act(CC)])

    totals = []

    def total_of(x):
        n = len(totals)
        for axis in ORDERS[n % 2]:
            for name in LAND.get((n, axis), ()):
                x = running[name].land(x)
                if (n, axis, name) in AT_ONCE:
                    running[name].launch()
            x = sum_over(x, axis)
            for name in LAUNCH.get((n, axis), ()):
                running[name].launch(x)
        totals.append(x)
        return x

    one, two = LAYERS - 1, LAYERS - 2
    r1, r0 = {}, {}
    slow_names, fast_names = ("gb", "tot_se", "tot_sk", "zse", "zsk"), ("tot_ss", "tot_lat", "zfe", "zfk")
    r1.update(stage(
        back_turn,
        dict(recv=recv, **layer("a_", one, *slow_names, *fast_names), slow_cot=Load(slow_cot2), fast_cot=Load(fast_cot4)),
        dict(out_slow=Out((rows, DS), F32), out_fast=Out((t, ALPHA, frame, DF), F32), du_s=act(DS), du_f=act(512), pay=pay(32)),
    ))
    recv = total_of(r1["pay"])
    r1.update(stage(
        back_expand,
        dict(recv=recv, **layer("a_", one, *slow_names, *fast_names, "zss", "zfs"), du_s=r1["du_s"], du_f=r1["du_f"],
             se_w=Weight(slow_expand_w, one), fe_bd=Layer(fe_bd, one)),
        dict(dz_se=act(DS, BF16), dz_sk=act(DS, BF16), dz_fe=act(512, BF16), dz_fk=act(512, BF16), dy=act(BS + LANES),
             **edge(2 * (BS + LANES)), pay=pay(8)),
    ))
    skip_back(one, r1)
    planes("A1", one, r1)
    recv = total_of(r1["pay"])
    r1.update(stage(
        back_spatial,
        dict(recv=recv, **layer("a_", one, "gb", "tot_sk", "tot_ss", "tot_lat", "zss", "zfs", "zst", "zft"), dy=r1["dy"],
             **around_of(r1), ss_w=Weight(slow_spatial_w, one), fs_bd=Layer(fs_bd, one)),
        dict(dz=act(BS + LANES, BF16), dy_st=act(BS), dy_ft=act(LANES), pay=pay(8)),
        [("pad", pad_both)],
    ))
    r1["dz_f"] = r1["dz"]
    recv = total_of(r1["pay"])
    r1.update(stage(
        back_temporal,
        dict(recv=recv, **layer("a_", one, "gb", "tot_sk", "tot_lat", "zst", "zft", "zlat"),
             **layer("b_", two, *slow_names), dy_st=r1["dy_st"], dy_ft=r1["dy_ft"], dlow=r1["dlow"], dz_fk=r1["dz_fk"],
             st_w=Weight(slow_temporal_w, one), ft_band=Layer(band, one), fk_w=Weight(fast_skip_w, one)),
        dict(dz_st=act(3 * BS, BF16), dz_ft=act(LANES, BF16), dfast=act(512), dy_lat=act(DL), du_s=act(DS), pay=pay(32)),
    ))
    bundle("ST1", rows_chain, ("ss", one, r1), ("st", one, r1))
    recv = total_of(r1["pay"])
    r0.update(stage(
        back_lateral,
        dict(recv=recv, **layer("a_", one, "gb", "tot_lat", "zlat"),
             **layer("b_", two, *slow_names, *fast_names, "zss"), dy_lat=r1["dy_lat"], dfast=r1["dfast"], du_s=r1["du_s"],
             lat_w=Weight(lateral_w, one), se_w=Weight(slow_expand_w, two)),
        dict(dz_lat=act(DL, BF16), du_f=act(512), dz_se=act(DS, BF16), dz_sk=act(DS, BF16), dy=act(BS), **edge(2 * BS), pay=pay(8)),
    ))
    r1["dz_lat"] = r0["dz_lat"]
    skip_back(two, r0)
    planes("A0", two, r0)
    recv = total_of(r0["pay"])
    fast = stage(
        back_low_spatial,
        dict(recv=recv, **layer("b_", two, "gb", "tot_sk", "tot_ss", "tot_lat", "zss", "zst", "zfe", "zfk", "zfs"),
             du_f=r0["du_f"], dy=r0["dy"], **around_of(r0), ss_w=Weight(slow_spatial_w, two), fe_bd=Layer(fe_bd, two)),
        dict(dz_fe=act(512, BF16), dz_fk=act(512, BF16), dy_fs=act(LANES), **edge(2 * LANES), dz=act(BS, BF16), dy_st=act(BS),
             pay=pay(8)),
        [("pad", pad_slow)],
    )
    r0.update(fast)
    bundle("SL", rows_chain, ("ss", two, r0), ("lat", one, r1), ("small", one, r1))
    recv = total_of(r0["pay"])
    r0.update(stage(
        back_low_temporal,
        dict(recv=recv, **layer("b_", two, "gb", "tot_sk", "tot_lat", "zst", "zft", "zlat", "zfs"), dy_fs=r0["dy_fs"],
             **around_of(r0), dy_st=r0["dy_st"], dlow=r0["dlow"], st_w=Weight(slow_temporal_w, two), fs_bd=Layer(fs_bd, two)),
        dict(dz_f=act(LANES, BF16), dy_ft=act(LANES), dz_st=act(3 * BS, BF16), dy_lat=act(DL), dslow=Out((rows, DS), F32),
             pay=pay(8)),
        [("pad", pad_fast)],
    ))
    bundle("T0", rows_chain, ("st", two, r0))
    recv = total_of(r0["pay"])
    r0.update(stage(
        back_low_lateral,
        dict(recv=recv, **layer("b_", two, "gb", "tot_lat", "zft", "zlat"), dy_ft=r0["dy_ft"], dy_lat=r0["dy_lat"],
             dz_fk=r0["dz_fk"], lat_w=Weight(lateral_w, two), ft_band=Layer(band, two), fk_w=Weight(fast_skip_w, two)),
        dict(dz_ft=act(LANES, BF16), dz_lat=act(DL, BF16), dfast=Out((t, ALPHA, frame, DF), F32)),
    ))
    bundle("L0", direct_chain, ("lat", two, r0), ("small", two, r0))
    ways = [chain.finish() for chain in running.values()]
    while ways:
        ways = [way for way in ways if next(way, 0) is None]
    out_slow, out_fast, grad_slow, grad_fast = r1["out_slow"], r1["out_fast"], r0["dslow"], r0["dfast"]
    where = [
        [(6, 0, 2, 2), (5, 0, 2, 2), (4, 0, 2, 2), (3, 8, 8, 8), (3, 8, 16, 8), (6, 4, 1, 1), (5, 4, 1, 1), (4, 4, 1, 1),
         (4, 4, 2, 1)],
        [(3, 0, 2, 2), (2, 0, 2, 2), (1, 0, 2, 2), (0, 0, 8, 8), (0, 0, 16, 8), (2, 4, 1, 1), (1, 4, 1, 1), (0, 24, 1, 1),
         (0, 24, 2, 1)],
    ]
    nst, nss, nla, nsm = CC // tiles, BS // tiles, DF // tiles, BF // tiles
    n, f, g = BS // clips, BF // clips, DF // clips
    sums = call(bind(kernel_norm_sums, where), (), totals, [Out(gains.shape, F32), Out(biases.shape, F32)])
    weights = [(LAYERS,) + dims for dims in (
        (5, nla, n), (3, nst, n), (3, 3, nss, n), (nss, DS // clips), (nst, DS // clips),
        (3, nla, f), (3, 3, nsm, f), (nsm, g), (nla, g),
    )]
    chains = list(running.values())
    if narrow:
        plan = [(chain.jobs, chain.layers, len(chain.state[0])) for chain in chains]
        parts = [x for chain in chains for x in chain.state[0]]
        weights = call(bind(kernel_finish, tiles, plan), places, parts, [Out(dims, F32) for dims in weights])
    else:
        found = {}
        for chain in chains:
            got = [x.astype(F32) for x in chain.state[0]]
            if chain.jobs == ("planes",) or chain.jobs != ("lat", "small"):
                total = jnp.concatenate([got[0] + got[1], got[2] + got[3]], axis=-2).astype(BF16)
            else:
                total = sum(got).astype(BF16)
            if chain.jobs == ("planes",):
                total = jnp.transpose(total, (1, 0, 2)).reshape(plane_rows, clips, DS // clips)
                total = lax.psum_scatter(total, "clip", scatter_dimension=1)
                found["sk", chain.layers[0]], found["se", chain.layers[0]] = total[:nst], total[nst:]
                continue
            count, small_rows = bundle_rows(chain.jobs, tiles)
            total = total.reshape(count, BS)
            small = lax.psum(total[count - small_rows :], "clip") if small_rows else None
            total = lax.psum_scatter(total[: count - small_rows].reshape(-1, clips, n), "clip", scatter_dimension=1)
            base = 0
            for job, l in zip(chain.jobs, chain.layers):
                if job == "small":
                    left = lax.dynamic_slice_in_dim(small[:, :LANES], place[2] * f, f, 1)
                    right = lax.dynamic_slice_in_dim(small[:, LANES:], place[2] * f, f, 1)
                    last = lax.dynamic_slice_in_dim(small[:, LANES:], place[2] * g, g, 1)
                    found["ft", l], found["fs", l] = left[: 3 * nla], right[: 9 * nsm]
                    found["fe", l], found["fk", l] = last[9 * nsm : 10 * nsm], last[10 * nsm : 10 * nsm + nla]
                else:
                    found[job, l] = total[base : base + job_rows(job, tiles)]
                    base += job_rows(job, tiles)
        names = ("lat", "st", "ss", "se", "sk", "ft", "fs", "fe", "fk")
        weights = [
            jnp.stack([found[name, l] for l in range(LAYERS)]).astype(F32).reshape(dims)
            for name, dims in zip(names, weights)
        ]
    return (
        out_slow.reshape(slow_in.shape),
        out_fast.reshape(fast_in.shape),
        grad_slow.reshape(slow_in.shape),
        grad_fast.reshape(fast_in.shape),
        *weights,
        *sums,
    )


def solution(mesh):
    pixels = P("clip", None, "ha", "wa", None)
    tile = ("ha", "wa")
    return jax.shard_map(
        local,
        mesh=mesh,
        in_specs=(pixels, pixels) + (P(),) * 12 + (pixels, pixels),
        out_specs=(
            (pixels,) * 4
            + (P(None, None, tile, "clip"),) * 2
            + (P(None, None, None, tile, "clip"),)
            + (P(None, tile, "clip"),) * 2
            + (P(None, None, tile, "clip"),)
            + (P(None, None, None, tile, "clip"),)
            + (P(None, tile, "clip"),) * 2
            + (P(),) * 2
        ),
        check_vma=False,
    )
```

```python
import functools

import jax
import jax.numpy as jnp
from jax import lax
from jax.experimental import pallas as pl
from jax.experimental.pallas import tpu as pltpu
from jax.sharding import PartitionSpec as P

DS = 1024
DL = 256
BS = 256
DF = 128
BF = 32
ST = 8
ALPHA = 4
HT = 16
WD = 16
LAYERS = 2
CC = DS + DL
EPSILON = 1e-05
LANES = 128
ALL_AXES = ("clip", "ha", "wa")


LAT, STM, SSP, SEX, SSK, FTM, FSP, FEX, FSK = 0, 2, 4, 6, 14, 22, 23, 24, 25
GB_ROWS = 32

F32 = jnp.float32
BF16 = jnp.bfloat16


def dot(a, b):
    return jnp.dot(a, b, preferred_element_type=F32)


def dot_nt(a, b):
    return lax.dot_general(a, b, (((1,), (1,)), ((), ())), preferred_element_type=F32)


def dot_tn(a, b):
    return lax.dot_general(a, b, (((0,), (0,)), ((), ())), preferred_element_type=F32)


def sigmoid(v):
    return 0.5 * jnp.tanh(0.5 * v) + 0.5


def silu(v):
    return v * sigmoid(v)


def slope(v):
    s = sigmoid(v)
    return s + v * s * (1.0 - s)


def silu_and_slope(v):
    s = sigmoid(v)
    act = v * s
    return act, s + act * (1.0 - s)


def wide(tile, row, count):
    if count == 1:
        return tile[row : row + 1, :]
    return jnp.concatenate([tile[row + i : row + i + 1, :] for i in range(count)], axis=1)


def fold_phases(tile):
    return tile + pltpu.roll(tile, 32, 1) + pltpu.roll(tile, 64, 1) + pltpu.roll(tile, 96, 1)


def down(x, frame):
    return jnp.concatenate([jnp.zeros_like(x[:frame]), x[:-frame]], axis=0)


def up(x, frame):
    return jnp.concatenate([x[frame:], jnp.zeros_like(x[:frame])], axis=0)


def col_sum(x):
    return jnp.sum(x, axis=0, keepdims=True)


class Norm:
    def __init__(self, total, row, gb, gb_row, count, inv_count):
        mean = wide(total, row, count) * inv_count
        square = wide(total, row + count, count) * inv_count
        self.mean = mean
        self.rstd = lax.rsqrt(square - mean * mean + EPSILON)
        self.gain = wide(gb[0], gb_row, count)
        self.bias = wide(gb[1], gb_row, count)
        self.scale = self.gain * self.rstd
        self.shift = self.bias - mean * self.scale

    def columns(self, start, size):
        other = object.__new__(Norm)
        for name in ("mean", "rstd", "gain", "bias", "scale", "shift"):
            setattr(other, name, getattr(self, name)[:, start : start + size])
        return other

    def out(self, z):
        return z * self.scale + self.shift

    def hat(self, z):
        return (z - self.mean) * self.rstd

    def back(self, dy, hat, inside, a_sum, b_sum, inv_count):
        return self.scale * (dy - jnp.where(inside, a_sum * inv_count + hat * (b_sum * inv_count), 0.0))


def inside_rows(rows, columns, limit):
    return lax.broadcasted_iota(jnp.int32, (rows, columns), 0) < limit


def moments(z, inside):
    masked = jnp.where(inside, z, 0.0)
    return col_sum(masked), col_sum(masked * z)


def put_rows(ref, row, vector):
    for i in range(vector.shape[1] // LANES):
        ref[row + i : row + i + 1, :] = vector[:, i * LANES : (i + 1) * LANES]


def spread(tile, ref):
    def body(i, carry):
        ref[i] = tile[...]
        return carry

    lax.fori_loop(0, ref.shape[0], body, 0)


def gathered(ref):
    return jnp.sum(ref[...], axis=0)


def phase(ref, p):
    return ref[:, p].reshape(ref.shape[0] * ref.shape[2], ref.shape[3])


def send_halo(z, shape, whole, top, bottom):
    t, h, w = shape
    four = z.reshape(t, h, w, z.shape[1])
    whole[...] = z.astype(BF16)
    top[...] = four[:, 0].reshape(t * w, z.shape[1]).astype(BF16)
    bottom[...] = four[:, h - 1].reshape(t * w, z.shape[1]).astype(BF16)


def fill_padded(pad, shape, own, above, below, others, has_left, has_right):
    t, h, w = shape
    c = own.shape[1]
    pad[:, 1 : h + 1, w : 2 * w, :] = own.reshape(t, h, w, c)
    pad[:, 0, w : 2 * w, :] = above.reshape(t, w, c)
    pad[:, h + 1, w : 2 * w, :] = below.reshape(t, w, c)
    o_above, o_own, o_below = others
    for start, has in ((0, has_left), (2 * w, has_right)):
        pad[:, 1 : h + 1, start : start + w, :] = (o_own * has).reshape(t, h, w, c)
        pad[:, 0, start : start + w, :] = (o_above * has).reshape(t, w, c)
        pad[:, h + 1, start : start + w, :] = (o_below * has).reshape(t, w, c)


def tap(pad, shape, a, b):
    t, h, w = shape
    part = pad[:, a : a + h, w - 1 + b : 2 * w - 1 + b, :]
    return part.reshape(t * h * w, part.shape[-1]).astype(BF16)


def activate_padded(pad, shape, norm, own, halo_refs, sf):
    def act(z):
        return silu(norm.out(z.astype(F32))).astype(BF16).astype(F32)

    above, below, o_above, o_own, o_below = (act(ref[...]) for ref in halo_refs)
    has_up, has_down = sf[2], sf[3]
    others = (o_above * has_up, o_own, o_below * has_down)
    fill_padded(pad, shape, act(own), above * has_up, below * has_down, others, sf[4], sf[5])


def fast_head(phases, shape, inside, lat_w, ft_band, fk_w, fb_out, zlat_out, zft_out, halo_out, zfk_out, pay, row):
    frame = shape[1] * shape[2]
    low = [v.astype(BF16) for v in phases]
    for p in range(ALPHA):
        fb_out[:, p * DF : (p + 1) * DF] = low[p]
    before2, before3, after0 = down(low[2], frame), down(low[3], frame), up(low[0], frame)
    z = (
        dot(before2, lat_w[0, 0])
        + dot(before3, lat_w[0, 1])
        + dot(low[0], lat_w[0, 2])
        + dot(low[1], lat_w[0, 3])
        + dot(low[2], lat_w[0, 4])
    )
    zlat_out[...] = z
    total, square = moments(z, inside[:, :DL])
    put_rows(pay, row, total)
    put_rows(pay, row + 2, square)
    six = [before3] + low + [after0]
    z = dot(six[0], ft_band[0])
    for j in range(1, 6):
        z = z + dot(six[j], ft_band[j])
    zft_out[...] = z
    send_halo(z, shape, *halo_out)
    total, square = moments(z, inside[:, :LANES])
    put_rows(pay, row + 4, total)
    put_rows(pay, row + 5, square)
    total, square = 0.0, 0.0
    for p in range(ALPHA):
        z = dot(low[p], fk_w[0])
        zfk_out[:, p * DF : (p + 1) * DF] = z
        one, two = moments(z, inside[:, :LANES])
        total, square = total + one, square + two
    put_rows(pay, row + 6, total)
    put_rows(pay, row + 7, square)


def place_columns(p):
    row = lax.broadcasted_iota(jnp.int32, (BF, LANES), 0)
    column = lax.broadcasted_iota(jnp.int32, (BF, LANES), 1)
    return jnp.where(column == row + BF * p, 1.0, 0.0).astype(BF16)


def kernel_start(shape, si, sf, fast, lat_w, ft_w, fk_w, fb, zlat, zft, z16, top, bottom, zfk, pay, ft_band):
    t, h, w = shape
    inside = inside_rows(t * h * w, DL, si[0])
    places = [place_columns(p) for p in range(ALPHA)]
    for l in range(LAYERS):
        for j in range(6):
            part = 0.0
            for p in range(ALPHA):
                if 0 <= j - p <= 2:
                    part = part + dot_tn(ft_w[l, j - p], places[p])
            ft_band[l, j] = part.astype(BF16)
    fast_head(
        [phase(fast, p) for p in range(ALPHA)],
        shape, inside, lat_w, ft_band.at[0], fk_w, fb, zlat, zft, (z16, top, bottom), zfk, pay, 0,
    )


def lane(shape):
    return lax.broadcasted_iota(jnp.int32, shape, len(shape) - 1)


def kernel_prepare(gains, biases, fs_w, fe_w, gb, fs_bd, fe_bd):
    for i, source in enumerate((gains, biases)):
        for l in range(LAYERS):
            for r in range(22):
                gb[l, i, r : r + 1, :] = source[l : l + 1, r * LANES : (r + 1) * LANES]
            v = source[l : l + 1, 22 * LANES : 23 * LANES]
            v2 = source[l : l + 1, 23 * LANES : 24 * LANES]
            v3 = jnp.concatenate([source[l : l + 1, 24 * LANES :], jnp.zeros((1, 64), F32)], axis=1)
            place = lane((1, LANES))
            gb[l, i, FTM : FTM + 1, :] = fold_phases(jnp.where(place < 32, v, 0.0))
            gb[l, i, FSP : FSP + 1, :] = fold_phases(jnp.where((place >= 32) & (place < 64), v, 0.0))
            v, v2, v3 = (pltpu.roll(x, 64, 1) for x in (v, v2, v3))
            gb[l, i, FEX : FEX + 1, :] = jnp.where(place < 64, v, v2)
            gb[l, i, FSK : FSK + 1, :] = jnp.where(place < 64, v2, v3)
            gb[l, i, 26:32, :] = jnp.zeros((6, LANES), F32)
    row = lax.broadcasted_iota(jnp.int32, (LANES, LANES), 0)
    column = lane((LANES, LANES))
    same = (row // BF) == (column // BF)
    spread_columns = 0.0
    for p in range(ALPHA):
        spread_columns = spread_columns + place_columns(p).astype(F32)
    spread_columns = spread_columns.astype(BF16)
    for l in range(LAYERS):
        for a in range(3):
            for b in range(3):
                part = dot(fs_w[l, a, b], spread_columns).astype(BF16)
                fs_bd[l, a, b] = jnp.where(same, dot_tn(spread_columns, part), 0.0).astype(BF16)
        fe_bd[l] = jnp.zeros((LANES, ALPHA * DF), BF16)
        for p in range(ALPHA):
            fe_bd[l, p * BF : (p + 1) * BF, p * DF : (p + 1) * DF] = fe_w[l]


def kernel_temporal(first, shape, si, sf, *refs):
    t, h, w = shape
    rows, frame = t * h * w, h * w
    if first:
        (recv, slow, gb, zlat, zft, h1, h2, h3, h4, h5, st_w, sk_w, fs_bd,
         low_out, zst, z16, top, bottom, zsk, af9, zfs, pay, pad) = refs
        row = 0
        total = recv[...]
    else:
        (recv, gb_before, tot_sk, zse_in, zsk_in, gb, zlat, zft, h1, h2, h3, h4, h5, st_w, sk_w, fs_bd,
         low_out, zst, z16, top, bottom, zsk, af9, zfs, pay, pad) = refs
        row = 16
        total = recv[...]
        inside = inside_rows(rows, 256, si[0])
        one = Norm(total, 0, gb_before, SEX, 8, sf[0])
        two = Norm(tot_sk[...], 8, gb_before, SSK, 8, sf[0])
        for c in range(0, DS, 256):
            u = one.columns(c, 256).out(zse_in[:, c : c + 256]) + two.columns(c, 256).out(zsk_in[:, c : c + 256])
            low_out[:, c : c + 256] = jnp.where(inside, silu(u), 0.0).astype(BF16)
    inside = inside_rows(rows, 256, si[0])
    lat = Norm(total, row, gb, LAT, 2, sf[0])
    ft = Norm(fold_phases(total), row + 4, gb, FTM, 1, sf[1])
    if first:
        low_out[:, :DS] = slow[...].astype(BF16)
    low_out[:, DS:] = silu(lat.out(zlat[...])).astype(BF16)
    activate_padded(pad, shape, ft, zft[...], (h1, h2, h3, h4, h5), sf)
    low = low_out[...]
    z = dot(low, st_w[0, 1])
    z = z + down(dot(low, st_w[0, 0]), frame)
    z = z + up(dot(low, st_w[0, 2]), frame)
    zst[...] = z
    send_halo(z, shape, z16, top, bottom)
    one, two = moments(z, inside)
    put_rows(pay, 0, one)
    put_rows(pay, 2, two)
    for a in range(3):
        for b in range(3):
            k = 3 * a + b
            af9[:, k * LANES : (k + 1) * LANES] = tap(pad, shape, a, b)
    z = dot(af9[...], fs_bd[...].reshape(9 * LANES, LANES))
    zfs[...] = z
    one, two = moments(z, inside[:, :LANES])
    put_rows(pay, 4, one)
    put_rows(pay, 5, two)
    pay[6:8, :] = jnp.zeros((2, LANES), F32)
    for c in range(0, DS, 256):
        z = dot(low, sk_w[0, :, c : c + 256])
        zsk[:, c : c + 256] = z
        one, two = moments(z, inside)
        put_rows(pay, 8 + c // LANES, one)
        put_rows(pay, 16 + c // LANES, two)


def kernel_spatial(shape, si, sf, recv, gb, zst, h1, h2, h3, h4, h5, zfs, ss_w, fe_bd,
                   a9, zss, bf, zfe, pays, pay, pad):
    t, h, w = shape
    inside = inside_rows(t * h * w, 256, si[0])
    total = recv[...]
    st = Norm(total, 0, gb, STM, 2, sf[0])
    fs = Norm(fold_phases(total), 4, gb, FSP, 1, sf[1])
    activate_padded(pad, shape, st, zst[...], (h1, h2, h3, h4, h5), sf)
    for a in range(3):
        for b in range(3):
            k = 3 * a + b
            a9[:, k * BS : (k + 1) * BS] = tap(pad, shape, a, b)
    z = dot(a9[...], ss_w[...].reshape(9 * BS, BS))
    zss[...] = z
    one, two = moments(z, inside)
    put_rows(pay, 0, one)
    put_rows(pay, 2, two)
    low = silu(fs.out(zfs[...])).astype(BF16)
    bf[...] = low
    total, square = 0.0, 0.0
    for p in range(ALPHA):
        z = dot(low, fe_bd[:, p * DF : (p + 1) * DF])
        zfe[:, p * DF : (p + 1) * DF] = z
        one, two = moments(z, inside[:, :LANES])
        total, square = total + one, square + two
    put_rows(pay, 4, total)
    put_rows(pay, 5, square)
    pay[6:8, :] = jnp.zeros((2, LANES), F32)
    spread(pay, pays)


def kernel_expand(last, shape, si, sf, *refs):
    t, h, w = shape
    inside = inside_rows(t * h * w, 256, si[0])
    if last:
        recv, gb, zss, se_w, bt, zse, pays, tot_out, pay = refs
    else:
        (recv, gb, zss, se_w, tot_fk, zfe, zfk, lat_w, ft_band, fk_w,
         bt, zse, pay, tot_out, fb, zlat, zft, z16, top, bottom, zfk_out) = refs
    total = gathered(recv)
    tot_out[...] = total
    ss = Norm(total, 0, gb, SSP, 2, sf[0])
    low = silu(ss.out(zss[...])).astype(BF16)
    bt[...] = low
    for c in range(0, DS, 256):
        z = dot(low, se_w[0, :, c : c + 256])
        zse[:, c : c + 256] = z
        one, two = moments(z, inside)
        put_rows(pay, c // LANES, one)
        put_rows(pay, 8 + c // LANES, two)
    if not last:
        fe = Norm(total, 4, gb, FEX, 1, sf[1])
        fk = Norm(tot_fk[...], tot_fk.shape[0] - 2, gb, FSK, 1, sf[1])
        phases = []
        for p in range(ALPHA):
            cols = slice(p * DF, (p + 1) * DF)
            u = fe.out(zfe[:, cols]) + fk.out(zfk[:, cols])
            phases.append(jnp.where(inside[:, :LANES], silu(u), 0.0))
        fast_head(
            phases, shape, inside, lat_w, ft_band, fk_w, fb, zlat, zft, (z16, top, bottom), zfk_out, pay, 16
        )
    else:
        spread(pay, pays)


class Refs:
    def __init__(self, names, refs):
        self.__dict__.update(zip(names, refs))

    def layer(self, prefix):
        own = {k[len(prefix) :]: v for k, v in self.__dict__.items() if k.startswith(prefix)}
        return Refs(own.keys(), own.values())


def norms_of(L, sf, *names):
    def make(name):
        if name == "se":
            return Norm(L.tot_se[...], 0, L.gb, SEX, 8, sf[0])
        if name == "sk":
            return Norm(L.tot_sk[...], 8, L.gb, SSK, 8, sf[0])
        if name == "ss":
            return Norm(L.tot_ss[...], 0, L.gb, SSP, 2, sf[0])
        if name == "st":
            return Norm(L.tot_sk[...], 0, L.gb, STM, 2, sf[0])
        if name == "lat":
            return Norm(L.tot_lat[...], L.tot_lat.shape[0] - 8, L.gb, LAT, 2, sf[0])
        if name == "ft":
            return Norm(fold_phases(L.tot_lat[...]), L.tot_lat.shape[0] - 4, L.gb, FTM, 1, sf[1])
        if name == "fk":
            return Norm(L.tot_lat[...], L.tot_lat.shape[0] - 2, L.gb, FSK, 1, sf[1])
        if name == "fs":
            return Norm(fold_phases(L.tot_sk[...]), 4, L.gb, FSP, 1, sf[1])
        return Norm(L.tot_ss[...], 4, L.gb, FEX, 1, sf[1])

    return [make(name) for name in names]


def fill_rows(pay, start, end):
    pay[start:end, :] = jnp.zeros((end - start, LANES), F32)


def top_slow(L, inside, sf, grad, du_out, pay, row, out=None):
    se, sk = norms_of(L, sf, "se", "sk")
    for c in range(0, DS, 256):
        cols = slice(c, c + 256)
        one, two = se.columns(c, 256), sk.columns(c, 256)
        hat1, hat2 = one.hat(L.zse[:, cols]), two.hat(L.zsk[:, cols])
        u = one.gain * hat1 + one.bias + (two.gain * hat2 + two.bias)
        act, rate = silu_and_slope(u)
        if out is not None:
            out[:, cols] = jnp.where(inside, act, 0.0)
        du = jnp.where(inside, grad(cols) * rate, 0.0)
        du_out[:, cols] = du
        put_rows(pay, row + c // LANES, col_sum(du))
        put_rows(pay, row + 8 + c // LANES, col_sum(du * hat1))
        put_rows(pay, row + 16 + c // LANES, col_sum(du * hat2))


def top_fast(L, inside, sf, grad, du_out, pay, row, out=None):
    fe, fk = norms_of(L, sf, "fe", "fk")
    inside = inside[:, :LANES]
    sums = [0.0, 0.0, 0.0]
    for p in range(ALPHA):
        cols = slice(p * DF, (p + 1) * DF)
        hat1, hat2 = fe.hat(L.zfe[:, cols]), fk.hat(L.zfk[:, cols])
        u = fe.gain * hat1 + fe.bias + (fk.gain * hat2 + fk.bias)
        act, rate = silu_and_slope(u)
        if out is not None:
            out[:, p] = jnp.where(inside, act, 0.0).reshape(out.shape[0], out.shape[2], DF)
        du = jnp.where(inside, grad(p) * rate, 0.0)
        du_out[:, cols] = du
        sums = [sums[0] + col_sum(du), sums[1] + col_sum(du * hat1), sums[2] + col_sum(du * hat2)]
    for i in range(3):
        put_rows(pay, row + i, sums[i])


def expand_slow(L, inside, sf, total, row, du_in, se_w, dz_se, dz_sk, pay, out_row):
    se, sk, ss = norms_of(L, sf, "se", "sk", "ss")
    back = 0.0
    for c in range(0, DS, 256):
        cols = slice(c, c + 256)
        r = row + c // LANES
        du = du_in[:, cols]
        a_sum = wide(total, r, 2)
        one, two = se.columns(c, 256), sk.columns(c, 256)
        dz = one.back(du, one.hat(L.zse[:, cols]), inside, a_sum, wide(total, 8 + r, 2), sf[0]).astype(BF16)
        dz_se[:, cols] = dz
        back = back + dot_nt(dz, se_w[0, :, cols])
        dz = two.back(du, two.hat(L.zsk[:, cols]), inside, a_sum, wide(total, 16 + r, 2), sf[0])
        dz_sk[:, cols] = dz.astype(BF16)
    z = L.zss[...]
    dy = back * slope(ss.out(z))
    put_rows(pay, out_row, col_sum(dy))
    put_rows(pay, out_row + 2, col_sum(dy * ss.hat(z)))
    return dy, z


def expand_fast(L, inside, sf, total, row, du_in, fe_bd, dz_fe, dz_fk, pay, out_row):
    fe, fk, fs = norms_of(L, sf, "fe", "fk", "fs")
    inside = inside[:, :LANES]
    back = 0.0
    a_sum = wide(total, row, 1)
    for p in range(ALPHA):
        cols = slice(p * DF, (p + 1) * DF)
        du = du_in[:, cols]
        dz = fe.back(du, fe.hat(L.zfe[:, cols]), inside, a_sum, wide(total, row + 1, 1), sf[1]).astype(BF16)
        dz_fe[:, cols] = dz
        back = back + dot_nt(dz, fe_bd[:, cols])
        dz = fk.back(du, fk.hat(L.zfk[:, cols]), inside, a_sum, wide(total, row + 2, 1), sf[1])
        dz_fk[:, cols] = dz.astype(BF16)
    z = L.zfs[...]
    dy = back * slope(fs.out(z))
    put_rows(pay, out_row, col_sum(dy))
    put_rows(pay, out_row + 1, col_sum(dy * fs.hat(z)))
    return dy, z


def pack_halo(pairs, shape, dy_out, halo_out):
    dy = jnp.concatenate([one for one, _ in pairs], axis=1) if len(pairs) > 1 else pairs[0][0]
    dy_out[...] = dy
    send_halo(jnp.concatenate([dy] + [z for _, z in pairs], axis=1), shape, *halo_out)


def spatial_gradient(parts, shape, si, sf, dy_in, halo_refs, pad, dz_out):
    t, h, w = shape
    width = dy_in.shape[1]

    def dz(dy, z, frame):
        inside = inside_rows(dy.shape[0], width, si[0] // (h * w) * frame)
        pieces, column = [], 0
        for norm, _, a_sum, b_sum, inv in parts:
            cols = slice(column, column + norm.mean.shape[1])
            pieces.append(norm.back(dy[:, cols], norm.hat(z[:, cols]), inside[:, cols], a_sum, b_sum, inv))
            column = cols.stop
        value = jnp.concatenate(pieces, axis=1) if len(pieces) > 1 else pieces[0]
        return value.astype(BF16)

    def arrived(ref, frame):
        value = ref[...].astype(F32)
        return dz(value[:, :width], value[:, width:], frame).astype(F32)

    z = jnp.concatenate([part[1] for part in parts], axis=1) if len(parts) > 1 else parts[0][1]
    own = dz(dy_in[...], z, h * w)
    dz_out[...] = own
    above, below, o_above, o_own, o_below = (
        arrived(ref, h * w if i == 3 else w) for i, ref in enumerate(halo_refs)
    )
    others = (o_above * sf[2], o_own, o_below * sf[3])
    fill_padded(pad, shape, own.astype(F32), above * sf[2], below * sf[3], others, sf[4], sf[5])


def spatial_part(norm, z, total, row, columns, inv):
    count = columns // LANES
    if columns == LANES:
        total = fold_phases(total)
    return norm, z, wide(total, row, count), wide(total, row + count, count), inv


def spatial_back(pad, shape, slow_w, fast_w):
    back, back_f = 0.0, 0.0
    for a in range(3):
        for b in range(3):
            part = tap(pad, shape, 2 - a, 2 - b)
            if slow_w is not None:
                back = back + dot_nt(part[:, :BS], slow_w[0, a, b])
            if fast_w is not None:
                back_f = back_f + dot_nt(part[:, part.shape[1] - LANES :], fast_w[a, b])
    return back, back_f


def finish_spatial(norm, z, back, dy_out, pay, row):
    dy = back * slope(norm.out(z))
    dy_out[...] = dy
    put_rows(pay, row, col_sum(dy))
    put_rows(pay, row + dy.shape[1] // LANES, col_sum(dy * norm.hat(z)))


def temporal_slow(L, frame, inside, sf, total, row, dy_in, dlow, st_w, dz_st, dy_lat, pay, out_row):
    st, lat = norms_of(L, sf, "st", "lat")
    dz = st.back(
        dy_in[...], st.hat(L.zst[...]), inside, wide(total, row, 2), wide(total, row + 2, 2), sf[0]
    ).astype(BF16)
    dz_st[:, :BS] = up(dz, frame)
    dz_st[:, BS : 2 * BS] = dz
    dz_st[:, 2 * BS :] = down(dz, frame)

    def back(cols):
        part = dlow[:, cols]
        for j in range(3):
            part = part + dot_nt(dz_st[:, j * BS : (j + 1) * BS], st_w[0, j, cols, :])
        return part

    z = L.zlat[...]
    dy = back(slice(DS, CC)) * slope(lat.out(z))
    dy_lat[...] = dy
    put_rows(pay, out_row, col_sum(dy))
    put_rows(pay, out_row + 2, col_sum(dy * lat.hat(z)))
    return back


def temporal_fast(L, frame, inside, sf, total, row, dy_in, dz_ft, dz_fk, fk_w, ft_band):
    (ft,) = norms_of(L, sf, "ft")
    folded = fold_phases(total)
    dz = ft.back(
        dy_in[...], ft.hat(L.zft[...]), inside[:, :LANES], wide(folded, row, 1), wide(folded, row + 1, 1), sf[1]
    ).astype(BF16)
    dz_ft[...] = dz

    def grad(p):
        part = dot_nt(dz_fk[:, p * DF : (p + 1) * DF], fk_w[0]) + dot_nt(dz, ft_band[p + 1])
        if p == ALPHA - 1:
            part = part + up(dot_nt(dz, ft_band[0]), frame)
        if p == 0:
            part = part + down(dot_nt(dz, ft_band[5]), frame)
        return part

    return grad


def lateral_back(L, frame, inside, sf, total, row, dy_in, lat_w, dz_lat, grad):
    (lat,) = norms_of(L, sf, "lat")
    dz = lat.back(
        dy_in[...], lat.hat(L.zlat[...]), inside, wide(total, row, 2), wide(total, row + 2, 2), sf[0]
    ).astype(BF16)
    dz_lat[...] = dz

    def whole(p):
        part = grad(p)
        if p < 3:
            part = part + dot_nt(dz, lat_w[0, p + 2])
        if p >= 2:
            part = part + up(dot_nt(dz, lat_w[0, p - 2]), frame)
        return part

    return whole


def back_turn(shape, R, inside, si, sf):
    L = R.layer("a_")
    L.tot_se = R.tot
    R.tot[...] = gathered(R.recv)
    top_slow(L, inside, sf, lambda cols: R.slow_cot[:, cols], R.du_s, R.pay, 0, R.out_slow)
    top_fast(L, inside, sf, lambda p: phase(R.fast_cot, p), R.du_f, R.pay, 24, R.out_fast)
    fill_rows(R.pay, 27, 32)


def back_expand(shape, R, inside, si, sf):
    L = R.layer("a_")
    total = R.recv[...]
    slow = expand_slow(L, inside, sf, total, 0, R.du_s, R.se_w, R.dz_se, R.dz_sk, R.pay, 0)
    fast = expand_fast(L, inside, sf, total, 24, R.du_f, R.fe_bd, R.dz_fe, R.dz_fk, R.pay, 4)
    fill_rows(R.pay, 6, 8)
    pack_halo([slow, fast], shape, R.dy, (R.whole, R.top, R.bottom))


def back_spatial(shape, R, inside, si, sf):
    L = R.layer("a_")
    total = R.recv[...]
    ss, fs, st, ft = norms_of(L, sf, "ss", "fs", "st", "ft")
    parts = [
        spatial_part(ss, L.zss[...], total, 0, BS, sf[0]),
        spatial_part(fs, L.zfs[...], total, 4, LANES, sf[1]),
    ]
    spatial_gradient(parts, shape, si, sf, R.dy, (R.h0, R.h1, R.h2, R.h3, R.h4), R.pad, R.dz)
    back, back_f = spatial_back(R.pad, shape, R.ss_w, R.fs_bd)
    finish_spatial(st, L.zst[...], back, R.dy_st, R.pay, 0)
    finish_spatial(ft, L.zft[...], back_f, R.dy_ft, R.pay, 4)
    fill_rows(R.pay, 6, 8)


def back_temporal(shape, R, inside, si, sf):
    L, below = R.layer("a_"), R.layer("b_")
    frame = shape[1] * shape[2]
    total = R.recv[...]
    back = temporal_slow(L, frame, inside, sf, total, 0, R.dy_st, R.dlow, R.st_w, R.dz_st, R.dy_lat, R.pay, 0)
    top_slow(below, inside, sf, back, R.du_s, R.pay, 8)
    fill_rows(R.pay, 4, 8)
    grad = temporal_fast(L, frame, inside, sf, total, 4, R.dy_ft, R.dz_ft, R.dz_fk, R.fk_w, R.ft_band)
    for p in range(ALPHA):
        R.dfast[:, p * DF : (p + 1) * DF] = grad(p)


def back_lateral(shape, R, inside, si, sf):
    L, below = R.layer("a_"), R.layer("b_")
    frame = shape[1] * shape[2]
    total = R.recv[...]
    slow = expand_slow(below, inside, sf, total, 8, R.du_s, R.se_w, R.dz_se, R.dz_sk, R.pay, 0)
    pack_halo([slow], shape, R.dy, (R.whole, R.top, R.bottom))
    grad = lateral_back(
        L, frame, inside, sf, total, 0, R.dy_lat, R.lat_w, R.dz_lat, lambda p: R.dfast[:, p * DF : (p + 1) * DF]
    )
    top_fast(below, inside, sf, grad, R.du_f, R.pay, 4)
    fill_rows(R.pay, 7, 8)


def back_low_spatial(shape, R, inside, si, sf):
    L = R.layer("b_")
    total = R.recv[...]
    fast = expand_fast(L, inside, sf, total, 4, R.du_f, R.fe_bd, R.dz_fe, R.dz_fk, R.pay, 4)
    pack_halo([fast], shape, R.dy_fs, (R.whole, R.top, R.bottom))
    ss, st = norms_of(L, sf, "ss", "st")
    parts = [spatial_part(ss, L.zss[...], total, 0, BS, sf[0])]
    spatial_gradient(parts, shape, si, sf, R.dy, (R.h0, R.h1, R.h2, R.h3, R.h4), R.pad, R.dz)
    back, _ = spatial_back(R.pad, shape, R.ss_w, None)
    finish_spatial(st, L.zst[...], back, R.dy_st, R.pay, 0)
    fill_rows(R.pay, 6, 8)


def back_low_temporal(shape, R, inside, si, sf):
    L = R.layer("b_")
    frame = shape[1] * shape[2]
    total = R.recv[...]
    fs, ft = norms_of(L, sf, "fs", "ft")
    parts = [spatial_part(fs, L.zfs[...], total, 4, LANES, sf[1])]
    spatial_gradient(parts, shape, si, sf, R.dy_fs, (R.h0, R.h1, R.h2, R.h3, R.h4), R.pad, R.dz_f)
    _, back_f = spatial_back(R.pad, shape, None, R.fs_bd)
    finish_spatial(ft, L.zft[...], back_f, R.dy_ft, R.pay, 4)
    back = temporal_slow(L, frame, inside, sf, total, 0, R.dy_st, R.dlow, R.st_w, R.dz_st, R.dy_lat, R.pay, 0)
    fill_rows(R.pay, 6, 8)
    for c in range(0, DS, 256):
        R.dslow[:, c : c + 256] = back(slice(c, c + 256))


def back_low_lateral(shape, R, inside, si, sf):
    L = R.layer("b_")
    frame = shape[1] * shape[2]
    total = R.recv[...]
    grad = temporal_fast(L, frame, inside, sf, total, 4, R.dy_ft, R.dz_ft, R.dz_fk, R.fk_w, R.ft_band)
    grad = lateral_back(L, frame, inside, sf, total, 0, R.dy_lat, R.lat_w, R.dz_lat, grad)
    for p in range(ALPHA):
        R.dfast[:, p] = grad(p).reshape(shape[0], frame, DF)


def kernel_back_skip(dz_sk, sk_w, dlow):
    for k in range(0, CC, 256):
        dlow[:, k : k + 256] = dot_nt(dz_sk[...], sk_w[0, k : k + 256, :])


def part_tiles(si, tiles, ref, keep, send):
    side = si[2]
    for i in range(tiles // 2):
        keep[i] = ref[2 * i + side]
        send[i] = ref[2 * i + 1 - side]


def pick_phases(parts):
    place = lane(parts[0].shape) // BF
    return fold_phases(sum(jnp.where(place == p, part, 0.0) for p, part in enumerate(parts)))


SMALL_ROWS = 64
ROW_JOBS = {"planes": 4, "st": 2, "ss": 2, "lat": 2, "small": 7}


def job_rows(job, tiles):
    rows = {"planes": 4 * (CC + BS), "st": 3 * CC, "ss": 9 * BS, "lat": 5 * DF, "small": SMALL_ROWS * tiles}
    return rows[job] // tiles


def bundle_rows(jobs, tiles):
    planes = job_rows("planes", tiles) if "planes" in jobs else 0
    small = SMALL_ROWS if "small" in jobs else 0
    rows = sum(job_rows(job, tiles) for job in jobs if job not in ("planes", "small"))
    return planes + -(-rows // 32) * 32 + small, planes, small


def share_rows(jobs, tiles):
    count, planes, small = bundle_rows(jobs, tiles)
    return planes // 2 + (count - planes - small) // 2 + 2 * small


def kernel_weights_rows(tiles, frame, jobs, si, *refs):
    kst, kss, kla, ksm = CC // tiles, BS // tiles, DF // tiles, BF // tiles
    count = sum(ROW_JOBS[job] for job in jobs)
    keep, send, blocks, small = refs[count:]
    rows, _, small_rows = bundle_rows(jobs, tiles)
    base = 0
    operands = list(refs[:count])
    for job in jobs:
        own = [operands.pop(0) for _ in range(ROW_JOBS[job])]
        if job == "planes":
            low, bt, dz_sk, dz_se = own
            ksk, kse = kst, kss
            for j in range(4):
                cols, start = slice(j * 256, (j + 1) * 256), base + j * (ksk + kse)
                d = dot_tn(low[...], dz_sk[:, cols]).astype(BF16)
                blocks[:, start : start + ksk, :] = d.reshape(tiles, ksk, 256)
                d = dot_tn(bt[...], dz_se[:, cols]).astype(BF16)
                blocks[:, start + ksk : start + ksk + kse, :] = d.reshape(tiles, kse, 256)
        elif job == "st":
            low, dz = own
            for j in range(3):
                d = dot_tn(low[...], dz[:, j * BS : (j + 1) * BS]).astype(BF16)
                blocks[:, base + j * kst : base + (j + 1) * kst, :] = d.reshape(tiles, kst, BS)
        elif job == "ss":
            a9, dz = own
            for k in range(9):
                d = dot_tn(a9[:, k * BS : (k + 1) * BS], dz[:, :BS]).astype(BF16)
                blocks[:, base + k * kss : base + (k + 1) * kss, :] = d.reshape(tiles, kss, BS)
        elif job == "lat":
            fb, dz = own
            f = [fb[:, p * DF : (p + 1) * DF] for p in range(3)] + [fb[:, 3 * DF :]]
            for k, x in enumerate([down(f[2], frame), down(f[3], frame), f[0], f[1], f[2]]):
                d = dot_tn(x, dz[...]).astype(BF16)
                blocks[:, base + k * kla : base + (k + 1) * kla, :] = d.reshape(tiles, kla, DL)
        else:
            af9, fb, bf, dz_f, dz_ft, dz_fe, dz_fk = own
            small[...] = jnp.zeros(small.shape, F32)
            last = dz_f.shape[1] - LANES
            for k in range(9):
                d = dot_tn(af9[:, k * LANES : (k + 1) * LANES], dz_f[:, last:])
                d = pick_phases([d[p * BF : (p + 1) * BF] for p in range(ALPHA)])
                for i in range(tiles):
                    small[i, k * ksm : (k + 1) * ksm, LANES:] = d[i * ksm : (i + 1) * ksm]
            f = [fb[:, p * DF : (p + 1) * DF] for p in range(ALPHA)]
            six = [dot_tn(x, dz_ft[...]) for x in [down(f[3], frame)] + f + [up(f[0], frame)]]
            for k in range(3):
                d = pick_phases([six[k + p] for p in range(ALPHA)])
                small[:, k * kla : (k + 1) * kla, :LANES] = d.reshape(tiles, kla, LANES)
            fe, fk = 0.0, 0.0
            for p in range(ALPHA):
                cols = slice(p * DF, (p + 1) * DF)
                fk = fk + dot_tn(fb[:, cols], dz_fk[:, cols])
                fe = fe + dot_tn(bf[...], dz_fe[:, cols])[p * BF : (p + 1) * BF, :]
            for i in range(tiles):
                small[i, 9 * ksm : 10 * ksm, LANES:] = fe[i * ksm : (i + 1) * ksm]
                small[i, 10 * ksm : 10 * ksm + kla, LANES:] = fk[i * kla : (i + 1) * kla]
            blocks[:, rows - small_rows :, :] = small[...].astype(BF16)
            continue
        base += job_rows(job, tiles)
    if rows - small_rows > base:
        blocks[:, base : rows - small_rows, :] = jnp.zeros((tiles, rows - small_rows - base, 256), BF16)
    part_tiles(si, tiles, blocks, keep, send)


def add(one, two):
    return (one.astype(F32) + two.astype(F32)).astype(BF16)


def kernel_halve_first(split, si, kept, got, keep_a, send_a, keep_b, send_b):
    low, high = si[1] % 2, si[1] // 2
    for i in range(2):
        for ref, side in ((keep_a, low), (send_a, 1 - low)):
            place = 2 * i + side
            ref[i] = add(kept[place, :split], got[place, :split])
        for ref, side in ((keep_b, high), (send_b, 1 - high)):
            place = 2 * side + i
            ref[i] = add(kept[place, split:], got[place, split:])


def kernel_halve_second(si, kept_a, got_a, kept_b, got_b, keep_a, send_a, keep_b, send_b):
    low, high = si[1] % 2, si[1] // 2
    for ref, place in ((keep_a, high), (send_a, 1 - high)):
        ref[...] = add(kept_a[place], got_a[place])
    for ref, place in ((keep_b, low), (send_b, 1 - low)):
        ref[...] = add(kept_b[place], got_b[place])


def kernel_halve_last(si, kept, got, keep, send):
    bit = si[3] // 2
    for ref, place in ((keep, bit), (send, 1 - bit)):
        ref[...] = add(kept[place], got[place])


def kernel_pick_places(si, kept, got, *outs):
    for i, ref in enumerate(outs):
        place = si[1] ^ i
        ref[...] = add(kept[place], got[place])


def whole_sum(parts):
    total = parts[0][...].astype(F32)
    for part in parts[1:]:
        total = total + part[...].astype(F32)
    return total


def columns_of(x, j):
    half = x.shape[0] // 2
    base = (j // 2) * LANES
    a, b = x[:half, base : base + LANES], x[half:, base : base + LANES]
    left = lane(a.shape) < 64
    if j % 2 == 0:
        return jnp.where(left, a, pltpu.roll(b, 64, 1))
    return jnp.where(left, pltpu.roll(a, 64, 1), b)


def column_blocks(jobs, tiles, total, blocks):
    count, planes, small_rows = bundle_rows(jobs, tiles)
    big = count - small_rows
    packed = (big - planes) // 2
    each = planes // 4
    for j in range(4):
        if planes:
            plane = total[j * each : (j + 1) * each].astype(BF16)
            blocks[j, :each, :] = plane[:, :LANES]
            blocks[j, each : 2 * each, :] = plane[:, LANES:]
        base = 2 * each
        if packed:
            blocks[j, base : base + packed, :] = columns_of(total[planes:big], j).astype(BF16)
        base += packed
        if small_rows:
            small = total[big:].astype(BF16)
            blocks[j, base : base + small_rows, :] = small[:, :LANES]
            blocks[j, base + small_rows :, :] = small[:, LANES:]


def kernel_pick_columns(jobs, tiles, si, a, b, c, d, out0, out1, out2, out3, blocks):
    column_blocks(jobs, tiles, whole_sum((a, b, c, d)), blocks)
    for i, ref in enumerate((out0, out1, out2, out3)):
        ref[...] = blocks[si[3] ^ i]


def kernel_join_columns(jobs, tiles, si, kept_a, got_a, kept_b, got_b, keep, send, blocks):
    total = jnp.concatenate([whole_sum((kept_a, got_a)), whole_sum((kept_b, got_b))], axis=0)
    column_blocks(jobs, tiles, total, blocks)
    bit = si[3] % 2
    for ref, side in ((keep, bit), (send, 1 - bit)):
        for i in range(2):
            ref[i] = blocks[2 * i + side]


def kernel_finish(tiles, plan, si, *refs):
    kst, kss, kla, ksm = CC // tiles, BS // tiles, DF // tiles, BF // tiles
    refs = list(refs)
    g_lat, g_st, g_ss, g_se, g_sk, g_ft, g_fs, g_fe, g_fk = refs[-9:]
    for jobs, layers, count in plan:
        total, refs = whole_sum(refs[:count]), refs[count:]
        rows, planes, small_rows = bundle_rows(jobs, tiles)
        start = planes // 2
        if planes:
            plane = jnp.concatenate([total[: start // 2], total[start // 2 : start]], axis=1)
            g_sk[layers[0]] = plane[:kst]
            g_se[layers[0]] = plane[kst:]
        packed = (rows - planes - small_rows) // 2
        big = total[start : start + packed]
        rows = [big[:, :64], pltpu.roll(big, 64, 1)[:, :64]] if packed else []
        tail = total[start + packed :]

        def part(start, size):
            end = start + size
            if end <= packed:
                return rows[0][start:end]
            if start >= packed:
                return rows[1][start - packed : end - packed]
            return jnp.concatenate([rows[0][start:], rows[1][: end - packed]], axis=0)

        base = 0
        for job, l in zip(jobs, layers):
            if job == "planes":
                continue
            if job == "st":
                for k in range(3):
                    g_st[l, k] = part(base + k * kst, kst).T
            elif job == "ss":
                for k in range(9):
                    g_ss[l, k // 3, k % 3] = part(base + k * kss, kss)
            elif job == "lat":
                for k in range(5):
                    g_lat[l, k] = part(base + k * kla, kla)
            else:
                small = tail[:SMALL_ROWS]
                eight = pltpu.roll(small, (LANES - 8 * si[3]) % LANES, 1)[:, :8]
                for k in range(3):
                    g_ft[l, k] = eight[k * kla : (k + 1) * kla].T
                small = tail[SMALL_ROWS:]
                eight = pltpu.roll(small, (LANES - 8 * si[3]) % LANES, 1)[:, :8]
                for k in range(9):
                    g_fs[l, k // 3, k % 3] = eight[k * ksm : (k + 1) * ksm]
                part32 = pltpu.roll(small, (LANES - 32 * si[3]) % LANES, 1)[:, :32]
                g_fe[l] = part32[9 * ksm : 10 * ksm]
                g_fk[l] = part32[10 * ksm : 10 * ksm + kla]
                continue
            base += job_rows(job, tiles)


def kernel_norm_sums(places, *refs):
    d_gains, d_biases = refs[-2:]
    for l in range(LAYERS):
        for i, out in ((0, d_biases), (1, d_gains)):
            column = 0
            for n, row, second, count in places[l][:5]:
                row += i * second
                for r in range(row, row + count):
                    out[l : l + 1, column : column + LANES] = refs[n][r : r + 1, :]
                    column += LANES
            ft, fs, fe, fk = (
                refs[n][row + i * second : row + i * second + 1, :] for n, row, second, _ in places[l][5:]
            )
            ft, fs = fold_phases(ft), fold_phases(fs)
            fe, fk = pltpu.roll(fe, 64, 1), pltpu.roll(fk, 64, 1)
            place = lane((1, LANES))
            out[l : l + 1, column : column + LANES] = jnp.where(place < 32, ft, jnp.where(place < 64, fs, fe))
            out[l : l + 1, column + LANES : column + 2 * LANES] = jnp.where(place < 64, fe, fk)
            out[l : l + 1, column + 2 * LANES :] = fk[:, :64]


SMEM = pltpu.MemorySpace.SMEM
VMEM = pltpu.MemorySpace.VMEM


class Weight:
    def __init__(self, array, layer):
        self.array = array
        self.layer = layer


class Layer:
    def __init__(self, array, layer):
        self.array = array
        self.layer = layer


class Load:
    def __init__(self, array):
        self.array = array


class Arriving:
    def __init__(self, copy, ref, layered):
        self.copy = copy
        self.ref = ref
        self.layered = layered
        self.shape = ref.shape

    def __getitem__(self, place):
        if self.copy is not None:
            self.copy.wait()
            self.copy = None
        if not self.layered:
            return self.ref[place]
        return self.ref[place[1:]] if isinstance(place, tuple) else self.ref[...]


class Out:
    def __init__(self, shape, kind):
        self.shape = shape
        self.kind = kind


def scalar_values(place, valid, frame, tiles):
    ha, wa, clip = place[0], place[1], place[2]
    total = valid[0]
    for i in range(1, valid.shape[0]):
        total = total + valid[i]
    count = jnp.full((1, LANES), total * (HT * WD), jnp.int32).astype(F32)
    inverse = 1.0 / count
    flags = [ha > 0, ha < tiles[0] - 1, wa > 0, wa < tiles[1] - 1]
    vectors = [jnp.where(jnp.full((1, LANES), jnp.where(f, 1, 0), jnp.int32) > 0, 1.0, 0.0) for f in flags]
    vectors = [inverse, inverse * (1.0 / ALPHA)] + vectors
    return (valid[clip] * frame, ha, wa, clip), [v[:, :1] for v in vectors]


def call(body, scalars, operands, outs, scratch=(), limit=16):
    mode, scalars = (None, ()) if not scalars else (scalars[0], scalars[1:3])
    count, first = len(operands), len(scalars)
    weights = [i for i, x in enumerate(operands) if isinstance(x, (Weight, Load))]
    results = [i for i, x in enumerate(outs) if isinstance(x, Out)]
    arrays = [x.array if isinstance(x, (Weight, Layer, Load)) else x for x in operands]
    layered = [isinstance(x, Weight) for x in operands]
    shapes = [(x.shape, x.kind) if isinstance(x, Out) else x for x in outs]
    buffers = [pltpu.VMEM(arrays[i].shape[1:] if layered[i] else arrays[i].shape, arrays[i].dtype) for i in weights]
    buffers += [pltpu.VMEM(*shapes[i]) for i in results]
    own = first + count + len(outs)

    def wrapped(*refs):
        refs = list(refs)
        inner, rest = refs[own : own + len(buffers)], refs[own + len(buffers) :]
        arriving, leaving = [], []
        for n, i in enumerate(weights):
            source = refs[first + i].at[operands[i].layer] if layered[i] else refs[first + i]
            copy = pltpu.make_async_copy(source, inner[n], rest[-1].at[n])
            copy.start()
            refs[first + i] = Arriving(copy, inner[n], layered[i])
            arriving.append(refs[first + i])
        for i, x in enumerate(operands):
            if isinstance(x, Layer):
                refs[first + i] = refs[first + i].at[x.layer]
        for n, i in enumerate(results):
            n += len(weights)
            leaving.append(pltpu.make_async_copy(inner[n], refs[first + count + i], rest[-1].at[n]))
            refs[first + count + i] = inner[n]
        given = ()
        if mode is not None:
            t_frame, tiles = mode[1], mode[2]
            ints, vectors = scalar_values(refs[0], refs[1], t_frame, tiles) if mode[0] == "all" else (
                (None, refs[0][0], refs[0][1], refs[0][2]), None)
            given = (ints, vectors) if mode[0] == "all" else (ints,)
        body(*given, *refs[first:own], *(rest[:-1] if buffers else rest))
        for copy in leaving:
            copy.start()
        for one in arriving:
            if one.copy is not None:
                one.copy.wait()
        for copy in leaving:
            copy.wait()

    def space(i, some):
        return pl.BlockSpec(memory_space=pltpu.HBM if i in some else VMEM)

    return pl.pallas_call(
        wrapped,
        out_shape=[jax.ShapeDtypeStruct(shape, kind) for shape, kind in shapes],
        in_specs=[pl.BlockSpec(memory_space=SMEM) for _ in scalars] + [space(i, weights) for i in range(count)],
        out_specs=[space(i, results) for i in range(len(outs))],
        scratch_shapes=buffers
        + [pltpu.VMEM(shape, kind) for shape, kind in scratch]
        + ([pltpu.SemaphoreType.DMA((len(buffers),))] if buffers else []),
        cost_estimate=pl.CostEstimate(flops=2000000000, bytes_accessed=4000000, transcendentals=0),
        compiler_params=pltpu.CompilerParams(vmem_limit_bytes=limit << 20),
    )(*scalars, *arrays)


def sum_over(x, axis):
    step, count = 1, lax.axis_size(axis)
    while step < count:
        pair = x + flip(x, axis, step)
        if 4 * step <= count:
            pair = pair + (flip(x, axis, 2 * step) + flip(x, axis, 3 * step))
            step *= 2
        x = pair
        step *= 2
    return x


def sum_all(x):
    for axis in ("wa", "ha", "clip"):
        x = sum_over(x, axis)
    return x


def exchange(block):
    return lax.all_to_all(block, ALL_AXES, 0, 0)


def swap(x):
    return lax.ppermute(x, "wa", [(0, 1), (1, 0)])


def halo(z, top, bottom):
    count = lax.axis_size("ha")
    above = lax.ppermute(bottom, "ha", [(i, i + 1) for i in range(count - 1)])
    below = lax.ppermute(top, "ha", [(i + 1, i) for i in range(count - 1)])
    return [above, below, swap(above), swap(z), swap(below)]


def after(first, *rest):
    return lax.optimization_barrier((first,) + rest)


def flip(x, axis, step):
    return lax.ppermute(x, axis, [(i, i ^ step) for i in range(lax.axis_size(axis))])


ORDERS = (("wa", "clip", "ha"), ("wa", "ha", "clip"))
LAUNCH = {(1, 'wa'): ('A1',), (3, 'wa'): ('ST1',), (5, 'wa'): ('A0',), (6, 'wa'): ('T0',), (3, 'ha'): ('A1',), (5, 'ha'): ('ST1',)}
LAND = {(1, 'clip'): ('A1',), (2, 'ha'): ('A1',), (3, 'clip'): ('ST1',), (4, 'ha'): ('A1', 'ST1'), (5, 'clip'): ('A1', 'A0'), (6, 'ha'): ('ST1', 'A0', 'T0')}
BUNDLES = {1: [('A1', False, [('planes', 1)])], 3: [('ST1', False, [('ss', 1), ('st', 1)])], 5: [('A0', False, [('planes', 0), ('ss', 0), ('lat', 1), ('small', 1)])], 6: [('T0', False, [('st', 0)])], 7: [('L0', True, [('lat', 0), ('small', 0)])]}
START_LIMIT = 60
WAIT = {(2, "ha", "A1"), (6, "ha", "T0"), (6, "ha", "ST1"), (4, "ha", "ST1")}


def local(
    slow_in,
    fast_in,
    valid_frames,
    lateral_w,
    slow_temporal_w,
    slow_spatial_w,
    slow_expand_w,
    slow_skip_w,
    fast_temporal_w,
    fast_spatial_w,
    fast_expand_w,
    fast_skip_w,
    gains,
    biases,
    slow_cot,
    fast_cot,
):
    devices = lax.axis_size(ALL_AXES)
    clips, n_ha, n_wa = (lax.axis_size(a) for a in ALL_AXES)
    tiles = n_ha * n_wa
    _, t, h, w, _ = slow_in.shape
    shape = (t, h, w)
    frame = h * w
    rows = t * frame

    place = jnp.stack([lax.axis_index(a) for a in ("ha", "wa", "clip")]).astype(jnp.int32)
    scalars = (("all", frame, (n_ha, n_wa)), place, valid_frames)
    places = (("place", frame, (n_ha, n_wa)), place, valid_frames)

    slow2 = slow_in.reshape(rows, DS)
    fast4 = fast_in.reshape(t, ALPHA, frame, DF)
    slow_cot2 = slow_cot.reshape(rows, DS)
    fast_cot4 = fast_cot.reshape(t, ALPHA, frame, DF)

    def act(columns, kind=F32):
        return ((rows, columns), kind)

    def edges(columns):
        return [act(columns, BF16), ((t * w, columns), BF16), ((t * w, columns), BF16)]

    def pay(count):
        return ((count, LANES), F32)

    def bind(body, *static):
        return functools.partial(body, *static)

    pad_slow = ((t, h + 2, 3 * w, BS), F32)
    pad_fast = ((t, h + 2, 3 * w, LANES), F32)
    pad_both = ((t, h + 2, 3 * w, BS + LANES), F32)
    saved = []
    fb, zlat, zft, z16, top, bottom, zfk, sent, band = call(
        bind(kernel_start, shape),
        scalars,
        [Load(fast4), Weight(lateral_w, 0), Load(jnp.swapaxes(fast_temporal_w, 2, 3)), Weight(fast_skip_w, 0)],
        [act(512, BF16), act(DL), act(LANES), *edges(LANES), act(512), pay(8), ((LAYERS, 6, LANES, LANES), BF16)],
        limit=START_LIMIT,
    )
    recv = sum_all(sent)
    gb_all, fs_bd, fe_bd = call(
        kernel_prepare,
        (),
        [Load(gains), Load(biases), Load(fast_spatial_w), Load(fast_expand_w)],
        [((LAYERS, 2, GB_ROWS, LANES), F32), ((LAYERS, 3, 3, LANES, LANES), BF16), ((LAYERS, LANES, ALPHA * DF), BF16)],
    )
    gb = [Layer(gb_all, l) for l in range(LAYERS)]
    before = None
    for l in range(LAYERS):
        around = halo(z16, top, bottom)
        last = l == LAYERS - 1
        start = [recv, Load(slow2), gb[l]] if l == 0 else [recv, gb[l - 1], before["tot_sk"], before["zse"], before["zsk"], gb[l]]
        low, zst, z16, top, bottom, zsk, af9, zfs, sent = call(
            bind(kernel_temporal, l == 0, shape),
            scalars,
            start + [zlat, zft, *around, Weight(slow_temporal_w, l), Weight(slow_skip_w, l), Layer(fs_bd, l)],
            [act(CC, BF16), act(BS), *edges(BS), act(DS), act(9 * LANES, BF16), act(LANES), pay(24)],
            [pad_fast],
        )
        tot_lat = recv
        if l > 0:
            before["tot_se"] = tot_lat
        recv = sum_all(sent)
        around = halo(z16, top, bottom)
        a9, zss, bf, zfe, sent = call(
            bind(kernel_spatial, shape),
            scalars,
            [recv, gb[l], zst, *around, zfs, Weight(slow_spatial_w, l), Layer(fe_bd, l)],
            [act(9 * BS, BF16), act(BS), act(LANES, BF16), act(512), ((devices, 8, LANES), F32)],
            [pay(8), pad_slow],
        )
        tot_st = recv
        recv = exchange(sent)
        keep = dict(
            fb=fb, zlat=zlat, zft=zft, zfk=zfk, low=low, zst=zst, zsk=zsk, af9=af9, zfs=zfs, a9=a9, zss=zss, bf=bf,
            zfe=zfe, tot_lat=tot_lat, tot_fk=tot_lat, tot_st=tot_st, tot_sk=tot_st,
        )
        if last:
            bt, zse, sent, tot_ss = call(
                bind(kernel_expand, True, shape),
                scalars,
                [recv, gb[l], zss, Weight(slow_expand_w, l)],
                [act(BS, BF16), act(DS), ((devices, 16, LANES), F32), pay(8)],
                [pay(16)],
            )
        else:
            bt, zse, sent, tot_ss, fb, zlat, zft, z16, top, bottom, zfk = call(
                bind(kernel_expand, False, shape),
                scalars,
                [recv, gb[l], zss, Weight(slow_expand_w, l), tot_lat, zfe, zfk,
                 Weight(lateral_w, l + 1), Layer(band, l + 1), Weight(fast_skip_w, l + 1)],
                [act(BS, BF16), act(DS), pay(24), pay(8),
                 act(512, BF16), act(DL), act(LANES), *edges(LANES), act(512)],
            )
        recv = exchange(sent) if last else sum_all(sent)
        keep.update(bt=bt, zse=zse, tot_ss=tot_ss, tot_fe=tot_ss)
        saved.append(keep)
        before = keep

    for l in range(LAYERS):
        saved[l]["gb"] = gb[l]

    def stage(body, ins, outs, scratch=(), limit=16):
        names = list(ins) + list(outs) + [name for name, _ in scratch]

        def named(ints, vectors, *refs):
            body(shape, Refs(names, refs), inside_rows(rows, 256, ints[0]), ints, vectors)

        results = call(
            named, scalars, list(ins.values()), list(outs.values()), [kind for _, kind in scratch], limit
        )
        return dict(zip(outs, results))

    def layer(prefix, l, *names):
        return {prefix + name: saved[l][name] for name in names}

    def edge(columns):
        return dict(zip(("whole", "top", "bottom"), edges(columns)))

    def around_of(r):
        return {f"h{i}": x for i, x in enumerate(halo(r["whole"], r["top"], r["bottom"]))}

    narrow = clips == 4

    def halves_chain(keep, send, jobs):
        count = bundle_rows(jobs, tiles)[0]
        (got,) = yield [keep], [(send, "wa", 1)]
        split = count // 32 * 16
        a, b = (split, 256), (count - split, 256)
        keep_a, send_a, keep_b, send_b = call(
            bind(kernel_halve_first, split), places, [keep, got], [((2,) + x, BF16) for x in (a, a, b, b)]
        )
        got_a, got_b = yield [keep_a, keep_b], [(send_a, "ha", 1), (send_b, "ha", 2)]
        keep_a, send_a, keep_b, send_b = call(
            kernel_halve_second, places, [keep_a, got_a, keep_b, got_b], [(x, BF16) for x in (a, a, b, b)]
        )
        got_a, got_b = yield [keep_a, keep_b], [(send_a, "ha", 2), (send_b, "ha", 1)]
        parts = [keep_a, got_a, keep_b, got_b]
        if narrow:
            block = (share_rows(jobs, tiles), LANES)
            keep, send = call(
                bind(kernel_join_columns, jobs, tiles), places, parts, [((2,) + block, BF16)] * 2, [((4,) + block, BF16)]
            )
            (got,) = yield [keep], [(send, "clip", 1)]
            keep, send = call(kernel_halve_last, places, [keep, got], [(block, BF16)] * 2)
            (got,) = yield [keep], [(send, "clip", 2)]
            parts = [keep, got]
        yield parts, None

    def direct_chain(keep, send, jobs):
        count = bundle_rows(jobs, tiles)[0]
        (got,) = yield [keep], [(send, "wa", 1)]
        mine, *others = call(kernel_pick_places, places, [keep, got], [((count, 256), BF16)] * 4)
        got = yield [mine], [(x, "ha", i + 1) for i, x in enumerate(others)]
        parts = [mine, *got]
        if narrow:
            block = (share_rows(jobs, tiles), LANES)
            mine, *others = call(
                bind(kernel_pick_columns, jobs, tiles), places, parts, [(block, BF16)] * 4, [((4,) + block, BF16)]
            )
            got = yield [mine], [(x, "clip", i + 1) for i, x in enumerate(others)]
            parts = [mine, *got]
        yield parts, None

    class Running:
        def __init__(self, chain, jobs, layers):
            self.chain = chain
            self.jobs = jobs
            self.layers = layers
            self.got = None
            self.state = next(chain)

        def done(self):
            return self.state[1] is None

        def launch(self, x=None):
            if self.done() or self.got is not None:
                return
            sends = [send for send, _, _ in self.state[1]]
            if x is not None:
                _, *sends = after(x, *sends)
            self.got = [flip(send, axis, step) for send, (_, axis, step) in zip(sends, self.state[1])]

        def land(self, x):
            if self.got is None:
                return x
            x, *got = after(x, *self.got)
            self.got = None
            self.state = self.chain.send(got)
            return x

        def finish(self):
            while not self.done():
                self.launch()
                got, self.got = self.got, None
                self.state = self.chain.send(got)
                yield

    running = {}

    def bundle(name, chain, *parts):
        jobs, layers = tuple(p[0] for p in parts), tuple(p[1] for p in parts)
        operands = []
        for job, l, r in parts:
            k = saved[l]
            operands += {
                "planes": lambda: [k["low"], k["bt"], r["dz_sk"], r["dz_se"]],
                "st": lambda: [k["low"], r["dz_st"]],
                "ss": lambda: [k["a9"], r["dz"]],
                "lat": lambda: [k["fb"], r["dz_lat"]],
                "small": lambda: [k["af9"], k["fb"], k["bf"], r["dz_f"], r["dz_ft"], r["dz_fe"], r["dz_fk"]],
            }[job]()
        count = bundle_rows(jobs, tiles)[0]
        pair = call(
            bind(kernel_weights_rows, tiles, frame, jobs),
            places,
            operands,
            [((tiles // 2, count, 256), BF16)] * 2,
            [((tiles, count, 256), BF16), ((tiles, SMALL_ROWS, 256), F32)],
            limit=24,
        )
        running[name] = Running(chain(*pair, jobs), jobs, layers)

    def skip_back(l, r):
        (r["dlow"],) = call(kernel_back_skip, (), [r["dz_sk"], Weight(slow_skip_w, l)], [act(CC)])

    totals = []

    def total_of(x):
        n = len(totals)
        for axis in ORDERS[n % 2]:
            for name in LAND.get((n, axis), ()):
                x = running[name].land(x)
                if (n, axis, name) not in WAIT:
                    running[name].launch()
            x = sum_over(x, axis)
            for name in LAUNCH.get((n, axis), ()) + tuple(w[2] for w in WAIT if w[:2] == (n, axis)):
                running[name].launch(x)
        totals.append(x)
        return x

    one, two = LAYERS - 1, LAYERS - 2
    r1, r0 = {}, {}

    def start_bundles():
        for name, direct, parts in BUNDLES.get(len(totals), ()):
            chain = direct_chain if direct else halves_chain
            bundle(name, chain, *[(job, l, (r0, r1)[l]) for job, l in parts])

    slow_names, fast_names = ("gb", "tot_se", "tot_sk", "zse", "zsk"), ("tot_ss", "tot_lat", "zfe", "zfk")
    r1.update(stage(
        back_turn,
        dict(recv=recv, **layer("a_", one, *slow_names[:1], *slow_names[2:], *fast_names), slow_cot=Load(slow_cot2), fast_cot=Load(fast_cot4)),
        dict(out_slow=Out((rows, DS), F32), out_fast=Out((t, ALPHA, frame, DF), F32), du_s=act(DS), du_f=act(512), pay=pay(32), tot=pay(16)),
    ))
    saved[-1]["tot_se"] = r1["tot"]
    recv = total_of(r1["pay"])
    r1.update(stage(
        back_expand,
        dict(recv=recv, **layer("a_", one, *slow_names, *fast_names, "zss", "zfs"), du_s=r1["du_s"], du_f=r1["du_f"],
             se_w=Weight(slow_expand_w, one), fe_bd=Layer(fe_bd, one)),
        dict(dz_se=act(DS, BF16), dz_sk=act(DS, BF16), dz_fe=act(512, BF16), dz_fk=act(512, BF16), dy=act(BS + LANES),
             **edge(2 * (BS + LANES)), pay=pay(8)),
    ))
    skip_back(one, r1)
    start_bundles()
    recv = total_of(r1["pay"])
    r1.update(stage(
        back_spatial,
        dict(recv=recv, **layer("a_", one, "gb", "tot_sk", "tot_ss", "tot_lat", "zss", "zfs", "zst", "zft"), dy=r1["dy"],
             **around_of(r1), ss_w=Weight(slow_spatial_w, one), fs_bd=Layer(fs_bd, one)),
        dict(dz=act(BS + LANES, BF16), dy_st=act(BS), dy_ft=act(LANES), pay=pay(8)),
        [("pad", pad_both)],
    ))
    r1["dz_f"] = r1["dz"]
    start_bundles()
    recv = total_of(r1["pay"])
    r1.update(stage(
        back_temporal,
        dict(recv=recv, **layer("a_", one, "gb", "tot_sk", "tot_lat", "zst", "zft", "zlat"),
             **layer("b_", two, *slow_names), dy_st=r1["dy_st"], dy_ft=r1["dy_ft"], dlow=r1["dlow"], dz_fk=r1["dz_fk"],
             st_w=Weight(slow_temporal_w, one), ft_band=Layer(band, one), fk_w=Weight(fast_skip_w, one)),
        dict(dz_st=act(3 * BS, BF16), dz_ft=act(LANES, BF16), dfast=act(512), dy_lat=act(DL), du_s=act(DS), pay=pay(32)),
    ))
    start_bundles()
    recv = total_of(r1["pay"])
    r0.update(stage(
        back_lateral,
        dict(recv=recv, **layer("a_", one, "gb", "tot_lat", "zlat"),
             **layer("b_", two, *slow_names, *fast_names, "zss"), dy_lat=r1["dy_lat"], dfast=r1["dfast"], du_s=r1["du_s"],
             lat_w=Weight(lateral_w, one), se_w=Weight(slow_expand_w, two)),
        dict(dz_lat=act(DL, BF16), du_f=act(512), dz_se=act(DS, BF16), dz_sk=act(DS, BF16), dy=act(BS), **edge(2 * BS), pay=pay(8)),
    ))
    r1["dz_lat"] = r0["dz_lat"]
    start_bundles()
    skip_back(two, r0)
    recv = total_of(r0["pay"])
    fast = stage(
        back_low_spatial,
        dict(recv=recv, **layer("b_", two, "gb", "tot_sk", "tot_ss", "tot_lat", "zss", "zst", "zfe", "zfk", "zfs"),
             du_f=r0["du_f"], dy=r0["dy"], **around_of(r0), ss_w=Weight(slow_spatial_w, two), fe_bd=Layer(fe_bd, two)),
        dict(dz_fe=act(512, BF16), dz_fk=act(512, BF16), dy_fs=act(LANES), **edge(2 * LANES), dz=act(BS, BF16), dy_st=act(BS),
             pay=pay(8)),
        [("pad", pad_slow)],
    )
    r0.update(fast)
    start_bundles()
    recv = total_of(r0["pay"])
    r0.update(stage(
        back_low_temporal,
        dict(recv=recv, **layer("b_", two, "gb", "tot_sk", "tot_lat", "zst", "zft", "zlat", "zfs"), dy_fs=r0["dy_fs"],
             **around_of(r0), dy_st=r0["dy_st"], dlow=r0["dlow"], st_w=Weight(slow_temporal_w, two), fs_bd=Layer(fs_bd, two)),
        dict(dz_f=act(LANES, BF16), dy_ft=act(LANES), dz_st=act(3 * BS, BF16), dy_lat=act(DL), dslow=Out((rows, DS), F32),
             pay=pay(8)),
        [("pad", pad_fast)],
    ))
    start_bundles()
    recv = total_of(r0["pay"])
    r0.update(stage(
        back_low_lateral,
        dict(recv=recv, **layer("b_", two, "gb", "tot_lat", "zft", "zlat"), dy_ft=r0["dy_ft"], dy_lat=r0["dy_lat"],
             dz_fk=r0["dz_fk"], lat_w=Weight(lateral_w, two), ft_band=Layer(band, two), fk_w=Weight(fast_skip_w, two)),
        dict(dz_ft=act(LANES, BF16), dz_lat=act(DL, BF16), dfast=Out((t, ALPHA, frame, DF), F32)),
    ))
    start_bundles()
    ways = [chain.finish() for chain in running.values()]
    while ways:
        ways = [way for way in ways if next(way, 0) is None]
    out_slow, out_fast, grad_slow, grad_fast = r1["out_slow"], r1["out_fast"], r0["dslow"], r0["dfast"]
    where = [
        [(6, 0, 2, 2), (5, 0, 2, 2), (4, 0, 2, 2), (3, 8, 8, 8), (3, 8, 16, 8), (6, 4, 1, 1), (5, 4, 1, 1), (4, 4, 1, 1),
         (4, 4, 2, 1)],
        [(3, 0, 2, 2), (2, 0, 2, 2), (1, 0, 2, 2), (0, 0, 8, 8), (0, 0, 16, 8), (2, 4, 1, 1), (1, 4, 1, 1), (0, 24, 1, 1),
         (0, 24, 2, 1)],
    ]
    nst, nss, nla, nsm = CC // tiles, BS // tiles, DF // tiles, BF // tiles
    n, f, g = BS // clips, BF // clips, DF // clips
    sums = call(bind(kernel_norm_sums, where), (), totals, [Out(gains.shape, F32), Out(biases.shape, F32)])
    weights = [(LAYERS,) + dims for dims in (
        (5, nla, n), (3, nst, n), (3, 3, nss, n), (nss, DS // clips), (nst, DS // clips),
        (3, nla, f), (3, 3, nsm, f), (nsm, g), (nla, g),
    )]
    chains = list(running.values())
    if narrow:
        plan = [(chain.jobs, chain.layers, len(chain.state[0])) for chain in chains]
        parts = [x for chain in chains for x in chain.state[0]]
        turned = (1, 5)
        weights = [dims[:-2] + dims[:-3:-1] if i in turned else dims for i, dims in enumerate(weights)]
        weights = call(bind(kernel_finish, tiles, plan), places, parts, [Out(dims, F32) for dims in weights])
        weights = [jnp.swapaxes(x, -1, -2) if i in turned else x for i, x in enumerate(weights)]
    else:
        found = {}
        for chain in chains:
            got = [x.astype(F32) for x in chain.state[0]]
            if chain.jobs != ("lat", "small"):
                total = jnp.concatenate([got[0] + got[1], got[2] + got[3]], axis=0).astype(BF16)
            else:
                total = sum(got).astype(BF16)
            count, planes, small_rows = bundle_rows(chain.jobs, tiles)
            if planes:
                plane = jnp.transpose(total[:planes].reshape(4, -1, 256), (1, 0, 2)).reshape(planes // 4, clips, DS // clips)
                plane = lax.psum_scatter(plane, "clip", scatter_dimension=1)
                found["sk", chain.layers[0]], found["se", chain.layers[0]] = plane[:nst], plane[nst:]
            small = lax.psum(total[count - small_rows :], "clip") if small_rows else None
            if count - small_rows > planes:
                total = lax.psum_scatter(
                    total[planes : count - small_rows].reshape(-1, clips, n), "clip", scatter_dimension=1
                )
            base = 0
            for job, l in zip(chain.jobs, chain.layers):
                if job == "small":
                    left = lax.dynamic_slice_in_dim(small[:, :LANES], place[2] * f, f, 1)
                    right = lax.dynamic_slice_in_dim(small[:, LANES:], place[2] * f, f, 1)
                    last = lax.dynamic_slice_in_dim(small[:, LANES:], place[2] * g, g, 1)
                    found["ft", l], found["fs", l] = left[: 3 * nla], right[: 9 * nsm]
                    found["fe", l], found["fk", l] = last[9 * nsm : 10 * nsm], last[10 * nsm : 10 * nsm + nla]
                elif job != "planes":
                    found[job, l] = total[base : base + job_rows(job, tiles)]
                    base += job_rows(job, tiles)
        names = ("lat", "st", "ss", "se", "sk", "ft", "fs", "fe", "fk")
        weights = [
            jnp.stack([found[name, l] for l in range(LAYERS)]).astype(F32).reshape(dims)
            for name, dims in zip(names, weights)
        ]
    return (
        out_slow.reshape(slow_in.shape),
        out_fast.reshape(fast_in.shape),
        grad_slow.reshape(slow_in.shape),
        grad_fast.reshape(fast_in.shape),
        *weights,
        *sums,
    )


def solution(mesh):
    pixels = P("clip", None, "ha", "wa", None)
    tile = ("ha", "wa")
    return jax.shard_map(
        local,
        mesh=mesh,
        in_specs=(pixels, pixels) + (P(),) * 12 + (pixels, pixels),
        out_specs=(
            (pixels,) * 4
            + (P(None, None, tile, "clip"),) * 2
            + (P(None, None, None, tile, "clip"),)
            + (P(None, tile, "clip"),) * 2
            + (P(None, None, tile, "clip"),)
            + (P(None, None, None, tile, "clip"),)
            + (P(None, tile, "clip"),) * 2
            + (P(),) * 2
        ),
        check_vma=False,
    )
```

```python
import functools

import jax
import jax.numpy as jnp
from jax import lax
from jax.experimental import pallas as pl
from jax.experimental.pallas import tpu as pltpu
from jax.sharding import PartitionSpec as P

DS = 1024
DL = 256
BS = 256
DF = 128
BF = 32
ST = 8
ALPHA = 4
HT = 16
WD = 16
LAYERS = 2
CC = DS + DL
EPSILON = 1e-05
LANES = 128
CLIP, HA, WA = "clip", "ha", "wa"
ALL_AXES = (CLIP, HA, WA)


LAT, STM, SSP, SEX, SSK, FTM, FSP, FEX, FSK = 0, 2, 4, 6, 14, 22, 23, 24, 25
GB_ROWS = 32

F32 = jnp.float32
BF16 = jnp.bfloat16


def dot(a, b):
    return jnp.dot(a, b, preferred_element_type=F32)


def dot_nt(a, b):
    return lax.dot_general(a, b, (((1,), (1,)), ((), ())), preferred_element_type=F32)


def dot_tn(a, b):
    return lax.dot_general(a, b, (((0,), (0,)), ((), ())), preferred_element_type=F32)


def sigmoid(v):
    return 0.5 * jnp.tanh(0.5 * v) + 0.5


def silu(v):
    return v * sigmoid(v)


def slope(v):
    s = sigmoid(v)
    return s + v * s * (1.0 - s)


def silu_and_slope(v):
    s = sigmoid(v)
    act = v * s
    return act, s + act * (1.0 - s)


def wide(tile, row, count):
    if count == 1:
        return tile[row : row + 1, :]
    return jnp.concatenate([tile[row + i : row + i + 1, :] for i in range(count)], axis=1)


def fold_phases(tile):
    return tile + pltpu.roll(tile, 32, 1) + pltpu.roll(tile, 64, 1) + pltpu.roll(tile, 96, 1)


def down(x, frame):
    return jnp.concatenate([jnp.zeros_like(x[:frame]), x[:-frame]], axis=0)


def up(x, frame):
    return jnp.concatenate([x[frame:], jnp.zeros_like(x[:frame])], axis=0)


def col_sum(x):
    return jnp.sum(x, axis=0, keepdims=True)


class Norm:
    def __init__(self, total, row, gb, gb_row, count, inv_count):
        mean = wide(total, row, count) * inv_count
        square = wide(total, row + count, count) * inv_count
        self.mean = mean
        self.rstd = lax.rsqrt(square - mean * mean + EPSILON)
        self.gain = wide(gb[0], gb_row, count)
        self.bias = wide(gb[1], gb_row, count)
        self.scale = self.gain * self.rstd
        self.shift = self.bias - mean * self.scale

    def columns(self, start, size):
        other = object.__new__(Norm)
        for name in ("mean", "rstd", "gain", "bias", "scale", "shift"):
            setattr(other, name, getattr(self, name)[:, start : start + size])
        return other

    def out(self, z):
        return z * self.scale + self.shift

    def hat(self, z):
        return (z - self.mean) * self.rstd

    def back(self, dy, hat, inside, a_sum, b_sum, inv_count):
        return self.scale * (dy - jnp.where(inside, a_sum * inv_count + hat * (b_sum * inv_count), 0.0))


def inside_rows(rows, columns, limit):
    return lax.broadcasted_iota(jnp.int32, (rows, columns), 0) < limit


def moments(z, inside):
    masked = jnp.where(inside, z, 0.0)
    return col_sum(masked), col_sum(masked * z)


def put_rows(ref, row, vector):
    for i in range(vector.shape[1] // LANES):
        ref[row + i : row + i + 1, :] = vector[:, i * LANES : (i + 1) * LANES]


def spread(tile, ref):
    def body(i, carry):
        ref[i] = tile[...]
        return carry

    lax.fori_loop(0, ref.shape[0], body, 0)


def gathered(ref):
    return jnp.sum(ref[...], axis=0)


def phase(ref, p):
    return ref[:, p].reshape(ref.shape[0] * ref.shape[2], ref.shape[3])


def send_halo(z, shape, si, whole, one, two):
    t, h, w = shape
    columns = z.shape[1]
    four = z.reshape(t, h, w, columns)
    whole[...] = z.astype(BF16)
    top, bottom = (four[:, i].reshape(t * w, columns) for i in (0, h - 1))
    if one.dtype == BF16:
        one[...] = top.astype(BF16)
        two[...] = bottom.astype(BF16)
        return
    even = jnp.full((t * w, columns), si[1] % 2, jnp.int32) == 0
    base = one.shape[0] - t * w * columns // LANES
    for ref, value in ((one, jnp.where(even, bottom, top)), (two, jnp.where(even, top, bottom))):
        for i in range(columns // LANES):
            ref[base + i * t * w : base + (i + 1) * t * w, :] = value[:, i * LANES : (i + 1) * LANES]


def send_sums(pay, one, two):
    if one.dtype == F32:
        for ref in (one, two):
            ref[: pay.shape[0], :] = pay[...]


def halo_values(si, edge, refs):
    one, two, other, o_one, o_two = refs
    if one.dtype == BF16:
        return [ref[...].astype(F32) for ref in (one, two, o_one, other, o_two)]
    columns = other.shape[1]
    base = one.shape[0] - edge * columns // LANES

    def rows(ref):
        parts = [ref[base + i * edge : base + (i + 1) * edge, :] for i in range(columns // LANES)]
        return jnp.concatenate(parts, axis=1) if len(parts) > 1 else parts[0]

    even = jnp.full((edge, columns), si[1] % 2, jnp.int32) == 0
    one, two, o_one, o_two = (rows(ref) for ref in (one, two, o_one, o_two))
    return [
        jnp.where(even, two, one), jnp.where(even, one, two),
        jnp.where(even, o_two, o_one), other[...].astype(F32), jnp.where(even, o_one, o_two),
    ]


def fill_padded(pad, shape, own, above, below, others, has_left, has_right):
    t, h, w = shape
    c = own.shape[1]
    pad[:, 1 : h + 1, w : 2 * w, :] = own.reshape(t, h, w, c)
    pad[:, 0, w : 2 * w, :] = above.reshape(t, w, c)
    pad[:, h + 1, w : 2 * w, :] = below.reshape(t, w, c)
    o_above, o_own, o_below = others
    for start, has in ((0, has_left), (2 * w, has_right)):
        pad[:, 1 : h + 1, start : start + w, :] = (o_own * has).reshape(t, h, w, c)
        pad[:, 0, start : start + w, :] = (o_above * has).reshape(t, w, c)
        pad[:, h + 1, start : start + w, :] = (o_below * has).reshape(t, w, c)


def tap(pad, shape, a, b):
    t, h, w = shape
    part = pad[:, a : a + h, w - 1 + b : 2 * w - 1 + b, :]
    return part.reshape(t * h * w, part.shape[-1]).astype(BF16)


def activate_padded(pad, shape, norm, own, halo_refs, si, sf):
    def act(z):
        return silu(norm.out(z.astype(F32))).astype(BF16).astype(F32)

    edge = shape[0] * shape[2]
    above, below, o_above, o_own, o_below = (act(x) for x in halo_values(si, edge, halo_refs))
    has_up, has_down = sf[2], sf[3]
    others = (o_above * has_up, o_own, o_below * has_down)
    fill_padded(pad, shape, act(own), above * has_up, below * has_down, others, sf[4], sf[5])


def fast_head(phases, shape, si, inside, lat_w, ft_band, fk_w, fb_out, zlat_out, zft_out, halo_out, zfk_out, pay, row):
    frame = shape[1] * shape[2]
    low = [v.astype(BF16) for v in phases]
    for p in range(ALPHA):
        fb_out[:, p * DF : (p + 1) * DF] = low[p]
    before2, before3, after0 = down(low[2], frame), down(low[3], frame), up(low[0], frame)
    z = (
        dot(before2, lat_w[0, 0])
        + dot(before3, lat_w[0, 1])
        + dot(low[0], lat_w[0, 2])
        + dot(low[1], lat_w[0, 3])
        + dot(low[2], lat_w[0, 4])
    )
    zlat_out[...] = z
    total, square = moments(z, inside[:, :DL])
    put_rows(pay, row, total)
    put_rows(pay, row + 2, square)
    six = [before3] + low + [after0]
    z = dot(six[0], ft_band[0])
    for j in range(1, 6):
        z = z + dot(six[j], ft_band[j])
    zft_out[...] = z
    send_halo(z, shape, si, *halo_out)
    total, square = moments(z, inside[:, :LANES])
    put_rows(pay, row + 4, total)
    put_rows(pay, row + 5, square)
    total, square = 0.0, 0.0
    for p in range(ALPHA):
        z = dot(low[p], fk_w[0])
        zfk_out[:, p * DF : (p + 1) * DF] = z
        one, two = moments(z, inside[:, :LANES])
        total, square = total + one, square + two
    put_rows(pay, row + 6, total)
    put_rows(pay, row + 7, square)


def place_columns(p):
    row = lax.broadcasted_iota(jnp.int32, (BF, LANES), 0)
    column = lax.broadcasted_iota(jnp.int32, (BF, LANES), 1)
    return jnp.where(column == row + BF * p, 1.0, 0.0).astype(BF16)


def kernel_start(shape, si, sf, fast, lat_w, ft_w, fk_w, fb, zlat, zft, z16, top, bottom, zfk, pay, ft_band):
    t, h, w = shape
    inside = inside_rows(t * h * w, DL, si[0])
    places = [place_columns(p) for p in range(ALPHA)]
    for l in range(LAYERS):
        for j in range(6):
            part = 0.0
            for p in range(ALPHA):
                if 0 <= j - p <= 2:
                    part = part + dot_tn(ft_w[l, j - p], places[p])
            ft_band[l, j] = part.astype(BF16)
    fast_head(
        [phase(fast, p) for p in range(ALPHA)],
        shape, si, inside, lat_w, ft_band.at[0], fk_w, fb, zlat, zft, (z16, top, bottom), zfk, pay, 0,
    )
    send_sums(pay, top, bottom)


def lane(shape):
    return lax.broadcasted_iota(jnp.int32, shape, len(shape) - 1)


def kernel_prepare(gains, biases, fs_w, fe_w, gb, fs_bd, fe_bd):
    for i, source in enumerate((gains, biases)):
        for l in range(LAYERS):
            for r in range(22):
                gb[l, i, r : r + 1, :] = source[l : l + 1, r * LANES : (r + 1) * LANES]
            v = source[l : l + 1, 22 * LANES : 23 * LANES]
            v2 = source[l : l + 1, 23 * LANES : 24 * LANES]
            v3 = jnp.concatenate([source[l : l + 1, 24 * LANES :], jnp.zeros((1, 64), F32)], axis=1)
            place = lane((1, LANES))
            gb[l, i, FTM : FTM + 1, :] = fold_phases(jnp.where(place < 32, v, 0.0))
            gb[l, i, FSP : FSP + 1, :] = fold_phases(jnp.where((place >= 32) & (place < 64), v, 0.0))
            v, v2, v3 = (pltpu.roll(x, 64, 1) for x in (v, v2, v3))
            gb[l, i, FEX : FEX + 1, :] = jnp.where(place < 64, v, v2)
            gb[l, i, FSK : FSK + 1, :] = jnp.where(place < 64, v2, v3)
            gb[l, i, 26:32, :] = jnp.zeros((6, LANES), F32)
    row = lax.broadcasted_iota(jnp.int32, (LANES, LANES), 0)
    column = lane((LANES, LANES))
    same = (row // BF) == (column // BF)
    spread_columns = 0.0
    for p in range(ALPHA):
        spread_columns = spread_columns + place_columns(p).astype(F32)
    spread_columns = spread_columns.astype(BF16)
    for l in range(LAYERS):
        for a in range(3):
            for b in range(3):
                part = dot(fs_w[l, a, b], spread_columns).astype(BF16)
                fs_bd[l, a, b] = jnp.where(same, dot_tn(spread_columns, part), 0.0).astype(BF16)
        fe_bd[l] = jnp.zeros((LANES, ALPHA * DF), BF16)
        for p in range(ALPHA):
            fe_bd[l, p * BF : (p + 1) * BF, p * DF : (p + 1) * DF] = fe_w[l]


def kernel_temporal(first, shape, si, sf, *refs):
    t, h, w = shape
    rows, frame = t * h * w, h * w
    if first:
        (recv, slow, gb, zlat, zft, h1, h2, h3, h4, h5, st_w, sk_w, fs_bd,
         low_out, zst, z16, top, bottom, zsk, af9, zfs, pay, pad) = refs
        row = 0
        total = recv[...]
    else:
        (recv, gb_before, tot_sk, zse_in, zsk_in, gb, zlat, zft, h1, h2, h3, h4, h5, st_w, sk_w, fs_bd,
         low_out, zst, z16, top, bottom, zsk, af9, zfs, pay, pad) = refs
        row = 16
        total = recv[...]
        inside = inside_rows(rows, 256, si[0])
        one = Norm(total, 0, gb_before, SEX, 8, sf[0])
        two = Norm(tot_sk[...], 8, gb_before, SSK, 8, sf[0])
        for c in range(0, DS, 256):
            u = one.columns(c, 256).out(zse_in[:, c : c + 256]) + two.columns(c, 256).out(zsk_in[:, c : c + 256])
            low_out[:, c : c + 256] = jnp.where(inside, silu(u), 0.0).astype(BF16)
    inside = inside_rows(rows, 256, si[0])
    lat = Norm(total, row, gb, LAT, 2, sf[0])
    ft = Norm(fold_phases(total), row + 4, gb, FTM, 1, sf[1])
    if first:
        low_out[:, :DS] = slow[...].astype(BF16)
    low_out[:, DS:] = silu(lat.out(zlat[...])).astype(BF16)
    activate_padded(pad, shape, ft, zft[...], (h1, h2, h3, h4, h5), si, sf)
    low = low_out[...]
    z = dot(low, st_w[0, 1])
    z = z + down(dot(low, st_w[0, 0]), frame)
    z = z + up(dot(low, st_w[0, 2]), frame)
    zst[...] = z
    send_halo(z, shape, si, z16, top, bottom)
    one, two = moments(z, inside)
    put_rows(pay, 0, one)
    put_rows(pay, 2, two)
    for a in range(3):
        for b in range(3):
            k = 3 * a + b
            af9[:, k * LANES : (k + 1) * LANES] = tap(pad, shape, a, b)
    z = dot(af9[...], fs_bd[...].reshape(9 * LANES, LANES))
    zfs[...] = z
    one, two = moments(z, inside[:, :LANES])
    put_rows(pay, 4, one)
    put_rows(pay, 5, two)
    pay[6:8, :] = jnp.zeros((2, LANES), F32)
    for c in range(0, DS, 256):
        z = dot(low, sk_w[0, :, c : c + 256])
        zsk[:, c : c + 256] = z
        one, two = moments(z, inside)
        put_rows(pay, 8 + c // LANES, one)
        put_rows(pay, 16 + c // LANES, two)
    send_sums(pay, top, bottom)


def kernel_spatial(shape, si, sf, recv, gb, zst, h1, h2, h3, h4, h5, zfs, ss_w, fe_bd,
                   a9, zss, bf, zfe, pays, pay, pad):
    t, h, w = shape
    inside = inside_rows(t * h * w, 256, si[0])
    total = recv[...]
    st = Norm(total, 0, gb, STM, 2, sf[0])
    fs = Norm(fold_phases(total), 4, gb, FSP, 1, sf[1])
    activate_padded(pad, shape, st, zst[...], (h1, h2, h3, h4, h5), si, sf)
    for a in range(3):
        for b in range(3):
            k = 3 * a + b
            a9[:, k * BS : (k + 1) * BS] = tap(pad, shape, a, b)
    z = dot(a9[...], ss_w[...].reshape(9 * BS, BS))
    zss[...] = z
    one, two = moments(z, inside)
    put_rows(pay, 0, one)
    put_rows(pay, 2, two)
    low = silu(fs.out(zfs[...])).astype(BF16)
    bf[...] = low
    total, square = 0.0, 0.0
    for p in range(ALPHA):
        z = dot(low, fe_bd[:, p * DF : (p + 1) * DF])
        zfe[:, p * DF : (p + 1) * DF] = z
        one, two = moments(z, inside[:, :LANES])
        total, square = total + one, square + two
    put_rows(pay, 4, total)
    put_rows(pay, 5, square)
    pay[6:8, :] = jnp.zeros((2, LANES), F32)
    spread(pay, pays)


def kernel_expand(last, shape, si, sf, *refs):
    t, h, w = shape
    inside = inside_rows(t * h * w, 256, si[0])
    if last:
        recv, gb, zss, se_w, bt, zse, pays, tot_out, pay = refs
    else:
        (recv, gb, zss, se_w, tot_fk, zfe, zfk, lat_w, ft_band, fk_w,
         bt, zse, pay, tot_out, fb, zlat, zft, z16, top, bottom, zfk_out) = refs
    total = gathered(recv)
    tot_out[...] = total
    ss = Norm(total, 0, gb, SSP, 2, sf[0])
    low = silu(ss.out(zss[...])).astype(BF16)
    bt[...] = low
    for c in range(0, DS, 256):
        z = dot(low, se_w[0, :, c : c + 256])
        zse[:, c : c + 256] = z
        one, two = moments(z, inside)
        put_rows(pay, c // LANES, one)
        put_rows(pay, 8 + c // LANES, two)
    if not last:
        fe = Norm(total, 4, gb, FEX, 1, sf[1])
        fk = Norm(tot_fk[...], tot_fk.shape[0] - 2, gb, FSK, 1, sf[1])
        phases = []
        for p in range(ALPHA):
            cols = slice(p * DF, (p + 1) * DF)
            u = fe.out(zfe[:, cols]) + fk.out(zfk[:, cols])
            phases.append(jnp.where(inside[:, :LANES], silu(u), 0.0))
        fast_head(
            phases, shape, si, inside, lat_w, ft_band, fk_w, fb, zlat, zft, (z16, top, bottom), zfk_out, pay, 16
        )
        send_sums(pay, top, bottom)
    else:
        spread(pay, pays)


class Refs:
    def __init__(self, names, refs):
        self.__dict__.update(zip(names, refs))

    def layer(self, prefix):
        own = {k[len(prefix) :]: v for k, v in self.__dict__.items() if k.startswith(prefix)}
        return Refs(own.keys(), own.values())


def norms_of(L, sf, *names):
    def make(name):
        if name == "se":
            return Norm(L.tot_se[...], 0, L.gb, SEX, 8, sf[0])
        if name == "sk":
            return Norm(L.tot_sk[...], 8, L.gb, SSK, 8, sf[0])
        if name == "ss":
            return Norm(L.tot_ss[...], 0, L.gb, SSP, 2, sf[0])
        if name == "st":
            return Norm(L.tot_sk[...], 0, L.gb, STM, 2, sf[0])
        if name == "lat":
            return Norm(L.tot_lat[...], L.tot_lat.shape[0] - 8, L.gb, LAT, 2, sf[0])
        if name == "ft":
            return Norm(fold_phases(L.tot_lat[...]), L.tot_lat.shape[0] - 4, L.gb, FTM, 1, sf[1])
        if name == "fk":
            return Norm(L.tot_lat[...], L.tot_lat.shape[0] - 2, L.gb, FSK, 1, sf[1])
        if name == "fs":
            return Norm(fold_phases(L.tot_sk[...]), 4, L.gb, FSP, 1, sf[1])
        return Norm(L.tot_ss[...], 4, L.gb, FEX, 1, sf[1])

    return [make(name) for name in names]


def fill_rows(pay, start, end):
    pay[start:end, :] = jnp.zeros((end - start, LANES), F32)


def top_slow(L, inside, sf, grad, du_out, pay, row, out=None):
    se, sk = norms_of(L, sf, "se", "sk")
    for c in range(0, DS, 256):
        cols = slice(c, c + 256)
        one, two = se.columns(c, 256), sk.columns(c, 256)
        hat1, hat2 = one.hat(L.zse[:, cols]), two.hat(L.zsk[:, cols])
        u = one.gain * hat1 + one.bias + (two.gain * hat2 + two.bias)
        act, rate = silu_and_slope(u)
        if out is not None:
            out[:, cols] = jnp.where(inside, act, 0.0)
        du = jnp.where(inside, grad(cols) * rate, 0.0)
        du_out[:, cols] = du
        put_rows(pay, row + c // LANES, col_sum(du))
        put_rows(pay, row + 8 + c // LANES, col_sum(du * hat1))
        put_rows(pay, row + 16 + c // LANES, col_sum(du * hat2))


def top_fast(L, inside, sf, grad, du_out, pay, row, out=None):
    fe, fk = norms_of(L, sf, "fe", "fk")
    inside = inside[:, :LANES]
    sums = [0.0, 0.0, 0.0]
    for p in range(ALPHA):
        cols = slice(p * DF, (p + 1) * DF)
        hat1, hat2 = fe.hat(L.zfe[:, cols]), fk.hat(L.zfk[:, cols])
        u = fe.gain * hat1 + fe.bias + (fk.gain * hat2 + fk.bias)
        act, rate = silu_and_slope(u)
        if out is not None:
            out[:, p] = jnp.where(inside, act, 0.0).reshape(out.shape[0], out.shape[2], DF)
        du = jnp.where(inside, grad(p) * rate, 0.0)
        du_out[:, cols] = du
        sums = [sums[0] + col_sum(du), sums[1] + col_sum(du * hat1), sums[2] + col_sum(du * hat2)]
    for i in range(3):
        put_rows(pay, row + i, sums[i])


def expand_slow(L, inside, sf, total, row, du_in, se_w, dz_se, dz_sk, pay, out_row):
    se, sk, ss = norms_of(L, sf, "se", "sk", "ss")
    back = 0.0
    for c in range(0, DS, 256):
        cols = slice(c, c + 256)
        r = row + c // LANES
        du = du_in[:, cols]
        a_sum = wide(total, r, 2)
        one, two = se.columns(c, 256), sk.columns(c, 256)
        dz = one.back(du, one.hat(L.zse[:, cols]), inside, a_sum, wide(total, 8 + r, 2), sf[0]).astype(BF16)
        dz_se[:, cols] = dz
        back = back + dot_nt(dz, se_w[0, :, cols])
        dz = two.back(du, two.hat(L.zsk[:, cols]), inside, a_sum, wide(total, 16 + r, 2), sf[0])
        dz_sk[:, cols] = dz.astype(BF16)
    z = L.zss[...]
    dy = back * slope(ss.out(z))
    put_rows(pay, out_row, col_sum(dy))
    put_rows(pay, out_row + 2, col_sum(dy * ss.hat(z)))
    return dy, z


def expand_fast(L, inside, sf, total, row, du_in, fe_bd, dz_fe, dz_fk, pay, out_row):
    fe, fk, fs = norms_of(L, sf, "fe", "fk", "fs")
    inside = inside[:, :LANES]
    back = 0.0
    a_sum = wide(total, row, 1)
    for p in range(ALPHA):
        cols = slice(p * DF, (p + 1) * DF)
        du = du_in[:, cols]
        dz = fe.back(du, fe.hat(L.zfe[:, cols]), inside, a_sum, wide(total, row + 1, 1), sf[1]).astype(BF16)
        dz_fe[:, cols] = dz
        back = back + dot_nt(dz, fe_bd[:, cols])
        dz = fk.back(du, fk.hat(L.zfk[:, cols]), inside, a_sum, wide(total, row + 2, 1), sf[1])
        dz_fk[:, cols] = dz.astype(BF16)
    z = L.zfs[...]
    dy = back * slope(fs.out(z))
    put_rows(pay, out_row, col_sum(dy))
    put_rows(pay, out_row + 1, col_sum(dy * fs.hat(z)))
    return dy, z


def pack_halo(pairs, shape, si, dy_out, halo_out):
    dy = jnp.concatenate([one for one, _ in pairs], axis=1) if len(pairs) > 1 else pairs[0][0]
    dy_out[...] = dy
    send_halo(jnp.concatenate([dy] + [z for _, z in pairs], axis=1), shape, si, *halo_out)


def spatial_gradient(parts, shape, si, sf, dy_in, halo_refs, pad, dz_out):
    t, h, w = shape
    width = dy_in.shape[1]

    def dz(dy, z, frame):
        inside = inside_rows(dy.shape[0], width, si[0] // (h * w) * frame)
        pieces, column = [], 0
        for norm, _, a_sum, b_sum, inv in parts:
            cols = slice(column, column + norm.mean.shape[1])
            pieces.append(norm.back(dy[:, cols], norm.hat(z[:, cols]), inside[:, cols], a_sum, b_sum, inv))
            column = cols.stop
        value = jnp.concatenate(pieces, axis=1) if len(pieces) > 1 else pieces[0]
        return value.astype(BF16)

    def arrived(value, frame):
        return dz(value[:, :width], value[:, width:], frame).astype(F32)

    z = jnp.concatenate([part[1] for part in parts], axis=1) if len(parts) > 1 else parts[0][1]
    own = dz(dy_in[...], z, h * w)
    dz_out[...] = own
    above, below, o_above, o_own, o_below = (
        arrived(x, h * w if i == 3 else w) for i, x in enumerate(halo_values(si, t * w, halo_refs))
    )
    others = (o_above * sf[2], o_own, o_below * sf[3])
    fill_padded(pad, shape, own.astype(F32), above * sf[2], below * sf[3], others, sf[4], sf[5])


def spatial_part(norm, z, total, row, columns, inv):
    count = columns // LANES
    if columns == LANES:
        total = fold_phases(total)
    return norm, z, wide(total, row, count), wide(total, row + count, count), inv


def spatial_back(pad, shape, slow_w, fast_w):
    back, back_f = 0.0, 0.0
    for a in range(3):
        for b in range(3):
            part = tap(pad, shape, 2 - a, 2 - b)
            if slow_w is not None:
                back = back + dot_nt(part[:, :BS], slow_w[0, a, b])
            if fast_w is not None:
                back_f = back_f + dot_nt(part[:, part.shape[1] - LANES :], fast_w[a, b])
    return back, back_f


def finish_spatial(norm, z, back, dy_out, pay, row):
    dy = back * slope(norm.out(z))
    dy_out[...] = dy
    put_rows(pay, row, col_sum(dy))
    put_rows(pay, row + dy.shape[1] // LANES, col_sum(dy * norm.hat(z)))


def temporal_slow(L, frame, inside, sf, total, row, dy_in, dlow, st_w, dz_st, dy_lat, pay, out_row):
    st, lat = norms_of(L, sf, "st", "lat")
    dz = st.back(
        dy_in[...], st.hat(L.zst[...]), inside, wide(total, row, 2), wide(total, row + 2, 2), sf[0]
    ).astype(BF16)
    dz_st[:, :BS] = up(dz, frame)
    dz_st[:, BS : 2 * BS] = dz
    dz_st[:, 2 * BS :] = down(dz, frame)

    def back(cols):
        part = dlow[:, cols]
        for j in range(3):
            part = part + dot_nt(dz_st[:, j * BS : (j + 1) * BS], st_w[0, j, cols, :])
        return part

    z = L.zlat[...]
    dy = back(slice(DS, CC)) * slope(lat.out(z))
    dy_lat[...] = dy
    put_rows(pay, out_row, col_sum(dy))
    put_rows(pay, out_row + 2, col_sum(dy * lat.hat(z)))
    return back


def temporal_fast(L, frame, inside, sf, total, row, dy_in, dz_ft, dz_fk, fk_w, ft_band):
    (ft,) = norms_of(L, sf, "ft")
    folded = fold_phases(total)
    dz = ft.back(
        dy_in[...], ft.hat(L.zft[...]), inside[:, :LANES], wide(folded, row, 1), wide(folded, row + 1, 1), sf[1]
    ).astype(BF16)
    dz_ft[...] = dz

    def grad(p):
        part = dot_nt(dz_fk[:, p * DF : (p + 1) * DF], fk_w[0]) + dot_nt(dz, ft_band[p + 1])
        if p == ALPHA - 1:
            part = part + up(dot_nt(dz, ft_band[0]), frame)
        if p == 0:
            part = part + down(dot_nt(dz, ft_band[5]), frame)
        return part

    return grad


def lateral_back(L, frame, inside, sf, total, row, dy_in, lat_w, dz_lat, grad):
    (lat,) = norms_of(L, sf, "lat")
    dz = lat.back(
        dy_in[...], lat.hat(L.zlat[...]), inside, wide(total, row, 2), wide(total, row + 2, 2), sf[0]
    ).astype(BF16)
    dz_lat[...] = dz

    def whole(p):
        part = grad(p)
        if p < 3:
            part = part + dot_nt(dz, lat_w[0, p + 2])
        if p >= 2:
            part = part + up(dot_nt(dz, lat_w[0, p - 2]), frame)
        return part

    return whole


def back_turn(shape, R, inside, si, sf):
    L = R.layer("a_")
    L.tot_se = R.tot
    R.tot[...] = gathered(R.recv)
    top_slow(L, inside, sf, lambda cols: R.slow_cot[:, cols], R.du_s, R.pay, 0, R.out_slow)
    top_fast(L, inside, sf, lambda p: phase(R.fast_cot, p), R.du_f, R.pay, 24, R.out_fast)
    fill_rows(R.pay, 27, 32)


def back_expand(shape, R, inside, si, sf):
    L = R.layer("a_")
    total = R.recv[...]
    slow = expand_slow(L, inside, sf, total, 0, R.du_s, R.se_w, R.dz_se, R.dz_sk, R.pay, 0)
    fast = expand_fast(L, inside, sf, total, 24, R.du_f, R.fe_bd, R.dz_fe, R.dz_fk, R.pay, 4)
    fill_rows(R.pay, 6, 8)
    pack_halo([slow, fast], shape, si, R.dy, (R.whole, R.top, R.bottom))
    send_sums(R.pay, R.top, R.bottom)


def back_spatial(shape, R, inside, si, sf):
    L = R.layer("a_")
    total = R.recv[...]
    ss, fs, st, ft = norms_of(L, sf, "ss", "fs", "st", "ft")
    parts = [
        spatial_part(ss, L.zss[...], total, 0, BS, sf[0]),
        spatial_part(fs, L.zfs[...], total, 4, LANES, sf[1]),
    ]
    spatial_gradient(parts, shape, si, sf, R.dy, (R.h0, R.h1, R.h2, R.h3, R.h4), R.pad, R.dz)
    back, back_f = spatial_back(R.pad, shape, R.ss_w, R.fs_bd)
    finish_spatial(st, L.zst[...], back, R.dy_st, R.pay, 0)
    finish_spatial(ft, L.zft[...], back_f, R.dy_ft, R.pay, 4)
    fill_rows(R.pay, 6, 8)


def back_temporal(shape, R, inside, si, sf):
    L, below = R.layer("a_"), R.layer("b_")
    frame = shape[1] * shape[2]
    total = R.recv[...]
    back = temporal_slow(L, frame, inside, sf, total, 0, R.dy_st, R.dlow, R.st_w, R.dz_st, R.dy_lat, R.pay, 0)
    top_slow(below, inside, sf, back, R.du_s, R.pay, 8)
    fill_rows(R.pay, 4, 8)
    grad = temporal_fast(L, frame, inside, sf, total, 4, R.dy_ft, R.dz_ft, R.dz_fk, R.fk_w, R.ft_band)
    for p in range(ALPHA):
        R.dfast[:, p * DF : (p + 1) * DF] = grad(p)


def back_lateral(shape, R, inside, si, sf):
    L, below = R.layer("a_"), R.layer("b_")
    frame = shape[1] * shape[2]
    total = R.recv[...]
    slow = expand_slow(below, inside, sf, total, 8, R.du_s, R.se_w, R.dz_se, R.dz_sk, R.pay, 0)
    pack_halo([slow], shape, si, R.dy, (R.whole, R.top, R.bottom))
    grad = lateral_back(
        L, frame, inside, sf, total, 0, R.dy_lat, R.lat_w, R.dz_lat, lambda p: R.dfast[:, p * DF : (p + 1) * DF]
    )
    top_fast(below, inside, sf, grad, R.du_f, R.pay, 4)
    fill_rows(R.pay, 7, 8)
    send_sums(R.pay, R.top, R.bottom)


def back_low_spatial(shape, R, inside, si, sf):
    L = R.layer("b_")
    total = R.recv[...]
    fast = expand_fast(L, inside, sf, total, 4, R.du_f, R.fe_bd, R.dz_fe, R.dz_fk, R.pay, 4)
    pack_halo([fast], shape, si, R.dy_fs, (R.whole, R.top, R.bottom))
    ss, st = norms_of(L, sf, "ss", "st")
    parts = [spatial_part(ss, L.zss[...], total, 0, BS, sf[0])]
    spatial_gradient(parts, shape, si, sf, R.dy, (R.h0, R.h1, R.h2, R.h3, R.h4), R.pad, R.dz)
    back, _ = spatial_back(R.pad, shape, R.ss_w, None)
    finish_spatial(st, L.zst[...], back, R.dy_st, R.pay, 0)
    fill_rows(R.pay, 6, 8)
    send_sums(R.pay, R.top, R.bottom)


def back_low_temporal(shape, R, inside, si, sf):
    L = R.layer("b_")
    frame = shape[1] * shape[2]
    total = R.recv[...]
    fs, ft = norms_of(L, sf, "fs", "ft")
    parts = [spatial_part(fs, L.zfs[...], total, 4, LANES, sf[1])]
    spatial_gradient(parts, shape, si, sf, R.dy_fs, (R.h0, R.h1, R.h2, R.h3, R.h4), R.pad, R.dz_f)
    _, back_f = spatial_back(R.pad, shape, None, R.fs_bd)
    finish_spatial(ft, L.zft[...], back_f, R.dy_ft, R.pay, 4)
    back = temporal_slow(L, frame, inside, sf, total, 0, R.dy_st, R.dlow, R.st_w, R.dz_st, R.dy_lat, R.pay, 0)
    fill_rows(R.pay, 6, 8)
    for c in range(0, DS, 256):
        R.dslow[:, c : c + 256] = back(slice(c, c + 256))


def back_low_lateral(shape, R, inside, si, sf):
    L = R.layer("b_")
    frame = shape[1] * shape[2]
    total = R.recv[...]
    grad = temporal_fast(L, frame, inside, sf, total, 4, R.dy_ft, R.dz_ft, R.dz_fk, R.fk_w, R.ft_band)
    grad = lateral_back(L, frame, inside, sf, total, 0, R.dy_lat, R.lat_w, R.dz_lat, grad)
    for p in range(ALPHA):
        R.dfast[:, p] = grad(p).reshape(shape[0], frame, DF)


def kernel_back_skip(dz_sk, sk_w, dlow):
    for k in range(0, CC, 256):
        dlow[:, k : k + 256] = dot_nt(dz_sk[...], sk_w[0, k : k + 256, :])


def part_tiles(si, tiles, ref, keep, send):
    side = si[2]
    for i in range(tiles // 2):
        keep[i] = ref[2 * i + side]
        send[i] = ref[2 * i + 1 - side]


def pick_phases(parts):
    place = lane(parts[0].shape) // BF
    return fold_phases(sum(jnp.where(place == p, part, 0.0) for p, part in enumerate(parts)))


SMALL_ROWS = 64
ROW_JOBS = {"pl": 4, "st": 2, "ss": 2, "lat": 2, "sm": 7}


def job_rows(job, tiles):
    rows = {"pl": 4 * (CC + BS), "st": 3 * CC, "ss": 9 * BS, "lat": 5 * DF, "sm": SMALL_ROWS * tiles}
    return rows[job] // tiles


def bundle_rows(jobs, tiles):
    planes = job_rows("pl", tiles) if "pl" in jobs else 0
    small = SMALL_ROWS if "sm" in jobs else 0
    rows = sum(job_rows(job, tiles) for job in jobs if job not in ("pl", "sm"))
    return planes + -(-rows // 32) * 32 + small, planes, small


def share_rows(jobs, tiles):
    count, planes, small = bundle_rows(jobs, tiles)
    return planes // 2 + (count - planes - small) // 2 + 2 * small


def kernel_weights_rows(tiles, frame, jobs, si, *refs):
    kst, kss, kla, ksm = CC // tiles, BS // tiles, DF // tiles, BF // tiles
    count = sum(ROW_JOBS[job] for job in jobs)
    keep, send, blocks, small = refs[count:]
    rows, _, small_rows = bundle_rows(jobs, tiles)
    base = 0
    operands = list(refs[:count])
    for job in jobs:
        own = [operands.pop(0) for _ in range(ROW_JOBS[job])]
        if job == "pl":
            low, bt, dz_sk, dz_se = own
            ksk, kse = kst, kss
            for j in range(4):
                cols, start = slice(j * 256, (j + 1) * 256), base + j * (ksk + kse)
                d = dot_tn(low[...], dz_sk[:, cols]).astype(BF16)
                blocks[:, start : start + ksk, :] = d.reshape(tiles, ksk, 256)
                d = dot_tn(bt[...], dz_se[:, cols]).astype(BF16)
                blocks[:, start + ksk : start + ksk + kse, :] = d.reshape(tiles, kse, 256)
        elif job == "st":
            low, dz = own
            for j in range(3):
                d = dot_tn(low[...], dz[:, j * BS : (j + 1) * BS]).astype(BF16)
                blocks[:, base + j * kst : base + (j + 1) * kst, :] = d.reshape(tiles, kst, BS)
        elif job == "ss":
            a9, dz = own
            for k in range(9):
                d = dot_tn(a9[:, k * BS : (k + 1) * BS], dz[:, :BS]).astype(BF16)
                blocks[:, base + k * kss : base + (k + 1) * kss, :] = d.reshape(tiles, kss, BS)
        elif job == "lat":
            fb, dz = own
            f = [fb[:, p * DF : (p + 1) * DF] for p in range(3)] + [fb[:, 3 * DF :]]
            for k, x in enumerate([down(f[2], frame), down(f[3], frame), f[0], f[1], f[2]]):
                d = dot_tn(x, dz[...]).astype(BF16)
                blocks[:, base + k * kla : base + (k + 1) * kla, :] = d.reshape(tiles, kla, DL)
        else:
            af9, fb, bf, dz_f, dz_ft, dz_fe, dz_fk = own
            small[...] = jnp.zeros(small.shape, F32)
            last = dz_f.shape[1] - LANES
            for k in range(9):
                d = dot_tn(af9[:, k * LANES : (k + 1) * LANES], dz_f[:, last:])
                d = pick_phases([d[p * BF : (p + 1) * BF] for p in range(ALPHA)])
                for i in range(tiles):
                    small[i, k * ksm : (k + 1) * ksm, LANES:] = d[i * ksm : (i + 1) * ksm]
            f = [fb[:, p * DF : (p + 1) * DF] for p in range(ALPHA)]
            six = [dot_tn(x, dz_ft[...]) for x in [down(f[3], frame)] + f + [up(f[0], frame)]]
            for k in range(3):
                d = pick_phases([six[k + p] for p in range(ALPHA)])
                small[:, k * kla : (k + 1) * kla, :LANES] = d.reshape(tiles, kla, LANES)
            fe, fk = 0.0, 0.0
            for p in range(ALPHA):
                cols = slice(p * DF, (p + 1) * DF)
                fk = fk + dot_tn(fb[:, cols], dz_fk[:, cols])
                fe = fe + dot_tn(bf[...], dz_fe[:, cols])[p * BF : (p + 1) * BF, :]
            for i in range(tiles):
                small[i, 9 * ksm : 10 * ksm, LANES:] = fe[i * ksm : (i + 1) * ksm]
                small[i, 10 * ksm : 10 * ksm + kla, LANES:] = fk[i * kla : (i + 1) * kla]
            blocks[:, rows - small_rows :, :] = small[...].astype(BF16)
            continue
        base += job_rows(job, tiles)
    if rows - small_rows > base:
        blocks[:, base : rows - small_rows, :] = jnp.zeros((tiles, rows - small_rows - base, 256), BF16)
    part_tiles(si, tiles, blocks, keep, send)


def add(one, two):
    return (one.astype(F32) + two.astype(F32)).astype(BF16)


def kernel_halve_first(split, si, kept, got, keep_a, send_a, keep_b, send_b):
    low, high = si[1] % 2, si[1] // 2
    for i in range(2):
        for ref, side in ((keep_a, low), (send_a, 1 - low)):
            place = 2 * i + side
            ref[i] = add(kept[place, :split], got[place, :split])
        for ref, side in ((keep_b, high), (send_b, 1 - high)):
            place = 2 * side + i
            ref[i] = add(kept[place, split:], got[place, split:])


def kernel_halve_second(si, kept_a, got_a, kept_b, got_b, keep_a, send_a, keep_b, send_b):
    low, high = si[1] % 2, si[1] // 2
    for ref, place in ((keep_a, high), (send_a, 1 - high)):
        ref[...] = add(kept_a[place], got_a[place])
    for ref, place in ((keep_b, low), (send_b, 1 - low)):
        ref[...] = add(kept_b[place], got_b[place])


def kernel_halve_last(si, kept, got, keep, send):
    bit = si[3] // 2
    for ref, place in ((keep, bit), (send, 1 - bit)):
        ref[...] = add(kept[place], got[place])


def kernel_pick_places(si, kept, got, *outs):
    for i, ref in enumerate(outs):
        place = si[1] ^ i
        ref[...] = add(kept[place], got[place])


def whole_sum(parts):
    total = parts[0][...].astype(F32)
    for part in parts[1:]:
        total = total + part[...].astype(F32)
    return total


def columns_of(x, j):
    half = x.shape[0] // 2
    base = (j // 2) * LANES
    a, b = x[:half, base : base + LANES], x[half:, base : base + LANES]
    left = lane(a.shape) < 64
    if j % 2 == 0:
        return jnp.where(left, a, pltpu.roll(b, 64, 1))
    return jnp.where(left, pltpu.roll(a, 64, 1), b)


def column_blocks(jobs, tiles, total, blocks):
    count, planes, small_rows = bundle_rows(jobs, tiles)
    big = count - small_rows
    packed = (big - planes) // 2
    each = planes // 4
    for j in range(4):
        if planes:
            plane = total[j * each : (j + 1) * each].astype(BF16)
            blocks[j, :each, :] = plane[:, :LANES]
            blocks[j, each : 2 * each, :] = plane[:, LANES:]
        base = 2 * each
        if packed:
            blocks[j, base : base + packed, :] = columns_of(total[planes:big], j).astype(BF16)
        base += packed
        if small_rows:
            small = total[big:].astype(BF16)
            blocks[j, base : base + small_rows, :] = small[:, :LANES]
            blocks[j, base + small_rows :, :] = small[:, LANES:]


def kernel_pick_columns(jobs, tiles, si, a, b, c, d, out0, out1, out2, out3, blocks):
    column_blocks(jobs, tiles, whole_sum((a, b, c, d)), blocks)
    for i, ref in enumerate((out0, out1, out2, out3)):
        ref[...] = blocks[si[3] ^ i]


def kernel_join_columns(jobs, tiles, si, kept_a, got_a, kept_b, got_b, keep, send, blocks):
    total = jnp.concatenate([whole_sum((kept_a, got_a)), whole_sum((kept_b, got_b))], axis=0)
    column_blocks(jobs, tiles, total, blocks)
    bit = si[3] % 2
    for ref, side in ((keep, bit), (send, 1 - bit)):
        for i in range(2):
            ref[i] = blocks[2 * i + side]


def kernel_finish(tiles, plan, si, *refs):
    kst, kss, kla, ksm = CC // tiles, BS // tiles, DF // tiles, BF // tiles
    refs = list(refs)
    g_lat, g_st, g_ss, g_se, g_sk, g_ft, g_fs, g_fe, g_fk = refs[-9:]
    for jobs, layers, count in plan:
        total, refs = whole_sum(refs[:count]), refs[count:]
        rows, planes, small_rows = bundle_rows(jobs, tiles)
        start = planes // 2
        if planes:
            plane = jnp.concatenate([total[: start // 2], total[start // 2 : start]], axis=1)
            g_sk[layers[0]] = plane[:kst]
            g_se[layers[0]] = plane[kst:]
        packed = (rows - planes - small_rows) // 2
        big = total[start : start + packed]
        rows = [big[:, :64], pltpu.roll(big, 64, 1)[:, :64]] if packed else []
        tail = total[start + packed :]

        def part(start, size):
            end = start + size
            if end <= packed:
                return rows[0][start:end]
            if start >= packed:
                return rows[1][start - packed : end - packed]
            return jnp.concatenate([rows[0][start:], rows[1][: end - packed]], axis=0)

        base = 0
        for job, l in zip(jobs, layers):
            if job == "pl":
                continue
            if job == "st":
                for k in range(3):
                    g_st[l, k] = part(base + k * kst, kst).T
            elif job == "ss":
                for k in range(9):
                    g_ss[l, k // 3, k % 3] = part(base + k * kss, kss)
            elif job == "lat":
                for k in range(5):
                    g_lat[l, k] = part(base + k * kla, kla)
            else:
                small = tail[:SMALL_ROWS]
                eight = pltpu.roll(small, (LANES - 8 * si[3]) % LANES, 1)[:, :8]
                for k in range(3):
                    g_ft[l, k] = eight[k * kla : (k + 1) * kla].T
                small = tail[SMALL_ROWS:]
                eight = pltpu.roll(small, (LANES - 8 * si[3]) % LANES, 1)[:, :8]
                for k in range(9):
                    g_fs[l, k // 3, k % 3] = eight[k * ksm : (k + 1) * ksm]
                part32 = pltpu.roll(small, (LANES - 32 * si[3]) % LANES, 1)[:, :32]
                g_fe[l] = part32[9 * ksm : 10 * ksm]
                g_fk[l] = part32[10 * ksm : 10 * ksm + kla]
                continue
            base += job_rows(job, tiles)


def kernel_norm_sums(places, *refs):
    d_gains, d_biases = refs[-2:]
    for l in range(LAYERS):
        for i, out in ((0, d_biases), (1, d_gains)):
            column = 0
            for n, row, second, count in places[l][:5]:
                row += i * second
                for r in range(row, row + count):
                    out[l : l + 1, column : column + LANES] = refs[n][r : r + 1, :]
                    column += LANES
            ft, fs, fe, fk = (
                refs[n][row + i * second : row + i * second + 1, :] for n, row, second, _ in places[l][5:]
            )
            ft, fs = fold_phases(ft), fold_phases(fs)
            fe, fk = pltpu.roll(fe, 64, 1), pltpu.roll(fk, 64, 1)
            place = lane((1, LANES))
            out[l : l + 1, column : column + LANES] = jnp.where(place < 32, ft, jnp.where(place < 64, fs, fe))
            out[l : l + 1, column + LANES : column + 2 * LANES] = jnp.where(place < 64, fe, fk)
            out[l : l + 1, column + 2 * LANES :] = fk[:, :64]


SMEM = pltpu.MemorySpace.SMEM
VMEM = pltpu.MemorySpace.VMEM


class Weight:
    def __init__(self, array, layer):
        self.array = array
        self.layer = layer


class Layer:
    def __init__(self, array, layer):
        self.array = array
        self.layer = layer


class Load:
    def __init__(self, array):
        self.array = array


class Arriving:
    def __init__(self, copy, ref, layered):
        self.copy = copy
        self.ref = ref
        self.layered = layered
        self.shape = ref.shape

    def __getitem__(self, place):
        if self.copy is not None:
            self.copy.wait()
            self.copy = None
        if not self.layered:
            return self.ref[place]
        return self.ref[place[1:]] if isinstance(place, tuple) else self.ref[...]


class Out:
    def __init__(self, shape, kind):
        self.shape = shape
        self.kind = kind


def scalar_values(place, valid, frame, tiles):
    ha, wa, clip = place[0], place[1], place[2]
    total = valid[0]
    for i in range(1, valid.shape[0]):
        total = total + valid[i]
    count = jnp.full((1, LANES), total * (HT * WD), jnp.int32).astype(F32)
    inverse = 1.0 / count
    flags = [ha > 0, ha < tiles[0] - 1, wa > 0, wa < tiles[1] - 1]
    vectors = [jnp.where(jnp.full((1, LANES), jnp.where(f, 1, 0), jnp.int32) > 0, 1.0, 0.0) for f in flags]
    vectors = [inverse, inverse * (1.0 / ALPHA)] + vectors
    return (valid[clip] * frame, ha, wa, clip), [v[:, :1] for v in vectors]


def call(body, scalars, operands, outs, scratch=(), limit=16, pinned=False):
    mode, scalars = (None, ()) if not scalars else (scalars[0], scalars[1:3])
    count, first = len(operands), len(scalars)
    weights = [i for i, x in enumerate(operands) if isinstance(x, (Weight, Load))]
    results = [i for i, x in enumerate(outs) if isinstance(x, Out)]
    arrays = [x.array if isinstance(x, (Weight, Layer, Load)) else x for x in operands]
    if pinned:
        for i in weights:
            arrays[i] = pltpu.with_memory_space_constraint(arrays[i], pltpu.HBM)
    layered = [isinstance(x, Weight) for x in operands]
    shapes = [(x.shape, x.kind) if isinstance(x, Out) else x for x in outs]
    buffers = [pltpu.VMEM(arrays[i].shape[1:] if layered[i] else arrays[i].shape, arrays[i].dtype) for i in weights]
    buffers += [pltpu.VMEM(*shapes[i]) for i in results]
    own = first + count + len(outs)

    def wrapped(*refs):
        refs = list(refs)
        inner, rest = refs[own : own + len(buffers)], refs[own + len(buffers) :]
        arriving, leaving = [], []
        for n, i in enumerate(weights):
            source = refs[first + i].at[operands[i].layer] if layered[i] else refs[first + i]
            copy = pltpu.make_async_copy(source, inner[n], rest[-1].at[n])
            copy.start()
            refs[first + i] = Arriving(copy, inner[n], layered[i])
            arriving.append(refs[first + i])
        for i, x in enumerate(operands):
            if isinstance(x, Layer):
                refs[first + i] = refs[first + i].at[x.layer]
        for n, i in enumerate(results):
            n += len(weights)
            leaving.append(pltpu.make_async_copy(inner[n], refs[first + count + i], rest[-1].at[n]))
            refs[first + count + i] = inner[n]
        given = ()
        if mode is not None:
            t_frame, tiles = mode[1], mode[2]
            ints, vectors = scalar_values(refs[0], refs[1], t_frame, tiles) if mode[0] == "all" else (
                (None, refs[0][0], refs[0][1], refs[0][2]), None)
            given = (ints, vectors) if mode[0] == "all" else (ints,)
        body(*given, *refs[first:own], *(rest[:-1] if buffers else rest))
        for copy in leaving:
            copy.start()
        for one in arriving:
            if one.copy is not None:
                one.copy.wait()
        for copy in leaving:
            copy.wait()

    def space(i, some):
        return pl.BlockSpec(memory_space=pltpu.HBM if i in some else VMEM)

    return pl.pallas_call(
        wrapped,
        out_shape=[jax.ShapeDtypeStruct(shape, kind) for shape, kind in shapes],
        in_specs=[pl.BlockSpec(memory_space=SMEM) for _ in scalars] + [space(i, weights) for i in range(count)],
        out_specs=[space(i, results) for i in range(len(outs))],
        scratch_shapes=buffers
        + [pltpu.VMEM(shape, kind) for shape, kind in scratch]
        + ([pltpu.SemaphoreType.DMA((len(buffers),))] if buffers else []),
        cost_estimate=pl.CostEstimate(flops=2000000000, bytes_accessed=4000000, transcendentals=0),
        compiler_params=pltpu.CompilerParams(vmem_limit_bytes=limit << 20),
    )(*scalars, *arrays)


def sum_over(x, axis):
    step, count = 1, lax.axis_size(axis)
    while step < count:
        pair = x + flip(x, axis, step)
        if 4 * step <= count:
            pair = pair + (flip(x, axis, 2 * step) + flip(x, axis, 3 * step))
            step *= 2
        x = pair
        step *= 2
    return x


def sum_all(x):
    for axis in (WA, HA, CLIP):
        x = sum_over(x, axis)
    return x


def exchange(block):
    return lax.all_to_all(block, ALL_AXES, 0, 0)


def swap(x):
    return lax.ppermute(x, WA, [(0, 1), (1, 0)])


def halo(z, top, bottom):
    count = lax.axis_size(HA)
    above = lax.ppermute(bottom, HA, [(i, i + 1) for i in range(count - 1)])
    below = lax.ppermute(top, HA, [(i + 1, i) for i in range(count - 1)])
    return [above, below, swap(z), swap(above), swap(below)]


def sum_with_halo(x, one, two, z):
    n = x.shape[0]
    one, two, across = flip(one, HA, 1), flip(two, HA, 3), flip(x, HA, 2)
    both = x + across
    o_one, o_two, o_both = swap(one), swap(two), swap(both)
    total = (both + (one[:n] + two[:n])) + (o_both + (o_one[:n] + o_two[:n]))
    return total, [one, two, swap(z), o_one, o_two]


def after(first, *rest):
    return lax.optimization_barrier((first,) + rest)


def flip(x, axis, step):
    return lax.ppermute(x, axis, [(i, i ^ step) for i in range(lax.axis_size(axis))])


ORDERS = ((WA, HA, CLIP), (WA, HA, CLIP), (WA, CLIP, HA), (WA, HA, CLIP), (WA, CLIP, HA), (WA, HA, CLIP), (WA, CLIP, HA))
LAUNCH = {(1, 'wa'): ('A1',), (3, 'wa'): ('ST1',), (5, 'wa'): ('A0',), (6, 'wa'): ('T0',), (3, 'ha'): ('A1',), (5, 'ha'): ('ST1',)}
LAND = {(1, 'clip'): ('A1',), (2, 'ha'): ('A1',), (3, 'clip'): ('ST1',), (4, 'ha'): ('A1', 'ST1'), (5, 'clip'): ('A1', 'A0'), (6, 'ha'): ('ST1', 'A0', 'T0')}
BUNDLES = {1: [('A1', False, [('pl', 1)])], 3: [('ST1', False, [('ss', 1), ('st', 1)])], 5: [('A0', False, [('pl', 0), ('ss', 0), ('lat', 1), ('sm', 1)])], 6: [('T0', False, [('st', 0)])], 7: [('L0', True, [('lat', 0), ('sm', 0)])]}
WAIT = {(2, HA, "A1"), (6, HA, "T0"), (6, HA, "ST1"), (4, HA, "ST1")}


def local(
    slow_in,
    fast_in,
    valid_frames,
    lateral_w,
    slow_temporal_w,
    slow_spatial_w,
    slow_expand_w,
    slow_skip_w,
    fast_temporal_w,
    fast_spatial_w,
    fast_expand_w,
    fast_skip_w,
    gains,
    biases,
    slow_cot,
    fast_cot,
):
    devices = lax.axis_size(ALL_AXES)
    clips, n_ha, n_wa = (lax.axis_size(a) for a in ALL_AXES)
    tiles = n_ha * n_wa
    _, t, h, w, _ = slow_in.shape
    shape = (t, h, w)
    frame = h * w
    rows = t * frame

    place = jnp.stack([lax.axis_index(a) for a in (HA, WA, CLIP)]).astype(jnp.int32)
    scalars = (("all", frame, (n_ha, n_wa)), place, valid_frames)
    places = (("place", frame, (n_ha, n_wa)), place, valid_frames)

    slow2 = slow_in.reshape(rows, DS)
    fast4 = fast_in.reshape(t, ALPHA, frame, DF)
    slow_cot2 = slow_cot.reshape(rows, DS)
    fast_cot4 = fast_cot.reshape(t, ALPHA, frame, DF)

    def act(columns, kind=F32):
        return ((rows, columns), kind)

    def edges(columns, sums=None):
        if sums is None:
            return [act(columns, BF16), ((t * w, columns), BF16), ((t * w, columns), BF16)]
        return [act(columns, BF16)] + [((sums + t * w * columns // LANES, LANES), F32)] * 2

    def pay(count):
        return ((count, LANES), F32)

    def bind(body, *static):
        return functools.partial(body, *static)

    pad_slow = ((t, h + 2, 3 * w, BS), F32)
    pad_fast = ((t, h + 2, 3 * w, LANES), F32)
    pad_both = ((t, h + 2, 3 * w, BS + LANES), F32)
    saved = []
    fb, zlat, zft, z16, top, bottom, zfk, sent, band = call(
        bind(kernel_start, shape),
        scalars,
        [Load(fast4), Weight(lateral_w, 0), Load(jnp.swapaxes(fast_temporal_w, 2, 3)), Weight(fast_skip_w, 0)],
        [act(512, BF16), act(DL), act(LANES), *edges(LANES, 8), act(512), pay(8), ((LAYERS, 6, LANES, LANES), BF16)],
        pinned=True,
    )
    recv, around = sum_with_halo(sent, top, bottom, z16)
    recv = sum_over(recv, CLIP)
    gb_all, fs_bd, fe_bd = call(
        kernel_prepare,
        (),
        [Load(gains), Load(biases), Load(fast_spatial_w), Load(fast_expand_w)],
        [((LAYERS, 2, GB_ROWS, LANES), F32), ((LAYERS, 3, 3, LANES, LANES), BF16), ((LAYERS, LANES, ALPHA * DF), BF16)],
        pinned=True,
    )
    gb = [Layer(gb_all, l) for l in range(LAYERS)]
    before = None
    for l in range(LAYERS):
        last = l == LAYERS - 1
        start = [recv, Load(slow2), gb[l]] if l == 0 else [recv, gb[l - 1], before["tot_sk"], before["zse"], before["zsk"], gb[l]]
        low, zst, z16, top, bottom, zsk, af9, zfs, sent = call(
            bind(kernel_temporal, l == 0, shape),
            scalars,
            start + [zlat, zft, *around, Weight(slow_temporal_w, l), Weight(slow_skip_w, l), Layer(fs_bd, l)],
            [act(CC, BF16), act(BS), *edges(BS, 24), act(DS), act(9 * LANES, BF16), act(LANES), pay(24)],
            [pad_fast],
            pinned=l == 0,
        )
        tot_lat = recv
        if l > 0:
            before["tot_se"] = tot_lat
        recv, around = sum_with_halo(sent, top, bottom, z16)
        recv = sum_over(recv, CLIP)
        a9, zss, bf, zfe, sent = call(
            bind(kernel_spatial, shape),
            scalars,
            [recv, gb[l], zst, *around, zfs, Weight(slow_spatial_w, l), Layer(fe_bd, l)],
            [act(9 * BS, BF16), act(BS), act(LANES, BF16), act(512), ((devices, 8, LANES), F32)],
            [pay(8), pad_slow],
        )
        tot_st = recv
        recv = exchange(sent)
        keep = dict(
            fb=fb, zlat=zlat, zft=zft, zfk=zfk, low=low, zst=zst, zsk=zsk, af9=af9, zfs=zfs, a9=a9, zss=zss, bf=bf,
            zfe=zfe, tot_lat=tot_lat, tot_fk=tot_lat, tot_st=tot_st, tot_sk=tot_st,
        )
        if last:
            bt, zse, sent, tot_ss = call(
                bind(kernel_expand, True, shape),
                scalars,
                [recv, gb[l], zss, Weight(slow_expand_w, l)],
                [act(BS, BF16), act(DS), ((devices, 16, LANES), F32), pay(8)],
                [pay(16)],
            )
        else:
            bt, zse, sent, tot_ss, fb, zlat, zft, z16, top, bottom, zfk = call(
                bind(kernel_expand, False, shape),
                scalars,
                [recv, gb[l], zss, Weight(slow_expand_w, l), tot_lat, zfe, zfk,
                 Weight(lateral_w, l + 1), Layer(band, l + 1), Weight(fast_skip_w, l + 1)],
                [act(BS, BF16), act(DS), pay(24), pay(8),
                 act(512, BF16), act(DL), act(LANES), *edges(LANES, 24), act(512)],
            )
        if last:
            recv = exchange(sent)
        else:
            recv, around = sum_with_halo(sent, top, bottom, z16)
            recv = sum_over(recv, CLIP)
        keep.update(bt=bt, zse=zse, tot_ss=tot_ss, tot_fe=tot_ss)
        saved.append(keep)
        before = keep

    for l in range(LAYERS):
        saved[l]["gb"] = gb[l]

    def stage(body, ins, outs, scratch=(), limit=16):
        names = list(ins) + list(outs) + [name for name, _ in scratch]

        def named(ints, vectors, *refs):
            body(shape, Refs(names, refs), inside_rows(rows, 256, ints[0]), ints, vectors)

        results = call(
            named, scalars, list(ins.values()), list(outs.values()), [kind for _, kind in scratch], limit
        )
        return dict(zip(outs, results))

    def layer(prefix, l, *names):
        return {prefix + name: saved[l][name] for name in names}

    def edge(columns, sums=None):
        return dict(zip(("whole", "top", "bottom"), edges(columns, sums)))

    def around_of(values):
        return {f"h{i}": x for i, x in enumerate(values)}

    narrow = clips == 4

    def halves_chain(keep, send, jobs):
        count = bundle_rows(jobs, tiles)[0]
        (got,) = yield [keep], [(send, WA, 1)]
        split = count // 32 * 16
        a, b = (split, 256), (count - split, 256)
        keep_a, send_a, keep_b, send_b = call(
            bind(kernel_halve_first, split), places, [keep, got], [((2,) + x, BF16) for x in (a, a, b, b)]
        )
        got_a, got_b = yield [keep_a, keep_b], [(send_a, HA, 1), (send_b, HA, 2)]
        keep_a, send_a, keep_b, send_b = call(
            kernel_halve_second, places, [keep_a, got_a, keep_b, got_b], [(x, BF16) for x in (a, a, b, b)]
        )
        got_a, got_b = yield [keep_a, keep_b], [(send_a, HA, 2), (send_b, HA, 1)]
        parts = [keep_a, got_a, keep_b, got_b]
        if narrow:
            block = (share_rows(jobs, tiles), LANES)
            keep, send = call(
                bind(kernel_join_columns, jobs, tiles), places, parts, [((2,) + block, BF16)] * 2, [((4,) + block, BF16)]
            )
            (got,) = yield [keep], [(send, CLIP, 1)]
            keep, send = call(kernel_halve_last, places, [keep, got], [(block, BF16)] * 2)
            (got,) = yield [keep], [(send, CLIP, 2)]
            parts = [keep, got]
        yield parts, None

    def direct_chain(keep, send, jobs):
        count = bundle_rows(jobs, tiles)[0]
        (got,) = yield [keep], [(send, WA, 1)]
        mine, *others = call(kernel_pick_places, places, [keep, got], [((count, 256), BF16)] * 4)
        got = yield [mine], [(x, HA, i + 1) for i, x in enumerate(others)]
        parts = [mine, *got]
        if narrow:
            block = (share_rows(jobs, tiles), LANES)
            mine, *others = call(
                bind(kernel_pick_columns, jobs, tiles), places, parts, [(block, BF16)] * 4, [((4,) + block, BF16)]
            )
            got = yield [mine], [(x, CLIP, i + 1) for i, x in enumerate(others)]
            parts = [mine, *got]
        yield parts, None

    class Running:
        def __init__(self, chain, jobs, layers):
            self.chain = chain
            self.jobs = jobs
            self.layers = layers
            self.got = None
            self.state = next(chain)

        def done(self):
            return self.state[1] is None

        def launch(self, x=None):
            if self.done() or self.got is not None:
                return
            sends = [send for send, _, _ in self.state[1]]
            if x is not None:
                _, *sends = after(x, *sends)
            self.got = [flip(send, axis, step) for send, (_, axis, step) in zip(sends, self.state[1])]

        def land(self, x):
            if self.got is None:
                return x
            x, *got = after(x, *self.got)
            self.got = None
            self.state = self.chain.send(got)
            return x

        def finish(self):
            while not self.done():
                self.launch()
                got, self.got = self.got, None
                self.state = self.chain.send(got)
                yield

    running = {}

    def bundle(name, chain, *parts):
        jobs, layers = tuple(p[0] for p in parts), tuple(p[1] for p in parts)
        operands = []
        for job, l, r in parts:
            k = saved[l]
            operands += {
                "pl": lambda: [k["low"], k["bt"], r["dz_sk"], r["dz_se"]],
                "st": lambda: [k["low"], r["dz_st"]],
                "ss": lambda: [k["a9"], r["dz"]],
                "lat": lambda: [k["fb"], r["dz_lat"]],
                "sm": lambda: [k["af9"], k["fb"], k["bf"], r["dz_f"], r["dz_ft"], r["dz_fe"], r["dz_fk"]],
            }[job]()
        count = bundle_rows(jobs, tiles)[0]
        pair = call(
            bind(kernel_weights_rows, tiles, frame, jobs),
            places,
            operands,
            [((tiles // 2, count, 256), BF16)] * 2,
            [((tiles, count, 256), BF16), ((tiles, SMALL_ROWS, 256), F32)],
            limit=24,
        )
        running[name] = Running(chain(*pair, jobs), jobs, layers)

    def skip_back(l, r):
        (r["dlow"],) = call(kernel_back_skip, (), [r["dz_sk"], Weight(slow_skip_w, l)], [act(CC)])

    totals = []

    around = []

    def total_of(x, edge_rows=None):
        n = len(totals)
        for axis in ORDERS[n]:
            for name in LAND.get((n, axis), ()):
                x = running[name].land(x)
                if (n, axis, name) not in WAIT:
                    running[name].launch()
            if edge_rows is None:
                x = sum_over(x, axis)
            elif axis == HA:
                x, around[:] = sum_with_halo(x, edge_rows["top"], edge_rows["bottom"], edge_rows["whole"])
            elif axis == CLIP:
                x = sum_over(x, axis)
            for name in LAUNCH.get((n, axis), ()) + tuple(w[2] for w in WAIT if w[:2] == (n, axis)):
                running[name].launch(x)
        totals.append(x)
        return x

    one, two = LAYERS - 1, LAYERS - 2
    r1, r0 = {}, {}

    def start_bundles():
        for name, direct, parts in BUNDLES.get(len(totals), ()):
            chain = direct_chain if direct else halves_chain
            bundle(name, chain, *[(job, l, (r0, r1)[l]) for job, l in parts])

    slow_names, fast_names = ("gb", "tot_se", "tot_sk", "zse", "zsk"), ("tot_ss", "tot_lat", "zfe", "zfk")
    r1.update(stage(
        back_turn,
        dict(recv=recv, **layer("a_", one, *slow_names[:1], *slow_names[2:], *fast_names), slow_cot=Load(slow_cot2), fast_cot=Load(fast_cot4)),
        dict(out_slow=Out((rows, DS), F32), out_fast=Out((t, ALPHA, frame, DF), F32), du_s=act(DS), du_f=act(512), pay=pay(32), tot=pay(16)),
    ))
    saved[-1]["tot_se"] = r1["tot"]
    recv = total_of(r1["pay"])
    r1.update(stage(
        back_expand,
        dict(recv=recv, **layer("a_", one, *slow_names, *fast_names, "zss", "zfs"), du_s=r1["du_s"], du_f=r1["du_f"],
             se_w=Weight(slow_expand_w, one), fe_bd=Layer(fe_bd, one)),
        dict(dz_se=act(DS, BF16), dz_sk=act(DS, BF16), dz_fe=act(512, BF16), dz_fk=act(512, BF16), dy=act(BS + LANES),
             **edge(2 * (BS + LANES)), pay=pay(8)),
    ))
    skip_back(one, r1)
    start_bundles()
    recv = total_of(r1["pay"])
    r1.update(stage(
        back_spatial,
        dict(recv=recv, **layer("a_", one, "gb", "tot_sk", "tot_ss", "tot_lat", "zss", "zfs", "zst", "zft"), dy=r1["dy"],
             **around_of(halo(r1["whole"], r1["top"], r1["bottom"])), ss_w=Weight(slow_spatial_w, one), fs_bd=Layer(fs_bd, one)),
        dict(dz=act(BS + LANES, BF16), dy_st=act(BS), dy_ft=act(LANES), pay=pay(8)),
        [("pad", pad_both)],
    ))
    r1["dz_f"] = r1["dz"]
    start_bundles()
    recv = total_of(r1["pay"])
    r1.update(stage(
        back_temporal,
        dict(recv=recv, **layer("a_", one, "gb", "tot_sk", "tot_lat", "zst", "zft", "zlat"),
             **layer("b_", two, *slow_names), dy_st=r1["dy_st"], dy_ft=r1["dy_ft"], dlow=r1["dlow"], dz_fk=r1["dz_fk"],
             st_w=Weight(slow_temporal_w, one), ft_band=Layer(band, one), fk_w=Weight(fast_skip_w, one)),
        dict(dz_st=act(3 * BS, BF16), dz_ft=act(LANES, BF16), dfast=act(512), dy_lat=act(DL), du_s=act(DS), pay=pay(32)),
    ))
    start_bundles()
    recv = total_of(r1["pay"])
    r0.update(stage(
        back_lateral,
        dict(recv=recv, **layer("a_", one, "gb", "tot_lat", "zlat"),
             **layer("b_", two, *slow_names, *fast_names, "zss"), dy_lat=r1["dy_lat"], dfast=r1["dfast"], du_s=r1["du_s"],
             lat_w=Weight(lateral_w, one), se_w=Weight(slow_expand_w, two)),
        dict(dz_lat=act(DL, BF16), du_f=act(512), dz_se=act(DS, BF16), dz_sk=act(DS, BF16), dy=act(BS), **edge(2 * BS), pay=pay(8)),
    ))
    r1["dz_lat"] = r0["dz_lat"]
    start_bundles()
    skip_back(two, r0)
    recv = total_of(r0["pay"])
    fast = stage(
        back_low_spatial,
        dict(recv=recv, **layer("b_", two, "gb", "tot_sk", "tot_ss", "tot_lat", "zss", "zst", "zfe", "zfk", "zfs"),
             du_f=r0["du_f"], dy=r0["dy"], **around_of(halo(r0["whole"], r0["top"], r0["bottom"])), ss_w=Weight(slow_spatial_w, two), fe_bd=Layer(fe_bd, two)),
        dict(dz_fe=act(512, BF16), dz_fk=act(512, BF16), dy_fs=act(LANES), **edge(2 * LANES), dz=act(BS, BF16), dy_st=act(BS),
             pay=pay(8)),
        [("pad", pad_slow)],
    )
    r0.update(fast)
    start_bundles()
    recv = total_of(r0["pay"])
    r0.update(stage(
        back_low_temporal,
        dict(recv=recv, **layer("b_", two, "gb", "tot_sk", "tot_lat", "zst", "zft", "zlat", "zfs"), dy_fs=r0["dy_fs"],
             **around_of(halo(r0["whole"], r0["top"], r0["bottom"])), dy_st=r0["dy_st"], dlow=r0["dlow"], st_w=Weight(slow_temporal_w, two), fs_bd=Layer(fs_bd, two)),
        dict(dz_f=act(LANES, BF16), dy_ft=act(LANES), dz_st=act(3 * BS, BF16), dy_lat=act(DL), dslow=Out((rows, DS), F32),
             pay=pay(8)),
        [("pad", pad_fast)],
    ))
    start_bundles()
    recv = total_of(r0["pay"])
    r0.update(stage(
        back_low_lateral,
        dict(recv=recv, **layer("b_", two, "gb", "tot_lat", "zft", "zlat"), dy_ft=r0["dy_ft"], dy_lat=r0["dy_lat"],
             dz_fk=r0["dz_fk"], lat_w=Weight(lateral_w, two), ft_band=Layer(band, two), fk_w=Weight(fast_skip_w, two)),
        dict(dz_ft=act(LANES, BF16), dz_lat=act(DL, BF16), dfast=Out((t, ALPHA, frame, DF), F32)),
    ))
    start_bundles()
    ways = [chain.finish() for chain in running.values()]
    while ways:
        ways = [way for way in ways if next(way, 0) is None]
    out_slow, out_fast, grad_slow, grad_fast = r1["out_slow"], r1["out_fast"], r0["dslow"], r0["dfast"]
    where = [
        [(6, 0, 2, 2), (5, 0, 2, 2), (4, 0, 2, 2), (3, 8, 8, 8), (3, 8, 16, 8), (6, 4, 1, 1), (5, 4, 1, 1), (4, 4, 1, 1),
         (4, 4, 2, 1)],
        [(3, 0, 2, 2), (2, 0, 2, 2), (1, 0, 2, 2), (0, 0, 8, 8), (0, 0, 16, 8), (2, 4, 1, 1), (1, 4, 1, 1), (0, 24, 1, 1),
         (0, 24, 2, 1)],
    ]
    nst, nss, nla, nsm = CC // tiles, BS // tiles, DF // tiles, BF // tiles
    n, f, g = BS // clips, BF // clips, DF // clips
    sums = call(bind(kernel_norm_sums, where), (), totals, [Out(gains.shape, F32), Out(biases.shape, F32)])
    weights = [(LAYERS,) + dims for dims in (
        (5, nla, n), (3, nst, n), (3, 3, nss, n), (nss, DS // clips), (nst, DS // clips),
        (3, nla, f), (3, 3, nsm, f), (nsm, g), (nla, g),
    )]
    chains = list(running.values())
    if narrow:
        plan = [(chain.jobs, chain.layers, len(chain.state[0])) for chain in chains]
        parts = [x for chain in chains for x in chain.state[0]]
        turned = (1, 5)
        weights = [dims[:-2] + dims[:-3:-1] if i in turned else dims for i, dims in enumerate(weights)]
        weights = call(bind(kernel_finish, tiles, plan), places, parts, [Out(dims, F32) for dims in weights])
        weights = [jnp.swapaxes(x, -1, -2) if i in turned else x for i, x in enumerate(weights)]
    else:
        found = {}
        for chain in chains:
            got = [x.astype(F32) for x in chain.state[0]]
            if chain.jobs != ("lat", "sm"):
                total = jnp.concatenate([got[0] + got[1], got[2] + got[3]], axis=0).astype(BF16)
            else:
                total = sum(got).astype(BF16)
            count, planes, small_rows = bundle_rows(chain.jobs, tiles)
            if planes:
                plane = jnp.transpose(total[:planes].reshape(4, -1, 256), (1, 0, 2)).reshape(planes // 4, clips, DS // clips)
                plane = lax.psum_scatter(plane, CLIP, scatter_dimension=1)
                found["sk", chain.layers[0]], found["se", chain.layers[0]] = plane[:nst], plane[nst:]
            small = lax.psum(total[count - small_rows :], CLIP) if small_rows else None
            if count - small_rows > planes:
                total = lax.psum_scatter(
                    total[planes : count - small_rows].reshape(-1, clips, n), CLIP, scatter_dimension=1
                )
            base = 0
            for job, l in zip(chain.jobs, chain.layers):
                if job == "sm":
                    left = lax.dynamic_slice_in_dim(small[:, :LANES], place[2] * f, f, 1)
                    right = lax.dynamic_slice_in_dim(small[:, LANES:], place[2] * f, f, 1)
                    last = lax.dynamic_slice_in_dim(small[:, LANES:], place[2] * g, g, 1)
                    found["ft", l], found["fs", l] = left[: 3 * nla], right[: 9 * nsm]
                    found["fe", l], found["fk", l] = last[9 * nsm : 10 * nsm], last[10 * nsm : 10 * nsm + nla]
                elif job != "pl":
                    found[job, l] = total[base : base + job_rows(job, tiles)]
                    base += job_rows(job, tiles)
        names = ("lat", "st", "ss", "se", "sk", "ft", "fs", "fe", "fk")
        weights = [
            jnp.stack([found[name, l] for l in range(LAYERS)]).astype(F32).reshape(dims)
            for name, dims in zip(names, weights)
        ]
    return (
        out_slow.reshape(slow_in.shape),
        out_fast.reshape(fast_in.shape),
        grad_slow.reshape(slow_in.shape),
        grad_fast.reshape(fast_in.shape),
        *weights,
        *sums,
    )


def solution(mesh):
    pixels = P(CLIP, None, HA, WA, None)
    tile = (HA, WA)
    return jax.shard_map(
        local,
        mesh=mesh,
        in_specs=(pixels, pixels) + (P(),) * 12 + (pixels, pixels),
        out_specs=(
            (pixels,) * 4
            + (P(None, None, tile, CLIP),) * 2
            + (P(None, None, None, tile, CLIP),)
            + (P(None, tile, CLIP),) * 2
            + (P(None, None, tile, CLIP),)
            + (P(None, None, None, tile, CLIP),)
            + (P(None, tile, CLIP),) * 2
            + (P(),) * 2
        ),
        check_vma=False,
    )
```

```python
import functools

import jax
import jax.numpy as jnp
from jax import lax
from jax.experimental import pallas as pl
from jax.experimental.pallas import tpu as pltpu
from jax.sharding import PartitionSpec as P

DS = 1024
DL = 256
BS = 256
DF = 128
BF = 32
ST = 8
ALPHA = 4
HT = 16
WD = 16
LAYERS = 2
CC = DS + DL
EPSILON = 1e-05
LANES = 128
CLIP, HA, WA = "clip", "ha", "wa"
ALL_AXES = (CLIP, HA, WA)


LAT, STM, SSP, SEX, SSK, FTM, FSP, FEX, FSK = 0, 2, 4, 6, 14, 22, 23, 24, 25
GB_ROWS = 32

F32 = jnp.float32
BF16 = jnp.bfloat16


def dot(a, b):
    return jnp.dot(a, b, preferred_element_type=F32)


def dot_nt(a, b):
    return lax.dot_general(a, b, (((1,), (1,)), ((), ())), preferred_element_type=F32)


def dot_tn(a, b):
    return lax.dot_general(a, b, (((0,), (0,)), ((), ())), preferred_element_type=F32)


def sigmoid(v):
    return 0.5 * jnp.tanh(0.5 * v) + 0.5


def silu(v):
    return v * sigmoid(v)


def slope(v):
    s = sigmoid(v)
    return s + v * s * (1.0 - s)


def silu_and_slope(v):
    s = sigmoid(v)
    act = v * s
    return act, s + act * (1.0 - s)


def wide(tile, row, count):
    if count == 1:
        return tile[row : row + 1, :]
    return jnp.concatenate([tile[row + i : row + i + 1, :] for i in range(count)], axis=1)


def fold_phases(tile):
    return tile + pltpu.roll(tile, 32, 1) + pltpu.roll(tile, 64, 1) + pltpu.roll(tile, 96, 1)


def down(x, frame):
    return jnp.concatenate([jnp.zeros_like(x[:frame]), x[:-frame]], axis=0)


def up(x, frame):
    return jnp.concatenate([x[frame:], jnp.zeros_like(x[:frame])], axis=0)


def col_sum(x):
    return jnp.sum(x, axis=0, keepdims=True)


class Norm:
    def __init__(self, total, row, gb, gb_row, count, inv_count):
        mean = wide(total, row, count) * inv_count
        square = wide(total, row + count, count) * inv_count
        self.mean = mean
        self.rstd = lax.rsqrt(square - mean * mean + EPSILON)
        self.gain = wide(gb[0], gb_row, count)
        self.bias = wide(gb[1], gb_row, count)
        self.scale = self.gain * self.rstd
        self.shift = self.bias - mean * self.scale

    def columns(self, start, size):
        other = object.__new__(Norm)
        for name in ("mean", "rstd", "gain", "bias", "scale", "shift"):
            setattr(other, name, getattr(self, name)[:, start : start + size])
        return other

    def out(self, z):
        return z * self.scale + self.shift

    def hat(self, z):
        return (z - self.mean) * self.rstd

    def back(self, dy, hat, inside, a_sum, b_sum, inv_count):
        return self.scale * (dy - jnp.where(inside, a_sum * inv_count + hat * (b_sum * inv_count), 0.0))


def inside_rows(rows, columns, limit):
    return lax.broadcasted_iota(jnp.int32, (rows, columns), 0) < limit


def moments(z, inside):
    masked = jnp.where(inside, z, 0.0)
    return col_sum(masked), col_sum(masked * z)


def put_rows(ref, row, vector):
    for i in range(vector.shape[1] // LANES):
        ref[row + i : row + i + 1, :] = vector[:, i * LANES : (i + 1) * LANES]


def spread(tile, ref):
    def body(i, carry):
        ref[i] = tile[...]
        return carry

    lax.fori_loop(0, ref.shape[0], body, 0)


def gathered(ref):
    return jnp.sum(ref[...], axis=0)


def phase(ref, p):
    return ref[:, p].reshape(ref.shape[0] * ref.shape[2], ref.shape[3])


def send_halo(z, shape, si, whole, one, two):
    t, h, w = shape
    columns = z.shape[1]
    four = z.reshape(t, h, w, columns)
    whole[...] = z.astype(BF16)
    top, bottom = (four[:, i].reshape(t * w, columns) for i in (0, h - 1))
    if one.dtype == BF16:
        one[...] = top.astype(BF16)
        two[...] = bottom.astype(BF16)
        return
    even = jnp.full((t * w, columns), si[1] % 2, jnp.int32) == 0
    base = one.shape[0] - t * w * columns // LANES
    for ref, value in ((one, jnp.where(even, bottom, top)), (two, jnp.where(even, top, bottom))):
        for i in range(columns // LANES):
            ref[base + i * t * w : base + (i + 1) * t * w, :] = value[:, i * LANES : (i + 1) * LANES]


def send_sums(pay, one, two):
    if one.dtype == F32:
        for ref in (one, two):
            ref[: pay.shape[0], :] = pay[...]


def halo_values(si, edge, refs):
    one, two, other, o_one, o_two = refs
    if one.dtype == BF16:
        return [ref[...].astype(F32) for ref in (one, two, o_one, other, o_two)]
    columns = other.shape[1]
    base = one.shape[0] - edge * columns // LANES

    def rows(ref):
        parts = [ref[base + i * edge : base + (i + 1) * edge, :] for i in range(columns // LANES)]
        return jnp.concatenate(parts, axis=1) if len(parts) > 1 else parts[0]

    even = jnp.full((edge, columns), si[1] % 2, jnp.int32) == 0
    one, two, o_one, o_two = (rows(ref) for ref in (one, two, o_one, o_two))
    return [
        jnp.where(even, two, one), jnp.where(even, one, two),
        jnp.where(even, o_two, o_one), other[...].astype(F32), jnp.where(even, o_one, o_two),
    ]


def fill_padded(pad, shape, own, above, below, others, has_left, has_right):
    t, h, w = shape
    c = own.shape[1]
    pad[:, 1 : h + 1, w : 2 * w, :] = own.reshape(t, h, w, c)
    pad[:, 0, w : 2 * w, :] = above.reshape(t, w, c)
    pad[:, h + 1, w : 2 * w, :] = below.reshape(t, w, c)
    o_above, o_own, o_below = others
    for start, has in ((0, has_left), (2 * w, has_right)):
        pad[:, 1 : h + 1, start : start + w, :] = (o_own * has).reshape(t, h, w, c)
        pad[:, 0, start : start + w, :] = (o_above * has).reshape(t, w, c)
        pad[:, h + 1, start : start + w, :] = (o_below * has).reshape(t, w, c)


def tap(pad, shape, a, b):
    t, h, w = shape
    part = pad[:, a : a + h, w - 1 + b : 2 * w - 1 + b, :]
    return part.reshape(t * h * w, part.shape[-1]).astype(BF16)


def activate_padded(pad, shape, norm, own, halo_refs, si, sf):
    def act(z):
        return silu(norm.out(z.astype(F32))).astype(BF16).astype(F32)

    edge = shape[0] * shape[2]
    above, below, o_above, o_own, o_below = (act(x) for x in halo_values(si, edge, halo_refs))
    has_up, has_down = sf[2], sf[3]
    others = (o_above * has_up, o_own, o_below * has_down)
    fill_padded(pad, shape, act(own), above * has_up, below * has_down, others, sf[4], sf[5])


def fast_head(phases, shape, si, inside, lat_w, ft_band, fk_w, fb_out, zlat_out, zft_out, halo_out, zfk_out, pay, row):
    frame = shape[1] * shape[2]
    low = [v.astype(BF16) for v in phases]
    for p in range(ALPHA):
        fb_out[:, p * DF : (p + 1) * DF] = low[p]
    before2, before3, after0 = down(low[2], frame), down(low[3], frame), up(low[0], frame)
    z = (
        dot(before2, lat_w[0, 0])
        + dot(before3, lat_w[0, 1])
        + dot(low[0], lat_w[0, 2])
        + dot(low[1], lat_w[0, 3])
        + dot(low[2], lat_w[0, 4])
    )
    zlat_out[...] = z
    total, square = moments(z, inside[:, :DL])
    put_rows(pay, row, total)
    put_rows(pay, row + 2, square)
    six = [before3] + low + [after0]
    z = dot(six[0], ft_band[0])
    for j in range(1, 6):
        z = z + dot(six[j], ft_band[j])
    zft_out[...] = z
    send_halo(z, shape, si, *halo_out)
    total, square = moments(z, inside[:, :LANES])
    put_rows(pay, row + 4, total)
    put_rows(pay, row + 5, square)
    total, square = 0.0, 0.0
    for p in range(ALPHA):
        z = dot(low[p], fk_w[0])
        zfk_out[:, p * DF : (p + 1) * DF] = z
        one, two = moments(z, inside[:, :LANES])
        total, square = total + one, square + two
    put_rows(pay, row + 6, total)
    put_rows(pay, row + 7, square)


def place_columns(p):
    row = lax.broadcasted_iota(jnp.int32, (BF, LANES), 0)
    column = lax.broadcasted_iota(jnp.int32, (BF, LANES), 1)
    return jnp.where(column == row + BF * p, 1.0, 0.0).astype(BF16)


def kernel_start(shape, si, sf, fast, lat_w, ft_w, fk_w, fb, zlat, zft, z16, top, bottom, zfk, pay, ft_band):
    t, h, w = shape
    inside = inside_rows(t * h * w, DL, si[0])
    places = [place_columns(p) for p in range(ALPHA)]
    for l in range(LAYERS):
        for j in range(6):
            part = 0.0
            for p in range(ALPHA):
                if 0 <= j - p <= 2:
                    part = part + dot_tn(ft_w[l, j - p], places[p])
            ft_band[l, j] = part.astype(BF16)
    fast_head(
        [phase(fast, p) for p in range(ALPHA)],
        shape, si, inside, lat_w, ft_band.at[0], fk_w, fb, zlat, zft, (z16, top, bottom), zfk, pay, 0,
    )
    send_sums(pay, top, bottom)


def lane(shape):
    return lax.broadcasted_iota(jnp.int32, shape, len(shape) - 1)


def kernel_prepare(gains, biases, fs_w, fe_w, gb, fs_bd, fe_bd):
    for i, source in enumerate((gains, biases)):
        for l in range(LAYERS):
            for r in range(22):
                gb[l, i, r : r + 1, :] = source[l : l + 1, r * LANES : (r + 1) * LANES]
            v = source[l : l + 1, 22 * LANES : 23 * LANES]
            v2 = source[l : l + 1, 23 * LANES : 24 * LANES]
            v3 = jnp.concatenate([source[l : l + 1, 24 * LANES :], jnp.zeros((1, 64), F32)], axis=1)
            place = lane((1, LANES))
            gb[l, i, FTM : FTM + 1, :] = fold_phases(jnp.where(place < 32, v, 0.0))
            gb[l, i, FSP : FSP + 1, :] = fold_phases(jnp.where((place >= 32) & (place < 64), v, 0.0))
            v, v2, v3 = (pltpu.roll(x, 64, 1) for x in (v, v2, v3))
            gb[l, i, FEX : FEX + 1, :] = jnp.where(place < 64, v, v2)
            gb[l, i, FSK : FSK + 1, :] = jnp.where(place < 64, v2, v3)
            gb[l, i, 26:32, :] = jnp.zeros((6, LANES), F32)
    row = lax.broadcasted_iota(jnp.int32, (LANES, LANES), 0)
    column = lane((LANES, LANES))
    same = (row // BF) == (column // BF)
    spread_columns = 0.0
    for p in range(ALPHA):
        spread_columns = spread_columns + place_columns(p).astype(F32)
    spread_columns = spread_columns.astype(BF16)
    for l in range(LAYERS):
        for a in range(3):
            for b in range(3):
                part = dot(fs_w[l, a, b], spread_columns).astype(BF16)
                fs_bd[l, a, b] = jnp.where(same, dot_tn(spread_columns, part), 0.0).astype(BF16)
        fe_bd[l] = jnp.zeros((LANES, ALPHA * DF), BF16)
        for p in range(ALPHA):
            fe_bd[l, p * BF : (p + 1) * BF, p * DF : (p + 1) * DF] = fe_w[l]


def kernel_temporal(first, shape, si, sf, *refs):
    t, h, w = shape
    rows, frame = t * h * w, h * w
    if first:
        (recv, slow, gb, zlat, zft, h1, h2, h3, h4, h5, st_w, sk_w, fs_bd,
         low_out, zst, z16, top, bottom, zsk, af9, zfs, pay, pad) = refs
        row = 0
        total = recv[...]
    else:
        (recv, gb_before, tot_sk, zse_in, zsk_in, gb, zlat, zft, h1, h2, h3, h4, h5, st_w, sk_w, fs_bd,
         low_out, zst, z16, top, bottom, zsk, af9, zfs, pay, pad) = refs
        row = 16
        total = recv[...]
        inside = inside_rows(rows, 256, si[0])
        one = Norm(total, 0, gb_before, SEX, 8, sf[0])
        two = Norm(tot_sk[...], 8, gb_before, SSK, 8, sf[0])
        for c in range(0, DS, 256):
            u = one.columns(c, 256).out(zse_in[:, c : c + 256]) + two.columns(c, 256).out(zsk_in[:, c : c + 256])
            low_out[:, c : c + 256] = jnp.where(inside, silu(u), 0.0).astype(BF16)
    inside = inside_rows(rows, 256, si[0])
    lat = Norm(total, row, gb, LAT, 2, sf[0])
    ft = Norm(fold_phases(total), row + 4, gb, FTM, 1, sf[1])
    if first:
        low_out[:, :DS] = slow[...].astype(BF16)
    low_out[:, DS:] = silu(lat.out(zlat[...])).astype(BF16)
    activate_padded(pad, shape, ft, zft[...], (h1, h2, h3, h4, h5), si, sf)
    low = low_out[...]
    z = dot(low, st_w[0, 1])
    z = z + down(dot(low, st_w[0, 0]), frame)
    z = z + up(dot(low, st_w[0, 2]), frame)
    zst[...] = z
    send_halo(z, shape, si, z16, top, bottom)
    one, two = moments(z, inside)
    put_rows(pay, 0, one)
    put_rows(pay, 2, two)
    for a in range(3):
        for b in range(3):
            k = 3 * a + b
            af9[:, k * LANES : (k + 1) * LANES] = tap(pad, shape, a, b)
    z = dot(af9[...], fs_bd[...].reshape(9 * LANES, LANES))
    zfs[...] = z
    one, two = moments(z, inside[:, :LANES])
    put_rows(pay, 4, one)
    put_rows(pay, 5, two)
    pay[6:8, :] = jnp.zeros((2, LANES), F32)
    for c in range(0, DS, 256):
        z = dot(low, sk_w[0, :, c : c + 256])
        zsk[:, c : c + 256] = z
        one, two = moments(z, inside)
        put_rows(pay, 8 + c // LANES, one)
        put_rows(pay, 16 + c // LANES, two)
    send_sums(pay, top, bottom)


def kernel_spatial(shape, si, sf, recv, gb, zst, h1, h2, h3, h4, h5, zfs, ss_w, fe_bd,
                   a9, zss, bf, zfe, pays, pay, pad):
    t, h, w = shape
    inside = inside_rows(t * h * w, 256, si[0])
    total = recv[...]
    st = Norm(total, 0, gb, STM, 2, sf[0])
    fs = Norm(fold_phases(total), 4, gb, FSP, 1, sf[1])
    activate_padded(pad, shape, st, zst[...], (h1, h2, h3, h4, h5), si, sf)
    for a in range(3):
        for b in range(3):
            k = 3 * a + b
            a9[:, k * BS : (k + 1) * BS] = tap(pad, shape, a, b)
    z = dot(a9[...], ss_w[...].reshape(9 * BS, BS))
    zss[...] = z
    one, two = moments(z, inside)
    put_rows(pay, 0, one)
    put_rows(pay, 2, two)
    low = silu(fs.out(zfs[...])).astype(BF16)
    bf[...] = low
    total, square = 0.0, 0.0
    for p in range(ALPHA):
        z = dot(low, fe_bd[:, p * DF : (p + 1) * DF])
        zfe[:, p * DF : (p + 1) * DF] = z
        one, two = moments(z, inside[:, :LANES])
        total, square = total + one, square + two
    put_rows(pay, 4, total)
    put_rows(pay, 5, square)
    pay[6:8, :] = jnp.zeros((2, LANES), F32)
    spread(pay, pays)


def kernel_expand(last, shape, si, sf, *refs):
    t, h, w = shape
    inside = inside_rows(t * h * w, 256, si[0])
    if last:
        recv, gb, zss, se_w, bt, zse, pays, tot_out, pay = refs
    else:
        (recv, gb, zss, se_w, tot_fk, zfe, zfk, lat_w, ft_band, fk_w,
         bt, zse, pay, tot_out, fb, zlat, zft, z16, top, bottom, zfk_out) = refs
    total = gathered(recv)
    tot_out[...] = total
    ss = Norm(total, 0, gb, SSP, 2, sf[0])
    low = silu(ss.out(zss[...])).astype(BF16)
    bt[...] = low
    for c in range(0, DS, 256):
        z = dot(low, se_w[0, :, c : c + 256])
        zse[:, c : c + 256] = z
        one, two = moments(z, inside)
        put_rows(pay, c // LANES, one)
        put_rows(pay, 8 + c // LANES, two)
    if not last:
        fe = Norm(total, 4, gb, FEX, 1, sf[1])
        fk = Norm(tot_fk[...], tot_fk.shape[0] - 2, gb, FSK, 1, sf[1])
        phases = []
        for p in range(ALPHA):
            cols = slice(p * DF, (p + 1) * DF)
            u = fe.out(zfe[:, cols]) + fk.out(zfk[:, cols])
            phases.append(jnp.where(inside[:, :LANES], silu(u), 0.0))
        fast_head(
            phases, shape, si, inside, lat_w, ft_band, fk_w, fb, zlat, zft, (z16, top, bottom), zfk_out, pay, 16
        )
        send_sums(pay, top, bottom)
    else:
        spread(pay, pays)


class Refs:
    def __init__(self, names, refs):
        self.__dict__.update(zip(names, refs))

    def layer(self, prefix):
        own = {k[len(prefix) :]: v for k, v in self.__dict__.items() if k.startswith(prefix)}
        return Refs(own.keys(), own.values())


def norms_of(L, sf, *names):
    def make(name):
        if name == "se":
            return Norm(L.tot_se[...], 0, L.gb, SEX, 8, sf[0])
        if name == "sk":
            return Norm(L.tot_sk[...], 8, L.gb, SSK, 8, sf[0])
        if name == "ss":
            return Norm(L.tot_ss[...], 0, L.gb, SSP, 2, sf[0])
        if name == "st":
            return Norm(L.tot_sk[...], 0, L.gb, STM, 2, sf[0])
        if name == "lat":
            return Norm(L.tot_lat[...], L.tot_lat.shape[0] - 8, L.gb, LAT, 2, sf[0])
        if name == "ft":
            return Norm(fold_phases(L.tot_lat[...]), L.tot_lat.shape[0] - 4, L.gb, FTM, 1, sf[1])
        if name == "fk":
            return Norm(L.tot_lat[...], L.tot_lat.shape[0] - 2, L.gb, FSK, 1, sf[1])
        if name == "fs":
            return Norm(fold_phases(L.tot_sk[...]), 4, L.gb, FSP, 1, sf[1])
        return Norm(L.tot_ss[...], 4, L.gb, FEX, 1, sf[1])

    return [make(name) for name in names]


def fill_rows(pay, start, end):
    pay[start:end, :] = jnp.zeros((end - start, LANES), F32)


def top_slow(L, inside, sf, grad, du_out, pay, row, out=None):
    se, sk = norms_of(L, sf, "se", "sk")
    for c in range(0, DS, 256):
        cols = slice(c, c + 256)
        one, two = se.columns(c, 256), sk.columns(c, 256)
        hat1, hat2 = one.hat(L.zse[:, cols]), two.hat(L.zsk[:, cols])
        u = one.gain * hat1 + one.bias + (two.gain * hat2 + two.bias)
        act, rate = silu_and_slope(u)
        if out is not None:
            out[:, cols] = jnp.where(inside, act, 0.0)
        du = jnp.where(inside, grad(cols) * rate, 0.0)
        du_out[:, cols] = du
        put_rows(pay, row + c // LANES, col_sum(du))
        put_rows(pay, row + 8 + c // LANES, col_sum(du * hat1))
        put_rows(pay, row + 16 + c // LANES, col_sum(du * hat2))


def top_fast(L, inside, sf, grad, du_out, pay, row, out=None):
    fe, fk = norms_of(L, sf, "fe", "fk")
    inside = inside[:, :LANES]
    sums = [0.0, 0.0, 0.0]
    for p in range(ALPHA):
        cols = slice(p * DF, (p + 1) * DF)
        hat1, hat2 = fe.hat(L.zfe[:, cols]), fk.hat(L.zfk[:, cols])
        u = fe.gain * hat1 + fe.bias + (fk.gain * hat2 + fk.bias)
        act, rate = silu_and_slope(u)
        if out is not None:
            out[:, p] = jnp.where(inside, act, 0.0).reshape(out.shape[0], out.shape[2], DF)
        du = jnp.where(inside, grad(p) * rate, 0.0)
        du_out[:, cols] = du
        sums = [sums[0] + col_sum(du), sums[1] + col_sum(du * hat1), sums[2] + col_sum(du * hat2)]
    for i in range(3):
        put_rows(pay, row + i, sums[i])


def expand_slow(L, inside, sf, total, row, du_in, se_w, dz_se, dz_sk, pay, out_row):
    se, sk, ss = norms_of(L, sf, "se", "sk", "ss")
    back = 0.0
    for c in range(0, DS, 256):
        cols = slice(c, c + 256)
        r = row + c // LANES
        du = du_in[:, cols]
        a_sum = wide(total, r, 2)
        one, two = se.columns(c, 256), sk.columns(c, 256)
        dz = one.back(du, one.hat(L.zse[:, cols]), inside, a_sum, wide(total, 8 + r, 2), sf[0]).astype(BF16)
        dz_se[:, cols] = dz
        back = back + dot_nt(dz, se_w[0, :, cols])
        dz = two.back(du, two.hat(L.zsk[:, cols]), inside, a_sum, wide(total, 16 + r, 2), sf[0])
        dz_sk[:, cols] = dz.astype(BF16)
    z = L.zss[...]
    dy = back * slope(ss.out(z))
    put_rows(pay, out_row, col_sum(dy))
    put_rows(pay, out_row + 2, col_sum(dy * ss.hat(z)))
    return dy, z


def expand_fast(L, inside, sf, total, row, du_in, fe_bd, dz_fe, dz_fk, pay, out_row):
    fe, fk, fs = norms_of(L, sf, "fe", "fk", "fs")
    inside = inside[:, :LANES]
    back = 0.0
    a_sum = wide(total, row, 1)
    for p in range(ALPHA):
        cols = slice(p * DF, (p + 1) * DF)
        du = du_in[:, cols]
        dz = fe.back(du, fe.hat(L.zfe[:, cols]), inside, a_sum, wide(total, row + 1, 1), sf[1]).astype(BF16)
        dz_fe[:, cols] = dz
        back = back + dot_nt(dz, fe_bd[:, cols])
        dz = fk.back(du, fk.hat(L.zfk[:, cols]), inside, a_sum, wide(total, row + 2, 1), sf[1])
        dz_fk[:, cols] = dz.astype(BF16)
    z = L.zfs[...]
    dy = back * slope(fs.out(z))
    put_rows(pay, out_row, col_sum(dy))
    put_rows(pay, out_row + 1, col_sum(dy * fs.hat(z)))
    return dy, z


def pack_halo(pairs, shape, si, dy_out, halo_out):
    dy = jnp.concatenate([one for one, _ in pairs], axis=1) if len(pairs) > 1 else pairs[0][0]
    dy_out[...] = dy
    send_halo(jnp.concatenate([dy] + [z for _, z in pairs], axis=1), shape, si, *halo_out)


def spatial_gradient(parts, shape, si, sf, dy_in, halo_refs, pad, dz_out):
    t, h, w = shape
    width = dy_in.shape[1]

    def dz(dy, z, frame):
        inside = inside_rows(dy.shape[0], width, si[0] // (h * w) * frame)
        pieces, column = [], 0
        for norm, _, a_sum, b_sum, inv in parts:
            cols = slice(column, column + norm.mean.shape[1])
            pieces.append(norm.back(dy[:, cols], norm.hat(z[:, cols]), inside[:, cols], a_sum, b_sum, inv))
            column = cols.stop
        value = jnp.concatenate(pieces, axis=1) if len(pieces) > 1 else pieces[0]
        return value.astype(BF16)

    def arrived(value, frame):
        return dz(value[:, :width], value[:, width:], frame).astype(F32)

    z = jnp.concatenate([part[1] for part in parts], axis=1) if len(parts) > 1 else parts[0][1]
    own = dz(dy_in[...], z, h * w)
    dz_out[...] = own
    above, below, o_above, o_own, o_below = (
        arrived(x, h * w if i == 3 else w) for i, x in enumerate(halo_values(si, t * w, halo_refs))
    )
    others = (o_above * sf[2], o_own, o_below * sf[3])
    fill_padded(pad, shape, own.astype(F32), above * sf[2], below * sf[3], others, sf[4], sf[5])


def spatial_part(norm, z, total, row, columns, inv):
    count = columns // LANES
    if columns == LANES:
        total = fold_phases(total)
    return norm, z, wide(total, row, count), wide(total, row + count, count), inv


def spatial_back(pad, shape, slow_w, fast_w):
    back, back_f = 0.0, 0.0
    for a in range(3):
        for b in range(3):
            part = tap(pad, shape, 2 - a, 2 - b)
            if slow_w is not None:
                back = back + dot_nt(part[:, :BS], slow_w[0, a, b])
            if fast_w is not None:
                back_f = back_f + dot_nt(part[:, part.shape[1] - LANES :], fast_w[a, b])
    return back, back_f


def finish_spatial(norm, z, back, dy_out, pay, row):
    dy = back * slope(norm.out(z))
    dy_out[...] = dy
    put_rows(pay, row, col_sum(dy))
    put_rows(pay, row + dy.shape[1] // LANES, col_sum(dy * norm.hat(z)))


def temporal_slow(L, frame, inside, sf, total, row, dy_in, dlow, st_w, dz_st, dy_lat, pay, out_row):
    st, lat = norms_of(L, sf, "st", "lat")
    dz = st.back(
        dy_in[...], st.hat(L.zst[...]), inside, wide(total, row, 2), wide(total, row + 2, 2), sf[0]
    ).astype(BF16)
    dz_st[:, :BS] = up(dz, frame)
    dz_st[:, BS : 2 * BS] = dz
    dz_st[:, 2 * BS :] = down(dz, frame)

    def back(cols):
        part = dlow[:, cols]
        for j in range(3):
            part = part + dot_nt(dz_st[:, j * BS : (j + 1) * BS], st_w[0, j, cols, :])
        return part

    z = L.zlat[...]
    dy = back(slice(DS, CC)) * slope(lat.out(z))
    dy_lat[...] = dy
    put_rows(pay, out_row, col_sum(dy))
    put_rows(pay, out_row + 2, col_sum(dy * lat.hat(z)))
    return back


def temporal_fast(L, frame, inside, sf, total, row, dy_in, dz_ft, dz_fk, fk_w, ft_band):
    (ft,) = norms_of(L, sf, "ft")
    folded = fold_phases(total)
    dz = ft.back(
        dy_in[...], ft.hat(L.zft[...]), inside[:, :LANES], wide(folded, row, 1), wide(folded, row + 1, 1), sf[1]
    ).astype(BF16)
    dz_ft[...] = dz

    def grad(p):
        part = dot_nt(dz_fk[:, p * DF : (p + 1) * DF], fk_w[0]) + dot_nt(dz, ft_band[p + 1])
        if p == ALPHA - 1:
            part = part + up(dot_nt(dz, ft_band[0]), frame)
        if p == 0:
            part = part + down(dot_nt(dz, ft_band[5]), frame)
        return part

    return grad


def lateral_back(L, frame, inside, sf, total, row, dy_in, lat_w, dz_lat, grad):
    (lat,) = norms_of(L, sf, "lat")
    dz = lat.back(
        dy_in[...], lat.hat(L.zlat[...]), inside, wide(total, row, 2), wide(total, row + 2, 2), sf[0]
    ).astype(BF16)
    dz_lat[...] = dz

    def whole(p):
        part = grad(p)
        if p < 3:
            part = part + dot_nt(dz, lat_w[0, p + 2])
        if p >= 2:
            part = part + up(dot_nt(dz, lat_w[0, p - 2]), frame)
        return part

    return whole


def back_turn(shape, R, inside, si, sf):
    L = R.layer("a_")
    L.tot_se = R.tot
    R.tot[...] = gathered(R.recv)
    top_slow(L, inside, sf, lambda cols: R.slow_cot[:, cols], R.du_s, R.pay, 0, R.out_slow)
    top_fast(L, inside, sf, lambda p: phase(R.fast_cot, p), R.du_f, R.pay, 24, R.out_fast)
    fill_rows(R.pay, 27, 32)


def back_expand(shape, R, inside, si, sf):
    L = R.layer("a_")
    total = R.recv[...]
    slow = expand_slow(L, inside, sf, total, 0, R.du_s, R.se_w, R.dz_se, R.dz_sk, R.pay, 0)
    fast = expand_fast(L, inside, sf, total, 24, R.du_f, R.fe_bd, R.dz_fe, R.dz_fk, R.pay, 4)
    fill_rows(R.pay, 6, 8)
    pack_halo([slow, fast], shape, si, R.dy, (R.whole, R.top, R.bottom))
    send_sums(R.pay, R.top, R.bottom)


def back_spatial(shape, R, inside, si, sf):
    L = R.layer("a_")
    total = R.recv[...]
    ss, fs, st, ft = norms_of(L, sf, "ss", "fs", "st", "ft")
    parts = [
        spatial_part(ss, L.zss[...], total, 0, BS, sf[0]),
        spatial_part(fs, L.zfs[...], total, 4, LANES, sf[1]),
    ]
    spatial_gradient(parts, shape, si, sf, R.dy, (R.h0, R.h1, R.h2, R.h3, R.h4), R.pad, R.dz)
    back, back_f = spatial_back(R.pad, shape, R.ss_w, R.fs_bd)
    finish_spatial(st, L.zst[...], back, R.dy_st, R.pay, 0)
    finish_spatial(ft, L.zft[...], back_f, R.dy_ft, R.pay, 4)
    fill_rows(R.pay, 6, 8)


def back_temporal(shape, R, inside, si, sf):
    L, below = R.layer("a_"), R.layer("b_")
    frame = shape[1] * shape[2]
    total = R.recv[...]
    back = temporal_slow(L, frame, inside, sf, total, 0, R.dy_st, R.dlow, R.st_w, R.dz_st, R.dy_lat, R.pay, 0)
    top_slow(below, inside, sf, back, R.du_s, R.pay, 8)
    fill_rows(R.pay, 4, 8)
    grad = temporal_fast(L, frame, inside, sf, total, 4, R.dy_ft, R.dz_ft, R.dz_fk, R.fk_w, R.ft_band)
    for p in range(ALPHA):
        R.dfast[:, p * DF : (p + 1) * DF] = grad(p)


def back_lateral(shape, R, inside, si, sf):
    L, below = R.layer("a_"), R.layer("b_")
    frame = shape[1] * shape[2]
    total = R.recv[...]
    slow = expand_slow(below, inside, sf, total, 8, R.du_s, R.se_w, R.dz_se, R.dz_sk, R.pay, 0)
    pack_halo([slow], shape, si, R.dy, (R.whole, R.top, R.bottom))
    grad = lateral_back(
        L, frame, inside, sf, total, 0, R.dy_lat, R.lat_w, R.dz_lat, lambda p: R.dfast[:, p * DF : (p + 1) * DF]
    )
    top_fast(below, inside, sf, grad, R.du_f, R.pay, 4)
    fill_rows(R.pay, 7, 8)
    send_sums(R.pay, R.top, R.bottom)


def back_low_spatial(shape, R, inside, si, sf):
    L = R.layer("b_")
    total = R.recv[...]
    fast = expand_fast(L, inside, sf, total, 4, R.du_f, R.fe_bd, R.dz_fe, R.dz_fk, R.pay, 4)
    pack_halo([fast], shape, si, R.dy_fs, (R.whole, R.top, R.bottom))
    ss, st = norms_of(L, sf, "ss", "st")
    parts = [spatial_part(ss, L.zss[...], total, 0, BS, sf[0])]
    spatial_gradient(parts, shape, si, sf, R.dy, (R.h0, R.h1, R.h2, R.h3, R.h4), R.pad, R.dz)
    back, _ = spatial_back(R.pad, shape, R.ss_w, None)
    finish_spatial(st, L.zst[...], back, R.dy_st, R.pay, 0)
    fill_rows(R.pay, 6, 8)
    send_sums(R.pay, R.top, R.bottom)


def back_low_temporal(shape, R, inside, si, sf):
    L = R.layer("b_")
    frame = shape[1] * shape[2]
    total = R.recv[...]
    fs, ft = norms_of(L, sf, "fs", "ft")
    parts = [spatial_part(fs, L.zfs[...], total, 4, LANES, sf[1])]
    spatial_gradient(parts, shape, si, sf, R.dy_fs, (R.h0, R.h1, R.h2, R.h3, R.h4), R.pad, R.dz_f)
    _, back_f = spatial_back(R.pad, shape, None, R.fs_bd)
    finish_spatial(ft, L.zft[...], back_f, R.dy_ft, R.pay, 4)
    temporal_slow(L, frame, inside, sf, total, 0, R.dy_st, R.dlow, R.st_w, R.dz_st, R.dy_lat, R.pay, 0)
    fill_rows(R.pay, 6, 8)


def kernel_low_input(dz_st, dlow, st_w, dslow):
    for c in range(0, DS, 256):
        cols = slice(c, c + 256)
        part = dlow[:, cols]
        for j in range(3):
            part = part + dot_nt(dz_st[:, j * BS : (j + 1) * BS], st_w[0, j, cols, :])
        dslow[:, cols] = part


def back_low_lateral(shape, R, inside, si, sf):
    L = R.layer("b_")
    lat, ft = norms_of(L, sf, "lat", "ft")
    total = R.recv[...]
    folded = fold_phases(total)
    R.dz_lat[...] = lat.back(
        R.dy_lat[...], lat.hat(L.zlat[...]), inside, wide(total, 0, 2), wide(total, 2, 2), sf[0]
    ).astype(BF16)
    R.dz_ft[...] = ft.back(
        R.dy_ft[...], ft.hat(L.zft[...]), inside[:, :LANES], wide(folded, 4, 1), wide(folded, 5, 1), sf[1]
    ).astype(BF16)


def kernel_low_fast_input(frame, dz_lat, dz_ft, dz_fk, lat_w, fk_w, ft_band, dfast):
    for p in range(ALPHA):
        part = dot_nt(dz_fk[:, p * DF : (p + 1) * DF], fk_w[0]) + dot_nt(dz_ft[...], ft_band[p + 1])
        if p == ALPHA - 1:
            part = part + up(dot_nt(dz_ft[...], ft_band[0]), frame)
        if p == 0:
            part = part + down(dot_nt(dz_ft[...], ft_band[5]), frame)
        if p < 3:
            part = part + dot_nt(dz_lat[...], lat_w[0, p + 2])
        if p >= 2:
            part = part + up(dot_nt(dz_lat[...], lat_w[0, p - 2]), frame)
        dfast[:, p] = part.reshape(dfast.shape[0], frame, DF)


def kernel_back_skip(dz_sk, sk_w, dlow):
    for k in range(0, CC, 256):
        dlow[:, k : k + 256] = dot_nt(dz_sk[...], sk_w[0, k : k + 256, :])


def part_tiles(si, tiles, ref, keep, send):
    side = si[2]
    for i in range(tiles // 2):
        keep[i] = ref[2 * i + side]
        send[i] = ref[2 * i + 1 - side]


def pick_phases(parts):
    place = lane(parts[0].shape) // BF
    return fold_phases(sum(jnp.where(place == p, part, 0.0) for p, part in enumerate(parts)))


SMALL_ROWS = 64
ROW_JOBS = {"pl": 4, "st": 2, "ss": 2, "lat": 2, "sm": 7}


def job_rows(job, tiles):
    rows = {"pl": 4 * (CC + BS), "st": 3 * CC, "ss": 9 * BS, "lat": 5 * DF, "sm": SMALL_ROWS * tiles}
    return rows[job] // tiles


def bundle_rows(jobs, tiles):
    planes = job_rows("pl", tiles) if "pl" in jobs else 0
    small = SMALL_ROWS if "sm" in jobs else 0
    rows = sum(job_rows(job, tiles) for job in jobs if job not in ("pl", "sm"))
    return planes + -(-rows // 32) * 32 + small, planes, small


def share_rows(jobs, tiles):
    count, planes, small = bundle_rows(jobs, tiles)
    return planes // 2 + (count - planes - small) // 2 + 2 * small


def kernel_weights_rows(tiles, frame, jobs, si, *refs):
    kst, kss, kla, ksm = CC // tiles, BS // tiles, DF // tiles, BF // tiles
    count = sum(ROW_JOBS[job] for job in jobs)
    keep, send, blocks, small = refs[count:]
    rows, _, small_rows = bundle_rows(jobs, tiles)
    base = 0
    operands = list(refs[:count])
    for job in jobs:
        own = [operands.pop(0) for _ in range(ROW_JOBS[job])]
        if job == "pl":
            low, bt, dz_sk, dz_se = own
            ksk, kse = kst, kss
            for j in range(4):
                cols, start = slice(j * 256, (j + 1) * 256), base + j * (ksk + kse)
                d = dot_tn(low[...], dz_sk[:, cols]).astype(BF16)
                blocks[:, start : start + ksk, :] = d.reshape(tiles, ksk, 256)
                d = dot_tn(bt[...], dz_se[:, cols]).astype(BF16)
                blocks[:, start + ksk : start + ksk + kse, :] = d.reshape(tiles, kse, 256)
        elif job == "st":
            low, dz = own
            for j in range(3):
                d = dot_tn(low[...], dz[:, j * BS : (j + 1) * BS]).astype(BF16)
                blocks[:, base + j * kst : base + (j + 1) * kst, :] = d.reshape(tiles, kst, BS)
        elif job == "ss":
            a9, dz = own
            for k in range(9):
                d = dot_tn(a9[:, k * BS : (k + 1) * BS], dz[:, :BS]).astype(BF16)
                blocks[:, base + k * kss : base + (k + 1) * kss, :] = d.reshape(tiles, kss, BS)
        elif job == "lat":
            fb, dz = own
            f = [fb[:, p * DF : (p + 1) * DF] for p in range(3)] + [fb[:, 3 * DF :]]
            for k, x in enumerate([down(f[2], frame), down(f[3], frame), f[0], f[1], f[2]]):
                d = dot_tn(x, dz[...]).astype(BF16)
                blocks[:, base + k * kla : base + (k + 1) * kla, :] = d.reshape(tiles, kla, DL)
        else:
            af9, fb, bf, dz_f, dz_ft, dz_fe, dz_fk = own
            small[...] = jnp.zeros(small.shape, F32)
            last = dz_f.shape[1] - LANES
            for k in range(9):
                d = dot_tn(af9[:, k * LANES : (k + 1) * LANES], dz_f[:, last:])
                d = pick_phases([d[p * BF : (p + 1) * BF] for p in range(ALPHA)])
                for i in range(tiles):
                    small[i, k * ksm : (k + 1) * ksm, LANES:] = d[i * ksm : (i + 1) * ksm]
            f = [fb[:, p * DF : (p + 1) * DF] for p in range(ALPHA)]
            six = [dot_tn(x, dz_ft[...]) for x in [down(f[3], frame)] + f + [up(f[0], frame)]]
            for k in range(3):
                d = pick_phases([six[k + p] for p in range(ALPHA)])
                small[:, k * kla : (k + 1) * kla, :LANES] = d.reshape(tiles, kla, LANES)
            fe, fk = 0.0, 0.0
            for p in range(ALPHA):
                cols = slice(p * DF, (p + 1) * DF)
                fk = fk + dot_tn(fb[:, cols], dz_fk[:, cols])
                fe = fe + dot_tn(bf[...], dz_fe[:, cols])[p * BF : (p + 1) * BF, :]
            for i in range(tiles):
                small[i, 9 * ksm : 10 * ksm, LANES:] = fe[i * ksm : (i + 1) * ksm]
                small[i, 10 * ksm : 10 * ksm + kla, LANES:] = fk[i * kla : (i + 1) * kla]
            blocks[:, rows - small_rows :, :] = small[...].astype(BF16)
            continue
        base += job_rows(job, tiles)
    if rows - small_rows > base:
        blocks[:, base : rows - small_rows, :] = jnp.zeros((tiles, rows - small_rows - base, 256), BF16)
    part_tiles(si, tiles, blocks, keep, send)


def add(one, two):
    return (one.astype(F32) + two.astype(F32)).astype(BF16)


def kernel_halve_first(split, si, kept, got, keep_a, send_a, keep_b, send_b):
    low, high = si[1] % 2, si[1] // 2
    for i in range(2):
        for ref, side in ((keep_a, low), (send_a, 1 - low)):
            place = 2 * i + side
            ref[i] = add(kept[place, :split], got[place, :split])
        for ref, side in ((keep_b, high), (send_b, 1 - high)):
            place = 2 * side + i
            ref[i] = add(kept[place, split:], got[place, split:])


def kernel_halve_second(si, kept_a, got_a, kept_b, got_b, keep_a, send_a, keep_b, send_b):
    low, high = si[1] % 2, si[1] // 2
    for ref, place in ((keep_a, high), (send_a, 1 - high)):
        ref[...] = add(kept_a[place], got_a[place])
    for ref, place in ((keep_b, low), (send_b, 1 - low)):
        ref[...] = add(kept_b[place], got_b[place])


def kernel_halve_last(si, kept, got, keep, send):
    bit = si[3] // 2
    for ref, place in ((keep, bit), (send, 1 - bit)):
        ref[...] = add(kept[place], got[place])


def kernel_pick_places(si, kept, got, *outs):
    for i, ref in enumerate(outs):
        place = si[1] ^ i
        ref[...] = add(kept[place], got[place])


def whole_sum(parts):
    total = parts[0][...].astype(F32)
    for part in parts[1:]:
        total = total + part[...].astype(F32)
    return total


def columns_of(x, j):
    half = x.shape[0] // 2
    base = (j // 2) * LANES
    a, b = x[:half, base : base + LANES], x[half:, base : base + LANES]
    left = lane(a.shape) < 64
    if j % 2 == 0:
        return jnp.where(left, a, pltpu.roll(b, 64, 1))
    return jnp.where(left, pltpu.roll(a, 64, 1), b)


def column_blocks(jobs, tiles, total, blocks):
    count, planes, small_rows = bundle_rows(jobs, tiles)
    big = count - small_rows
    packed = (big - planes) // 2
    each = planes // 4
    for j in range(4):
        if planes:
            plane = total[j * each : (j + 1) * each].astype(BF16)
            blocks[j, :each, :] = plane[:, :LANES]
            blocks[j, each : 2 * each, :] = plane[:, LANES:]
        base = 2 * each
        if packed:
            blocks[j, base : base + packed, :] = columns_of(total[planes:big], j).astype(BF16)
        base += packed
        if small_rows:
            small = total[big:].astype(BF16)
            blocks[j, base : base + small_rows, :] = small[:, :LANES]
            blocks[j, base + small_rows :, :] = small[:, LANES:]


def kernel_pick_columns(jobs, tiles, si, a, b, c, d, out0, out1, out2, out3, blocks):
    column_blocks(jobs, tiles, whole_sum((a, b, c, d)), blocks)
    for i, ref in enumerate((out0, out1, out2, out3)):
        ref[...] = blocks[si[3] ^ i]


def kernel_join_columns(jobs, tiles, si, kept_a, got_a, kept_b, got_b, keep, send, blocks):
    total = jnp.concatenate([whole_sum((kept_a, got_a)), whole_sum((kept_b, got_b))], axis=0)
    column_blocks(jobs, tiles, total, blocks)
    bit = si[3] % 2
    for ref, side in ((keep, bit), (send, 1 - bit)):
        for i in range(2):
            ref[i] = blocks[2 * i + side]


def kernel_finish(tiles, plan, si, *refs):
    kst, kss, kla, ksm = CC // tiles, BS // tiles, DF // tiles, BF // tiles
    refs = list(refs)
    g_lat, g_st, g_ss, g_se, g_sk, g_ft, g_fs, g_fe, g_fk = refs[-9:]
    for jobs, layers, count in plan:
        total, refs = whole_sum(refs[:count]), refs[count:]
        rows, planes, small_rows = bundle_rows(jobs, tiles)
        start = planes // 2
        if planes:
            plane = jnp.concatenate([total[: start // 2], total[start // 2 : start]], axis=1)
            g_sk[layers[0]] = plane[:kst]
            g_se[layers[0]] = plane[kst:]
        packed = (rows - planes - small_rows) // 2
        big = total[start : start + packed]
        rows = [big[:, :64], pltpu.roll(big, 64, 1)[:, :64]] if packed else []
        tail = total[start + packed :]

        def part(start, size):
            end = start + size
            if end <= packed:
                return rows[0][start:end]
            if start >= packed:
                return rows[1][start - packed : end - packed]
            return jnp.concatenate([rows[0][start:], rows[1][: end - packed]], axis=0)

        base = 0
        for job, l in zip(jobs, layers):
            if job == "pl":
                continue
            if job == "st":
                for k in range(3):
                    g_st[l, k] = part(base + k * kst, kst).T
            elif job == "ss":
                for k in range(9):
                    g_ss[l, k // 3, k % 3] = part(base + k * kss, kss)
            elif job == "lat":
                for k in range(5):
                    g_lat[l, k] = part(base + k * kla, kla)
            else:
                small = tail[:SMALL_ROWS]
                eight = pltpu.roll(small, (LANES - 8 * si[3]) % LANES, 1)[:, :8]
                for k in range(3):
                    g_ft[l, k] = eight[k * kla : (k + 1) * kla].T
                small = tail[SMALL_ROWS:]
                eight = pltpu.roll(small, (LANES - 8 * si[3]) % LANES, 1)[:, :8]
                for k in range(9):
                    g_fs[l, k // 3, k % 3] = eight[k * ksm : (k + 1) * ksm]
                part32 = pltpu.roll(small, (LANES - 32 * si[3]) % LANES, 1)[:, :32]
                g_fe[l] = part32[9 * ksm : 10 * ksm]
                g_fk[l] = part32[10 * ksm : 10 * ksm + kla]
                continue
            base += job_rows(job, tiles)


def kernel_norm_sums(places, *refs):
    d_gains, d_biases = refs[-2:]
    for l in range(LAYERS):
        for i, out in ((0, d_biases), (1, d_gains)):
            column = 0
            for n, row, second, count in places[l][:5]:
                row += i * second
                for r in range(row, row + count):
                    out[l : l + 1, column : column + LANES] = refs[n][r : r + 1, :]
                    column += LANES
            ft, fs, fe, fk = (
                refs[n][row + i * second : row + i * second + 1, :] for n, row, second, _ in places[l][5:]
            )
            ft, fs = fold_phases(ft), fold_phases(fs)
            fe, fk = pltpu.roll(fe, 64, 1), pltpu.roll(fk, 64, 1)
            place = lane((1, LANES))
            out[l : l + 1, column : column + LANES] = jnp.where(place < 32, ft, jnp.where(place < 64, fs, fe))
            out[l : l + 1, column + LANES : column + 2 * LANES] = jnp.where(place < 64, fe, fk)
            out[l : l + 1, column + 2 * LANES :] = fk[:, :64]


SMEM = pltpu.MemorySpace.SMEM
VMEM = pltpu.MemorySpace.VMEM


class Weight:
    def __init__(self, array, layer):
        self.array = array
        self.layer = layer


class Layer:
    def __init__(self, array, layer):
        self.array = array
        self.layer = layer


class Ready:
    def __init__(self, array):
        self.array = array


class Load:
    def __init__(self, array):
        self.array = array


class Arriving:
    def __init__(self, copy, ref, layered):
        self.copy = copy
        self.ref = ref
        self.layered = layered
        self.shape = ref.shape

    def __getitem__(self, place):
        if self.copy is not None:
            self.copy.wait()
            self.copy = None
        if not self.layered:
            return self.ref[place]
        return self.ref[place[1:]] if isinstance(place, tuple) else self.ref[...]


class Out:
    def __init__(self, shape, kind):
        self.shape = shape
        self.kind = kind


def scalar_values(place, valid, frame, tiles):
    ha, wa, clip = place[0], place[1], place[2]
    total = valid[0]
    for i in range(1, valid.shape[0]):
        total = total + valid[i]
    count = jnp.full((1, LANES), total * (HT * WD), jnp.int32).astype(F32)
    inverse = 1.0 / count
    flags = [ha > 0, ha < tiles[0] - 1, wa > 0, wa < tiles[1] - 1]
    vectors = [jnp.where(jnp.full((1, LANES), jnp.where(f, 1, 0), jnp.int32) > 0, 1.0, 0.0) for f in flags]
    vectors = [inverse, inverse * (1.0 / ALPHA)] + vectors
    return (valid[clip] * frame, ha, wa, clip), [v[:, :1] for v in vectors]


def call(body, scalars, operands, outs, scratch=(), limit=16, pinned=False, ahead=()):
    mode, scalars = (None, ()) if not scalars else (scalars[0], scalars[1:3])
    operands = list(operands) + list(ahead)
    count, first = len(operands), len(scalars)
    kept = len(outs)
    outs = list(outs) + [(x.array.shape[1:], x.array.dtype) for x in ahead]
    weights = [i for i, x in enumerate(operands) if isinstance(x, (Weight, Load))]
    results = [i for i, x in enumerate(outs) if isinstance(x, Out)]
    arrays = [x.array if isinstance(x, (Weight, Layer, Load, Ready)) else x for x in operands]
    if pinned:
        for i in weights:
            arrays[i] = pltpu.with_memory_space_constraint(arrays[i], pltpu.HBM)
    layered = [isinstance(x, Weight) for x in operands]
    shapes = [(x.shape, x.kind) if isinstance(x, Out) else x for x in outs]
    inward = weights[: len(weights) - len(ahead)]
    buffers = [pltpu.VMEM(arrays[i].shape[1:] if layered[i] else arrays[i].shape, arrays[i].dtype) for i in inward]
    buffers += [pltpu.VMEM(*shapes[i]) for i in results]
    own = first + count + len(outs)
    copies = len(buffers) + len(ahead)

    def wrapped(*refs):
        refs = list(refs)
        inner, rest = refs[own : own + len(buffers)], refs[own + len(buffers) :]
        arriving, leaving = [], []
        for n, i in enumerate(inward):
            source = refs[first + i].at[operands[i].layer] if layered[i] else refs[first + i]
            copy = pltpu.make_async_copy(source, inner[n], rest[-1].at[n])
            copy.start()
            refs[first + i] = Arriving(copy, inner[n], layered[i])
            arriving.append(refs[first + i])
        for i, x in enumerate(operands):
            if isinstance(x, Layer):
                refs[first + i] = refs[first + i].at[x.layer]
            if isinstance(x, Ready):
                refs[first + i] = Arriving(None, refs[first + i], True)
        later = []
        for n, x in enumerate(ahead):
            source = refs[first + count - len(ahead) + n].at[x.layer]
            later.append(pltpu.make_async_copy(source, refs[first + count + kept + n], rest[-1].at[len(buffers) + n]))
            later[-1].start()
        for n, i in enumerate(results):
            n += len(inward)
            leaving.append(pltpu.make_async_copy(inner[n], refs[first + count + i], rest[-1].at[n]))
            refs[first + count + i] = inner[n]
        given = ()
        if mode is not None:
            t_frame, tiles = mode[1], mode[2]
            ints, vectors = scalar_values(refs[0], refs[1], t_frame, tiles) if mode[0] == "all" else (
                (None, refs[0][0], refs[0][1], refs[0][2]), None)
            given = (ints, vectors) if mode[0] == "all" else (ints,)
        given_refs = refs[first : first + count - len(ahead)] + refs[first + count : first + count + kept]
        body(*given, *given_refs, *(rest[:-1] if copies else rest))
        for copy in leaving:
            copy.start()
        for one in arriving:
            if one.copy is not None:
                one.copy.wait()
        for copy in leaving + later:
            copy.wait()

    def space(i, some):
        return pl.BlockSpec(memory_space=pltpu.HBM if i in some else VMEM)

    return pl.pallas_call(
        wrapped,
        out_shape=[jax.ShapeDtypeStruct(shape, kind) for shape, kind in shapes],
        in_specs=[pl.BlockSpec(memory_space=SMEM) for _ in scalars] + [space(i, weights) for i in range(count)],
        out_specs=[space(i, results) for i in range(len(outs))],
        scratch_shapes=buffers
        + [pltpu.VMEM(shape, kind) for shape, kind in scratch]
        + ([pltpu.SemaphoreType.DMA((copies,))] if copies else []),
        cost_estimate=pl.CostEstimate(flops=3000000000, bytes_accessed=6000000, transcendentals=0),
        compiler_params=pltpu.CompilerParams(vmem_limit_bytes=limit << 20),
    )(*scalars, *arrays)


def sum_over(x, axis):
    step, count = 1, lax.axis_size(axis)
    while step < count:
        pair = x + flip(x, axis, step)
        if 4 * step <= count:
            pair = pair + (flip(x, axis, 2 * step) + flip(x, axis, 3 * step))
            step *= 2
        x = pair
        step *= 2
    return x


def sum_all(x):
    for axis in (WA, HA, CLIP):
        x = sum_over(x, axis)
    return x


def exchange(block):
    return lax.all_to_all(block, ALL_AXES, 0, 0)


def swap(x):
    return lax.ppermute(x, WA, [(0, 1), (1, 0)])


def halo(z, top, bottom):
    count = lax.axis_size(HA)
    above = lax.ppermute(bottom, HA, [(i, i + 1) for i in range(count - 1)])
    below = lax.ppermute(top, HA, [(i + 1, i) for i in range(count - 1)])
    return [above, below, swap(z), swap(above), swap(below)]


def sum_with_halo(x, one, two, z):
    n = x.shape[0]
    one, two, across = flip(one, HA, 1), flip(two, HA, 3), flip(x, HA, 2)
    both = x + across
    o_one, o_two, o_both = swap(one), swap(two), swap(both)
    total = (both + (one[:n] + two[:n])) + (o_both + (o_one[:n] + o_two[:n]))
    return total, [one, two, swap(z), o_one, o_two]


def after(first, *rest):
    return lax.optimization_barrier((first,) + rest)


def flip(x, axis, step):
    return lax.ppermute(x, axis, [(i, i ^ step) for i in range(lax.axis_size(axis))])


ORDERS = ((WA, HA, CLIP), (WA, HA, CLIP), (WA, CLIP, HA), (WA, HA, CLIP), (WA, CLIP, HA), (WA, HA, CLIP), (WA, CLIP, HA))
LAUNCH = {(1, 'wa'): ('A1',), (3, 'wa'): ('ST1',), (5, 'wa'): ('A0',), (3, 'ha'): ('A1',), (5, 'ha'): ('ST1',), (6, 'ha'): ('A0',)}
LAND = {(1, 'clip'): ('A1',), (2, 'ha'): ('A1',), (3, 'clip'): ('ST1',), (4, 'ha'): ('A1', 'ST1'), (5, 'clip'): ('A1', 'A0'), (6, 'ha'): ('ST1',)}
BUNDLES = {1: [('A1', False, [('pl', 1)])], 3: [('ST1', False, [('ss', 1), ('st', 1)])], 5: [('A0', False, [('pl', 0), ('ss', 0), ('lat', 1), ('sm', 1)])], 7: [('L0', True, [('st', 0), ('lat', 0), ('sm', 0)])]}
WAIT = {(5, CLIP, "A0"), (2, HA, "A1"), (6, HA, "ST1"), (4, HA, "ST1")}


def local(
    slow_in,
    fast_in,
    valid_frames,
    lateral_w,
    slow_temporal_w,
    slow_spatial_w,
    slow_expand_w,
    slow_skip_w,
    fast_temporal_w,
    fast_spatial_w,
    fast_expand_w,
    fast_skip_w,
    gains,
    biases,
    slow_cot,
    fast_cot,
):
    devices = lax.axis_size(ALL_AXES)
    clips, n_ha, n_wa = (lax.axis_size(a) for a in ALL_AXES)
    tiles = n_ha * n_wa
    _, t, h, w, _ = slow_in.shape
    shape = (t, h, w)
    frame = h * w
    rows = t * frame

    place = jnp.stack([lax.axis_index(a) for a in (HA, WA, CLIP)]).astype(jnp.int32)
    scalars = (("all", frame, (n_ha, n_wa)), place, valid_frames)
    places = (("place", frame, (n_ha, n_wa)), place, valid_frames)

    slow2 = slow_in.reshape(rows, DS)
    fast4 = fast_in.reshape(t, ALPHA, frame, DF)
    slow_cot2 = slow_cot.reshape(rows, DS)
    fast_cot4 = fast_cot.reshape(t, ALPHA, frame, DF)

    def act(columns, kind=F32):
        return ((rows, columns), kind)

    def edges(columns, sums=None):
        if sums is None:
            return [act(columns, BF16), ((t * w, columns), BF16), ((t * w, columns), BF16)]
        return [act(columns, BF16)] + [((sums + t * w * columns // LANES, LANES), F32)] * 2

    def pay(count):
        return ((count, LANES), F32)

    def bind(body, *static):
        return functools.partial(body, *static)

    pad_slow = ((t, h + 2, 3 * w, BS), F32)
    pad_fast = ((t, h + 2, 3 * w, LANES), F32)
    pad_both = ((t, h + 2, 3 * w, BS + LANES), F32)
    saved = []
    fb, zlat, zft, z16, top, bottom, zfk, sent, band = call(
        bind(kernel_start, shape),
        scalars,
        [Load(fast4), Weight(lateral_w, 0), Load(jnp.swapaxes(fast_temporal_w, 2, 3)), Weight(fast_skip_w, 0)],
        [act(512, BF16), act(DL), act(LANES), *edges(LANES, 8), act(512), pay(8), ((LAYERS, 6, LANES, LANES), BF16)],
        pinned=True,
    )
    recv, around = sum_with_halo(sent, top, bottom, z16)
    recv = sum_over(recv, CLIP)
    gb_all, fs_bd, fe_bd, *ahead = call(
        kernel_prepare,
        (),
        [Load(gains), Load(biases), Load(fast_spatial_w), Load(fast_expand_w)],
        [((LAYERS, 2, GB_ROWS, LANES), F32), ((LAYERS, 3, 3, LANES, LANES), BF16), ((LAYERS, LANES, ALPHA * DF), BF16)],
        pinned=True,
        ahead=[Weight(slow_temporal_w, 0), Weight(slow_skip_w, 0)],
    )
    gb = [Layer(gb_all, l) for l in range(LAYERS)]
    before = None
    for l in range(LAYERS):
        last = l == LAYERS - 1
        start = [recv, Load(slow2), gb[l]] if l == 0 else [recv, gb[l - 1], before["tot_sk"], before["zse"], before["zsk"], gb[l]]
        low, zst, z16, top, bottom, zsk, af9, zfs, sent = call(
            bind(kernel_temporal, l == 0, shape),
            scalars,
            start + [zlat, zft, *around, Ready(ahead[0]), Ready(ahead[1]), Layer(fs_bd, l)],
            [act(CC, BF16), act(BS), *edges(BS, 24), act(DS), act(9 * LANES, BF16), act(LANES), pay(24)],
            [pad_fast],
        )
        tot_lat = recv
        if l > 0:
            before["tot_se"] = tot_lat
        recv, around = sum_with_halo(sent, top, bottom, z16)
        recv = sum_over(recv, CLIP)
        a9, zss, bf, zfe, sent = call(
            bind(kernel_spatial, shape),
            scalars,
            [recv, gb[l], zst, *around, zfs, Weight(slow_spatial_w, l), Layer(fe_bd, l)],
            [act(9 * BS, BF16), act(BS), act(LANES, BF16), act(512), ((devices, 8, LANES), F32)],
            [pay(8), pad_slow],
        )
        tot_st = recv
        recv = exchange(sent)
        keep = dict(
            fb=fb, zlat=zlat, zft=zft, zfk=zfk, low=low, zst=zst, zsk=zsk, af9=af9, zfs=zfs, a9=a9, zss=zss, bf=bf,
            zfe=zfe, tot_lat=tot_lat, tot_fk=tot_lat, tot_st=tot_st, tot_sk=tot_st,
        )
        if last:
            bt, zse, sent, tot_ss = call(
                bind(kernel_expand, True, shape),
                scalars,
                [recv, gb[l], zss, Weight(slow_expand_w, l)],
                [act(BS, BF16), act(DS), ((devices, 16, LANES), F32), pay(8)],
                [pay(16)],
            )
        else:
            bt, zse, sent, tot_ss, fb, zlat, zft, z16, top, bottom, zfk, *ahead = call(
                bind(kernel_expand, False, shape),
                scalars,
                [recv, gb[l], zss, Weight(slow_expand_w, l), tot_lat, zfe, zfk,
                 Weight(lateral_w, l + 1), Layer(band, l + 1), Weight(fast_skip_w, l + 1)],
                [act(BS, BF16), act(DS), pay(24), pay(8),
                 act(512, BF16), act(DL), act(LANES), *edges(LANES, 24), act(512)],
                ahead=[Weight(slow_temporal_w, l + 1), Weight(slow_skip_w, l + 1)],
            )
        if last:
            recv = exchange(sent)
        else:
            recv, around = sum_with_halo(sent, top, bottom, z16)
            recv = sum_over(recv, CLIP)
        keep.update(bt=bt, zse=zse, tot_ss=tot_ss, tot_fe=tot_ss)
        saved.append(keep)
        before = keep

    for l in range(LAYERS):
        saved[l]["gb"] = gb[l]

    def stage(body, ins, outs, scratch=(), limit=16, ahead=()):
        names = list(ins) + list(outs) + [name for name, _ in scratch]

        def named(ints, vectors, *refs):
            body(shape, Refs(names, refs), inside_rows(rows, 256, ints[0]), ints, vectors)

        results = call(
            named, scalars, list(ins.values()), list(outs.values()), [kind for _, kind in scratch], limit,
            ahead=list(ahead),
        )
        return dict(zip(outs, results[: len(outs)]), ahead=results[len(outs) :])

    def layer(prefix, l, *names):
        return {prefix + name: saved[l][name] for name in names}

    def edge(columns, sums=None):
        return dict(zip(("whole", "top", "bottom"), edges(columns, sums)))

    def around_of(values):
        return {f"h{i}": x for i, x in enumerate(values)}

    narrow = clips == 4

    def halves_chain(keep, send, jobs):
        count = bundle_rows(jobs, tiles)[0]
        (got,) = yield [keep], [(send, WA, 1)]
        split = count // 32 * 16
        a, b = (split, 256), (count - split, 256)
        keep_a, send_a, keep_b, send_b = call(
            bind(kernel_halve_first, split), places, [keep, got], [((2,) + x, BF16) for x in (a, a, b, b)]
        )
        got_a, got_b = yield [keep_a, keep_b], [(send_a, HA, 1), (send_b, HA, 2)]
        keep_a, send_a, keep_b, send_b = call(
            kernel_halve_second, places, [keep_a, got_a, keep_b, got_b], [(x, BF16) for x in (a, a, b, b)]
        )
        got_a, got_b = yield [keep_a, keep_b], [(send_a, HA, 2), (send_b, HA, 1)]
        parts = [keep_a, got_a, keep_b, got_b]
        if narrow:
            block = (share_rows(jobs, tiles), LANES)
            keep, send = call(
                bind(kernel_join_columns, jobs, tiles), places, parts, [((2,) + block, BF16)] * 2, [((4,) + block, BF16)]
            )
            (got,) = yield [keep], [(send, CLIP, 1)]
            keep, send = call(kernel_halve_last, places, [keep, got], [(block, BF16)] * 2)
            (got,) = yield [keep], [(send, CLIP, 2)]
            parts = [keep, got]
        yield parts, None

    def direct_chain(keep, send, jobs):
        count = bundle_rows(jobs, tiles)[0]
        (got,) = yield [keep], [(send, WA, 1)]
        mine, *others = call(kernel_pick_places, places, [keep, got], [((count, 256), BF16)] * 4)
        got = yield [mine], [(x, HA, i + 1) for i, x in enumerate(others)]
        parts = [mine, *got]
        if narrow:
            block = (share_rows(jobs, tiles), LANES)
            mine, *others = call(
                bind(kernel_pick_columns, jobs, tiles), places, parts, [(block, BF16)] * 4, [((4,) + block, BF16)]
            )
            got = yield [mine], [(x, CLIP, i + 1) for i, x in enumerate(others)]
            parts = [mine, *got]
        yield parts, None

    class Running:
        def __init__(self, chain, jobs, layers):
            self.chain = chain
            self.jobs = jobs
            self.layers = layers
            self.got = None
            self.state = next(chain)

        def done(self):
            return self.state[1] is None

        def launch(self, x=None):
            if self.done() or self.got is not None:
                return
            sends = [send for send, _, _ in self.state[1]]
            if x is not None:
                _, *sends = after(x, *sends)
            self.got = [flip(send, axis, step) for send, (_, axis, step) in zip(sends, self.state[1])]

        def land(self, x):
            if self.got is None:
                return x
            x, *got = after(x, *self.got)
            self.got = None
            self.state = self.chain.send(got)
            return x

        def finish(self):
            while not self.done():
                self.launch()
                got, self.got = self.got, None
                self.state = self.chain.send(got)
                yield

    running = {}

    def bundle(name, chain, *parts):
        jobs, layers = tuple(p[0] for p in parts), tuple(p[1] for p in parts)
        operands = []
        for job, l, r in parts:
            k = saved[l]
            operands += {
                "pl": lambda: [k["low"], k["bt"], r["dz_sk"], r["dz_se"]],
                "st": lambda: [k["low"], r["dz_st"]],
                "ss": lambda: [k["a9"], r["dz"]],
                "lat": lambda: [k["fb"], r["dz_lat"]],
                "sm": lambda: [k["af9"], k["fb"], k["bf"], r["dz_f"], r["dz_ft"], r["dz_fe"], r["dz_fk"]],
            }[job]()
        count = bundle_rows(jobs, tiles)[0]
        pair = call(
            bind(kernel_weights_rows, tiles, frame, jobs),
            places,
            operands,
            [((tiles // 2, count, 256), BF16)] * 2,
            [((tiles, count, 256), BF16), ((tiles, SMALL_ROWS, 256), F32)],
            limit=24,
        )
        running[name] = Running(chain(*pair, jobs), jobs, layers)
        running[name].direct = chain is direct_chain

    def skip_back(l, r):
        (r["dlow"],) = call(kernel_back_skip, (), [r["dz_sk"], Weight(slow_skip_w, l)], [act(CC)])

    totals = []

    around = []

    def total_of(x, edge_rows=None):
        n = len(totals)
        for axis in ORDERS[n]:
            for name in LAND.get((n, axis), ()):
                x = running[name].land(x)
                if (n, axis, name) not in WAIT:
                    running[name].launch()
            if edge_rows is None:
                x = sum_over(x, axis)
            elif axis == HA:
                x, around[:] = sum_with_halo(x, edge_rows["top"], edge_rows["bottom"], edge_rows["whole"])
            elif axis == CLIP:
                x = sum_over(x, axis)
            for name in LAUNCH.get((n, axis), ()) + tuple(w[2] for w in WAIT if w[:2] == (n, axis) and w != (5, CLIP, "A0")):
                running[name].launch(x)
        totals.append(x)
        return x

    one, two = LAYERS - 1, LAYERS - 2
    r1, r0 = {}, {}

    def start_bundles():
        for name, direct, parts in BUNDLES.get(len(totals), ()):
            chain = direct_chain if direct else halves_chain
            bundle(name, chain, *[(job, l, (r0, r1)[l]) for job, l in parts])

    slow_names, fast_names = ("gb", "tot_se", "tot_sk", "zse", "zsk"), ("tot_ss", "tot_lat", "zfe", "zfk")
    r1.update(stage(
        back_turn,
        dict(recv=recv, **layer("a_", one, *slow_names[:1], *slow_names[2:], *fast_names), slow_cot=Load(slow_cot2), fast_cot=Load(fast_cot4)),
        dict(out_slow=Out((rows, DS), F32), out_fast=Out((t, ALPHA, frame, DF), F32), du_s=act(DS), du_f=act(512), pay=pay(32), tot=pay(16)),
    ))
    saved[-1]["tot_se"] = r1["tot"]
    recv = total_of(r1["pay"])
    r1.update(stage(
        back_expand,
        dict(recv=recv, **layer("a_", one, *slow_names, *fast_names, "zss", "zfs"), du_s=r1["du_s"], du_f=r1["du_f"],
             se_w=Weight(slow_expand_w, one), fe_bd=Layer(fe_bd, one)),
        dict(dz_se=act(DS, BF16), dz_sk=act(DS, BF16), dz_fe=act(512, BF16), dz_fk=act(512, BF16), dy=act(BS + LANES),
             **edge(2 * (BS + LANES)), pay=pay(8)),
    ))
    skip_back(one, r1)
    start_bundles()
    recv = total_of(r1["pay"])
    r1.update(stage(
        back_spatial,
        dict(recv=recv, **layer("a_", one, "gb", "tot_sk", "tot_ss", "tot_lat", "zss", "zfs", "zst", "zft"), dy=r1["dy"],
             **around_of(halo(r1["whole"], r1["top"], r1["bottom"])), ss_w=Weight(slow_spatial_w, one), fs_bd=Layer(fs_bd, one)),
        dict(dz=act(BS + LANES, BF16), dy_st=act(BS), dy_ft=act(LANES), pay=pay(8)),
        [("pad", pad_both)],
        ahead=[Weight(slow_temporal_w, one)],
    ))
    r1["dz_f"] = r1["dz"]
    start_bundles()
    recv = total_of(r1["pay"])
    r1.update(stage(
        back_temporal,
        dict(recv=recv, **layer("a_", one, "gb", "tot_sk", "tot_lat", "zst", "zft", "zlat"),
             **layer("b_", two, *slow_names), dy_st=r1["dy_st"], dy_ft=r1["dy_ft"], dlow=r1["dlow"], dz_fk=r1["dz_fk"],
             st_w=Ready(r1["ahead"][0]), ft_band=Layer(band, one), fk_w=Weight(fast_skip_w, one)),
        dict(dz_st=act(3 * BS, BF16), dz_ft=act(LANES, BF16), dfast=act(512), dy_lat=act(DL), du_s=act(DS), pay=pay(32)),
    ))
    start_bundles()
    recv = total_of(r1["pay"])
    r0.update(stage(
        back_lateral,
        dict(recv=recv, **layer("a_", one, "gb", "tot_lat", "zlat"),
             **layer("b_", two, *slow_names, *fast_names, "zss"), dy_lat=r1["dy_lat"], dfast=r1["dfast"], du_s=r1["du_s"],
             lat_w=Weight(lateral_w, one), se_w=Weight(slow_expand_w, two)),
        dict(dz_lat=act(DL, BF16), du_f=act(512), dz_se=act(DS, BF16), dz_sk=act(DS, BF16), dy=act(BS), **edge(2 * BS), pay=pay(8)),
    ))
    r1["dz_lat"] = r0["dz_lat"]
    start_bundles()
    skip_back(two, r0)
    recv = total_of(r0["pay"])
    fast = stage(
        back_low_spatial,
        dict(recv=recv, **layer("b_", two, "gb", "tot_sk", "tot_ss", "tot_lat", "zss", "zst", "zfe", "zfk", "zfs"),
             du_f=r0["du_f"], dy=r0["dy"], **around_of(halo(r0["whole"], r0["top"], r0["bottom"])), ss_w=Weight(slow_spatial_w, two), fe_bd=Layer(fe_bd, two)),
        dict(dz_fe=act(512, BF16), dz_fk=act(512, BF16), dy_fs=act(LANES), **edge(2 * LANES), dz=act(BS, BF16), dy_st=act(BS),
             pay=pay(8)),
        [("pad", pad_slow)],
        ahead=[Weight(slow_temporal_w, two)],
    )
    r0.update(fast)
    start_bundles()
    recv = total_of(r0["pay"])
    r0.update(stage(
        back_low_temporal,
        dict(recv=recv, **layer("b_", two, "gb", "tot_sk", "tot_lat", "zst", "zft", "zlat", "zfs"), dy_fs=r0["dy_fs"],
             **around_of(halo(r0["whole"], r0["top"], r0["bottom"])), dy_st=r0["dy_st"], dlow=r0["dlow"], st_w=Ready(r0["ahead"][0]), fs_bd=Layer(fs_bd, two)),
        dict(dz_f=act(LANES, BF16), dy_ft=act(LANES), dz_st=act(3 * BS, BF16), dy_lat=act(DL), pay=pay(8)),
        [("pad", pad_fast)],
    ))
    start_bundles()
    recv = total_of(r0["pay"])
    r0.update(stage(
        back_low_lateral,
        dict(recv=recv, **layer("b_", two, "gb", "tot_lat", "zft", "zlat"), dy_ft=r0["dy_ft"], dy_lat=r0["dy_lat"]),
        dict(dz_ft=act(LANES, BF16), dz_lat=act(DL, BF16)),
    ))
    start_bundles()
    ways = [chain.finish() for chain in running.values()]
    _, late_lat, late_st = after(running["L0"].state[1][0][0], r0["dz_lat"], r0["dz_st"])
    while ways:
        ways = [way for way in ways if next(way, 0) is None]
    out_slow, out_fast = r1["out_slow"], r1["out_fast"]
    (grad_slow,) = call(
        kernel_low_input, (), [late_st, r0["dlow"], Weight(slow_temporal_w, two)], [Out((rows, DS), F32)]
    )
    (grad_fast,) = call(
        bind(kernel_low_fast_input, frame),
        (),
        [late_lat, r0["dz_ft"], r0["dz_fk"], Weight(lateral_w, two), Weight(fast_skip_w, two), Layer(band, two)],
        [Out((t, ALPHA, frame, DF), F32)],
    )
    where = [
        [(6, 0, 2, 2), (5, 0, 2, 2), (4, 0, 2, 2), (3, 8, 8, 8), (3, 8, 16, 8), (6, 4, 1, 1), (5, 4, 1, 1), (4, 4, 1, 1),
         (4, 4, 2, 1)],
        [(3, 0, 2, 2), (2, 0, 2, 2), (1, 0, 2, 2), (0, 0, 8, 8), (0, 0, 16, 8), (2, 4, 1, 1), (1, 4, 1, 1), (0, 24, 1, 1),
         (0, 24, 2, 1)],
    ]
    nst, nss, nla, nsm = CC // tiles, BS // tiles, DF // tiles, BF // tiles
    n, f, g = BS // clips, BF // clips, DF // clips
    sums = call(bind(kernel_norm_sums, where), (), totals, [Out(gains.shape, F32), Out(biases.shape, F32)])
    weights = [(LAYERS,) + dims for dims in (
        (5, nla, n), (3, nst, n), (3, 3, nss, n), (nss, DS // clips), (nst, DS // clips),
        (3, nla, f), (3, 3, nsm, f), (nsm, g), (nla, g),
    )]
    chains = list(running.values())
    if narrow:
        plan = [(chain.jobs, chain.layers, len(chain.state[0])) for chain in chains]
        parts = [x for chain in chains for x in chain.state[0]]
        turned = (1, 5)
        weights = [dims[:-2] + dims[:-3:-1] if i in turned else dims for i, dims in enumerate(weights)]
        weights = call(bind(kernel_finish, tiles, plan), places, parts, [Out(dims, F32) for dims in weights])
        weights = [jnp.swapaxes(x, -1, -2) if i in turned else x for i, x in enumerate(weights)]
    else:
        found = {}
        for chain in chains:
            got = [x.astype(F32) for x in chain.state[0]]
            if not chain.direct:
                total = jnp.concatenate([got[0] + got[1], got[2] + got[3]], axis=0).astype(BF16)
            else:
                total = sum(got).astype(BF16)
            count, planes, small_rows = bundle_rows(chain.jobs, tiles)
            if planes:
                plane = jnp.transpose(total[:planes].reshape(4, -1, 256), (1, 0, 2)).reshape(planes // 4, clips, DS // clips)
                plane = lax.psum_scatter(plane, CLIP, scatter_dimension=1)
                found["sk", chain.layers[0]], found["se", chain.layers[0]] = plane[:nst], plane[nst:]
            small = lax.psum(total[count - small_rows :], CLIP) if small_rows else None
            if count - small_rows > planes:
                total = lax.psum_scatter(
                    total[planes : count - small_rows].reshape(-1, clips, n), CLIP, scatter_dimension=1
                )
            base = 0
            for job, l in zip(chain.jobs, chain.layers):
                if job == "sm":
                    left = lax.dynamic_slice_in_dim(small[:, :LANES], place[2] * f, f, 1)
                    right = lax.dynamic_slice_in_dim(small[:, LANES:], place[2] * f, f, 1)
                    last = lax.dynamic_slice_in_dim(small[:, LANES:], place[2] * g, g, 1)
                    found["ft", l], found["fs", l] = left[: 3 * nla], right[: 9 * nsm]
                    found["fe", l], found["fk", l] = last[9 * nsm : 10 * nsm], last[10 * nsm : 10 * nsm + nla]
                elif job != "pl":
                    found[job, l] = total[base : base + job_rows(job, tiles)]
                    base += job_rows(job, tiles)
        names = ("lat", "st", "ss", "se", "sk", "ft", "fs", "fe", "fk")
        weights = [
            jnp.stack([found[name, l] for l in range(LAYERS)]).astype(F32).reshape(dims)
            for name, dims in zip(names, weights)
        ]
    return (
        out_slow.reshape(slow_in.shape),
        out_fast.reshape(fast_in.shape),
        grad_slow.reshape(slow_in.shape),
        grad_fast.reshape(fast_in.shape),
        *weights,
        *sums,
    )


def solution(mesh):
    pixels = P(CLIP, None, HA, WA, None)
    tile = (HA, WA)
    return jax.shard_map(
        local,
        mesh=mesh,
        in_specs=(pixels, pixels) + (P(),) * 12 + (pixels, pixels),
        out_specs=(
            (pixels,) * 4
            + (P(None, None, tile, CLIP),) * 2
            + (P(None, None, None, tile, CLIP),)
            + (P(None, tile, CLIP),) * 2
            + (P(None, None, tile, CLIP),)
            + (P(None, None, None, tile, CLIP),)
            + (P(None, tile, CLIP),) * 2
            + (P(),) * 2
        ),
        check_vma=False,
    )
```

```python
import functools

import jax
import jax.numpy as jnp
from jax import lax
from jax.experimental import pallas as pl
from jax.experimental.pallas import tpu as pltpu
from jax.sharding import PartitionSpec as P

DS = 1024
DL = 256
BS = 256
DF = 128
BF = 32
ST = 8
ALPHA = 4
HT = 16
WD = 16
LAYERS = 2
CC = DS + DL
EPSILON = 1e-05
LANES = 128
CLIP, HA, WA = "clip", "ha", "wa"
ALL_AXES = (CLIP, HA, WA)


LAT, STM, SSP, SEX, SSK, FTM, FSP, FEX, FSK = 0, 2, 4, 6, 14, 22, 23, 24, 25
GB_ROWS = 32

F32 = jnp.float32
BF16 = jnp.bfloat16


def dot(a, b):
    return jnp.dot(a, b, preferred_element_type=F32)


def dot_nt(a, b):
    return lax.dot_general(a, b, (((1,), (1,)), ((), ())), preferred_element_type=F32)


def dot_tn(a, b):
    return lax.dot_general(a, b, (((0,), (0,)), ((), ())), preferred_element_type=F32)


def sigmoid(v):
    return 0.5 * jnp.tanh(0.5 * v) + 0.5


def silu(v):
    return v * sigmoid(v)


def slope(v):
    s = sigmoid(v)
    return s + v * s * (1.0 - s)


def silu_and_slope(v):
    s = sigmoid(v)
    act = v * s
    return act, s + act * (1.0 - s)


def wide(tile, row, count):
    if count == 1:
        return tile[row : row + 1, :]
    return jnp.concatenate([tile[row + i : row + i + 1, :] for i in range(count)], axis=1)


def fold_phases(tile):
    return tile + pltpu.roll(tile, 32, 1) + pltpu.roll(tile, 64, 1) + pltpu.roll(tile, 96, 1)


def down(x, frame):
    return jnp.concatenate([jnp.zeros_like(x[:frame]), x[:-frame]], axis=0)


def up(x, frame):
    return jnp.concatenate([x[frame:], jnp.zeros_like(x[:frame])], axis=0)


def col_sum(x):
    return jnp.sum(x, axis=0, keepdims=True)


class Norm:
    def __init__(self, total, row, gb, gb_row, count, inv_count):
        mean = wide(total, row, count) * inv_count
        square = wide(total, row + count, count) * inv_count
        self.mean = mean
        self.rstd = lax.rsqrt(square - mean * mean + EPSILON)
        self.gain = wide(gb[0], gb_row, count)
        self.bias = wide(gb[1], gb_row, count)
        self.scale = self.gain * self.rstd
        self.shift = self.bias - mean * self.scale

    def columns(self, start, size):
        other = object.__new__(Norm)
        for name in ("mean", "rstd", "gain", "bias", "scale", "shift"):
            setattr(other, name, getattr(self, name)[:, start : start + size])
        return other

    def out(self, z):
        return z * self.scale + self.shift

    def hat(self, z):
        return (z - self.mean) * self.rstd

    def back(self, dy, hat, inside, a_sum, b_sum, inv_count):
        return self.scale * (dy - jnp.where(inside, a_sum * inv_count + hat * (b_sum * inv_count), 0.0))


def inside_rows(rows, columns, limit):
    return lax.broadcasted_iota(jnp.int32, (rows, columns), 0) < limit


def moments(z, inside):
    masked = jnp.where(inside, z, 0.0)
    return col_sum(masked), col_sum(masked * z)


def put_rows(ref, row, vector):
    for i in range(vector.shape[1] // LANES):
        ref[row + i : row + i + 1, :] = vector[:, i * LANES : (i + 1) * LANES]


def spread(tile, ref):
    def body(i, carry):
        ref[i] = tile[...]
        return carry

    lax.fori_loop(0, ref.shape[0], body, 0)


def gathered(ref):
    return jnp.sum(ref[...], axis=0)


def phase(ref, p):
    return ref[:, p].reshape(ref.shape[0] * ref.shape[2], ref.shape[3])


def send_halo(z, shape, si, whole, one, two):
    t, h, w = shape
    columns = z.shape[1]
    four = z.reshape(t, h, w, columns)
    whole[...] = z.astype(BF16)
    top, bottom = (four[:, i].reshape(t * w, columns) for i in (0, h - 1))
    if one.dtype == BF16:
        one[...] = top.astype(BF16)
        two[...] = bottom.astype(BF16)
        return
    even = jnp.full((t * w, columns), si[1] % 2, jnp.int32) == 0
    base = one.shape[0] - t * w * columns // LANES
    for ref, value in ((one, jnp.where(even, bottom, top)), (two, jnp.where(even, top, bottom))):
        for i in range(columns // LANES):
            ref[base + i * t * w : base + (i + 1) * t * w, :] = value[:, i * LANES : (i + 1) * LANES]


def send_sums(pay, one, two):
    if one.dtype == F32:
        for ref in (one, two):
            ref[: pay.shape[0], :] = pay[...]


def halo_values(si, edge, refs):
    one, two, other, o_one, o_two = refs
    if one.dtype == BF16:
        return [ref[...].astype(F32) for ref in (one, two, o_one, other, o_two)]
    columns = other.shape[1]
    base = one.shape[0] - edge * columns // LANES

    def rows(ref):
        parts = [ref[base + i * edge : base + (i + 1) * edge, :] for i in range(columns // LANES)]
        return jnp.concatenate(parts, axis=1) if len(parts) > 1 else parts[0]

    even = jnp.full((edge, columns), si[1] % 2, jnp.int32) == 0
    one, two, o_one, o_two = (rows(ref) for ref in (one, two, o_one, o_two))
    return [
        jnp.where(even, two, one), jnp.where(even, one, two),
        jnp.where(even, o_two, o_one), other[...].astype(F32), jnp.where(even, o_one, o_two),
    ]


def fill_padded(pad, shape, own, above, below, others, has_left, has_right):
    t, h, w = shape
    c = own.shape[1]
    pad[:, 1 : h + 1, w : 2 * w, :] = own.reshape(t, h, w, c)
    pad[:, 0, w : 2 * w, :] = above.reshape(t, w, c)
    pad[:, h + 1, w : 2 * w, :] = below.reshape(t, w, c)
    o_above, o_own, o_below = others
    for start, has in ((0, has_left), (2 * w, has_right)):
        pad[:, 1 : h + 1, start : start + w, :] = (o_own * has).reshape(t, h, w, c)
        pad[:, 0, start : start + w, :] = (o_above * has).reshape(t, w, c)
        pad[:, h + 1, start : start + w, :] = (o_below * has).reshape(t, w, c)


def tap(pad, shape, a, b):
    t, h, w = shape
    part = pad[:, a : a + h, w - 1 + b : 2 * w - 1 + b, :]
    return part.reshape(t * h * w, part.shape[-1]).astype(BF16)


def activate_padded(pad, shape, norm, own, halo_refs, si, sf):
    def act(z):
        return silu(norm.out(z.astype(F32))).astype(BF16).astype(F32)

    edge = shape[0] * shape[2]
    above, below, o_above, o_own, o_below = (act(x) for x in halo_values(si, edge, halo_refs))
    has_up, has_down = sf[2], sf[3]
    others = (o_above * has_up, o_own, o_below * has_down)
    fill_padded(pad, shape, act(own), above * has_up, below * has_down, others, sf[4], sf[5])


def fast_head(phases, shape, si, inside, lat_w, ft_band, fk_w, fb_out, zlat_out, zft_out, halo_out, zfk_out, pay, row):
    frame = shape[1] * shape[2]
    low = [v.astype(BF16) for v in phases]
    for p in range(ALPHA):
        fb_out[:, p * DF : (p + 1) * DF] = low[p]
    before2, before3, after0 = down(low[2], frame), down(low[3], frame), up(low[0], frame)
    z = (
        dot(before2, lat_w[0, 0])
        + dot(before3, lat_w[0, 1])
        + dot(low[0], lat_w[0, 2])
        + dot(low[1], lat_w[0, 3])
        + dot(low[2], lat_w[0, 4])
    )
    zlat_out[...] = z
    total, square = moments(z, inside[:, :DL])
    put_rows(pay, row, total)
    put_rows(pay, row + 2, square)
    six = [before3] + low + [after0]
    z = dot(six[0], ft_band[0])
    for j in range(1, 6):
        z = z + dot(six[j], ft_band[j])
    zft_out[...] = z
    send_halo(z, shape, si, *halo_out)
    total, square = moments(z, inside[:, :LANES])
    put_rows(pay, row + 4, total)
    put_rows(pay, row + 5, square)
    total, square = 0.0, 0.0
    for p in range(ALPHA):
        z = dot(low[p], fk_w[0])
        zfk_out[:, p * DF : (p + 1) * DF] = z
        one, two = moments(z, inside[:, :LANES])
        total, square = total + one, square + two
    put_rows(pay, row + 6, total)
    put_rows(pay, row + 7, square)


def place_columns(p):
    row = lax.broadcasted_iota(jnp.int32, (BF, LANES), 0)
    column = lax.broadcasted_iota(jnp.int32, (BF, LANES), 1)
    return jnp.where(column == row + BF * p, 1.0, 0.0).astype(BF16)


def kernel_start(shape, si, sf, fast, lat_w, ft_w, fk_w, fb, zlat, zft, z16, top, bottom, zfk, pay, ft_band):
    t, h, w = shape
    inside = inside_rows(t * h * w, DL, si[0])
    places = [place_columns(p) for p in range(ALPHA)]
    for l in range(LAYERS):
        for j in range(6):
            part = 0.0
            for p in range(ALPHA):
                if 0 <= j - p <= 2:
                    part = part + dot_tn(ft_w[l, j - p], places[p])
            ft_band[l, j] = part.astype(BF16)
    fast_head(
        [phase(fast, p) for p in range(ALPHA)],
        shape, si, inside, lat_w, ft_band.at[0], fk_w, fb, zlat, zft, (z16, top, bottom), zfk, pay, 0,
    )
    send_sums(pay, top, bottom)


def lane(shape):
    return lax.broadcasted_iota(jnp.int32, shape, len(shape) - 1)


def kernel_prepare(gains, biases, fs_w, fe_w, gb, fs_bd, fe_bd):
    for i, source in enumerate((gains, biases)):
        for l in range(LAYERS):
            for r in range(22):
                gb[l, i, r : r + 1, :] = source[l : l + 1, r * LANES : (r + 1) * LANES]
            v = source[l : l + 1, 22 * LANES : 23 * LANES]
            v2 = source[l : l + 1, 23 * LANES : 24 * LANES]
            v3 = jnp.concatenate([source[l : l + 1, 24 * LANES :], jnp.zeros((1, 64), F32)], axis=1)
            place = lane((1, LANES))
            gb[l, i, FTM : FTM + 1, :] = fold_phases(jnp.where(place < 32, v, 0.0))
            gb[l, i, FSP : FSP + 1, :] = fold_phases(jnp.where((place >= 32) & (place < 64), v, 0.0))
            v, v2, v3 = (pltpu.roll(x, 64, 1) for x in (v, v2, v3))
            gb[l, i, FEX : FEX + 1, :] = jnp.where(place < 64, v, v2)
            gb[l, i, FSK : FSK + 1, :] = jnp.where(place < 64, v2, v3)
            gb[l, i, 26:32, :] = jnp.zeros((6, LANES), F32)
    row = lax.broadcasted_iota(jnp.int32, (LANES, LANES), 0)
    column = lane((LANES, LANES))
    same = (row // BF) == (column // BF)
    spread_columns = 0.0
    for p in range(ALPHA):
        spread_columns = spread_columns + place_columns(p).astype(F32)
    spread_columns = spread_columns.astype(BF16)
    for l in range(LAYERS):
        for a in range(3):
            for b in range(3):
                part = dot(fs_w[l, a, b], spread_columns).astype(BF16)
                fs_bd[l, a, b] = jnp.where(same, dot_tn(spread_columns, part), 0.0).astype(BF16)
        fe_bd[l] = jnp.zeros((LANES, ALPHA * DF), BF16)
        for p in range(ALPHA):
            fe_bd[l, p * BF : (p + 1) * BF, p * DF : (p + 1) * DF] = fe_w[l]


def kernel_temporal(first, shape, si, sf, *refs):
    t, h, w = shape
    rows, frame = t * h * w, h * w
    if first:
        (recv, slow, gb, zlat, zft, h1, h2, h3, h4, h5, st_w, sk_w, fs_bd,
         low_out, zst, z16, top, bottom, zsk, af9, zfs, pay, pad) = refs
        row = 0
        total = recv[...]
    else:
        (recv, gb_before, tot_sk, zse_in, zsk_in, gb, zlat, zft, h1, h2, h3, h4, h5, st_w, sk_w, fs_bd,
         low_out, zst, z16, top, bottom, zsk, af9, zfs, pay, pad) = refs
        row = 16
        total = recv[...]
        inside = inside_rows(rows, 256, si[0])
        one = Norm(total, 0, gb_before, SEX, 8, sf[0])
        two = Norm(tot_sk[...], 8, gb_before, SSK, 8, sf[0])
        for c in range(0, DS, 256):
            u = one.columns(c, 256).out(zse_in[:, c : c + 256]) + two.columns(c, 256).out(zsk_in[:, c : c + 256])
            low_out[:, c : c + 256] = jnp.where(inside, silu(u), 0.0).astype(BF16)
    inside = inside_rows(rows, 256, si[0])
    lat = Norm(total, row, gb, LAT, 2, sf[0])
    ft = Norm(fold_phases(total), row + 4, gb, FTM, 1, sf[1])
    if first:
        low_out[:, :DS] = slow[...].astype(BF16)
    low_out[:, DS:] = silu(lat.out(zlat[...])).astype(BF16)
    activate_padded(pad, shape, ft, zft[...], (h1, h2, h3, h4, h5), si, sf)
    low = low_out[...]
    z = dot(low, st_w[0, 1])
    z = z + down(dot(low, st_w[0, 0]), frame)
    z = z + up(dot(low, st_w[0, 2]), frame)
    zst[...] = z
    send_halo(z, shape, si, z16, top, bottom)
    one, two = moments(z, inside)
    put_rows(pay, 0, one)
    put_rows(pay, 2, two)
    for a in range(3):
        for b in range(3):
            k = 3 * a + b
            af9[:, k * LANES : (k + 1) * LANES] = tap(pad, shape, a, b)
    z = dot(af9[...], fs_bd[...].reshape(9 * LANES, LANES))
    zfs[...] = z
    one, two = moments(z, inside[:, :LANES])
    put_rows(pay, 4, one)
    put_rows(pay, 5, two)
    pay[6:8, :] = jnp.zeros((2, LANES), F32)
    for c in range(0, DS, 256):
        z = dot(low, sk_w[0, :, c : c + 256])
        zsk[:, c : c + 256] = z
        one, two = moments(z, inside)
        put_rows(pay, 8 + c // LANES, one)
        put_rows(pay, 16 + c // LANES, two)
    send_sums(pay, top, bottom)


def kernel_spatial(shape, si, sf, recv, gb, zst, h1, h2, h3, h4, h5, zfs, ss_w, fe_bd,
                   a9, zss, bf, zfe, pays, pay, pad):
    t, h, w = shape
    inside = inside_rows(t * h * w, 256, si[0])
    total = recv[...]
    st = Norm(total, 0, gb, STM, 2, sf[0])
    fs = Norm(fold_phases(total), 4, gb, FSP, 1, sf[1])
    activate_padded(pad, shape, st, zst[...], (h1, h2, h3, h4, h5), si, sf)
    for a in range(3):
        for b in range(3):
            k = 3 * a + b
            a9[:, k * BS : (k + 1) * BS] = tap(pad, shape, a, b)
    z = dot(a9[...], ss_w[...].reshape(9 * BS, BS))
    zss[...] = z
    one, two = moments(z, inside)
    put_rows(pay, 0, one)
    put_rows(pay, 2, two)
    low = silu(fs.out(zfs[...])).astype(BF16)
    bf[...] = low
    total, square = 0.0, 0.0
    for p in range(ALPHA):
        z = dot(low, fe_bd[:, p * DF : (p + 1) * DF])
        zfe[:, p * DF : (p + 1) * DF] = z
        one, two = moments(z, inside[:, :LANES])
        total, square = total + one, square + two
    put_rows(pay, 4, total)
    put_rows(pay, 5, square)
    pay[6:8, :] = jnp.zeros((2, LANES), F32)
    spread(pay, pays)


def kernel_expand(last, shape, si, sf, *refs):
    t, h, w = shape
    inside = inside_rows(t * h * w, 256, si[0])
    if last:
        recv, gb, zss, se_w, bt, zse, pays, tot_out, pay = refs
    else:
        (recv, gb, zss, se_w, tot_fk, zfe, zfk, lat_w, ft_band, fk_w,
         bt, zse, pay, tot_out, fb, zlat, zft, z16, top, bottom, zfk_out) = refs
    total = gathered(recv)
    tot_out[...] = total
    ss = Norm(total, 0, gb, SSP, 2, sf[0])
    low = silu(ss.out(zss[...])).astype(BF16)
    bt[...] = low
    for c in range(0, DS, 256):
        z = dot(low, se_w[0, :, c : c + 256])
        zse[:, c : c + 256] = z
        one, two = moments(z, inside)
        put_rows(pay, c // LANES, one)
        put_rows(pay, 8 + c // LANES, two)
    if not last:
        fe = Norm(total, 4, gb, FEX, 1, sf[1])
        fk = Norm(tot_fk[...], tot_fk.shape[0] - 2, gb, FSK, 1, sf[1])
        phases = []
        for p in range(ALPHA):
            cols = slice(p * DF, (p + 1) * DF)
            u = fe.out(zfe[:, cols]) + fk.out(zfk[:, cols])
            phases.append(jnp.where(inside[:, :LANES], silu(u), 0.0))
        fast_head(
            phases, shape, si, inside, lat_w, ft_band, fk_w, fb, zlat, zft, (z16, top, bottom), zfk_out, pay, 16
        )
        send_sums(pay, top, bottom)
    else:
        spread(pay, pays)


class Refs:
    def __init__(self, names, refs):
        self.__dict__.update(zip(names, refs))

    def layer(self, prefix):
        own = {k[len(prefix) :]: v for k, v in self.__dict__.items() if k.startswith(prefix)}
        return Refs(own.keys(), own.values())


def norms_of(L, sf, *names):
    def make(name):
        if name == "se":
            return Norm(L.tot_se[...], 0, L.gb, SEX, 8, sf[0])
        if name == "sk":
            return Norm(L.tot_sk[...], 8, L.gb, SSK, 8, sf[0])
        if name == "ss":
            return Norm(L.tot_ss[...], 0, L.gb, SSP, 2, sf[0])
        if name == "st":
            return Norm(L.tot_sk[...], 0, L.gb, STM, 2, sf[0])
        if name == "lat":
            return Norm(L.tot_lat[...], L.tot_lat.shape[0] - 8, L.gb, LAT, 2, sf[0])
        if name == "ft":
            return Norm(fold_phases(L.tot_lat[...]), L.tot_lat.shape[0] - 4, L.gb, FTM, 1, sf[1])
        if name == "fk":
            return Norm(L.tot_lat[...], L.tot_lat.shape[0] - 2, L.gb, FSK, 1, sf[1])
        if name == "fs":
            return Norm(fold_phases(L.tot_sk[...]), 4, L.gb, FSP, 1, sf[1])
        return Norm(L.tot_ss[...], 4, L.gb, FEX, 1, sf[1])

    return [make(name) for name in names]


def fill_rows(pay, start, end):
    pay[start:end, :] = jnp.zeros((end - start, LANES), F32)


def top_slow(L, inside, sf, grad, du_out, pay, row, out=None):
    se, sk = norms_of(L, sf, "se", "sk")
    for c in range(0, DS, 256):
        cols = slice(c, c + 256)
        one, two = se.columns(c, 256), sk.columns(c, 256)
        hat1, hat2 = one.hat(L.zse[:, cols]), two.hat(L.zsk[:, cols])
        u = one.gain * hat1 + one.bias + (two.gain * hat2 + two.bias)
        act, rate = silu_and_slope(u)
        if out is not None:
            out[:, cols] = jnp.where(inside, act, 0.0)
        du = jnp.where(inside, grad(cols) * rate, 0.0)
        du_out[:, cols] = du
        put_rows(pay, row + c // LANES, col_sum(du))
        put_rows(pay, row + 8 + c // LANES, col_sum(du * hat1))
        put_rows(pay, row + 16 + c // LANES, col_sum(du * hat2))


def top_fast(L, inside, sf, grad, du_out, pay, row, out=None):
    fe, fk = norms_of(L, sf, "fe", "fk")
    inside = inside[:, :LANES]
    sums = [0.0, 0.0, 0.0]
    for p in range(ALPHA):
        cols = slice(p * DF, (p + 1) * DF)
        hat1, hat2 = fe.hat(L.zfe[:, cols]), fk.hat(L.zfk[:, cols])
        u = fe.gain * hat1 + fe.bias + (fk.gain * hat2 + fk.bias)
        act, rate = silu_and_slope(u)
        if out is not None:
            out[:, p] = jnp.where(inside, act, 0.0).reshape(out.shape[0], out.shape[2], DF)
        du = jnp.where(inside, grad(p) * rate, 0.0)
        du_out[:, cols] = du
        sums = [sums[0] + col_sum(du), sums[1] + col_sum(du * hat1), sums[2] + col_sum(du * hat2)]
    for i in range(3):
        put_rows(pay, row + i, sums[i])


def expand_slow(L, inside, sf, total, row, du_in, se_w, dz_se, dz_sk, pay, out_row):
    se, sk, ss = norms_of(L, sf, "se", "sk", "ss")
    back = 0.0
    for c in range(0, DS, 256):
        cols = slice(c, c + 256)
        r = row + c // LANES
        du = du_in[:, cols]
        a_sum = wide(total, r, 2)
        one, two = se.columns(c, 256), sk.columns(c, 256)
        dz = one.back(du, one.hat(L.zse[:, cols]), inside, a_sum, wide(total, 8 + r, 2), sf[0]).astype(BF16)
        dz_se[:, cols] = dz
        back = back + dot_nt(dz, se_w[0, :, cols])
        dz = two.back(du, two.hat(L.zsk[:, cols]), inside, a_sum, wide(total, 16 + r, 2), sf[0])
        dz_sk[:, cols] = dz.astype(BF16)
    z = L.zss[...]
    dy = back * slope(ss.out(z))
    put_rows(pay, out_row, col_sum(dy))
    put_rows(pay, out_row + 2, col_sum(dy * ss.hat(z)))
    return dy, z


def expand_fast(L, inside, sf, total, row, du_in, fe_bd, dz_fe, dz_fk, pay, out_row):
    fe, fk, fs = norms_of(L, sf, "fe", "fk", "fs")
    inside = inside[:, :LANES]
    back = 0.0
    a_sum = wide(total, row, 1)
    for p in range(ALPHA):
        cols = slice(p * DF, (p + 1) * DF)
        du = du_in[:, cols]
        dz = fe.back(du, fe.hat(L.zfe[:, cols]), inside, a_sum, wide(total, row + 1, 1), sf[1]).astype(BF16)
        dz_fe[:, cols] = dz
        back = back + dot_nt(dz, fe_bd[:, cols])
        dz = fk.back(du, fk.hat(L.zfk[:, cols]), inside, a_sum, wide(total, row + 2, 1), sf[1])
        dz_fk[:, cols] = dz.astype(BF16)
    z = L.zfs[...]
    dy = back * slope(fs.out(z))
    put_rows(pay, out_row, col_sum(dy))
    put_rows(pay, out_row + 1, col_sum(dy * fs.hat(z)))
    return dy, z


def pack_halo(pairs, shape, si, dy_out, halo_out):
    dy = jnp.concatenate([one for one, _ in pairs], axis=1) if len(pairs) > 1 else pairs[0][0]
    dy_out[...] = dy
    send_halo(jnp.concatenate([dy] + [z for _, z in pairs], axis=1), shape, si, *halo_out)


def spatial_gradient(parts, shape, si, sf, dy_in, halo_refs, pad, dz_out):
    t, h, w = shape
    width = dy_in.shape[1]

    def dz(dy, z, frame):
        inside = inside_rows(dy.shape[0], width, si[0] // (h * w) * frame)
        pieces, column = [], 0
        for norm, _, a_sum, b_sum, inv in parts:
            cols = slice(column, column + norm.mean.shape[1])
            pieces.append(norm.back(dy[:, cols], norm.hat(z[:, cols]), inside[:, cols], a_sum, b_sum, inv))
            column = cols.stop
        value = jnp.concatenate(pieces, axis=1) if len(pieces) > 1 else pieces[0]
        return value.astype(BF16)

    def arrived(value, frame):
        return dz(value[:, :width], value[:, width:], frame).astype(F32)

    z = jnp.concatenate([part[1] for part in parts], axis=1) if len(parts) > 1 else parts[0][1]
    own = dz(dy_in[...], z, h * w)
    dz_out[...] = own
    above, below, o_above, o_own, o_below = (
        arrived(x, h * w if i == 3 else w) for i, x in enumerate(halo_values(si, t * w, halo_refs))
    )
    others = (o_above * sf[2], o_own, o_below * sf[3])
    fill_padded(pad, shape, own.astype(F32), above * sf[2], below * sf[3], others, sf[4], sf[5])


def spatial_part(norm, z, total, row, columns, inv):
    count = columns // LANES
    if columns == LANES:
        total = fold_phases(total)
    return norm, z, wide(total, row, count), wide(total, row + count, count), inv


def spatial_back(pad, shape, slow_w, fast_w):
    back, back_f = 0.0, 0.0
    for a in range(3):
        for b in range(3):
            part = tap(pad, shape, 2 - a, 2 - b)
            if slow_w is not None:
                back = back + dot_nt(part[:, :BS], slow_w[0, a, b])
            if fast_w is not None:
                back_f = back_f + dot_nt(part[:, part.shape[1] - LANES :], fast_w[a, b])
    return back, back_f


def finish_spatial(norm, z, back, dy_out, pay, row):
    dy = back * slope(norm.out(z))
    dy_out[...] = dy
    put_rows(pay, row, col_sum(dy))
    put_rows(pay, row + dy.shape[1] // LANES, col_sum(dy * norm.hat(z)))


def temporal_slow(L, frame, inside, sf, total, row, dy_in, dlow, st_w, dz_st, dy_lat, pay, out_row):
    st, lat = norms_of(L, sf, "st", "lat")
    dz = st.back(
        dy_in[...], st.hat(L.zst[...]), inside, wide(total, row, 2), wide(total, row + 2, 2), sf[0]
    ).astype(BF16)
    dz_st[:, :BS] = up(dz, frame)
    dz_st[:, BS : 2 * BS] = dz
    dz_st[:, 2 * BS :] = down(dz, frame)

    def back(cols):
        part = dlow[:, cols]
        for j in range(3):
            part = part + dot_nt(dz_st[:, j * BS : (j + 1) * BS], st_w[0, j, cols, :])
        return part

    z = L.zlat[...]
    dy = back(slice(DS, CC)) * slope(lat.out(z))
    dy_lat[...] = dy
    put_rows(pay, out_row, col_sum(dy))
    put_rows(pay, out_row + 2, col_sum(dy * lat.hat(z)))
    return back


def temporal_fast(L, frame, inside, sf, total, row, dy_in, dz_ft, dz_fk, fk_w, ft_band):
    (ft,) = norms_of(L, sf, "ft")
    folded = fold_phases(total)
    dz = ft.back(
        dy_in[...], ft.hat(L.zft[...]), inside[:, :LANES], wide(folded, row, 1), wide(folded, row + 1, 1), sf[1]
    ).astype(BF16)
    dz_ft[...] = dz

    def grad(p):
        part = dot_nt(dz_fk[:, p * DF : (p + 1) * DF], fk_w[0]) + dot_nt(dz, ft_band[p + 1])
        if p == ALPHA - 1:
            part = part + up(dot_nt(dz, ft_band[0]), frame)
        if p == 0:
            part = part + down(dot_nt(dz, ft_band[5]), frame)
        return part

    return grad


def lateral_back(L, frame, inside, sf, total, row, dy_in, lat_w, dz_lat, grad):
    (lat,) = norms_of(L, sf, "lat")
    dz = lat.back(
        dy_in[...], lat.hat(L.zlat[...]), inside, wide(total, row, 2), wide(total, row + 2, 2), sf[0]
    ).astype(BF16)
    dz_lat[...] = dz

    def whole(p):
        part = grad(p)
        if p < 3:
            part = part + dot_nt(dz, lat_w[0, p + 2])
        if p >= 2:
            part = part + up(dot_nt(dz, lat_w[0, p - 2]), frame)
        return part

    return whole


def back_turn(shape, R, inside, si, sf):
    L = R.layer("a_")
    L.tot_se = R.tot
    R.tot[...] = gathered(R.recv)
    top_slow(L, inside, sf, lambda cols: R.slow_cot[:, cols], R.du_s, R.pay, 0, R.out_slow)
    top_fast(L, inside, sf, lambda p: phase(R.fast_cot, p), R.du_f, R.pay, 24, R.out_fast)
    fill_rows(R.pay, 27, 32)


def back_expand(shape, R, inside, si, sf):
    L = R.layer("a_")
    total = R.recv[...]
    slow = expand_slow(L, inside, sf, total, 0, R.du_s, R.se_w, R.dz_se, R.dz_sk, R.pay, 0)
    fast = expand_fast(L, inside, sf, total, 24, R.du_f, R.fe_bd, R.dz_fe, R.dz_fk, R.pay, 4)
    fill_rows(R.pay, 6, 8)
    pack_halo([slow, fast], shape, si, R.dy, (R.whole, R.top, R.bottom))
    send_sums(R.pay, R.top, R.bottom)


def back_spatial(shape, R, inside, si, sf):
    L = R.layer("a_")
    total = R.recv[...]
    ss, fs, st, ft = norms_of(L, sf, "ss", "fs", "st", "ft")
    parts = [
        spatial_part(ss, L.zss[...], total, 0, BS, sf[0]),
        spatial_part(fs, L.zfs[...], total, 4, LANES, sf[1]),
    ]
    spatial_gradient(parts, shape, si, sf, R.dy, (R.h0, R.h1, R.h2, R.h3, R.h4), R.pad, R.dz)
    back, back_f = spatial_back(R.pad, shape, R.ss_w, R.fs_bd)
    finish_spatial(st, L.zst[...], back, R.dy_st, R.pay, 0)
    finish_spatial(ft, L.zft[...], back_f, R.dy_ft, R.pay, 4)
    fill_rows(R.pay, 6, 8)


def back_temporal(shape, R, inside, si, sf):
    L, below = R.layer("a_"), R.layer("b_")
    frame = shape[1] * shape[2]
    total = R.recv[...]
    back = temporal_slow(L, frame, inside, sf, total, 0, R.dy_st, R.dlow, R.st_w, R.dz_st, R.dy_lat, R.pay, 0)
    top_slow(below, inside, sf, back, R.du_s, R.pay, 8)
    fill_rows(R.pay, 4, 8)
    grad = temporal_fast(L, frame, inside, sf, total, 4, R.dy_ft, R.dz_ft, R.dz_fk, R.fk_w, R.ft_band)
    for p in range(ALPHA):
        R.dfast[:, p * DF : (p + 1) * DF] = grad(p)


def back_lateral(shape, R, inside, si, sf):
    L, below = R.layer("a_"), R.layer("b_")
    frame = shape[1] * shape[2]
    total = R.recv[...]
    slow = expand_slow(below, inside, sf, total, 8, R.du_s, R.se_w, R.dz_se, R.dz_sk, R.pay, 0)
    pack_halo([slow], shape, si, R.dy, (R.whole, R.top, R.bottom))
    grad = lateral_back(
        L, frame, inside, sf, total, 0, R.dy_lat, R.lat_w, R.dz_lat, lambda p: R.dfast[:, p * DF : (p + 1) * DF]
    )
    top_fast(below, inside, sf, grad, R.du_f, R.pay, 4)
    fill_rows(R.pay, 7, 8)
    send_sums(R.pay, R.top, R.bottom)


def back_low_spatial(shape, R, inside, si, sf):
    L = R.layer("b_")
    total = R.recv[...]
    fast = expand_fast(L, inside, sf, total, 4, R.du_f, R.fe_bd, R.dz_fe, R.dz_fk, R.pay, 4)
    pack_halo([fast], shape, si, R.dy_fs, (R.whole, R.top, R.bottom))
    ss, st = norms_of(L, sf, "ss", "st")
    parts = [spatial_part(ss, L.zss[...], total, 0, BS, sf[0])]
    spatial_gradient(parts, shape, si, sf, R.dy, (R.h0, R.h1, R.h2, R.h3, R.h4), R.pad, R.dz)
    back, _ = spatial_back(R.pad, shape, R.ss_w, None)
    finish_spatial(st, L.zst[...], back, R.dy_st, R.pay, 0)
    fill_rows(R.pay, 6, 8)
    send_sums(R.pay, R.top, R.bottom)


def back_low_temporal(shape, R, inside, si, sf):
    L = R.layer("b_")
    frame = shape[1] * shape[2]
    total = R.recv[...]
    fs, ft = norms_of(L, sf, "fs", "ft")
    parts = [spatial_part(fs, L.zfs[...], total, 4, LANES, sf[1])]
    spatial_gradient(parts, shape, si, sf, R.dy_fs, (R.h0, R.h1, R.h2, R.h3, R.h4), R.pad, R.dz_f)
    _, back_f = spatial_back(R.pad, shape, None, R.fs_bd)
    finish_spatial(ft, L.zft[...], back_f, R.dy_ft, R.pay, 4)
    temporal_slow(L, frame, inside, sf, total, 0, R.dy_st, R.dlow, R.st_w, R.dz_st, R.dy_lat, R.pay, 0)
    fill_rows(R.pay, 6, 8)


def kernel_low_input(dz_st, dlow, st_w, dslow):
    for c in range(0, DS, 256):
        cols = slice(c, c + 256)
        part = dlow[:, cols]
        for j in range(3):
            part = part + dot_nt(dz_st[:, j * BS : (j + 1) * BS], st_w[0, j, cols, :])
        dslow[:, cols] = part


def back_low_lateral(shape, R, inside, si, sf):
    L = R.layer("b_")
    lat, ft = norms_of(L, sf, "lat", "ft")
    total = R.recv[...]
    folded = fold_phases(total)
    R.dz_lat[...] = lat.back(
        R.dy_lat[...], lat.hat(L.zlat[...]), inside, wide(total, 0, 2), wide(total, 2, 2), sf[0]
    ).astype(BF16)
    R.dz_ft[...] = ft.back(
        R.dy_ft[...], ft.hat(L.zft[...]), inside[:, :LANES], wide(folded, 4, 1), wide(folded, 5, 1), sf[1]
    ).astype(BF16)


def kernel_low_fast_input(frame, dz_lat, dz_ft, dz_fk, lat_w, fk_w, ft_band, dfast):
    for p in range(ALPHA):
        part = dot_nt(dz_fk[:, p * DF : (p + 1) * DF], fk_w[0]) + dot_nt(dz_ft[...], ft_band[p + 1])
        if p == ALPHA - 1:
            part = part + up(dot_nt(dz_ft[...], ft_band[0]), frame)
        if p == 0:
            part = part + down(dot_nt(dz_ft[...], ft_band[5]), frame)
        if p < 3:
            part = part + dot_nt(dz_lat[...], lat_w[0, p + 2])
        if p >= 2:
            part = part + up(dot_nt(dz_lat[...], lat_w[0, p - 2]), frame)
        dfast[:, p] = part.reshape(dfast.shape[0], frame, DF)


def kernel_back_skip(dz_sk, sk_w, dlow):
    for k in range(0, CC, 256):
        dlow[:, k : k + 256] = dot_nt(dz_sk[...], sk_w[0, k : k + 256, :])


def part_tiles(si, tiles, ref, keep, send):
    side = si[2]
    for i in range(tiles // 2):
        keep[i] = ref[2 * i + side]
        send[i] = ref[2 * i + 1 - side]


def pick_phases(parts):
    place = lane(parts[0].shape) // BF
    return fold_phases(sum(jnp.where(place == p, part, 0.0) for p, part in enumerate(parts)))


SMALL_ROWS = 64
ROW_JOBS = {"pl": 4, "st": 2, "ss": 2, "lat": 2, "sm": 7}


def job_rows(job, tiles):
    rows = {"pl": 4 * (CC + BS), "st": 3 * CC, "ss": 9 * BS, "lat": 5 * DF, "sm": SMALL_ROWS * tiles}
    return rows[job] // tiles


def bundle_rows(jobs, tiles):
    planes = job_rows("pl", tiles) if "pl" in jobs else 0
    small = SMALL_ROWS if "sm" in jobs else 0
    rows = sum(job_rows(job, tiles) for job in jobs if job not in ("pl", "sm"))
    return planes + -(-rows // 32) * 32 + small, planes, small


def share_rows(jobs, tiles):
    count, planes, small = bundle_rows(jobs, tiles)
    return planes // 2 + (count - planes - small) // 2 + 2 * small


def kernel_weights_rows(tiles, frame, jobs, si, *refs):
    kst, kss, kla, ksm = CC // tiles, BS // tiles, DF // tiles, BF // tiles
    count = sum(ROW_JOBS[job] for job in jobs)
    keep, send, blocks, small = refs[count:]
    rows, _, small_rows = bundle_rows(jobs, tiles)
    base = 0
    operands = list(refs[:count])
    for job in jobs:
        own = [operands.pop(0) for _ in range(ROW_JOBS[job])]
        if job == "pl":
            low, bt, dz_sk, dz_se = own
            ksk, kse = kst, kss
            for j in range(4):
                cols, start = slice(j * 256, (j + 1) * 256), base + j * (ksk + kse)
                d = dot_tn(low[...], dz_sk[:, cols]).astype(BF16)
                blocks[:, start : start + ksk, :] = d.reshape(tiles, ksk, 256)
                d = dot_tn(bt[...], dz_se[:, cols]).astype(BF16)
                blocks[:, start + ksk : start + ksk + kse, :] = d.reshape(tiles, kse, 256)
        elif job == "st":
            low, dz = own
            for j in range(3):
                d = dot_tn(low[...], dz[:, j * BS : (j + 1) * BS]).astype(BF16)
                blocks[:, base + j * kst : base + (j + 1) * kst, :] = d.reshape(tiles, kst, BS)
        elif job == "ss":
            a9, dz = own
            for k in range(9):
                d = dot_tn(a9[:, k * BS : (k + 1) * BS], dz[:, :BS]).astype(BF16)
                blocks[:, base + k * kss : base + (k + 1) * kss, :] = d.reshape(tiles, kss, BS)
        elif job == "lat":
            fb, dz = own
            f = [fb[:, p * DF : (p + 1) * DF] for p in range(3)] + [fb[:, 3 * DF :]]
            for k, x in enumerate([down(f[2], frame), down(f[3], frame), f[0], f[1], f[2]]):
                d = dot_tn(x, dz[...]).astype(BF16)
                blocks[:, base + k * kla : base + (k + 1) * kla, :] = d.reshape(tiles, kla, DL)
        else:
            af9, fb, bf, dz_f, dz_ft, dz_fe, dz_fk = own
            small[...] = jnp.zeros(small.shape, F32)
            last = dz_f.shape[1] - LANES
            for k in range(9):
                d = dot_tn(af9[:, k * LANES : (k + 1) * LANES], dz_f[:, last:])
                d = pick_phases([d[p * BF : (p + 1) * BF] for p in range(ALPHA)])
                for i in range(tiles):
                    small[i, k * ksm : (k + 1) * ksm, LANES:] = d[i * ksm : (i + 1) * ksm]
            f = [fb[:, p * DF : (p + 1) * DF] for p in range(ALPHA)]
            six = [dot_tn(x, dz_ft[...]) for x in [down(f[3], frame)] + f + [up(f[0], frame)]]
            for k in range(3):
                d = pick_phases([six[k + p] for p in range(ALPHA)])
                small[:, k * kla : (k + 1) * kla, :LANES] = d.reshape(tiles, kla, LANES)
            fe, fk = 0.0, 0.0
            for p in range(ALPHA):
                cols = slice(p * DF, (p + 1) * DF)
                fk = fk + dot_tn(fb[:, cols], dz_fk[:, cols])
                fe = fe + dot_tn(bf[...], dz_fe[:, cols])[p * BF : (p + 1) * BF, :]
            for i in range(tiles):
                small[i, 9 * ksm : 10 * ksm, LANES:] = fe[i * ksm : (i + 1) * ksm]
                small[i, 10 * ksm : 10 * ksm + kla, LANES:] = fk[i * kla : (i + 1) * kla]
            blocks[:, rows - small_rows :, :] = small[...].astype(BF16)
            continue
        base += job_rows(job, tiles)
    if rows - small_rows > base:
        blocks[:, base : rows - small_rows, :] = jnp.zeros((tiles, rows - small_rows - base, 256), BF16)
    part_tiles(si, tiles, blocks, keep, send)


def add(one, two):
    return (one.astype(F32) + two.astype(F32)).astype(BF16)


def kernel_halve_first(split, si, kept, got, keep_a, send_a, keep_b, send_b):
    low, high = si[1] % 2, si[1] // 2
    for i in range(2):
        for ref, side in ((keep_a, low), (send_a, 1 - low)):
            place = 2 * i + side
            ref[i] = add(kept[place, :split], got[place, :split])
        for ref, side in ((keep_b, high), (send_b, 1 - high)):
            place = 2 * side + i
            ref[i] = add(kept[place, split:], got[place, split:])


def kernel_halve_second(si, kept_a, got_a, kept_b, got_b, keep_a, send_a, keep_b, send_b):
    low, high = si[1] % 2, si[1] // 2
    for ref, place in ((keep_a, high), (send_a, 1 - high)):
        ref[...] = add(kept_a[place], got_a[place])
    for ref, place in ((keep_b, low), (send_b, 1 - low)):
        ref[...] = add(kept_b[place], got_b[place])


def kernel_halve_last(si, kept, got, keep, send):
    bit = si[3] // 2
    for ref, place in ((keep, bit), (send, 1 - bit)):
        ref[...] = add(kept[place], got[place])


def kernel_pick_places(si, kept, got, *outs):
    for i, ref in enumerate(outs):
        place = si[1] ^ i
        ref[...] = add(kept[place], got[place])


def whole_sum(parts):
    total = parts[0][...].astype(F32)
    for part in parts[1:]:
        total = total + part[...].astype(F32)
    return total


def columns_of(x, j):
    half = x.shape[0] // 2
    base = (j // 2) * LANES
    a, b = x[:half, base : base + LANES], x[half:, base : base + LANES]
    left = lane(a.shape) < 64
    if j % 2 == 0:
        return jnp.where(left, a, pltpu.roll(b, 64, 1))
    return jnp.where(left, pltpu.roll(a, 64, 1), b)


def column_blocks(jobs, tiles, total, blocks):
    count, planes, small_rows = bundle_rows(jobs, tiles)
    big = count - small_rows
    packed = (big - planes) // 2
    each = planes // 4
    for j in range(4):
        if planes:
            plane = total[j * each : (j + 1) * each].astype(BF16)
            blocks[j, :each, :] = plane[:, :LANES]
            blocks[j, each : 2 * each, :] = plane[:, LANES:]
        base = 2 * each
        if packed:
            blocks[j, base : base + packed, :] = columns_of(total[planes:big], j).astype(BF16)
        base += packed
        if small_rows:
            small = total[big:].astype(BF16)
            blocks[j, base : base + small_rows, :] = small[:, :LANES]
            blocks[j, base + small_rows :, :] = small[:, LANES:]


def kernel_pick_columns(jobs, tiles, si, a, b, c, d, out0, out1, out2, out3, blocks):
    column_blocks(jobs, tiles, whole_sum((a, b, c, d)), blocks)
    for i, ref in enumerate((out0, out1, out2, out3)):
        ref[...] = blocks[si[3] ^ i]


def kernel_join_columns(jobs, tiles, si, kept_a, got_a, kept_b, got_b, keep, send, blocks):
    total = jnp.concatenate([whole_sum((kept_a, got_a)), whole_sum((kept_b, got_b))], axis=0)
    column_blocks(jobs, tiles, total, blocks)
    bit = si[3] % 2
    for ref, side in ((keep, bit), (send, 1 - bit)):
        for i in range(2):
            ref[i] = blocks[2 * i + side]


def kernel_finish(tiles, plan, si, *refs):
    kst, kss, kla, ksm = CC // tiles, BS // tiles, DF // tiles, BF // tiles
    refs = list(refs)
    g_lat, g_st, g_ss, g_se, g_sk, g_ft, g_fs, g_fe, g_fk = refs[-9:]
    for jobs, layers, count in plan:
        total, refs = whole_sum(refs[:count]), refs[count:]
        rows, planes, small_rows = bundle_rows(jobs, tiles)
        start = planes // 2
        if planes:
            plane = jnp.concatenate([total[: start // 2], total[start // 2 : start]], axis=1)
            g_sk[layers[0]] = plane[:kst]
            g_se[layers[0]] = plane[kst:]
        packed = (rows - planes - small_rows) // 2
        big = total[start : start + packed]
        rows = [big[:, :64], pltpu.roll(big, 64, 1)[:, :64]] if packed else []
        tail = total[start + packed :]

        def part(start, size):
            end = start + size
            if end <= packed:
                return rows[0][start:end]
            if start >= packed:
                return rows[1][start - packed : end - packed]
            return jnp.concatenate([rows[0][start:], rows[1][: end - packed]], axis=0)

        base = 0
        for job, l in zip(jobs, layers):
            if job == "pl":
                continue
            if job == "st":
                for k in range(3):
                    g_st[l, k] = part(base + k * kst, kst).T
            elif job == "ss":
                for k in range(9):
                    g_ss[l, k // 3, k % 3] = part(base + k * kss, kss)
            elif job == "lat":
                for k in range(5):
                    g_lat[l, k] = part(base + k * kla, kla)
            else:
                small = tail[:SMALL_ROWS]
                eight = pltpu.roll(small, (LANES - 8 * si[3]) % LANES, 1)[:, :8]
                for k in range(3):
                    g_ft[l, k] = eight[k * kla : (k + 1) * kla].T
                small = tail[SMALL_ROWS:]
                eight = pltpu.roll(small, (LANES - 8 * si[3]) % LANES, 1)[:, :8]
                for k in range(9):
                    g_fs[l, k // 3, k % 3] = eight[k * ksm : (k + 1) * ksm]
                part32 = pltpu.roll(small, (LANES - 32 * si[3]) % LANES, 1)[:, :32]
                g_fe[l] = part32[9 * ksm : 10 * ksm]
                g_fk[l] = part32[10 * ksm : 10 * ksm + kla]
                continue
            base += job_rows(job, tiles)


def kernel_norm_sums(places, *refs):
    d_gains, d_biases = refs[-2:]
    for l in range(LAYERS):
        for i, out in ((0, d_biases), (1, d_gains)):
            column = 0
            for n, row, second, count in places[l][:5]:
                row += i * second
                for r in range(row, row + count):
                    out[l : l + 1, column : column + LANES] = refs[n][r : r + 1, :]
                    column += LANES
            ft, fs, fe, fk = (
                refs[n][row + i * second : row + i * second + 1, :] for n, row, second, _ in places[l][5:]
            )
            ft, fs = fold_phases(ft), fold_phases(fs)
            fe, fk = pltpu.roll(fe, 64, 1), pltpu.roll(fk, 64, 1)
            place = lane((1, LANES))
            out[l : l + 1, column : column + LANES] = jnp.where(place < 32, ft, jnp.where(place < 64, fs, fe))
            out[l : l + 1, column + LANES : column + 2 * LANES] = jnp.where(place < 64, fe, fk)
            out[l : l + 1, column + 2 * LANES :] = fk[:, :64]


SMEM = pltpu.MemorySpace.SMEM
VMEM = pltpu.MemorySpace.VMEM


class Weight:
    def __init__(self, array, layer):
        self.array = array
        self.layer = layer


class Layer:
    def __init__(self, array, layer):
        self.array = array
        self.layer = layer


class Ready:
    def __init__(self, array):
        self.array = array


class Load:
    def __init__(self, array):
        self.array = array


class Arriving:
    def __init__(self, copy, ref, layered):
        self.copy = copy
        self.ref = ref
        self.layered = layered
        self.shape = ref.shape

    def __getitem__(self, place):
        if self.copy is not None:
            self.copy.wait()
            self.copy = None
        if not self.layered:
            return self.ref[place]
        return self.ref[place[1:]] if isinstance(place, tuple) else self.ref[...]


class Out:
    def __init__(self, shape, kind, spare=0):
        self.shape = shape
        self.kind = kind
        self.spare = spare


def scalar_values(place, valid, frame, tiles):
    ha, wa, clip = place[0], place[1], place[2]
    total = valid[0]
    for i in range(1, valid.shape[0]):
        total = total + valid[i]
    count = jnp.full((1, LANES), total * (HT * WD), jnp.int32).astype(F32)
    inverse = 1.0 / count
    flags = [ha > 0, ha < tiles[0] - 1, wa > 0, wa < tiles[1] - 1]
    vectors = [jnp.where(jnp.full((1, LANES), jnp.where(f, 1, 0), jnp.int32) > 0, 1.0, 0.0) for f in flags]
    vectors = [inverse, inverse * (1.0 / ALPHA)] + vectors
    return (valid[clip] * frame, ha, wa, clip), [v[:, :1] for v in vectors]


def call(body, scalars, operands, outs, scratch=(), limit=16, pinned=False, ahead=()):
    mode, scalars = (None, ()) if not scalars else (scalars[0], scalars[1:3])
    operands = list(operands) + list(ahead)
    count, first = len(operands), len(scalars)
    kept = len(outs)
    outs = list(outs) + [(x.array.shape[1:], x.array.dtype) for x in ahead]
    weights = [i for i, x in enumerate(operands) if isinstance(x, (Weight, Load))]
    results = [i for i, x in enumerate(outs) if isinstance(x, Out)]
    arrays = [x.array if isinstance(x, (Weight, Layer, Load, Ready)) else x for x in operands]
    if pinned:
        for i in weights:
            arrays[i] = pltpu.with_memory_space_constraint(arrays[i], pltpu.HBM)
    layered = [isinstance(x, Weight) for x in operands]
    shapes = [(x.shape, x.kind) if isinstance(x, Out) else x for x in outs]
    inward = weights[: len(weights) - len(ahead)]
    buffers = [pltpu.VMEM(arrays[i].shape[1:] if layered[i] else arrays[i].shape, arrays[i].dtype) for i in inward]
    buffers += [pltpu.VMEM((outs[i].shape[0] + outs[i].spare,) + outs[i].shape[1:], outs[i].kind) for i in results]
    own = first + count + len(outs)
    copies = len(buffers) + len(ahead)

    def wrapped(*refs):
        refs = list(refs)
        inner, rest = refs[own : own + len(buffers)], refs[own + len(buffers) :]
        arriving, leaving = [], []
        for n, i in enumerate(inward):
            source = refs[first + i].at[operands[i].layer] if layered[i] else refs[first + i]
            copy = pltpu.make_async_copy(source, inner[n], rest[-1].at[n])
            copy.start()
            refs[first + i] = Arriving(copy, inner[n], layered[i])
            arriving.append(refs[first + i])
        for i, x in enumerate(operands):
            if isinstance(x, Layer):
                refs[first + i] = refs[first + i].at[x.layer]
            if isinstance(x, Ready):
                refs[first + i] = Arriving(None, refs[first + i], True)
        later = []
        for n, x in enumerate(ahead):
            source = refs[first + count - len(ahead) + n].at[x.layer]
            later.append(pltpu.make_async_copy(source, refs[first + count + kept + n], rest[-1].at[len(buffers) + n]))
            later[-1].start()
        for n, i in enumerate(results):
            n += len(inward)
            whole = inner[n].at[pl.ds(0, outs[i].shape[0])] if outs[i].spare else inner[n]
            leaving.append(pltpu.make_async_copy(whole, refs[first + count + i], rest[-1].at[n]))
            refs[first + count + i] = inner[n]
        given = ()
        if mode is not None:
            t_frame, tiles = mode[1], mode[2]
            ints, vectors = scalar_values(refs[0], refs[1], t_frame, tiles) if mode[0] == "all" else (
                (None, refs[0][0], refs[0][1], refs[0][2]), None)
            given = (ints, vectors) if mode[0] == "all" else (ints,)
        given_refs = refs[first : first + count - len(ahead)] + refs[first + count : first + count + kept]
        body(*given, *given_refs, *(rest[:-1] if copies else rest))
        for copy in leaving:
            copy.start()
        for one in arriving:
            if one.copy is not None:
                one.copy.wait()
        for copy in leaving + later:
            copy.wait()

    def space(i, some):
        return pl.BlockSpec(memory_space=pltpu.HBM if i in some else VMEM)

    return pl.pallas_call(
        wrapped,
        out_shape=[jax.ShapeDtypeStruct(shape, kind) for shape, kind in shapes],
        in_specs=[pl.BlockSpec(memory_space=SMEM) for _ in scalars] + [space(i, weights) for i in range(count)],
        out_specs=[space(i, results) for i in range(len(outs))],
        scratch_shapes=buffers
        + [pltpu.VMEM(shape, kind) for shape, kind in scratch]
        + ([pltpu.SemaphoreType.DMA((copies,))] if copies else []),
        cost_estimate=pl.CostEstimate(flops=3000000000, bytes_accessed=6000000, transcendentals=0),
        compiler_params=pltpu.CompilerParams(vmem_limit_bytes=limit << 20),
    )(*scalars, *arrays)


def sum_over(x, axis):
    step, count = 1, lax.axis_size(axis)
    while step < count:
        pair = x + flip(x, axis, step)
        if 4 * step <= count:
            pair = pair + (flip(x, axis, 2 * step) + flip(x, axis, 3 * step))
            step *= 2
        x = pair
        step *= 2
    return x


def sum_all(x):
    for axis in (WA, HA, CLIP):
        x = sum_over(x, axis)
    return x


def exchange(block):
    return lax.all_to_all(block, ALL_AXES, 0, 0)


def swap(x):
    return lax.ppermute(x, WA, [(0, 1), (1, 0)])


def halo(z, top, bottom):
    count = lax.axis_size(HA)
    above = lax.ppermute(bottom, HA, [(i, i + 1) for i in range(count - 1)])
    below = lax.ppermute(top, HA, [(i + 1, i) for i in range(count - 1)])
    return [above, below, swap(z), swap(above), swap(below)]


def sum_with_halo(x, one, two, z):
    n = x.shape[0]
    one, two, across = flip(one, HA, 1), flip(two, HA, 3), flip(x, HA, 2)
    both = x + across
    o_one, o_two, o_both = swap(one), swap(two), swap(both)
    total = (both + (one[:n] + two[:n])) + (o_both + (o_one[:n] + o_two[:n]))
    return total, [one, two, swap(z), o_one, o_two]


def after(first, *rest):
    return lax.optimization_barrier((first,) + rest)


def flip(x, axis, step):
    return lax.ppermute(x, axis, [(i, i ^ step) for i in range(lax.axis_size(axis))])


ORDERS = ((WA, HA, CLIP), (WA, HA, CLIP), (WA, CLIP, HA), (WA, HA, CLIP), (WA, CLIP, HA), (WA, HA, CLIP), (WA, CLIP, HA))
LAUNCH = {(1, 'wa'): ('A1',), (3, 'wa'): ('ST1',), (5, 'wa'): ('A0',), (3, 'ha'): ('A1',), (5, 'ha'): ('ST1',), (6, 'ha'): ('A0',)}
LAND = {(1, 'clip'): ('A1',), (2, 'ha'): ('A1',), (3, 'clip'): ('ST1',), (4, 'ha'): ('A1', 'ST1'), (5, 'clip'): ('A1', 'A0'), (6, 'ha'): ('ST1',)}
BUNDLES = {1: [('A1', False, [('pl', 1)])], 3: [('ST1', False, [('ss', 1), ('st', 1)])], 5: [('A0', False, [('pl', 0), ('ss', 0), ('lat', 1), ('sm', 1)])], 7: [('L0', True, [('st', 0), ('lat', 0), ('sm', 0)])]}
WAIT = {(5, CLIP, "A0"), (2, HA, "A1"), (6, HA, "ST1"), (4, HA, "ST1")}


def local(
    slow_in,
    fast_in,
    valid_frames,
    lateral_w,
    slow_temporal_w,
    slow_spatial_w,
    slow_expand_w,
    slow_skip_w,
    fast_temporal_w,
    fast_spatial_w,
    fast_expand_w,
    fast_skip_w,
    gains,
    biases,
    slow_cot,
    fast_cot,
):
    devices = lax.axis_size(ALL_AXES)
    clips, n_ha, n_wa = (lax.axis_size(a) for a in ALL_AXES)
    tiles = n_ha * n_wa
    _, t, h, w, _ = slow_in.shape
    shape = (t, h, w)
    frame = h * w
    rows = t * frame

    place = jnp.stack([lax.axis_index(a) for a in (HA, WA, CLIP)]).astype(jnp.int32)
    scalars = (("all", frame, (n_ha, n_wa)), place, valid_frames)
    places = (("place", frame, (n_ha, n_wa)), place, valid_frames)

    slow2 = slow_in.reshape(rows, DS)
    fast4 = fast_in.reshape(t, ALPHA, frame, DF)
    slow_cot2 = slow_cot.reshape(rows, DS)
    fast_cot4 = fast_cot.reshape(t, ALPHA, frame, DF)

    def act(columns, kind=F32):
        return ((rows, columns), kind)

    def edges(columns, sums=None):
        if sums is None:
            return [act(columns, BF16), ((t * w, columns), BF16), ((t * w, columns), BF16)]
        return [act(columns, BF16)] + [((sums + t * w * columns // LANES, LANES), F32)] * 2

    def pay(count):
        return ((count, LANES), F32)

    def bind(body, *static):
        return functools.partial(body, *static)

    pad_slow = ((t, h + 2, 3 * w, BS), F32)
    pad_fast = ((t, h + 2, 3 * w, LANES), F32)
    pad_both = ((t, h + 2, 3 * w, BS + LANES), F32)
    saved = []
    fb, zlat, zft, z16, top, bottom, zfk, sent, band = call(
        bind(kernel_start, shape),
        scalars,
        [Load(fast4), Weight(lateral_w, 0), Load(jnp.swapaxes(fast_temporal_w, 2, 3)), Weight(fast_skip_w, 0)],
        [act(512, BF16), act(DL), act(LANES), *edges(LANES, 8), act(512), pay(8), ((LAYERS, 6, LANES, LANES), BF16)],
        pinned=True,
    )
    recv, around = sum_with_halo(sent, top, bottom, z16)
    recv = sum_over(recv, CLIP)
    gb_all, fs_bd, fe_bd, *ahead = call(
        kernel_prepare,
        (),
        [Load(gains), Load(biases), Load(fast_spatial_w), Load(fast_expand_w)],
        [((LAYERS, 2, GB_ROWS, LANES), F32), ((LAYERS, 3, 3, LANES, LANES), BF16), ((LAYERS, LANES, ALPHA * DF), BF16)],
        pinned=True,
        ahead=[Weight(slow_temporal_w, 0), Weight(slow_skip_w, 0)],
    )
    gb = [Layer(gb_all, l) for l in range(LAYERS)]
    before = None
    for l in range(LAYERS):
        last = l == LAYERS - 1
        start = [recv, Load(slow2), gb[l]] if l == 0 else [recv, gb[l - 1], before["tot_sk"], before["zse"], before["zsk"], gb[l]]
        low, zst, z16, top, bottom, zsk, af9, zfs, sent = call(
            bind(kernel_temporal, l == 0, shape),
            scalars,
            start + [zlat, zft, *around, Ready(ahead[0]), Ready(ahead[1]), Layer(fs_bd, l)],
            [act(CC, BF16), act(BS), *edges(BS, 24), act(DS), act(9 * LANES, BF16), act(LANES), pay(24)],
            [pad_fast],
        )
        tot_lat = recv
        if l > 0:
            before["tot_se"] = tot_lat
        recv, around = sum_with_halo(sent, top, bottom, z16)
        recv = sum_over(recv, CLIP)
        a9, zss, bf, zfe, sent = call(
            bind(kernel_spatial, shape),
            scalars,
            [recv, gb[l], zst, *around, zfs, Weight(slow_spatial_w, l), Layer(fe_bd, l)],
            [act(9 * BS, BF16), act(BS), act(LANES, BF16), act(512), ((devices, 8, LANES), F32)],
            [pay(8), pad_slow],
        )
        tot_st = recv
        recv = exchange(sent)
        keep = dict(
            fb=fb, zlat=zlat, zft=zft, zfk=zfk, low=low, zst=zst, zsk=zsk, af9=af9, zfs=zfs, a9=a9, zss=zss, bf=bf,
            zfe=zfe, tot_lat=tot_lat, tot_fk=tot_lat, tot_st=tot_st, tot_sk=tot_st,
        )
        if last:
            bt, zse, sent, tot_ss = call(
                bind(kernel_expand, True, shape),
                scalars,
                [recv, gb[l], zss, Weight(slow_expand_w, l)],
                [act(BS, BF16), act(DS), ((devices, 16, LANES), F32), pay(8)],
                [pay(16)],
            )
        else:
            bt, zse, sent, tot_ss, fb, zlat, zft, z16, top, bottom, zfk, *ahead = call(
                bind(kernel_expand, False, shape),
                scalars,
                [recv, gb[l], zss, Weight(slow_expand_w, l), tot_lat, zfe, zfk,
                 Weight(lateral_w, l + 1), Layer(band, l + 1), Weight(fast_skip_w, l + 1)],
                [act(BS, BF16), act(DS), pay(24), pay(8),
                 act(512, BF16), act(DL), act(LANES), *edges(LANES, 24), act(512)],
                ahead=[Weight(slow_temporal_w, l + 1), Weight(slow_skip_w, l + 1)],
            )
        if last:
            recv = exchange(sent)
        else:
            recv, around = sum_with_halo(sent, top, bottom, z16)
            recv = sum_over(recv, CLIP)
        keep.update(bt=bt, zse=zse, tot_ss=tot_ss, tot_fe=tot_ss)
        saved.append(keep)
        before = keep

    for l in range(LAYERS):
        saved[l]["gb"] = gb[l]

    def stage(body, ins, outs, scratch=(), limit=16, ahead=()):
        names = list(ins) + list(outs) + [name for name, _ in scratch]

        def named(ints, vectors, *refs):
            body(shape, Refs(names, refs), inside_rows(rows, 256, ints[0]), ints, vectors)

        results = call(
            named, scalars, list(ins.values()), list(outs.values()), [kind for _, kind in scratch], limit,
            ahead=list(ahead),
        )
        return dict(zip(outs, results[: len(outs)]), ahead=results[len(outs) :])

    def layer(prefix, l, *names):
        return {prefix + name: saved[l][name] for name in names}

    def edge(columns, sums=None):
        return dict(zip(("whole", "top", "bottom"), edges(columns, sums)))

    def around_of(values):
        return {f"h{i}": x for i, x in enumerate(values)}

    narrow = clips == 4

    def halves_chain(keep, send, jobs):
        count = bundle_rows(jobs, tiles)[0]
        (got,) = yield [keep], [(send, WA, 1)]
        split = count // 32 * 16
        a, b = (split, 256), (count - split, 256)
        keep_a, send_a, keep_b, send_b = call(
            bind(kernel_halve_first, split), places, [keep, got], [((2,) + x, BF16) for x in (a, a, b, b)]
        )
        got_a, got_b = yield [keep_a, keep_b], [(send_a, HA, 1), (send_b, HA, 2)]
        keep_a, send_a, keep_b, send_b = call(
            kernel_halve_second, places, [keep_a, got_a, keep_b, got_b], [(x, BF16) for x in (a, a, b, b)]
        )
        got_a, got_b = yield [keep_a, keep_b], [(send_a, HA, 2), (send_b, HA, 1)]
        parts = [keep_a, got_a, keep_b, got_b]
        if narrow:
            block = (share_rows(jobs, tiles), LANES)
            keep, send = call(
                bind(kernel_join_columns, jobs, tiles), places, parts, [((2,) + block, BF16)] * 2, [((4,) + block, BF16)]
            )
            (got,) = yield [keep], [(send, CLIP, 1)]
            keep, send = call(kernel_halve_last, places, [keep, got], [(block, BF16)] * 2)
            (got,) = yield [keep], [(send, CLIP, 2)]
            parts = [keep, got]
        yield parts, None

    def direct_chain(keep, send, jobs):
        count = bundle_rows(jobs, tiles)[0]
        (got,) = yield [keep], [(send, WA, 1)]
        mine, *others = call(kernel_pick_places, places, [keep, got], [((count, 256), BF16)] * 4)
        got = yield [mine], [(x, HA, i + 1) for i, x in enumerate(others)]
        parts = [mine, *got]
        if narrow:
            block = (share_rows(jobs, tiles), LANES)
            mine, *others = call(
                bind(kernel_pick_columns, jobs, tiles), places, parts, [(block, BF16)] * 4, [((4,) + block, BF16)]
            )
            got = yield [mine], [(x, CLIP, i + 1) for i, x in enumerate(others)]
            parts = [mine, *got]
        yield parts, None

    class Running:
        def __init__(self, chain, jobs, layers):
            self.chain = chain
            self.jobs = jobs
            self.layers = layers
            self.got = None
            self.state = next(chain)

        def done(self):
            return self.state[1] is None

        def launch(self, x=None):
            if self.done() or self.got is not None:
                return
            sends = [send for send, _, _ in self.state[1]]
            if x is not None:
                _, *sends = after(x, *sends)
            self.got = [flip(send, axis, step) for send, (_, axis, step) in zip(sends, self.state[1])]

        def land(self, x):
            if self.got is None:
                return x
            x, *got = after(x, *self.got)
            self.got = None
            self.state = self.chain.send(got)
            return x

        def finish(self):
            while not self.done():
                self.launch()
                got, self.got = self.got, None
                self.state = self.chain.send(got)
                yield

    running = {}

    def bundle(name, chain, *parts):
        jobs, layers = tuple(p[0] for p in parts), tuple(p[1] for p in parts)
        operands = []
        for job, l, r in parts:
            k = saved[l]
            operands += {
                "pl": lambda: [k["low"], k["bt"], r["dz_sk"], r["dz_se"]],
                "st": lambda: [k["low"], r["dz_st"]],
                "ss": lambda: [k["a9"], r["dz"]],
                "lat": lambda: [k["fb"], r["dz_lat"]],
                "sm": lambda: [k["af9"], k["fb"], k["bf"], r["dz_f"], r["dz_ft"], r["dz_fe"], r["dz_fk"]],
            }[job]()
        count = bundle_rows(jobs, tiles)[0]
        pair = call(
            bind(kernel_weights_rows, tiles, frame, jobs),
            places,
            operands,
            [((tiles // 2, count, 256), BF16)] * 2,
            [((tiles, count, 256), BF16), ((tiles, SMALL_ROWS, 256), F32)],
            limit=24,
        )
        running[name] = Running(chain(*pair, jobs), jobs, layers)
        running[name].direct = chain is direct_chain

    def skip_back(l, r):
        (r["dlow"],) = call(kernel_back_skip, (), [r["dz_sk"], Weight(slow_skip_w, l)], [act(CC)])

    totals = []

    around = []

    def total_of(x, edge_rows=None):
        n = len(totals)
        for axis in ORDERS[n]:
            for name in LAND.get((n, axis), ()):
                x = running[name].land(x)
                if (n, axis, name) not in WAIT:
                    running[name].launch()
            if edge_rows is None:
                x = sum_over(x, axis)
            elif axis == HA:
                x, around[:] = sum_with_halo(x, edge_rows["top"], edge_rows["bottom"], edge_rows["whole"])
            elif axis == CLIP:
                x = sum_over(x, axis)
            for name in LAUNCH.get((n, axis), ()) + tuple(w[2] for w in WAIT if w[:2] == (n, axis) and w != (5, CLIP, "A0")):
                running[name].launch(x)
        totals.append(x)
        return x

    one, two = LAYERS - 1, LAYERS - 2
    r1, r0 = {}, {}

    def start_bundles():
        for name, direct, parts in BUNDLES.get(len(totals), ()):
            chain = direct_chain if direct else halves_chain
            bundle(name, chain, *[(job, l, (r0, r1)[l]) for job, l in parts])

    slow_names, fast_names = ("gb", "tot_se", "tot_sk", "zse", "zsk"), ("tot_ss", "tot_lat", "zfe", "zfk")
    r1.update(stage(
        back_turn,
        dict(recv=recv, **layer("a_", one, *slow_names[:1], *slow_names[2:], *fast_names), slow_cot=Load(slow_cot2), fast_cot=Load(fast_cot4)),
        dict(out_slow=Out((rows, DS), F32), out_fast=Out((t, ALPHA, frame, DF), F32), du_s=act(DS), du_f=act(512), pay=pay(32), tot=pay(16)),
    ))
    saved[-1]["tot_se"] = r1["tot"]
    recv = total_of(r1["pay"])
    r1.update(stage(
        back_expand,
        dict(recv=recv, **layer("a_", one, *slow_names, *fast_names, "zss", "zfs"), du_s=r1["du_s"], du_f=r1["du_f"],
             se_w=Weight(slow_expand_w, one), fe_bd=Layer(fe_bd, one)),
        dict(dz_se=act(DS, BF16), dz_sk=act(DS, BF16), dz_fe=act(512, BF16), dz_fk=act(512, BF16), dy=act(BS + LANES),
             **edge(2 * (BS + LANES)), pay=pay(8)),
    ))
    skip_back(one, r1)
    start_bundles()
    recv = total_of(r1["pay"])
    r1.update(stage(
        back_spatial,
        dict(recv=recv, **layer("a_", one, "gb", "tot_sk", "tot_ss", "tot_lat", "zss", "zfs", "zst", "zft"), dy=r1["dy"],
             **around_of(halo(r1["whole"], r1["top"], r1["bottom"])), ss_w=Weight(slow_spatial_w, one), fs_bd=Layer(fs_bd, one)),
        dict(dz=act(BS + LANES, BF16), dy_st=act(BS), dy_ft=act(LANES), pay=pay(8)),
        [("pad", pad_both)],
        ahead=[Weight(slow_temporal_w, one)],
    ))
    r1["dz_f"] = r1["dz"]
    start_bundles()
    recv = total_of(r1["pay"])
    r1.update(stage(
        back_temporal,
        dict(recv=recv, **layer("a_", one, "gb", "tot_sk", "tot_lat", "zst", "zft", "zlat"),
             **layer("b_", two, *slow_names), dy_st=r1["dy_st"], dy_ft=r1["dy_ft"], dlow=r1["dlow"], dz_fk=r1["dz_fk"],
             st_w=Ready(r1["ahead"][0]), ft_band=Layer(band, one), fk_w=Weight(fast_skip_w, one)),
        dict(dz_st=act(3 * BS, BF16), dz_ft=act(LANES, BF16), dfast=act(512), dy_lat=act(DL), du_s=act(DS), pay=pay(32)),
    ))
    start_bundles()
    recv = total_of(r1["pay"])
    r0.update(stage(
        back_lateral,
        dict(recv=recv, **layer("a_", one, "gb", "tot_lat", "zlat"),
             **layer("b_", two, *slow_names, *fast_names, "zss"), dy_lat=r1["dy_lat"], dfast=r1["dfast"], du_s=r1["du_s"],
             lat_w=Weight(lateral_w, one), se_w=Weight(slow_expand_w, two)),
        dict(dz_lat=act(DL, BF16), du_f=act(512), dz_se=act(DS, BF16), dz_sk=act(DS, BF16), dy=act(BS), **edge(2 * BS), pay=pay(8)),
    ))
    r1["dz_lat"] = r0["dz_lat"]
    start_bundles()
    skip_back(two, r0)
    recv = total_of(r0["pay"])
    fast = stage(
        back_low_spatial,
        dict(recv=recv, **layer("b_", two, "gb", "tot_sk", "tot_ss", "tot_lat", "zss", "zst", "zfe", "zfk", "zfs"),
             du_f=r0["du_f"], dy=r0["dy"], **around_of(halo(r0["whole"], r0["top"], r0["bottom"])), ss_w=Weight(slow_spatial_w, two), fe_bd=Layer(fe_bd, two)),
        dict(dz_fe=act(512, BF16), dz_fk=act(512, BF16), dy_fs=act(LANES), **edge(2 * LANES), dz=act(BS, BF16), dy_st=act(BS),
             pay=pay(8)),
        [("pad", pad_slow)],
        ahead=[Weight(slow_temporal_w, two)],
    )
    r0.update(fast)
    start_bundles()
    recv = total_of(r0["pay"])
    r0.update(stage(
        back_low_temporal,
        dict(recv=recv, **layer("b_", two, "gb", "tot_sk", "tot_lat", "zst", "zft", "zlat", "zfs"), dy_fs=r0["dy_fs"],
             **around_of(halo(r0["whole"], r0["top"], r0["bottom"])), dy_st=r0["dy_st"], dlow=r0["dlow"], st_w=Ready(r0["ahead"][0]), fs_bd=Layer(fs_bd, two)),
        dict(dz_f=act(LANES, BF16), dy_ft=act(LANES), dz_st=act(3 * BS, BF16), dy_lat=act(DL), pay=pay(8)),
        [("pad", pad_fast)],
    ))
    start_bundles()
    recv = total_of(r0["pay"])
    r0.update(stage(
        back_low_lateral,
        dict(recv=recv, **layer("b_", two, "gb", "tot_lat", "zft", "zlat"), dy_ft=r0["dy_ft"], dy_lat=r0["dy_lat"]),
        dict(dz_ft=act(LANES, BF16), dz_lat=act(DL, BF16)),
    ))
    start_bundles()
    ways = [chain.finish() for chain in running.values()]
    _, late_lat, late_st = after(running["L0"].state[1][0][0], r0["dz_lat"], r0["dz_st"])
    while ways:
        ways = [way for way in ways if next(way, 0) is None]
    out_slow, out_fast = r1["out_slow"], r1["out_fast"]
    (grad_slow,) = call(
        kernel_low_input, (), [late_st, r0["dlow"], Weight(slow_temporal_w, two)], [Out((rows, DS), F32)]
    )
    (grad_fast,) = call(
        bind(kernel_low_fast_input, frame),
        (),
        [late_lat, r0["dz_ft"], r0["dz_fk"], Weight(lateral_w, two), Weight(fast_skip_w, two), Layer(band, two)],
        [Out((t, ALPHA, frame, DF), F32)],
    )
    where = [
        [(6, 0, 2, 2), (5, 0, 2, 2), (4, 0, 2, 2), (3, 8, 8, 8), (3, 8, 16, 8), (6, 4, 1, 1), (5, 4, 1, 1), (4, 4, 1, 1),
         (4, 4, 2, 1)],
        [(3, 0, 2, 2), (2, 0, 2, 2), (1, 0, 2, 2), (0, 0, 8, 8), (0, 0, 16, 8), (2, 4, 1, 1), (1, 4, 1, 1), (0, 24, 1, 1),
         (0, 24, 2, 1)],
    ]
    nst, nss, nla, nsm = CC // tiles, BS // tiles, DF // tiles, BF // tiles
    n, f, g = BS // clips, BF // clips, DF // clips
    sums = call(bind(kernel_norm_sums, where), (), totals, [Out(gains.shape, F32), Out(biases.shape, F32)])
    weights = [(LAYERS,) + dims for dims in (
        (5, nla, n), (3, nst, n), (3, 3, nss, n), (nss, DS // clips), (nst, DS // clips),
        (3, nla, f), (3, 3, nsm, f), (nsm, g), (nla, g),
    )]
    chains = list(running.values())
    if narrow:
        plan = [(chain.jobs, chain.layers, len(chain.state[0])) for chain in chains]
        parts = [x for chain in chains for x in chain.state[0]]
        turned = (1, 5)
        weights = [dims[:-2] + dims[:-3:-1] if i in turned else dims for i, dims in enumerate(weights)]
        weights = call(bind(kernel_finish, tiles, plan), places, parts, [Out(dims, F32, 1) for dims in weights])
        weights = [jnp.swapaxes(x, -1, -2) if i in turned else x for i, x in enumerate(weights)]
    else:
        found = {}
        for chain in chains:
            got = [x.astype(F32) for x in chain.state[0]]
            if not chain.direct:
                total = jnp.concatenate([got[0] + got[1], got[2] + got[3]], axis=0).astype(BF16)
            else:
                total = sum(got).astype(BF16)
            count, planes, small_rows = bundle_rows(chain.jobs, tiles)
            if planes:
                plane = jnp.transpose(total[:planes].reshape(4, -1, 256), (1, 0, 2)).reshape(planes // 4, clips, DS // clips)
                plane = lax.psum_scatter(plane, CLIP, scatter_dimension=1)
                found["sk", chain.layers[0]], found["se", chain.layers[0]] = plane[:nst], plane[nst:]
            small = lax.psum(total[count - small_rows :], CLIP) if small_rows else None
            if count - small_rows > planes:
                total = lax.psum_scatter(
                    total[planes : count - small_rows].reshape(-1, clips, n), CLIP, scatter_dimension=1
                )
            base = 0
            for job, l in zip(chain.jobs, chain.layers):
                if job == "sm":
                    left = lax.dynamic_slice_in_dim(small[:, :LANES], place[2] * f, f, 1)
                    right = lax.dynamic_slice_in_dim(small[:, LANES:], place[2] * f, f, 1)
                    last = lax.dynamic_slice_in_dim(small[:, LANES:], place[2] * g, g, 1)
                    found["ft", l], found["fs", l] = left[: 3 * nla], right[: 9 * nsm]
                    found["fe", l], found["fk", l] = last[9 * nsm : 10 * nsm], last[10 * nsm : 10 * nsm + nla]
                elif job != "pl":
                    found[job, l] = total[base : base + job_rows(job, tiles)]
                    base += job_rows(job, tiles)
        names = ("lat", "st", "ss", "se", "sk", "ft", "fs", "fe", "fk")
        weights = [
            jnp.stack([found[name, l] for l in range(LAYERS)]).astype(F32).reshape(dims)
            for name, dims in zip(names, weights)
        ]
    return (
        out_slow.reshape(slow_in.shape),
        out_fast.reshape(fast_in.shape),
        grad_slow.reshape(slow_in.shape),
        grad_fast.reshape(fast_in.shape),
        *weights,
        *sums,
    )


def solution(mesh):
    pixels = P(CLIP, None, HA, WA, None)
    tile = (HA, WA)
    return jax.shard_map(
        local,
        mesh=mesh,
        in_specs=(pixels, pixels) + (P(),) * 12 + (pixels, pixels),
        out_specs=(
            (pixels,) * 4
            + (P(None, None, tile, CLIP),) * 2
            + (P(None, None, None, tile, CLIP),)
            + (P(None, tile, CLIP),) * 2
            + (P(None, None, tile, CLIP),)
            + (P(None, None, None, tile, CLIP),)
            + (P(None, tile, CLIP),) * 2
            + (P(),) * 2
        ),
        check_vma=False,
    )
```
